32 devices in a mesh: seq: 8 (over z, x), rows: 4 (over y, core).
Axes of the slice: x: 2, y: 2, z: 4, core: 2. Of those that a mesh axis runs over, the one named last changes fastest.
Arguments:
- frames: bfloat16 [64, 64, 4096], P('seq', 'rows'), may hold values from -12 to 12
- cotangent: bfloat16 [64, 64, 4096], P('seq', 'rows'), may hold values from -12 to 12
- actions: int32 [64], P('seq'), may hold values from 0 to 17
- noise_ids: int32 [64], P('seq'), may hold values from 0 to 31
- valid: int32 [64], P('seq'), may hold values 0 or 1
- act_table: bfloat16 [18, 256], P(None, 'seq'), may hold values from -5 to 5
- noise_table: bfloat16 [32, 256], P(None, 'seq'), may hold values from -5 to 5
- ada_one: bfloat16 [256, 128], P('seq'), may hold values from -0.1875 to 0.1875
- ada_two: bfloat16 [256, 128], P('seq'), may hold values from -0.1875 to 0.1875
- conv_one: bfloat16 [576, 64], P('seq'), may hold values from -0.25 to 0.25
- conv_two: bfloat16 [576, 64], P('seq'), may hold values from -0.25 to 0.25
- down_kernel: bfloat16 [576, 64], P('seq'), may hold values from -0.25 to 0.25
- up_kernel: bfloat16 [1152, 64], P('seq'), may hold values from -0.1875 to 0.1875
- bias_one: bfloat16 [64], P('seq'), may hold values from -3 to 3
- bias_two: bfloat16 [64], P('seq'), may hold values from -3 to 3
- bias_down: bfloat16 [64], P('seq'), may hold values from -3 to 3
- bias_up: bfloat16 [64], P('seq'), may hold values from -3 to 3
Outputs:
- output: bfloat16 [64, 64, 4096], P('seq', 'rows')
- frames_grad: float32 [64, 64, 4096], P('seq', 'rows')
- act_table_grad: float32 [18, 256], P(None, 'seq')
- noise_table_grad: float32 [32, 256], P(None, 'seq')
- ada_one_grad: float32 [256, 128], P('seq')
- ada_two_grad: float32 [256, 128], P('seq')
- conv_one_grad: float32 [576, 64], P('seq')
- conv_two_grad: float32 [576, 64], P('seq')
- down_grad: float32 [576, 64], P('seq')
- up_grad: float32 [1152, 64], P('seq')
- bias_one_grad: float32 [64], P('seq')
- bias_two_grad: float32 [64], P('seq')
- bias_down_grad: float32 [64], P('seq')
- bias_up_grad: float32 [64], P('seq')
The draws below stay inside these ranges and needn't reach their ends.
All inputs are finite; a program needn't handle non-finite values. No bound on the sum of `valid` on one device may be relied on, other than what follows from the above.
Results may differ from the reference program's by a relative error of at most 0.0066.
Values may be sent and summed in bfloat16 or wider, within the bound.
No kernel may reach another device: no remote copies, remote signals or barrier semaphores. Data moves between devices by JAX's collectives and lax.ppermute only.
A program may use at most 192 MiB of HBM per device.

```python
import math
import jax
import jax.numpy as jnp
import numpy as np
from jax import lax

C = 64
E = 256
NACT = 18
GROUPS = 32
NLEV = 32
H = 64
W = 64
FR_MB = 4
FRAMES = 64


def draw_frames(key, part):
    key = jax.random.fold_in(key, 11)
    noise_key = jax.random.fold_in(key, 0)
    growth = jnp.exp(jnp.log(3.0) * jnp.arange(H, dtype=jnp.float32) / (H - 1))
    sample = jax.random.normal(noise_key, (FRAMES, H, W * C), jnp.float32)
    values = sample * growth[None, :, None]
    return jnp.clip(values, -12.0, 12.0).astype(jnp.bfloat16)


def draw_cotangent(key, part):
    key = jax.random.fold_in(key, 23)
    noise_key = jax.random.fold_in(key, 0)
    growth = jnp.exp(jnp.log(3.0) * jnp.arange(H, dtype=jnp.float32) / (H - 1))
    sample = jax.random.normal(noise_key, (FRAMES, H, W * C), jnp.float32)
    values = sample * growth[None, :, None]
    return jnp.clip(values, -12.0, 12.0).astype(jnp.bfloat16)


def plant(entries, own_key, low, top_value):
    longest = entries.shape.index(max(entries.shape))
    spots = []
    for shift in (0, 1):
        where = [jax.random.randint(jax.random.fold_in(own_key, axis), (), 0, length) for axis, length in enumerate(entries.shape)]
        where[longest] = (where[longest] + shift) % entries.shape[longest]
        spots.append(tuple(where))
    return entries.at[spots[0]].set(low).at[spots[1]].set(top_value)


def block_scale(key, shape, cuts, smallest, high):
    def one(axis_at, blocks):
        steps = jax.random.uniform(jax.random.fold_in(jax.random.fold_in(key, 6), axis_at), (blocks,), jnp.float32, smallest / len(cuts), high / len(cuts))
        return jnp.repeat(jnp.exp(steps), shape[axis_at] // blocks).reshape((-1,) + (1,) * (len(shape) - axis_at - 1))

    level = one(*cuts[0])
    for cut in cuts[1:]:
        level = level * one(*cut)
    return level


def rank_bounds(count, slope):
    portions = [(1 << 20) // math.isqrt(rank ** slope) + 1 for rank in range(1, count + 1)]
    scale = 1 + sum(portions) // (1 << 30)
    return np.cumsum(np.array([max(1, weight // scale) for weight in portions]))


def skewed_ids(rng, shape, number_of, skew):
    grid = rank_bounds(number_of, skew)
    ticket = jax.random.randint(jax.random.fold_in(rng, 1), shape, 0, int(grid[number_of - 1]))
    grade = jnp.searchsorted(jnp.asarray(grid, jnp.int32), ticket, side="right")
    return jax.random.permutation(jax.random.fold_in(rng, 2), number_of)[grade].astype(jnp.int32)


def bell_draw(key, shape, spread, reach, cuts=(), kind=jnp.bfloat16):
    entries = jax.random.normal(key, shape, jnp.float32) * spread
    if len(cuts) > 0:
        entries = block_scale(key, shape, cuts, -0.22, 0.18) * entries
    return jnp.clip(entries, min=-reach, max=reach).astype(kind)


def setup_inputs(seed: int = 0) -> dict:
    arg_keys = jax.random.split(jax.random.key(seed), 18)
    frames = draw_frames(jax.random.fold_in(arg_keys[17], 71), 0)
    cotangent = draw_cotangent(jax.random.fold_in(arg_keys[17], 71), 0)
    actions = plant(skewed_ids(arg_keys[2], (FRAMES,), NACT, 2), jax.random.fold_in(arg_keys[2], 3), 0, NACT - 1).astype(jnp.int32)
    noise_ids = plant(jax.random.randint(arg_keys[3], (FRAMES,), 0, NLEV), jax.random.fold_in(arg_keys[3], 1), 0, NLEV - 1).astype(jnp.int32)
    valid = plant((jax.random.randint(arg_keys[4], (FRAMES,), 0, 4) < 3).astype(jnp.int32), jax.random.fold_in(arg_keys[4], 1), 0, 1)
    act_table = bell_draw(arg_keys[5], (NACT, E), 1.0, 5.0, ((1, 8),))
    noise_table = bell_draw(arg_keys[6], (NLEV, E), 1.0, 5.0, ((1, 8),))
    ada_one = bell_draw(arg_keys[7], (E, 2 * C), (4 * E) ** -0.5, 0.1875, ((0, 8),))
    ada_two = bell_draw(arg_keys[8], (E, 2 * C), (4 * E) ** -0.5, 0.1875, ((0, 8),))
    conv_one = bell_draw(arg_keys[9], (9 * C, C), (9 * C) ** -0.5, 0.25, ((0, 8),))
    conv_two = bell_draw(arg_keys[10], (9 * C, C), (9 * C) ** -0.5, 0.25, ((0, 8),))
    down_kernel = bell_draw(arg_keys[11], (9 * C, C), (9 * C) ** -0.5, 0.25, ((0, 8),))
    up_kernel = bell_draw(arg_keys[12], (18 * C, C), (18 * C) ** -0.5, 0.1875, ((0, 8),))
    bias_one = bell_draw(arg_keys[13], (C,), 0.5, 3.0, ((0, 8),))
    bias_two = bell_draw(arg_keys[14], (C,), 0.5, 3.0, ((0, 8),))
    bias_down = bell_draw(arg_keys[15], (C,), 0.5, 3.0, ((0, 8),))
    bias_up = bell_draw(arg_keys[16], (C,), 0.5, 3.0, ((0, 8),))
    return dict(frames=frames, cotangent=cotangent, actions=actions, noise_ids=noise_ids, valid=valid, act_table=act_table, noise_table=noise_table, ada_one=ada_one, ada_two=ada_two, conv_one=conv_one, conv_two=conv_two, down_kernel=down_kernel, up_kernel=up_kernel, bias_one=bias_one, bias_two=bias_two, bias_down=bias_down, bias_up=bias_up)


@jax.custom_vjp
def low(v):
    return lax.optimization_barrier(v.astype(jnp.bfloat16)).astype(jnp.float32)

@jax.custom_vjp
def low_back(v):
    return v

def low_keep(v):
    return (low(v), None)

def low_pass(kept, grad):
    return (grad,)

def back_keep(v):
    return (v, None)

def back_low(kept, grad):
    return (low(grad),)
low.defvjp(low_keep, low_pass)
low_back.defvjp(back_keep, back_low)

def convolve(values, kernel, stride):
    shaped = kernel.reshape(3, 3, values.shape[-1], kernel.shape[1])
    return lax.conv_general_dilated(values, shaped, (stride, stride), ((1, 1), (1, 1)), dimension_numbers=('NHWC', 'HWIO', 'NHWC'), precision=lax.Precision.HIGHEST)

def adaptive_norm(values, styles):
    frame_count = values.shape[0]
    group_view = values.reshape(frame_count, H, W, GROUPS, C // GROUPS)
    average = lax.optimization_barrier(jnp.mean(group_view, axis=(1, 2, 4), keepdims=True))
    variance = lax.optimization_barrier(jnp.mean(jnp.square(group_view - average), axis=(1, 2, 4), keepdims=True))
    normed = ((group_view - average) * lax.rsqrt(variance + 1e-05)).reshape(values.shape)
    return normed * (1.0 + styles[:, None, None, :C]) + styles[:, None, None, C:]

def layers(values, actions, noise_ids, valid, act_table, noise_table, ada_one, ada_two, conv_one, conv_two, down_kernel, up_kernel, bias_one, bias_two, bias_down, bias_up):
    embed = valid.astype(jnp.float32)[:, None] * act_table[actions] + noise_table[noise_ids]
    style_one = jnp.dot(embed, ada_one, precision=lax.Precision.HIGHEST)
    style_two = jnp.dot(embed, ada_two, precision=lax.Precision.HIGHEST)
    act_one = low(jax.nn.silu(adaptive_norm(values, style_one)))
    middle = low_back(convolve(act_one, conv_one, 1)) + bias_one
    act_two = low(jax.nn.silu(adaptive_norm(middle, style_two)))
    level = values + low_back(convolve(act_two, conv_two, 1)) + bias_two
    level_low = low(level)
    down = low_back(convolve(level_low, down_kernel, 2)) + bias_down
    coarse = low(jax.nn.silu(down))
    upsampled = jnp.repeat(jnp.repeat(coarse, 2, axis=1), 2, axis=2)
    joined = jnp.concatenate([upsampled, level_low], axis=-1)
    return level + low_back(convolve(joined, up_kernel, 1)) + bias_up

def reference(frames, cotangent, actions, noise_ids, valid, act_table, noise_table, ada_one, ada_two, conv_one, conv_two, down_kernel, up_kernel, bias_one, bias_two, bias_down, bias_up):
    params = tuple((item.astype(jnp.float32) for item in (act_table, noise_table, ada_one, ada_two, conv_one, conv_two, down_kernel, up_kernel, bias_one, bias_two, bias_down, bias_up)))
    blocks = FRAMES // FR_MB
    frame_view = frames.reshape(blocks, FR_MB, H, W, C)
    cot_view = cotangent.reshape(blocks, FR_MB, H, W, C)

    def block_step(summed, inputs):
        block_frames, block_cot, block_actions, block_noise, block_valid = inputs

        def forward(values, *weights):
            return layers(values, block_actions, block_noise, block_valid, *weights)
        result, pullback = jax.vjp(forward, block_frames.astype(jnp.float32), *params)
        gradients = pullback(block_cot.astype(jnp.float32))
        summed = tuple((left_term + right_term for left_term, right_term in zip(summed, gradients[1:])))
        return (summed, (result.astype(jnp.bfloat16), gradients[0]))
    initial = tuple((jnp.zeros_like(item) for item in params))
    summed, outputs = lax.scan(block_step, initial, (frame_view, cot_view, actions.reshape(blocks, FR_MB), noise_ids.reshape(blocks, FR_MB), valid.reshape(blocks, FR_MB)))
    results, input_grads = outputs
    return (results.reshape(FRAMES, H, W * C), input_grads.reshape(FRAMES, H, W * C), summed[0], summed[1], summed[2], summed[3], summed[4], summed[5], summed[6], summed[7], summed[8], summed[9], summed[10], summed[11])
```

```python
import jax
import jax.numpy as jnp
from jax import lax
from jax.experimental import pallas as pl
from jax.experimental.pallas import tpu as pltpu
from jax.sharding import PartitionSpec as P

C = 64
NACT = 18
GROUPS = 32
NLEV = 32
H = 64
W = 64
PAIRS = W // 2
HALF = H // 2
LANES = 2 * C
BLOCK = PAIRS * HALF
MEMBERS = float(H * W * (C // GROUPS))
EPS = 1e-05

precise = lax.Precision.HIGHEST
f32 = jnp.float32
bf16 = jnp.bfloat16
VMEM_LIMIT = 60 * 2**20


def lane_ids(shape):
    return lax.broadcasted_iota(jnp.int32, shape, len(shape) - 1)


def swap_halves(x):
    return pltpu.roll(x, C, axis=x.ndim - 1)


def row_before(x):
    rows = lax.broadcasted_iota(jnp.int32, x.shape, 0)
    return jnp.where(rows == 0, 0.0, pltpu.roll(x, 1, axis=0))


def row_after(x):
    rows = lax.broadcasted_iota(jnp.int32, x.shape, 0)
    return jnp.where(rows == x.shape[0] - 1, 0.0, pltpu.roll(x, x.shape[0] - 1, axis=0))


def both_parities(x):
    x = jnp.broadcast_to(x, (8, LANES))
    return x + swap_halves(x)


def group_sum(x):
    even = lane_ids(x.shape) % 2 == 0
    return x + jnp.where(even, pltpu.roll(x, LANES - 1, axis=1), pltpu.roll(x, 1, axis=1))


def total(x):
    return jnp.sum(x, axis=0, keepdims=True)


def build_windows(windows, tile):
    low_lanes = lane_ids((HALF, LANES)) < C
    zero = jnp.zeros((HALF, LANES), f32)

    def write(j, even, odd):
        windows[0, j] = row_before(odd).astype(bf16)
        windows[1, j] = even.astype(bf16)
        windows[2, j] = odd.astype(bf16)
        windows[3, j] = row_after(even).astype(bf16)

    def body(j, carry):
        even_past, odd_past = carry
        even = swap_halves(tile(0, j))
        odd = swap_halves(tile(1, j))
        write(j, jnp.where(low_lanes, even_past, even), jnp.where(low_lanes, odd_past, odd))
        return even, odd

    even, odd = lax.fori_loop(0, PAIRS, body, (zero, zero), unroll=4)
    write(PAIRS, jnp.where(low_lanes, even, 0.0), jnp.where(low_lanes, odd, 0.0))


def window_operand(windows, slots):
    parts = []
    for slot in slots:
        for shift in (0, 1):
            parts.append(windows[slot, shift : shift + PAIRS].reshape(BLOCK, LANES))
    return jnp.concatenate(parts, axis=1)


def matmul(left, right):
    return jnp.dot(left, right, preferred_element_type=f32)


def tiles_of(y):
    return y.reshape(PAIRS, HALF, LANES)


def norm_stats(sums, squares):
    average = group_sum(both_parities(sums)) / MEMBERS
    variance = group_sum(both_parities(squares)) / MEMBERS - average * average
    return average, lax.rsqrt(variance + EPS)


def strip_start(member, offset, strip):
    return pl.multiple_of((member ^ offset) * strip, strip)


def load_strips(member, strips, image):
    for offset, strip in enumerate(strips):
        rows = strip.shape[1]
        start = strip_start(member, offset, rows)
        for j in range(PAIRS):
            image[j, pl.ds(start, rows), :] = strip[0, :, j * LANES : (j + 1) * LANES].astype(f32)


def store_strips(member, image, strips):
    for offset in range(strips.shape[0]):
        rows = strips.shape[2]
        start = strip_start(member, offset, rows)
        for j in range(PAIRS):
            strips[offset, 0, :, j * LANES : (j + 1) * LANES] = image[j, pl.ds(start, rows), :].astype(strips.dtype)


def parity_rows(image, parity, j):
    return image[j, pl.ds(parity, HALF, stride=2), :]


def forward_kernel(count, *refs):
    member_ref = refs[0]
    strips = refs[1 : 1 + count]
    styles, biases, w_one, w_two, w_down, w_up = refs[1 + count : 7 + count]
    out, win_one, win_two, win_level, win_coarse, middle, down, stats = refs[7 + count : 15 + count]
    image, level = refs[15 + count :]
    member = member_ref[0]
    win_one, win_two, win_level, win_coarse = (ref.at[0] for ref in (win_one, win_two, win_level, win_coarse))
    middle, down = middle.at[0], down.at[0]

    load_strips(member, strips, image)

    def add_stats(j, carry):
        x = image[j]
        s, q = carry
        return s + x, q + x * x

    zero = jnp.zeros((H, LANES), f32)
    s, q = lax.fori_loop(0, PAIRS, add_stats, (zero, zero), unroll=4)
    average_one, inverse_one = norm_stats(total(s), total(q))
    gain_one = inverse_one * styles[0, 0:1, :]
    half_gain = 0.5 * gain_one[0:1]
    half_shift = 0.5 * (styles[0, 1:2, :] - average_one[0:1] * gain_one[0:1])

    def act_one(parity, j):
        h = parity_rows(image, parity, j) * half_gain + half_shift
        return h * jnp.tanh(h) + h

    build_windows(win_one, act_one)
    y = matmul(window_operand(win_one, range(4)), w_one[...])
    sums = jnp.zeros((1, LANES), f32)
    squares = jnp.zeros((1, LANES), f32)
    for a in range(2):
        v = y[:, a * LANES : (a + 1) * LANES] + biases[0:1, :]
        sums = sums + total(v)
        squares = squares + total(v * v)
        middle[a] = tiles_of(v)
    average_two, inverse_two = norm_stats(sums, squares)
    stats[0, 0:1, :] = average_one[0:1]
    stats[0, 1:2, :] = inverse_one[0:1]
    stats[0, 2:3, :] = average_two[0:1]
    stats[0, 3:4, :] = inverse_two[0:1]
    stats[0, 4:8, :] = jnp.zeros((4, LANES), f32)
    gain_two = inverse_two * styles[0, 2:3, :]
    half_gain_two = 0.5 * gain_two[0:1]
    half_shift_two = 0.5 * (styles[0, 3:4, :] - average_two[0:1] * gain_two[0:1])

    def act_two(parity, j):
        h = middle[parity, j] * half_gain_two + half_shift_two
        return h * jnp.tanh(h) + h

    build_windows(win_two, act_two)
    y = matmul(window_operand(win_two, range(4)), w_two[...])
    for a in range(2):
        v = y[:, a * LANES : (a + 1) * LANES] + biases[1:2, :]
        level[a] = tiles_of(v) + image[:, pl.ds(a, HALF, stride=2), :]

    build_windows(win_level, lambda parity, j: level[parity, j])
    operand = window_operand(win_level, range(4))
    y = matmul(operand[:, : 6 * LANES], w_down[...]) + biases[2:3, :]
    down[...] = tiles_of(y)

    low_lanes = lane_ids((HALF, LANES)) < C

    def write_coarse(j, cells):
        win_coarse[0, j] = row_before(cells).astype(bf16)
        win_coarse[1, j] = cells.astype(bf16)
        win_coarse[2, j] = row_after(cells).astype(bf16)

    def coarse_body(j, past):
        h = down[j] * 0.5
        coarse = h * jnp.tanh(h) + h
        write_coarse(j, jnp.where(low_lanes, past, coarse))
        return coarse

    past = lax.fori_loop(0, PAIRS, coarse_body, jnp.zeros((HALF, LANES), f32), unroll=4)
    write_coarse(PAIRS, jnp.where(low_lanes, past, 0.0))

    operand = window_operand(win_level, range(4))
    coarse_operand = window_operand(win_coarse, (0, 1, 1, 2))
    y = matmul(operand, w_up[: 16 * C, :]) + matmul(coarse_operand, w_up[16 * C :, :])
    for a in range(2):
        v = y[:, a * LANES : (a + 1) * LANES] + biases[3:4, :]
        image[:, pl.ds(a, HALF, stride=2), :] = tiles_of(v) + level[a]
    store_strips(member, image, out)


def slope_twice(h):
    t = jnp.tanh(h)
    return (1.0 + t) + h * (1.0 - t * t)


def backward_kernel(count, *refs):
    member_ref = refs[0]
    cot_strips = refs[1 : 1 + count]
    frame_strips = refs[1 + count : 1 + 2 * count]
    styles, stats, middle, down, w_up, w_down, w_two, w_one = refs[1 + 2 * count : 9 + 2 * count]
    out, tile_out, tile_level, tile_mid, coarse_pairs, pieces, bias_sums = refs[9 + 2 * count : 16 + 2 * count]
    image, level_grad, pre_grad, windows, coarse_below, row_sums = refs[16 + 2 * count :]
    member = member_ref[0]
    tile_out, tile_level, tile_mid, coarse_pairs = (ref.at[0] for ref in (tile_out, tile_level, tile_mid, coarse_pairs))
    middle, down = middle.at[0], down.at[0]
    low_lanes = lane_ids((HALF, LANES)) < C

    load_strips(member, cot_strips, image)

    def add_rows(j, s):
        return s + image[j]

    sums = lax.fori_loop(0, PAIRS, add_rows, jnp.zeros((H, LANES), f32), unroll=4)
    bias_up_sum = both_parities(total(sums))

    def out_tile(parity, j):
        x = parity_rows(image, parity, j)
        tile_out[parity, j] = x.astype(bf16)
        return x

    build_windows(windows, out_tile)
    y = matmul(window_operand(windows, range(4)), w_up[...])
    for a in range(2):
        level_grad[a] = tiles_of(y[:, (2 + a) * LANES : (3 + a) * LANES]) + image[:, pl.ds(a, HALF, stride=2), :]
    coarse = y[:, :LANES] + y[:, LANES : 2 * LANES]
    pre_grad[0] = tiles_of(coarse)

    def coarse_body(t, carry):
        after, sums = carry
        j = PAIRS - 1 - t
        g = pre_grad[0, j]
        g = g + swap_halves(g)
        h = down[j] * 0.5
        d = 0.5 * g * slope_twice(h)
        pair = jnp.where(low_lanes, d, after)
        coarse_pairs[j] = pair.astype(bf16)
        coarse_below[j] = row_after(pair).astype(bf16)
        return d, sums + d

    zero = jnp.zeros((HALF, LANES), f32)
    _, sums = lax.fori_loop(0, PAIRS, coarse_body, (zero, zero), unroll=4)
    bias_down_sum = jnp.broadcast_to(total(sums), (8, LANES))

    operand = jnp.concatenate(
        [coarse_pairs[...].reshape(BLOCK, LANES), coarse_below[...].reshape(BLOCK, LANES)], axis=1
    )
    y = matmul(operand, w_down[...])
    sums = jnp.zeros((1, LANES), f32)
    for a in range(2):
        v = y[:, a * LANES : (a + 1) * LANES] + level_grad[a].reshape(BLOCK, LANES)
        sums = sums + total(v)
        level_grad[a] = tiles_of(v)
    bias_two_sum = both_parities(sums)

    def level_tile(parity, j):
        x = level_grad[parity, j]
        tile_level[parity, j] = x.astype(bf16)
        return x

    build_windows(windows, level_tile)

    def norm_slopes(y, value, k):
        average, inverse = stats[0, 2 * k : 2 * k + 1, :], stats[0, 2 * k + 1 : 2 * k + 2, :]
        gain = inverse * styles[0, 2 * k : 2 * k + 1, :]
        half_gain = 0.5 * gain
        half_shift = 0.5 * (styles[0, 2 * k + 1 : 2 * k + 2, :] - average * gain)
        scale_sum = jnp.zeros((1, LANES), f32)
        shift_sum = jnp.zeros((1, LANES), f32)
        for a in range(2):
            v = value(a)
            g = 0.5 * y[:, a * LANES : (a + 1) * LANES] * slope_twice(v * half_gain + half_shift)
            pre_grad[a] = tiles_of(g)
            shift_sum = shift_sum + total(g)
            scale_sum = scale_sum + total(g * ((v - average) * inverse))
        scale_sum, shift_sum = both_parities(scale_sum), both_parities(shift_sum)
        factor = styles[0, 2 * k : 2 * k + 1, :]
        center = group_sum(factor * shift_sum) / MEMBERS
        tilt = group_sum(factor * scale_sum) / MEMBERS
        return scale_sum, shift_sum, gain, (inverse * center)[0:1], (inverse * tilt)[0:1], average, inverse

    y = matmul(window_operand(windows, range(4)), w_two[...])
    scale_two, shift_two, gain, center, tilt, average, inverse = norm_slopes(
        y, lambda a: middle[a].reshape(BLOCK, LANES), 1
    )
    tilt_slope = tilt * inverse
    constant = tilt_slope * average - center

    def mid_tile(parity, j):
        x = pre_grad[parity, j] * gain + (constant - middle[parity, j] * tilt_slope)
        tile_mid[parity, j] = x.astype(bf16)
        row_sums[...] += x
        return x

    row_sums[...] = jnp.zeros_like(row_sums)
    build_windows(windows, mid_tile)
    bias_one_sum = both_parities(total(row_sums[...]))

    load_strips(member, frame_strips, image)
    y = matmul(window_operand(windows, range(4)), w_one[...])
    scale_one, shift_one, gain_one, center_one, tilt_one, average_one, inverse_one = norm_slopes(
        y, lambda a: image[:, pl.ds(a, HALF, stride=2), :].reshape(BLOCK, LANES), 0
    )
    slope_one = tilt_one * inverse_one
    constant_one = slope_one * average_one - center_one

    def frame_body(j, carry):
        for parity in range(2):
            x = parity_rows(image, parity, j)
            g = pre_grad[parity, j] * gain_one + (constant_one - x * slope_one) + level_grad[parity, j]
            image[j, pl.ds(parity, HALF, stride=2), :] = g
        return carry

    lax.fori_loop(0, PAIRS, frame_body, 0, unroll=4)
    store_strips(member, image, out)
    for k, value in enumerate((scale_one, shift_one, scale_two, shift_two)):
        pieces[0, k : k + 1, :] = value[0:1]
    pieces[0, 4:8, :] = jnp.zeros((4, LANES), f32)
    for k, value in enumerate((bias_one_sum, bias_two_sum, bias_down_sum, bias_up_sum)):
        bias_sums[0, k : k + 1, :] = value[0:1]
    bias_sums[0, 4:8, :] = jnp.zeros((4, LANES), f32)


def outer(left, right):
    return lax.dot_general(left, right, (((0,), (0,)), ((), ())), preferred_element_type=f32)


def weight_kernel(
    win_one, win_two, win_level, win_coarse, tile_out, tile_level, tile_mid, coarse_pairs,
    g_one, g_two, g_down, g_up,
    sum_one, sum_two, sum_down, sum_up,
):
    step = pl.program_id(0)

    @pl.when(step == 0)
    def _():
        for ref in (sum_one, sum_two, sum_down, sum_up):
            ref[...] = jnp.zeros_like(ref)

    def blocks(tiles):
        return jnp.concatenate([tiles[0, a].reshape(BLOCK, LANES) for a in range(2)], axis=1)

    level_operand = window_operand(win_level.at[0], range(4))
    out_blocks = blocks(tile_out)
    sum_up[16 * C :, :] += outer(window_operand(win_coarse.at[0], (0, 1, 1, 2)), out_blocks)
    sum_up[: 16 * C, :] += outer(level_operand, out_blocks)
    sum_down[...] += outer(level_operand[:, : 6 * LANES], coarse_pairs[0].reshape(BLOCK, LANES))
    sum_two[...] += outer(window_operand(win_two.at[0], range(4)), blocks(tile_level))
    sum_one[...] += outer(window_operand(win_one.at[0], range(4)), blocks(tile_mid))

    @pl.when(step == pl.num_programs(0) - 1)
    def _():
        def fold(sums, base, p, q):
            halves = []
            for b in range(2):
                rows = [base + ((a + p) * 4 + b + q) * C for a in range(2)]
                halves.append(sums[rows[0] : rows[0] + C, :LANES] + sums[rows[1] : rows[1] + C, LANES:])
            return halves[0] + swap_halves(halves[1])

        for p in range(3):
            for q in range(3):
                at = (3 * p + q) * C
                g_one[at : at + C, :] = fold(sum_one, 0, p, q)[:, :C]
                g_two[at : at + C, :] = fold(sum_two, 0, p, q)[:, :C]
                g_up[2 * at : 2 * at + C, :] = fold(sum_up, 16 * C, p, q)[:, :C]
                g_up[2 * at + C : 2 * at + 2 * C, :] = fold(sum_up, 0, p, q)[:, :C]
                place = (p * 4 + q) * C
                g_down[at : at + C, :] = sum_down[place : place + C, :C]


def expand_kernel(conv_one, conv_two, down_kernel, up_kernel, f_one, f_two, f_down, f_up, b_one, b_two, b_down, b_up):
    low_lanes = lane_ids((C, LANES)) < C
    zero = jnp.zeros((C, LANES), f32)

    def taps(ref, base, step):
        plain, turned = {}, {}
        for p in range(3):
            for q in range(3):
                at = (3 * p + q) * step + base
                k = ref[at : at + C, :].astype(f32)
                plain[p, q] = jnp.concatenate([k, k], axis=1)
                turned[p, q] = jnp.concatenate([k, k], axis=0).T
        return plain, turned

    def write_forward(ref, base, plain):
        for w in range(4):
            for p in range(3):
                tile = jnp.where(low_lanes, plain.get((p, w), zero), plain.get((p, w - 1), zero)).astype(bf16)
                for a in range(2):
                    at = base + ((a + p) * 4 + w) * C
                    ref[at : at + C, a * LANES : (a + 1) * LANES] = tile
            for a in range(2):
                for r in range(4):
                    if not 0 <= r - a < 3:
                        at = base + (r * 4 + w) * C
                        ref[at : at + C, a * LANES : (a + 1) * LANES] = zero.astype(bf16)

    def write_backward(ref, lane, turned):
        for w in range(4):
            for p in range(3):
                tile = jnp.where(low_lanes, turned.get((p, 2 - w), zero), turned.get((p, 3 - w), zero)).astype(bf16)
                for a in range(2):
                    at = ((a + 2 - p) * 4 + w) * C
                    ref[at : at + C, lane + a * LANES : lane + (a + 1) * LANES] = tile
            for a in range(2):
                for r in range(4):
                    if not 0 <= a + 2 - r < 3:
                        at = (r * 4 + w) * C
                        ref[at : at + C, lane + a * LANES : lane + (a + 1) * LANES] = zero.astype(bf16)

    for ref, forward, backward in ((conv_one, f_one, b_one), (conv_two, f_two, b_two)):
        plain, turned = taps(ref, 0, C)
        write_forward(forward, 0, plain)
        write_backward(backward, 0, turned)
    plain, turned = taps(up_kernel, 0, 2 * C)
    write_forward(f_up, 16 * C, plain)
    write_backward(b_up, 0, turned)
    plain, turned = taps(up_kernel, C, 2 * C)
    write_forward(f_up, 0, plain)
    write_backward(b_up, 2 * LANES, turned)
    plain, turned = taps(down_kernel, 0, C)
    for p in range(3):
        for w in range(4):
            at = (p * 4 + w) * C
            f_down[at : at + C, :] = plain.get((p, w), zero).astype(bf16)
    for below in range(2):
        for right in range(2):
            at = (below * 2 + right) * C
            for a in range(2):
                p = {(0, 0): 1, (0, 1): 2, (1, 1): 0}.get((below, a))
                first, second = zero, zero
                if p is not None:
                    first = turned[p, 1] if right == 0 else zero
                    second = turned[p, 2] if right == 0 else turned[p, 0]
                b_down[at : at + C, a * LANES : (a + 1) * LANES] = jnp.where(low_lanes, first, second).astype(bf16)


def shape(dims, kind):
    return jax.ShapeDtypeStruct(dims, kind)


def whole(dims):
    return pl.BlockSpec(dims, lambda f: (0,) * len(dims))


def per_frame(dims):
    return pl.BlockSpec((1,) + dims, lambda f: (f,) + (0,) * len(dims))


def strip_specs(count, strip):
    return [pl.BlockSpec((1, strip, W * C), lambda f: (f, 0, 0))] * count


def out_strips(count, strip):
    return pl.BlockSpec((count, 1, strip, W * C), lambda f: (0, f, 0, 0))


SMALL = (8, LANES)
WINDOWS = (4, PAIRS + 1, HALF, LANES)
COARSE_WINDOWS = (3, PAIRS + 1, HALF, LANES)
TILES = (2, PAIRS, HALF, LANES)
COARSE = (PAIRS, HALF, LANES)
IMAGE = (PAIRS, H, LANES)
KEYS = 16 * C


def params():
    return pltpu.CompilerParams(vmem_limit_bytes=VMEM_LIMIT)


def expand(conv_one, conv_two, down_kernel, up_kernel):
    vmem = pl.BlockSpec(memory_space=pltpu.VMEM)
    return pl.pallas_call(
        expand_kernel,
        in_specs=[vmem] * 4,
        out_specs=[vmem] * 8,
        out_shape=[
            shape((KEYS, 2 * LANES), bf16),
            shape((KEYS, 2 * LANES), bf16),
            shape((6 * LANES, LANES), bf16),
            shape((2 * KEYS, 2 * LANES), bf16),
            shape((KEYS, 2 * LANES), bf16),
            shape((KEYS, 2 * LANES), bf16),
            shape((2 * LANES, 2 * LANES), bf16),
            shape((KEYS, 4 * LANES), bf16),
        ],
        compiler_params=params(),
        name="expand",
    )(conv_one, conv_two, down_kernel, up_kernel)


def forward(member, strips, styles, biases, w_one, w_two, w_down, w_up):
    count = len(strips)
    frames, strip, _ = strips[0].shape
    return pl.pallas_call(
        lambda *refs: forward_kernel(count, *refs),
        grid=(frames,),
        in_specs=[pl.BlockSpec(memory_space=pltpu.SMEM)]
        + strip_specs(count, strip)
        + [per_frame(SMALL), whole(SMALL)]
        + [whole(w.shape) for w in (w_one, w_two, w_down, w_up)],
        out_specs=[out_strips(count, strip)]
        + [per_frame(d) for d in (WINDOWS, WINDOWS, WINDOWS, COARSE_WINDOWS, TILES, COARSE, SMALL)],
        out_shape=[
            shape((count, frames, strip, W * C), bf16),
            shape((frames,) + WINDOWS, bf16),
            shape((frames,) + WINDOWS, bf16),
            shape((frames,) + WINDOWS, bf16),
            shape((frames,) + COARSE_WINDOWS, bf16),
            shape((frames,) + TILES, f32),
            shape((frames,) + COARSE, f32),
            shape((frames,) + SMALL, f32),
        ],
        scratch_shapes=[pltpu.VMEM(IMAGE, f32), pltpu.VMEM(TILES, f32)],
        compiler_params=params(),
        name="forward",
    )(member, *strips, styles, biases, w_one, w_two, w_down, w_up)


def backward(member, cot_strips, frame_strips, styles, stats, middle, down, w_up, w_down, w_two, w_one):
    count = len(cot_strips)
    frames, strip, _ = cot_strips[0].shape
    return pl.pallas_call(
        lambda *refs: backward_kernel(count, *refs),
        grid=(frames,),
        in_specs=[pl.BlockSpec(memory_space=pltpu.SMEM)]
        + strip_specs(2 * count, strip)
        + [per_frame(d) for d in (SMALL, SMALL, TILES, COARSE)]
        + [whole(w.shape) for w in (w_up, w_down, w_two, w_one)],
        out_specs=[out_strips(count, strip)]
        + [per_frame(d) for d in (TILES, TILES, TILES, COARSE, SMALL, SMALL)],
        out_shape=[
            shape((count, frames, strip, W * C), bf16),
            shape((frames,) + TILES, bf16),
            shape((frames,) + TILES, bf16),
            shape((frames,) + TILES, bf16),
            shape((frames,) + COARSE, bf16),
            shape((frames,) + SMALL, f32),
            shape((frames,) + SMALL, f32),
        ],
        scratch_shapes=[
            pltpu.VMEM(IMAGE, f32),
            pltpu.VMEM(TILES, f32),
            pltpu.VMEM(TILES, f32),
            pltpu.VMEM(WINDOWS, bf16),
            pltpu.VMEM(COARSE, bf16),
            pltpu.VMEM((HALF, LANES), f32),
        ],
        compiler_params=params(),
        name="backward",
    )(member, *cot_strips, *frame_strips, styles, stats, middle, down, w_up, w_down, w_two, w_one)


def weight_grads(win_one, win_two, win_level, win_coarse, tile_out, tile_level, tile_mid, coarse_pairs):
    frames = win_one.shape[0]
    return pl.pallas_call(
        weight_kernel,
        grid=(frames,),
        in_specs=[
            per_frame(d) for d in (WINDOWS, WINDOWS, WINDOWS, COARSE_WINDOWS, TILES, TILES, TILES, COARSE)
        ],
        out_specs=[whole((9 * C, C)), whole((9 * C, C)), whole((9 * C, C)), whole((18 * C, C))],
        out_shape=[shape((9 * C, C), f32)] * 3 + [shape((18 * C, C), f32)],
        scratch_shapes=[
            pltpu.VMEM((KEYS, 2 * LANES), f32),
            pltpu.VMEM((KEYS, 2 * LANES), f32),
            pltpu.VMEM((6 * LANES, LANES), f32),
            pltpu.VMEM((2 * KEYS, 2 * LANES), f32),
        ],
        compiler_params=params(),
        name="weights",
    )(win_one, win_two, win_level, win_coarse, tile_out, tile_level, tile_mid, coarse_pairs)


def twice(values):
    return jnp.concatenate([values, values], axis=-1)


def pad_small(rows):
    stacked = jnp.stack(rows, axis=-2)
    gaps = [(0, 0)] * (stacked.ndim - 2) + [(0, 8 - len(rows)), (0, 0)]
    return jnp.pad(stacked, gaps)


def trade(value, offset):
    if offset == 0:
        return value
    count = lax.axis_size("rows")
    return lax.ppermute(value, "rows", [(i, i ^ offset) for i in range(count)])


def spread_strips(array, member):
    count = lax.axis_size("rows")
    share = array.shape[0] // count
    return [
        trade(lax.dynamic_slice_in_dim(array, (member ^ offset) * share, share, axis=0), offset)
        for offset in range(count)
    ]


def collect_strips(strips, member, kind):
    count, share = strips.shape[:2]
    result = jnp.zeros((count * share,) + strips.shape[2:], kind)
    for offset in range(count):
        part = trade(strips[offset], offset).astype(kind)
        result = lax.dynamic_update_slice_in_dim(result, part, (member ^ offset) * share, axis=0)
    return result


def local(
    frames,
    cotangent,
    actions,
    noise_ids,
    valid,
    act_table,
    noise_table,
    ada_one,
    ada_two,
    conv_one,
    conv_two,
    down_kernel,
    up_kernel,
    bias_one,
    bias_two,
    bias_down,
    bias_up,
):
    member = lax.axis_index("rows")
    count = lax.axis_size("rows")
    share = frames.shape[0] // count
    member_box = member.astype(jnp.int32).reshape(1)

    def gathered(value, axis):
        return lax.all_gather(value, "seq", axis=axis, tiled=True)

    frame_strips = spread_strips(frames, member)
    cot_strips = spread_strips(cotangent, member)
    act_full = gathered(act_table, 1)
    noise_full = gathered(noise_table, 1)
    ada_full = gathered(jnp.concatenate([ada_one, ada_two], axis=1), 0).astype(f32)
    biases = gathered(jnp.stack([bias_one, bias_two, bias_down, bias_up]), 1).astype(f32)
    expanded = expand(gathered(conv_one, 0), gathered(conv_two, 0), gathered(down_kernel, 0), gathered(up_kernel, 0))
    f_one, f_two, f_down, f_up, b_one, b_two, b_down, b_up = expanded

    own = lambda ids: lax.dynamic_slice_in_dim(ids, member * share, share)
    own_actions, own_noise, own_valid = own(actions), own(noise_ids), own(valid)
    action_hot = (own_actions[:, None] == jnp.arange(NACT, dtype=jnp.int32)[None, :]).astype(f32) * own_valid[
        :, None
    ].astype(f32)
    noise_hot = (own_noise[:, None] == jnp.arange(NLEV, dtype=jnp.int32)[None, :]).astype(f32)
    embed = jnp.dot(action_hot, act_full.astype(f32), precision=precise) + jnp.dot(
        noise_hot, noise_full.astype(f32), precision=precise
    )
    style = jnp.dot(embed, ada_full, precision=precise)
    styles = pad_small(
        [
            twice(1.0 + style[:, :C]),
            twice(style[:, C : 2 * C]),
            twice(1.0 + style[:, 2 * C : 3 * C]),
            twice(style[:, 3 * C :]),
        ]
    )
    bias_rows = pad_small([twice(biases[k]) for k in range(4)])

    out, win_one, win_two, win_level, win_coarse, middle, down, stats = forward(
        member_box, frame_strips, styles, bias_rows, f_one, f_two, f_down, f_up
    )
    result = collect_strips(out, member, bf16)
    grad_strips, tile_out, tile_level, tile_mid, coarse_pairs, pieces, bias_sums = backward(
        member_box, cot_strips, frame_strips, styles, stats, middle, down, b_up, b_down, b_two, b_one
    )
    frames_grad = collect_strips(grad_strips, member, f32)
    g_one, g_two, g_down, g_up = weight_grads(
        win_one, win_two, win_level, win_coarse, tile_out, tile_level, tile_mid, coarse_pairs
    )

    pieces_one = jnp.concatenate([pieces[:, 0, :C], pieces[:, 1, :C]], axis=1)
    pieces_two = jnp.concatenate([pieces[:, 2, :C], pieces[:, 3, :C]], axis=1)
    ada_one_grad = jnp.dot(embed.T, pieces_one, precision=precise)
    ada_two_grad = jnp.dot(embed.T, pieces_two, precision=precise)
    embed_grad = jnp.dot(jnp.concatenate([pieces_one, pieces_two], axis=1), ada_full.T, precision=precise)
    act_table_grad = jnp.dot(action_hot.T, embed_grad, precision=precise)
    noise_table_grad = jnp.dot(noise_hot.T, embed_grad, precision=precise)
    bias_total = jnp.sum(bias_sums, axis=0)[:4, :C]

    def shard(value, axis):
        return lax.psum_scatter(value, "seq", scatter_dimension=axis, tiled=True)

    shards = (
        shard(act_table_grad, 1),
        shard(noise_table_grad, 1),
        shard(ada_one_grad, 0),
        shard(ada_two_grad, 0),
        shard(g_one, 0),
        shard(g_two, 0),
        shard(g_down, 0),
        shard(g_up, 0),
        shard(bias_total[0], 0),
        shard(bias_total[1], 0),
        shard(bias_total[2], 0),
        shard(bias_total[3], 0),
    )
    return (result, frames_grad) + lax.psum(shards, "rows")


def solution(mesh):
    in_specs = (
        P("seq", "rows", None),
        P("seq", "rows", None),
        P("seq"),
        P("seq"),
        P("seq"),
        P(None, "seq"),
        P(None, "seq"),
        P("seq", None),
        P("seq", None),
        P("seq", None),
        P("seq", None),
        P("seq", None),
        P("seq", None),
        P("seq"),
        P("seq"),
        P("seq"),
        P("seq"),
    )
    out_specs = (
        P("seq", "rows", None),
        P("seq", "rows", None),
        P(None, "seq"),
        P(None, "seq"),
        P("seq", None),
        P("seq", None),
        P("seq", None),
        P("seq", None),
        P("seq", None),
        P("seq", None),
        P("seq"),
        P("seq"),
        P("seq"),
        P("seq"),
    )
    return jax.shard_map(local, mesh=mesh, in_specs=in_specs, out_specs=out_specs, check_vma=False)
```

```python
import jax
import jax.numpy as jnp
from jax import lax
from jax.experimental import pallas as pl
from jax.experimental.pallas import tpu as pltpu
from jax.sharding import PartitionSpec as P

C = 64
NACT = 18
GROUPS = 32
NLEV = 32
H = 64
W = 64
PAIRS = W // 2
HALF = H // 2
LANES = 2 * C
BLOCK = PAIRS * HALF
MEMBERS = float(H * W * (C // GROUPS))
EPS = 1e-05

precise = lax.Precision.HIGHEST
f32 = jnp.float32
bf16 = jnp.bfloat16
VMEM_LIMIT = 60 * 2**20


def lane_ids(shape):
    return lax.broadcasted_iota(jnp.int32, shape, len(shape) - 1)


def swap_halves(x):
    return pltpu.roll(x, C, axis=x.ndim - 1)


def row_before(x):
    rows = lax.broadcasted_iota(jnp.int32, x.shape, 0)
    return jnp.where(rows == 0, 0.0, pltpu.roll(x, 1, axis=0))


def row_after(x):
    rows = lax.broadcasted_iota(jnp.int32, x.shape, 0)
    return jnp.where(rows == x.shape[0] - 1, 0.0, pltpu.roll(x, x.shape[0] - 1, axis=0))


def both_parities(x):
    x = jnp.broadcast_to(x, (8, LANES))
    return x + swap_halves(x)


def group_sum(x):
    even = lane_ids(x.shape) % 2 == 0
    return x + jnp.where(even, pltpu.roll(x, LANES - 1, axis=1), pltpu.roll(x, 1, axis=1))


def total(x):
    return jnp.sum(x, axis=0, keepdims=True)


def build_windows(windows, tile):
    low_lanes = lane_ids((HALF, LANES)) < C
    zero = jnp.zeros((HALF, LANES), f32)

    def write(j, even, odd):
        windows[0, j] = row_before(odd).astype(bf16)
        windows[1, j] = even.astype(bf16)
        windows[2, j] = odd.astype(bf16)
        windows[3, j] = row_after(even).astype(bf16)

    def body(j, carry):
        even_past, odd_past = carry
        even = swap_halves(tile(0, j))
        odd = swap_halves(tile(1, j))
        write(j, jnp.where(low_lanes, even_past, even), jnp.where(low_lanes, odd_past, odd))
        return even, odd

    even, odd = lax.fori_loop(0, PAIRS, body, (zero, zero), unroll=4)
    write(PAIRS, jnp.where(low_lanes, even, 0.0), jnp.where(low_lanes, odd, 0.0))


def window_operand(windows, slots):
    parts = []
    for slot in slots:
        for shift in (0, 1):
            parts.append(windows[slot, shift : shift + PAIRS].reshape(BLOCK, LANES))
    return jnp.concatenate(parts, axis=1)


def matmul(left, right):
    return jnp.dot(left, right, preferred_element_type=f32)


def tiles_of(y):
    return y.reshape(PAIRS, HALF, LANES)


def norm_stats(sums, squares):
    average = group_sum(both_parities(sums)) / MEMBERS
    variance = group_sum(both_parities(squares)) / MEMBERS - average * average
    return average, lax.rsqrt(variance + EPS)


def strip_start(member, offset, strip):
    return pl.multiple_of((member ^ offset) * strip, strip)


def load_strips(member, strips, image):
    for offset, strip in enumerate(strips):
        rows = strip.shape[1]
        start = strip_start(member, offset, rows)
        for j in range(PAIRS):
            image[j, pl.ds(start, rows), :] = strip[0, :, j * LANES : (j + 1) * LANES].astype(f32)


def store_strips(member, image, strips):
    for offset in range(strips.shape[0]):
        rows = strips.shape[2]
        start = strip_start(member, offset, rows)
        for j in range(PAIRS):
            strips[offset, 0, :, j * LANES : (j + 1) * LANES] = image[j, pl.ds(start, rows), :].astype(strips.dtype)


def parity_rows(image, parity, j):
    return image[j, pl.ds(parity, HALF, stride=2), :]


def forward_kernel(count, *refs):
    member_ref = refs[0]
    strips = refs[1 : 1 + count]
    styles, biases, w_one, w_two, w_down, w_up = refs[1 + count : 7 + count]
    out, win_one, win_two, win_level, win_coarse, middle, down, stats = refs[7 + count : 15 + count]
    image, level = refs[15 + count :]
    member = member_ref[0]
    win_one, win_two, win_level, win_coarse = (ref.at[0] for ref in (win_one, win_two, win_level, win_coarse))
    middle, down = middle.at[0], down.at[0]

    load_strips(member, strips, image)

    def add_stats(j, carry):
        x = image[j]
        s, q = carry
        return s + x, q + x * x

    zero = jnp.zeros((H, LANES), f32)
    s, q = lax.fori_loop(0, PAIRS, add_stats, (zero, zero), unroll=4)
    average_one, inverse_one = norm_stats(total(s), total(q))
    gain_one = inverse_one * styles[0, 0:1, :]
    half_gain = 0.5 * gain_one[0:1]
    half_shift = 0.5 * (styles[0, 1:2, :] - average_one[0:1] * gain_one[0:1])

    def act_one(parity, j):
        h = parity_rows(image, parity, j) * half_gain + half_shift
        return h * jnp.tanh(h) + h

    build_windows(win_one, act_one)
    y = matmul(window_operand(win_one, range(4)), w_one[...])
    sums = jnp.zeros((1, LANES), f32)
    squares = jnp.zeros((1, LANES), f32)
    for a in range(2):
        v = y[:, a * LANES : (a + 1) * LANES] + biases[0:1, :]
        sums = sums + total(v)
        squares = squares + total(v * v)
        middle[a] = tiles_of(v)
    average_two, inverse_two = norm_stats(sums, squares)
    stats[0, 0:1, :] = average_one[0:1]
    stats[0, 1:2, :] = inverse_one[0:1]
    stats[0, 2:3, :] = average_two[0:1]
    stats[0, 3:4, :] = inverse_two[0:1]
    stats[0, 4:8, :] = jnp.zeros((4, LANES), f32)
    gain_two = inverse_two * styles[0, 2:3, :]
    half_gain_two = 0.5 * gain_two[0:1]
    half_shift_two = 0.5 * (styles[0, 3:4, :] - average_two[0:1] * gain_two[0:1])

    def act_two(parity, j):
        h = middle[parity, j] * half_gain_two + half_shift_two
        return h * jnp.tanh(h) + h

    build_windows(win_two, act_two)
    y = matmul(window_operand(win_two, range(4)), w_two[...])
    for a in range(2):
        v = y[:, a * LANES : (a + 1) * LANES] + biases[1:2, :]
        level[a] = tiles_of(v) + image[:, pl.ds(a, HALF, stride=2), :]

    build_windows(win_level, lambda parity, j: level[parity, j])
    operand = window_operand(win_level, range(4))
    y = matmul(operand[:, : 6 * LANES], w_down[...]) + biases[2:3, :]
    down[...] = tiles_of(y)

    low_lanes = lane_ids((HALF, LANES)) < C

    def write_coarse(j, cells):
        win_coarse[0, j] = row_before(cells).astype(bf16)
        win_coarse[1, j] = cells.astype(bf16)
        win_coarse[2, j] = row_after(cells).astype(bf16)

    def coarse_body(j, past):
        h = down[j] * 0.5
        coarse = h * jnp.tanh(h) + h
        write_coarse(j, jnp.where(low_lanes, past, coarse))
        return coarse

    past = lax.fori_loop(0, PAIRS, coarse_body, jnp.zeros((HALF, LANES), f32), unroll=4)
    write_coarse(PAIRS, jnp.where(low_lanes, past, 0.0))

    operand = window_operand(win_level, range(4))
    coarse_operand = window_operand(win_coarse, (0, 1, 1, 2))
    y = matmul(operand, w_up[: 16 * C, :]) + matmul(coarse_operand, w_up[16 * C :, :])
    for a in range(2):
        v = y[:, a * LANES : (a + 1) * LANES] + biases[3:4, :]
        image[:, pl.ds(a, HALF, stride=2), :] = tiles_of(v) + level[a]
    store_strips(member, image, out)


def slope_twice(h):
    t = jnp.tanh(h)
    return (1.0 + t) + h * (1.0 - t * t)


def backward_kernel(count, *refs):
    member_ref = refs[0]
    cot_strips = refs[1 : 1 + count]
    frame_strips = refs[1 + count : 1 + 2 * count]
    styles, stats, middle, down, w_up, w_down, w_two, w_one = refs[1 + 2 * count : 9 + 2 * count]
    out, tile_out, tile_level, tile_mid, coarse_pairs, pieces, bias_sums = refs[9 + 2 * count : 16 + 2 * count]
    image, level_grad, pre_grad, windows, coarse_below, row_sums = refs[16 + 2 * count :]
    member = member_ref[0]
    tile_out, tile_level, tile_mid, coarse_pairs = (ref.at[0] for ref in (tile_out, tile_level, tile_mid, coarse_pairs))
    middle, down = middle.at[0], down.at[0]
    low_lanes = lane_ids((HALF, LANES)) < C

    load_strips(member, cot_strips, image)

    def add_rows(j, s):
        return s + image[j]

    sums = lax.fori_loop(0, PAIRS, add_rows, jnp.zeros((H, LANES), f32), unroll=4)
    bias_up_sum = both_parities(total(sums))

    def out_tile(parity, j):
        x = parity_rows(image, parity, j)
        tile_out[parity, j] = x.astype(bf16)
        return x

    build_windows(windows, out_tile)
    y = matmul(window_operand(windows, range(4)), w_up[...])
    for a in range(2):
        level_grad[a] = tiles_of(y[:, (2 + a) * LANES : (3 + a) * LANES]) + image[:, pl.ds(a, HALF, stride=2), :]
    coarse = y[:, :LANES] + y[:, LANES : 2 * LANES]
    pre_grad[0] = tiles_of(coarse)

    def coarse_body(t, carry):
        after, sums = carry
        j = PAIRS - 1 - t
        g = pre_grad[0, j]
        g = g + swap_halves(g)
        h = down[j] * 0.5
        d = 0.5 * g * slope_twice(h)
        pair = jnp.where(low_lanes, d, after)
        coarse_pairs[j] = pair.astype(bf16)
        coarse_below[j] = row_after(pair).astype(bf16)
        return d, sums + d

    zero = jnp.zeros((HALF, LANES), f32)
    _, sums = lax.fori_loop(0, PAIRS, coarse_body, (zero, zero), unroll=4)
    bias_down_sum = jnp.broadcast_to(total(sums), (8, LANES))

    operand = jnp.concatenate(
        [coarse_pairs[...].reshape(BLOCK, LANES), coarse_below[...].reshape(BLOCK, LANES)], axis=1
    )
    y = matmul(operand, w_down[...])
    sums = jnp.zeros((1, LANES), f32)
    for a in range(2):
        v = y[:, a * LANES : (a + 1) * LANES] + level_grad[a].reshape(BLOCK, LANES)
        sums = sums + total(v)
        level_grad[a] = tiles_of(v)
    bias_two_sum = both_parities(sums)

    def level_tile(parity, j):
        x = level_grad[parity, j]
        tile_level[parity, j] = x.astype(bf16)
        return x

    build_windows(windows, level_tile)

    def norm_slopes(y, value, k):
        average, inverse = stats[0, 2 * k : 2 * k + 1, :], stats[0, 2 * k + 1 : 2 * k + 2, :]
        gain = inverse * styles[0, 2 * k : 2 * k + 1, :]
        half_gain = 0.5 * gain
        half_shift = 0.5 * (styles[0, 2 * k + 1 : 2 * k + 2, :] - average * gain)
        scale_sum = jnp.zeros((1, LANES), f32)
        shift_sum = jnp.zeros((1, LANES), f32)
        for a in range(2):
            v = value(a)
            g = 0.5 * y[:, a * LANES : (a + 1) * LANES] * slope_twice(v * half_gain + half_shift)
            pre_grad[a] = tiles_of(g)
            shift_sum = shift_sum + total(g)
            scale_sum = scale_sum + total(g * ((v - average) * inverse))
        scale_sum, shift_sum = both_parities(scale_sum), both_parities(shift_sum)
        factor = styles[0, 2 * k : 2 * k + 1, :]
        center = group_sum(factor * shift_sum) / MEMBERS
        tilt = group_sum(factor * scale_sum) / MEMBERS
        return scale_sum, shift_sum, gain, (inverse * center)[0:1], (inverse * tilt)[0:1], average, inverse

    y = matmul(window_operand(windows, range(4)), w_two[...])
    scale_two, shift_two, gain, center, tilt, average, inverse = norm_slopes(
        y, lambda a: middle[a].reshape(BLOCK, LANES), 1
    )
    tilt_slope = tilt * inverse
    constant = tilt_slope * average - center

    def mid_tile(parity, j):
        x = pre_grad[parity, j] * gain + (constant - middle[parity, j] * tilt_slope)
        tile_mid[parity, j] = x.astype(bf16)
        row_sums[...] += x
        return x

    row_sums[...] = jnp.zeros_like(row_sums)
    build_windows(windows, mid_tile)
    bias_one_sum = both_parities(total(row_sums[...]))

    load_strips(member, frame_strips, image)
    y = matmul(window_operand(windows, range(4)), w_one[...])
    scale_one, shift_one, gain_one, center_one, tilt_one, average_one, inverse_one = norm_slopes(
        y, lambda a: image[:, pl.ds(a, HALF, stride=2), :].reshape(BLOCK, LANES), 0
    )
    slope_one = tilt_one * inverse_one
    constant_one = slope_one * average_one - center_one

    def frame_body(j, carry):
        for parity in range(2):
            x = parity_rows(image, parity, j)
            g = pre_grad[parity, j] * gain_one + (constant_one - x * slope_one) + level_grad[parity, j]
            image[j, pl.ds(parity, HALF, stride=2), :] = g
        return carry

    lax.fori_loop(0, PAIRS, frame_body, 0, unroll=4)
    store_strips(member, image, out)
    for k, value in enumerate((scale_one, shift_one, scale_two, shift_two)):
        pieces[0, k : k + 1, :] = value[0:1]
    pieces[0, 4:8, :] = jnp.zeros((4, LANES), f32)
    for k, value in enumerate((bias_one_sum, bias_two_sum, bias_down_sum, bias_up_sum)):
        bias_sums[0, k : k + 1, :] = value[0:1]
    bias_sums[0, 4:8, :] = jnp.zeros((4, LANES), f32)


def outer(left, right):
    return lax.dot_general(left, right, (((0,), (0,)), ((), ())), preferred_element_type=f32)


def accumulate(wins, tiles, sums):
    win_one, win_two, win_level, win_coarse = wins
    tile_out, tile_level, tile_mid, coarse_pairs = tiles
    sum_one, sum_two, sum_down, sum_up = sums

    @pl.when(pl.program_id(0) == 0)
    def _():
        for ref in sums:
            ref[...] = jnp.zeros_like(ref)

    def blocks(tiles):
        return jnp.concatenate([tiles[0, a].reshape(BLOCK, LANES) for a in range(2)], axis=1)

    level_operand = window_operand(win_level.at[0], range(4))
    out_blocks = blocks(tile_out)
    sum_up[16 * C :, :] += outer(window_operand(win_coarse.at[0], (0, 1, 1, 2)), out_blocks)
    sum_up[: 16 * C, :] += outer(level_operand, out_blocks)
    sum_down[...] += outer(level_operand[:, : 6 * LANES], coarse_pairs[0].reshape(BLOCK, LANES))
    sum_two[...] += outer(window_operand(win_two.at[0], range(4)), blocks(tile_level))
    sum_one[...] += outer(window_operand(win_one.at[0], range(4)), blocks(tile_mid))


def fold(sums, base, p, q):
    halves = []
    for b in range(2):
        rows = [base + ((a + p) * 4 + b + q) * C for a in range(2)]
        halves.append(sums[rows[0] : rows[0] + C, :LANES] + sums[rows[1] : rows[1] + C, LANES:])
    return halves[0] + swap_halves(halves[1])


def weight_kernel(*refs):
    wins, tiles, grads, sums = refs[:4], refs[4:8], refs[8:12], refs[12:]
    g_one, g_two, g_down, g_up = grads
    sum_one, sum_two, sum_down, sum_up = sums
    accumulate(wins, tiles, sums)

    @pl.when(pl.program_id(0) == pl.num_programs(0) - 1)
    def _():
        for p in range(3):
            for q in range(3):
                at = (3 * p + q) * C
                g_one[at : at + C, :] = fold(sum_one, 0, p, q)[:, :C]
                g_two[at : at + C, :] = fold(sum_two, 0, p, q)[:, :C]
                g_up[2 * at : 2 * at + C, :] = fold(sum_up, 16 * C, p, q)[:, :C]
                g_up[2 * at + C : 2 * at + 2 * C, :] = fold(sum_up, 0, p, q)[:, :C]
                place = (p * 4 + q) * C
                g_down[at : at + C, :] = sum_down[place : place + C, :C]


PARTS = 16


def message_kernel(count, rows, *refs):
    where_ref, wins, tiles = refs[0], refs[1:5], refs[5:9]
    pieces, bias_sums, own, messages = refs[9:13]
    sums = refs[13:17]
    g_pair, g_up, g_down, small = refs[17:]
    sum_one, sum_two, sum_down, sum_up = sums
    accumulate(wins, tiles, sums)

    @pl.when(pl.program_id(0) == pl.num_programs(0) - 1)
    def _():
        low_lanes = lane_ids((C, LANES)) < C
        for p in range(3):
            for q in range(3):
                at = (3 * p + q) * C
                g_pair[at : at + C, :] = jnp.where(
                    low_lanes, fold(sum_one, 0, p, q), swap_halves(fold(sum_two, 0, p, q))
                )
                g_up[2 * at : 2 * at + C, :] = fold(sum_up, 16 * C, p, q)
                g_up[2 * at + C : 2 * at + 2 * C, :] = fold(sum_up, 0, p, q)
                place = (p * 4 + q) * C
                g_down[at : at + C, :] = sum_down[place : place + C, :]
        frames = pieces.shape[0]
        small[...] = jnp.zeros_like(small)
        total_bias = bias_sums[0, 0:4, :]
        for f in range(frames):
            small[4 * f : 4 * f + 4, :] = pieces[f, 0:4, :]
            if f > 0:
                total_bias = total_bias + bias_sums[f, 0:4, :]
        small[4 * frames : 4 * frames + 4, :] = total_bias
        exact = small[...]
        high = exact.astype(bf16).astype(f32)
        rest = exact - high
        mid = rest.astype(bf16).astype(f32)
        parts = (high, mid, rest - mid)
        low_lanes = lane_ids((rows, LANES)) < C
        nothing = jnp.zeros((rows - 3 * PARTS, LANES), f32)
        sent = jnp.concatenate([*parts, nothing], axis=0)
        kept = jnp.concatenate([exact, jnp.zeros((2 * PARTS, LANES), f32), nothing], axis=0)
        for offset in range(count):
            start = pl.multiple_of(seq_owner(where_ref[0], offset) * rows, 8)
            block = jnp.concatenate(
                [
                    g_pair[pl.ds(start, rows), :],
                    jnp.where(
                        low_lanes,
                        g_up[pl.ds(pl.multiple_of(2 * start, 8), rows), :],
                        swap_halves(g_up[pl.ds(pl.multiple_of(2 * start + rows, 8), rows), :]),
                    ),
                    jnp.where(low_lanes, g_down[pl.ds(start, rows), :], kept if offset == 0 else sent),
                ],
                axis=0,
            )
            if offset == 0:
                own[...] = block
            else:
                messages[offset - 1] = block.astype(bf16)


def reduce_kernel(count, rows, cells, frames, *refs):
    where_ref, own = refs[:2]
    messages = refs[2 : 1 + count]
    packs = refs[1 + count : 1 + 2 * count]
    act_table, noise_table, ada_one, ada_two, out, pieces_one, pieces_two, table = refs[1 + 2 * count :]
    place, member = where_ref[0], where_ref[1]
    taken = 4 * frames
    bias = jnp.zeros((4, LANES), f32)
    sums = own[...]
    lanes = lane_ids((1, LANES))
    low_lanes = lanes < C
    hot = []
    for offset in range(count):
        if offset == 0:
            small = sums[2 * rows : 2 * rows + PARTS]
        else:
            message = messages[offset - 1][...].astype(f32)
            sums = sums + message
            first = 2 * rows
            small = (
                message[first : first + PARTS]
                + message[first + PARTS : first + 2 * PARTS]
                + message[first + 2 * PARTS : first + 3 * PARTS]
            )
        turned = swap_halves(small)
        bias = bias + small[taken : taken + 4]
        ids = packs[offset][2 * rows + ID_ROW : 2 * rows + ID_ROW + 8, :].astype(f32)
        for f in range(frames):
            at = offset * frames + f
            for k, ref in ((0, pieces_one), (2, pieces_two)):
                ref[at : at + 1, :] = jnp.where(low_lanes, turned[4 * f + k : 4 * f + k + 1], small[4 * f + k + 1 : 4 * f + k + 2])
            mine = jnp.where(lane_ids(ids.shape) == C + member * frames + f, ids, 0.0)
            mine = jnp.sum(mine, axis=1, keepdims=True)
            action, noise, valid = mine[0:1], mine[1:2], mine[2:3]
            place_at = lanes.astype(f32)
            hot.append(jnp.where(place_at == action + ACT_ROW, valid, 0.0) + jnp.where(place_at == noise + NOISE_ROW, 1.0, 0.0))
    hot = jnp.concatenate(hot, axis=0)[:, :TABLE_ROWS]
    table[...] = jnp.zeros_like(table)
    table[ACT_ROW : ACT_ROW + NACT, :] = act_table[...].astype(f32)
    table[NOISE_ROW : NOISE_ROW + NLEV, :] = noise_table[...].astype(f32)
    embed = matmul(hot.astype(bf16), table[...].astype(bf16))

    def exact(left, right, dims):
        return lax.dot_general(left, right, (dims, ((), ())), precision=precise, preferred_element_type=f32)

    one, two = pieces_one[...], pieces_two[...]
    at = 3 * rows
    out[:at, :] = sums
    out[at : at + cells, :] = exact(embed, one, ((0,), (0,)))
    out[at + cells : at + 2 * cells, :] = exact(embed, two, ((0,), (0,)))
    embed_grad = exact(one, ada_one[...].astype(f32), ((1,), (1,))) + exact(two, ada_two[...].astype(f32), ((1,), (1,)))
    at = at + 2 * cells
    out[at : at + TABLE_ROWS, :] = jnp.zeros((TABLE_ROWS, LANES), f32)
    out[at : at + TABLE_ROWS, :cells] = exact(hot, embed_grad, ((0,), (0,)))
    at = at + TABLE_ROWS
    bias = jnp.concatenate([bias, jnp.zeros((4, LANES), f32)], axis=0)
    width = C // count
    out[at : at + 8, :] = pltpu.roll(bias, (C - place * width) % LANES, axis=1)


def finish_kernel(rows, cells, width, first, second, *outs):
    act_grad, noise_grad, ada_one, ada_two, g_one, g_two, g_down, g_up = outs[:8]
    bias_grads = outs[8]
    sums = first[...] + second[...]
    pair, halves, down = (sums[k * rows : (k + 1) * rows] for k in range(3))
    g_one[...] = pair[:, :C]
    g_two[...] = swap_halves(pair)[:, :C]
    g_up[:rows, :] = halves[:, :C]
    g_up[rows:, :] = swap_halves(halves)[:, :C]
    g_down[...] = down[:, :C]
    at = 3 * rows
    ada_one[...] = sums[at : at + cells]
    ada_two[...] = sums[at + cells : at + 2 * cells]
    at = at + 2 * cells
    act_grad[...] = sums[at + ACT_ROW : at + ACT_ROW + NACT, :cells]
    noise_grad[...] = sums[at + NOISE_ROW : at + NOISE_ROW + NLEV, :cells]
    at = at + TABLE_ROWS
    bias_grads[...] = sums[at : at + 4, :width]


def write_operands(block, f_one, f_two, f_down, f_up, b_one, b_two, b_down, b_up):
    low_lanes = lane_ids((C, LANES)) < C
    zero = jnp.zeros((C, LANES), f32)

    def taps(name, base, step):
        plain, turned = {}, {}
        for p in range(3):
            for q in range(3):
                k = block(name, (3 * p + q) * step + base)
                plain[p, q] = k
                turned[p, q] = jnp.concatenate([k, k], axis=0).T[:C]
        return plain, turned

    def write_forward(ref, base, plain):
        for w in range(4):
            for p in range(3):
                tile = jnp.where(low_lanes, plain.get((p, w), zero), plain.get((p, w - 1), zero)).astype(bf16)
                for a in range(2):
                    at = base + ((a + p) * 4 + w) * C
                    ref[at : at + C, a * LANES : (a + 1) * LANES] = tile
            for a in range(2):
                for r in range(4):
                    if not 0 <= r - a < 3:
                        at = base + (r * 4 + w) * C
                        ref[at : at + C, a * LANES : (a + 1) * LANES] = zero.astype(bf16)

    def write_backward(ref, lane, turned):
        for w in range(4):
            for p in range(3):
                tile = jnp.where(low_lanes, turned.get((p, 2 - w), zero), turned.get((p, 3 - w), zero)).astype(bf16)
                for a in range(2):
                    at = ((a + 2 - p) * 4 + w) * C
                    ref[at : at + C, lane + a * LANES : lane + (a + 1) * LANES] = tile
            for a in range(2):
                for r in range(4):
                    if not 0 <= a + 2 - r < 3:
                        at = (r * 4 + w) * C
                        ref[at : at + C, lane + a * LANES : lane + (a + 1) * LANES] = zero.astype(bf16)

    for name, forward_ref, backward_ref in (("one", f_one, b_one), ("two", f_two, b_two)):
        plain, turned = taps(name, 0, C)
        write_forward(forward_ref, 0, plain)
        write_backward(backward_ref, 0, turned)
    plain, turned = taps("up", 0, 2 * C)
    write_forward(f_up, 16 * C, plain)
    write_backward(b_up, 0, turned)
    plain, turned = taps("up", C, 2 * C)
    write_forward(f_up, 0, plain)
    write_backward(b_up, 2 * LANES, turned)
    plain, turned = taps("down", 0, C)
    for p in range(3):
        for w in range(4):
            at = (p * 4 + w) * C
            f_down[at : at + C, :] = plain.get((p, w), zero).astype(bf16)
    for below in range(2):
        for right in range(2):
            at = (below * 2 + right) * C
            for a in range(2):
                p = {(0, 0): 1, (0, 1): 2, (1, 1): 0}.get((below, a))
                first, second = zero, zero
                if p is not None:
                    first = turned[p, 1] if right == 0 else zero
                    second = turned[p, 2] if right == 0 else turned[p, 0]
                b_down[at : at + C, a * LANES : (a + 1) * LANES] = jnp.where(low_lanes, first, second).astype(bf16)


def expand_kernel(conv_one, conv_two, down_kernel, up_kernel, *outs):
    kernels = {"one": conv_one, "two": conv_two, "down": down_kernel, "up": up_kernel}

    def block(name, row):
        k = kernels[name][row : row + C, :].astype(f32)
        return jnp.concatenate([k, k], axis=1)

    write_operands(block, *outs)


ACT_ROW, NOISE_ROW, TABLE_ROWS = 0, 24, 56
BIAS_ROW, ID_ROW = 56, 64


def pack_sizes(rows, cells):
    return 3 * rows, 3 * rows + 2 * cells, -(-(3 * rows + 2 * cells) // 16) * 16


def pack_kernel(conv_one, conv_two, down_kernel, up_kernel, ada_one, ada_two, act_table, noise_table, biases, ids, out, work):
    rows, cells = conv_one.shape[0], ada_one.shape[0]
    style_at, end, _ = pack_sizes(rows, cells)
    work[...] = jnp.zeros_like(work)
    wide = lambda ref: ref[...].astype(f32)
    work[:rows, :] = jnp.concatenate([wide(conv_one), wide(conv_two)], axis=1)
    work[rows : 2 * rows, :] = jnp.concatenate([wide(up_kernel)[:rows], wide(up_kernel)[rows:]], axis=1)
    work[2 * rows : 3 * rows, :C] = wide(down_kernel)
    for at, ref in ((ACT_ROW, act_table), (NOISE_ROW, noise_table), (BIAS_ROW, biases), (ID_ROW, ids)):
        size = ref.shape
        work[2 * rows + at : 2 * rows + at + size[0], C : C + size[1]] = wide(ref)
    work[style_at : style_at + cells, :] = wide(ada_one)
    work[style_at + cells : end, :] = wide(ada_two)
    out[...] = work[...].astype(bf16)


def seq_owner(place, offset):
    return place ^ offset


def prepare_kernel(count, rows, cells, *refs):
    where_ref, actions, noise_ids, valid = refs[:4]
    packs = refs[4 : 4 + count]
    outs = refs[4 + count : 12 + count]
    styles, biases = refs[12 + count : 14 + count]
    work_pair, work_up, work_down, work_one, work_two, work_table = refs[14 + count :]
    place, member, frames = where_ref[0], where_ref[1], styles.shape[0]
    style_at, _, _ = pack_sizes(rows, cells)
    bias_rows = jnp.zeros(SMALL, f32)
    for offset, ref in enumerate(packs):
        pack = ref[...].astype(f32)
        owner = seq_owner(place, offset)
        start = pl.multiple_of(owner * rows, 8)
        work_pair[pl.ds(start, rows), :] = pack[:rows]
        halves = pack[rows : 2 * rows]
        work_up[pl.ds(2 * start, rows), :] = halves
        work_up[pl.ds(pl.multiple_of(2 * start + rows, 8), rows), :] = swap_halves(halves)
        extra = pack[2 * rows : 3 * rows]
        work_down[pl.ds(start, rows), :] = extra
        work_one[offset * cells : (offset + 1) * cells, :] = pack[style_at : style_at + cells]
        work_two[offset * cells : (offset + 1) * cells, :] = pack[style_at + cells : style_at + 2 * cells]
        lane = (offset * cells) % LANES
        tables = pltpu.roll(extra[:TABLE_ROWS], (lane - C) % LANES, axis=1)
        kept = (lane_ids(tables.shape) >= lane) & (lane_ids(tables.shape) < lane + cells)
        column = offset * cells // LANES
        tables = jnp.where(kept, tables, 0.0)
        if lane == 0:
            work_table[column] = tables
        else:
            work_table[column] += tables
        slots = extra[BIAS_ROW : BIAS_ROW + 8]
        width = C // count
        slots = jnp.where((lane_ids(SMALL) >= C) & (lane_ids(SMALL) < C + width), slots, 0.0)
        bias_rows = bias_rows + pltpu.roll(slots, (owner * width + C) % LANES, axis=1)
    biases[...] = bias_rows + swap_halves(bias_rows)

    lanes = lane_ids((8, LANES))
    row_at = lax.broadcasted_iota(jnp.int32, (8, LANES), 0)
    hot = jnp.zeros((8, LANES), f32)
    for f in range(frames):
        at = member * frames + f
        here = jnp.where(lanes == actions[at] + ACT_ROW, valid[at], 0) + jnp.where(lanes == noise_ids[at] + NOISE_ROW, 1, 0)
        hot = jnp.where(row_at == f, here.astype(f32), hot)
    hot = hot[:, :TABLE_ROWS].astype(bf16)
    embed = jnp.concatenate([matmul(hot, work_table[k].astype(bf16)) for k in range(work_table.shape[0])], axis=1)
    low_lanes = lanes < C
    for k, work in enumerate((work_one, work_two)):
        style = jnp.dot(embed, work[...], precision=precise, preferred_element_type=f32)
        other = swap_halves(style)
        scale = 1.0 + jnp.where(low_lanes, style, other)
        shift = jnp.where(low_lanes, other, style)
        for f in range(frames):
            styles[f, 2 * k : 2 * k + 1, :] = scale[f : f + 1]
            styles[f, 2 * k + 1 : 2 * k + 2, :] = shift[f : f + 1]
    for f in range(frames):
        styles[f, 4:8, :] = jnp.zeros((4, LANES), f32)

    def block(name, row):
        work = {"one": work_pair, "two": work_pair, "down": work_down, "up": work_up}[name]
        k = work[row : row + C, :]
        low = lane_ids(k.shape) < C
        if name == "two":
            return jnp.where(low, swap_halves(k), k)
        return jnp.where(low, k, swap_halves(k))

    write_operands(block, *outs)


def shape(dims, kind):
    return jax.ShapeDtypeStruct(dims, kind)


def whole(dims):
    return pl.BlockSpec(dims, lambda f: (0,) * len(dims))


def per_frame(dims):
    return pl.BlockSpec((1,) + dims, lambda f: (f,) + (0,) * len(dims))


def strip_specs(count, strip):
    return [pl.BlockSpec((1, strip, W * C), lambda f: (f, 0, 0))] * count


def out_strips(count, strip):
    return pl.BlockSpec((count, 1, strip, W * C), lambda f: (0, f, 0, 0))


SMALL = (8, LANES)
WINDOWS = (4, PAIRS + 1, HALF, LANES)
COARSE_WINDOWS = (3, PAIRS + 1, HALF, LANES)
TILES = (2, PAIRS, HALF, LANES)
COARSE = (PAIRS, HALF, LANES)
IMAGE = (PAIRS, H, LANES)
KEYS = 16 * C


def params():
    return pltpu.CompilerParams(vmem_limit_bytes=VMEM_LIMIT)


def expand(conv_one, conv_two, down_kernel, up_kernel):
    vmem = pl.BlockSpec(memory_space=pltpu.VMEM)
    return pl.pallas_call(
        expand_kernel,
        in_specs=[vmem] * 4,
        out_specs=[vmem] * 8,
        out_shape=[
            shape((KEYS, 2 * LANES), bf16),
            shape((KEYS, 2 * LANES), bf16),
            shape((6 * LANES, LANES), bf16),
            shape((2 * KEYS, 2 * LANES), bf16),
            shape((KEYS, 2 * LANES), bf16),
            shape((KEYS, 2 * LANES), bf16),
            shape((2 * LANES, 2 * LANES), bf16),
            shape((KEYS, 4 * LANES), bf16),
        ],
        compiler_params=params(),
        name="expand",
    )(conv_one, conv_two, down_kernel, up_kernel)


def forward(member, strips, styles, biases, w_one, w_two, w_down, w_up):
    count = len(strips)
    frames, strip, _ = strips[0].shape
    return pl.pallas_call(
        lambda *refs: forward_kernel(count, *refs),
        grid=(frames,),
        in_specs=[pl.BlockSpec(memory_space=pltpu.SMEM)]
        + strip_specs(count, strip)
        + [per_frame(SMALL), whole(SMALL)]
        + [whole(w.shape) for w in (w_one, w_two, w_down, w_up)],
        out_specs=[out_strips(count, strip)]
        + [per_frame(d) for d in (WINDOWS, WINDOWS, WINDOWS, COARSE_WINDOWS, TILES, COARSE, SMALL)],
        out_shape=[
            shape((count, frames, strip, W * C), bf16),
            shape((frames,) + WINDOWS, bf16),
            shape((frames,) + WINDOWS, bf16),
            shape((frames,) + WINDOWS, bf16),
            shape((frames,) + COARSE_WINDOWS, bf16),
            shape((frames,) + TILES, f32),
            shape((frames,) + COARSE, f32),
            shape((frames,) + SMALL, f32),
        ],
        scratch_shapes=[pltpu.VMEM(IMAGE, f32), pltpu.VMEM(TILES, f32)],
        compiler_params=params(),
        name="forward",
    )(member, *strips, styles, biases, w_one, w_two, w_down, w_up)


def backward(member, cot_strips, frame_strips, styles, stats, middle, down, w_up, w_down, w_two, w_one):
    count = len(cot_strips)
    frames, strip, _ = cot_strips[0].shape
    return pl.pallas_call(
        lambda *refs: backward_kernel(count, *refs),
        grid=(frames,),
        in_specs=[pl.BlockSpec(memory_space=pltpu.SMEM)]
        + strip_specs(2 * count, strip)
        + [per_frame(d) for d in (SMALL, SMALL, TILES, COARSE)]
        + [whole(w.shape) for w in (w_up, w_down, w_two, w_one)],
        out_specs=[out_strips(count, strip)]
        + [per_frame(d) for d in (TILES, TILES, TILES, COARSE, SMALL, SMALL)],
        out_shape=[
            shape((count, frames, strip, W * C), bf16),
            shape((frames,) + TILES, bf16),
            shape((frames,) + TILES, bf16),
            shape((frames,) + TILES, bf16),
            shape((frames,) + COARSE, bf16),
            shape((frames,) + SMALL, f32),
            shape((frames,) + SMALL, f32),
        ],
        scratch_shapes=[
            pltpu.VMEM(IMAGE, f32),
            pltpu.VMEM(TILES, f32),
            pltpu.VMEM(TILES, f32),
            pltpu.VMEM(WINDOWS, bf16),
            pltpu.VMEM(COARSE, bf16),
            pltpu.VMEM((HALF, LANES), f32),
        ],
        compiler_params=params(),
        name="backward",
    )(member, *cot_strips, *frame_strips, styles, stats, middle, down, w_up, w_down, w_two, w_one)


def weight_grads(win_one, win_two, win_level, win_coarse, tile_out, tile_level, tile_mid, coarse_pairs):
    frames = win_one.shape[0]
    return pl.pallas_call(
        weight_kernel,
        grid=(frames,),
        in_specs=[
            per_frame(d) for d in (WINDOWS, WINDOWS, WINDOWS, COARSE_WINDOWS, TILES, TILES, TILES, COARSE)
        ],
        out_specs=[whole((9 * C, C)), whole((9 * C, C)), whole((9 * C, C)), whole((18 * C, C))],
        out_shape=[shape((9 * C, C), f32)] * 3 + [shape((18 * C, C), f32)],
        scratch_shapes=[
            pltpu.VMEM((KEYS, 2 * LANES), f32),
            pltpu.VMEM((KEYS, 2 * LANES), f32),
            pltpu.VMEM((6 * LANES, LANES), f32),
            pltpu.VMEM((2 * KEYS, 2 * LANES), f32),
        ],
        compiler_params=params(),
        name="weights",
    )(win_one, win_two, win_level, win_coarse, tile_out, tile_level, tile_mid, coarse_pairs)


def in_vmem():
    return pl.BlockSpec(memory_space=pltpu.VMEM)


def in_smem():
    return pl.BlockSpec(memory_space=pltpu.SMEM)


def pack(conv_one, conv_two, down_kernel, up_kernel, ada_one, ada_two, act_table, noise_table, biases, ids):
    args = (conv_one, conv_two, down_kernel, up_kernel, ada_one, ada_two, act_table, noise_table, biases, ids)
    _, _, size = pack_sizes(conv_one.shape[0], ada_one.shape[0])
    return pl.pallas_call(
        pack_kernel,
        in_specs=[in_vmem()] * len(args),
        out_specs=in_vmem(),
        out_shape=shape((size, LANES), bf16),
        scratch_shapes=[pltpu.VMEM((size, LANES), f32)],
        compiler_params=params(),
        name="pack",
    )(*args)


OPERANDS = (
    (KEYS, 2 * LANES),
    (KEYS, 2 * LANES),
    (6 * LANES, LANES),
    (2 * KEYS, 2 * LANES),
    (KEYS, 2 * LANES),
    (KEYS, 2 * LANES),
    (2 * LANES, 2 * LANES),
    (KEYS, 4 * LANES),
)


def prepare(where, actions, noise_ids, valid, packs, rows, cells, frames):
    count = len(packs)
    return pl.pallas_call(
        lambda *refs: prepare_kernel(count, rows, cells, *refs),
        in_specs=[in_smem()] * 4 + [in_vmem()] * count,
        out_specs=[in_vmem()] * 10,
        out_shape=[shape(d, bf16) for d in OPERANDS] + [shape((frames,) + SMALL, f32), shape(SMALL, f32)],
        scratch_shapes=[
            pltpu.VMEM((9 * C, LANES), f32),
            pltpu.VMEM((18 * C, LANES), f32),
            pltpu.VMEM((9 * C, LANES), f32),
            pltpu.VMEM((count * cells, LANES), f32),
            pltpu.VMEM((count * cells, LANES), f32),
            pltpu.VMEM((count * cells // LANES, TABLE_ROWS, LANES), f32),
        ],
        compiler_params=params(),
        name="prepare",
    )(where, actions, noise_ids, valid, *packs)


def weight_messages(where, wins, tiles, pieces, bias_sums, count, rows):
    frames = pieces.shape[0]
    return pl.pallas_call(
        lambda *refs: message_kernel(count, rows, *refs),
        grid=(frames,),
        in_specs=[in_smem()]
        + [per_frame(d) for d in (WINDOWS, WINDOWS, WINDOWS, COARSE_WINDOWS, TILES, TILES, TILES, COARSE)]
        + [whole((frames,) + SMALL)] * 2,
        out_specs=[whole((3 * rows, LANES)), whole((count - 1, 3 * rows, LANES))],
        out_shape=[shape((3 * rows, LANES), f32), shape((count - 1, 3 * rows, LANES), bf16)],
        scratch_shapes=[
            pltpu.VMEM((KEYS, 2 * LANES), f32),
            pltpu.VMEM((KEYS, 2 * LANES), f32),
            pltpu.VMEM((6 * LANES, LANES), f32),
            pltpu.VMEM((2 * KEYS, 2 * LANES), f32),
            pltpu.VMEM((9 * C, LANES), f32),
            pltpu.VMEM((18 * C, LANES), f32),
            pltpu.VMEM((9 * C, LANES), f32),
            pltpu.VMEM((PARTS, LANES), f32),
        ],
        compiler_params=params(),
        name="weights",
    )(where, *wins, *tiles, pieces, bias_sums)


def reduce_messages(where, own, messages, packs, act_table, noise_table, ada_one, ada_two, rows, cells, frames):
    count = len(packs)
    return pl.pallas_call(
        lambda *refs: reduce_kernel(count, rows, cells, frames, *refs),
        in_specs=[in_smem()] + [in_vmem()] * (2 * count + 4),
        out_specs=in_vmem(),
        out_shape=shape((3 * rows + 2 * cells + TABLE_ROWS + 8, LANES), f32),
        scratch_shapes=[
            pltpu.VMEM((count * frames, LANES), f32),
            pltpu.VMEM((count * frames, LANES), f32),
            pltpu.VMEM((TABLE_ROWS, cells), f32),
        ],
        compiler_params=params(),
        name="reduce",
    )(where, own, *messages, *packs, act_table, noise_table, ada_one, ada_two)


def finish(first, second, rows, cells, width):
    return pl.pallas_call(
        lambda *refs: finish_kernel(rows, cells, width, *refs),
        in_specs=[in_vmem()] * 2,
        out_specs=[in_vmem()] * 9,
        out_shape=[
            shape((NACT, cells), f32),
            shape((NLEV, cells), f32),
            shape((cells, LANES), f32),
            shape((cells, LANES), f32),
            shape((rows, C), f32),
            shape((rows, C), f32),
            shape((rows, C), f32),
            shape((2 * rows, C), f32),
            shape((4, width), f32),
        ],
        compiler_params=params(),
        name="finish",
    )(first, second)


def twice(values):
    return jnp.concatenate([values, values], axis=-1)


def pad_small(rows):
    stacked = jnp.stack(rows, axis=-2)
    gaps = [(0, 0)] * (stacked.ndim - 2) + [(0, 8 - len(rows)), (0, 0)]
    return jnp.pad(stacked, gaps)


def trade(value, offset):
    if offset == 0:
        return value
    count = lax.axis_size("rows")
    return lax.ppermute(value, "rows", [(i, i ^ offset) for i in range(count)])


def spread_strips(array, member):
    count = lax.axis_size("rows")
    share = array.shape[0] // count
    return [
        trade(lax.dynamic_slice_in_dim(array, (member ^ offset) * share, share, axis=0), offset)
        for offset in range(count)
    ]


def collect_strips(strips, member, kind):
    count, share = strips.shape[:2]
    result = jnp.zeros((count * share,) + strips.shape[2:], kind)
    for offset in range(count):
        part = trade(strips[offset], offset).astype(kind)
        result = lax.dynamic_update_slice_in_dim(result, part, (member ^ offset) * share, axis=0)
    return result


def seq_trade(value, offset):
    count = lax.axis_size("seq")
    return lax.ppermute(value, "seq", [(i, i ^ offset) for i in range(count)])


def layers(member_box, frame_strips, cot_strips, styles, bias_rows, operands):
    f_one, f_two, f_down, f_up, b_one, b_two, b_down, b_up = operands
    member = member_box[0]
    out, win_one, win_two, win_level, win_coarse, middle, down, stats = forward(
        member_box, frame_strips, styles, bias_rows, f_one, f_two, f_down, f_up
    )
    result = collect_strips(out, member, bf16)
    grad_strips, tile_out, tile_level, tile_mid, coarse_pairs, pieces, bias_sums = backward(
        member_box, cot_strips, frame_strips, styles, stats, middle, down, b_up, b_down, b_two, b_one
    )
    frames_grad = collect_strips(grad_strips, member, f32)
    wins = (win_one, win_two, win_level, win_coarse)
    tiles = (tile_out, tile_level, tile_mid, coarse_pairs)
    return result, frames_grad, wins, tiles, pieces, bias_sums


def local_direct(
    frames,
    cotangent,
    actions,
    noise_ids,
    valid,
    act_table,
    noise_table,
    ada_one,
    ada_two,
    conv_one,
    conv_two,
    down_kernel,
    up_kernel,
    bias_one,
    bias_two,
    bias_down,
    bias_up,
):
    member = lax.axis_index("rows").astype(jnp.int32)
    place = lax.axis_index("seq").astype(jnp.int32)
    count = lax.axis_size("seq")
    share = frames.shape[0] // lax.axis_size("rows")
    rows, cells, width = conv_one.shape[0], ada_one.shape[0], bias_one.shape[0]
    member_box = member.reshape(1)
    where = jnp.stack([place, member])
    biases = jnp.stack([bias_one, bias_two, bias_down, bias_up])
    ids = jnp.stack([actions, noise_ids, valid])
    packed = pack(conv_one, conv_two, down_kernel, up_kernel, ada_one, ada_two, act_table, noise_table, biases, ids)
    packs = [packed] + [seq_trade(packed, offset) for offset in range(1, count)]
    frame_strips = spread_strips(frames, member)
    cot_strips = spread_strips(cotangent, member)
    *operands, styles, bias_rows = prepare(where, actions, noise_ids, valid, packs, rows, cells, share)
    result, frames_grad, wins, tiles, pieces, bias_sums = layers(
        member_box, frame_strips, cot_strips, styles, bias_rows, operands
    )
    own, messages = weight_messages(where, wins, tiles, pieces, bias_sums, count, rows)
    received = [seq_trade(messages[offset - 1], offset) for offset in range(1, count)]
    sums = reduce_messages(where, own, received, packs, act_table, noise_table, ada_one, ada_two, rows, cells, share)
    offset = 1
    while 2 * offset < lax.axis_size("rows"):
        sums = sums + trade(sums, offset)
        offset *= 2
    *grads, bias_grads = finish(sums, trade(sums, offset), rows, cells, width)
    return (result, frames_grad, *grads, bias_grads[0], bias_grads[1], bias_grads[2], bias_grads[3])


def local_general(
    frames,
    cotangent,
    actions,
    noise_ids,
    valid,
    act_table,
    noise_table,
    ada_one,
    ada_two,
    conv_one,
    conv_two,
    down_kernel,
    up_kernel,
    bias_one,
    bias_two,
    bias_down,
    bias_up,
):
    member = lax.axis_index("rows").astype(jnp.int32)
    share = frames.shape[0] // lax.axis_size("rows")
    member_box = member.reshape(1)

    def gathered(value, axis):
        return lax.all_gather(value, "seq", axis=axis, tiled=True)

    frame_strips = spread_strips(frames, member)
    cot_strips = spread_strips(cotangent, member)
    act_full = gathered(act_table, 1)
    noise_full = gathered(noise_table, 1)
    ada_full = gathered(jnp.concatenate([ada_one, ada_two], axis=1), 0).astype(f32)
    biases = gathered(jnp.stack([bias_one, bias_two, bias_down, bias_up]), 1).astype(f32)
    operands = expand(gathered(conv_one, 0), gathered(conv_two, 0), gathered(down_kernel, 0), gathered(up_kernel, 0))

    own = lambda ids: lax.dynamic_slice_in_dim(ids, member * share, share)
    own_actions, own_noise, own_valid = own(actions), own(noise_ids), own(valid)
    action_hot = (own_actions[:, None] == jnp.arange(NACT, dtype=jnp.int32)[None, :]).astype(f32) * own_valid[
        :, None
    ].astype(f32)
    noise_hot = (own_noise[:, None] == jnp.arange(NLEV, dtype=jnp.int32)[None, :]).astype(f32)
    embed = jnp.dot(action_hot, act_full.astype(f32), precision=precise) + jnp.dot(
        noise_hot, noise_full.astype(f32), precision=precise
    )
    style = jnp.dot(embed, ada_full, precision=precise)
    styles = pad_small(
        [
            twice(1.0 + style[:, :C]),
            twice(style[:, C : 2 * C]),
            twice(1.0 + style[:, 2 * C : 3 * C]),
            twice(style[:, 3 * C :]),
        ]
    )
    bias_rows = pad_small([twice(biases[k]) for k in range(4)])
    result, frames_grad, wins, tiles, pieces, bias_sums = layers(
        member_box, frame_strips, cot_strips, styles, bias_rows, operands
    )
    g_one, g_two, g_down, g_up = weight_grads(*wins, *tiles)

    pieces_one = jnp.concatenate([pieces[:, 0, :C], pieces[:, 1, :C]], axis=1)
    pieces_two = jnp.concatenate([pieces[:, 2, :C], pieces[:, 3, :C]], axis=1)
    ada_one_grad = jnp.dot(embed.T, pieces_one, precision=precise)
    ada_two_grad = jnp.dot(embed.T, pieces_two, precision=precise)
    embed_grad = jnp.dot(jnp.concatenate([pieces_one, pieces_two], axis=1), ada_full.T, precision=precise)
    act_table_grad = jnp.dot(action_hot.T, embed_grad, precision=precise)
    noise_table_grad = jnp.dot(noise_hot.T, embed_grad, precision=precise)
    bias_total = jnp.sum(bias_sums, axis=0)[:4, :C]

    def shard(value, axis):
        return lax.psum_scatter(value, "seq", scatter_dimension=axis, tiled=True)

    shards = (
        shard(act_table_grad, 1),
        shard(noise_table_grad, 1),
        shard(ada_one_grad, 0),
        shard(ada_two_grad, 0),
        shard(g_one, 0),
        shard(g_two, 0),
        shard(g_down, 0),
        shard(g_up, 0),
        shard(bias_total[0], 0),
        shard(bias_total[1], 0),
        shard(bias_total[2], 0),
        shard(bias_total[3], 0),
    )
    return (result, frames_grad) + lax.psum(shards, "rows")


def fits_direct(mesh):
    count = mesh.shape["seq"]
    rows, cells = 9 * C // count, 256 // count
    return count in (2, 4, 8) and rows % 8 == 0 and rows >= ID_ROW + 8 and cells % 8 == 0 and mesh.shape["rows"] == 4


def solution(mesh):
    in_specs = (
        P("seq", "rows", None),
        P("seq", "rows", None),
        P("seq"),
        P("seq"),
        P("seq"),
        P(None, "seq"),
        P(None, "seq"),
        P("seq", None),
        P("seq", None),
        P("seq", None),
        P("seq", None),
        P("seq", None),
        P("seq", None),
        P("seq"),
        P("seq"),
        P("seq"),
        P("seq"),
    )
    out_specs = (
        P("seq", "rows", None),
        P("seq", "rows", None),
        P(None, "seq"),
        P(None, "seq"),
        P("seq", None),
        P("seq", None),
        P("seq", None),
        P("seq", None),
        P("seq", None),
        P("seq", None),
        P("seq"),
        P("seq"),
        P("seq"),
        P("seq"),
    )
    local = local_direct if fits_direct(mesh) else local_general
    return jax.shard_map(local, mesh=mesh, in_specs=in_specs, out_specs=out_specs, check_vma=False)
```

```python
import jax
import jax.numpy as jnp
from jax import lax
from jax.experimental import pallas as pl
from jax.experimental.pallas import tpu as pltpu
from jax.sharding import PartitionSpec as P

C = 64
NACT = 18
GROUPS = 32
NLEV = 32
H = 64
W = 64
PAIRS = W // 2
HALF = H // 2
LANES = 2 * C
BLOCK = PAIRS * HALF
MEMBERS = float(H * W * (C // GROUPS))
EPS = 1e-05

precise = lax.Precision.HIGHEST
f32 = jnp.float32
bf16 = jnp.bfloat16
VMEM_LIMIT = 60 * 2**20


def lane_ids(shape):
    return lax.broadcasted_iota(jnp.int32, shape, len(shape) - 1)


def swap_halves(x):
    return pltpu.roll(x, C, axis=x.ndim - 1)


def row_before(x):
    rows = lax.broadcasted_iota(jnp.int32, x.shape, 0)
    return jnp.where(rows == 0, 0.0, pltpu.roll(x, 1, axis=0))


def row_after(x):
    rows = lax.broadcasted_iota(jnp.int32, x.shape, 0)
    return jnp.where(rows == x.shape[0] - 1, 0.0, pltpu.roll(x, x.shape[0] - 1, axis=0))


def both_parities(x):
    x = jnp.broadcast_to(x, (8, LANES))
    return x + swap_halves(x)


def group_sum(x):
    even = lane_ids(x.shape) % 2 == 0
    return x + jnp.where(even, pltpu.roll(x, LANES - 1, axis=1), pltpu.roll(x, 1, axis=1))


def total(x):
    return jnp.sum(x, axis=0, keepdims=True)


def build_windows(windows, tile):
    low_lanes = lane_ids((HALF, LANES)) < C
    zero = jnp.zeros((HALF, LANES), f32)

    def write(j, even, odd):
        windows[0, j] = row_before(odd).astype(bf16)
        windows[1, j] = even.astype(bf16)
        windows[2, j] = odd.astype(bf16)
        windows[3, j] = row_after(even).astype(bf16)

    def body(j, carry):
        even_past, odd_past = carry
        even = swap_halves(tile(0, j))
        odd = swap_halves(tile(1, j))
        write(j, jnp.where(low_lanes, even_past, even), jnp.where(low_lanes, odd_past, odd))
        return even, odd

    even, odd = lax.fori_loop(0, PAIRS, body, (zero, zero), unroll=4)
    write(PAIRS, jnp.where(low_lanes, even, 0.0), jnp.where(low_lanes, odd, 0.0))


def window_operand(windows, slots):
    parts = []
    for slot in slots:
        for shift in (0, 1):
            parts.append(windows[slot, shift : shift + PAIRS].reshape(BLOCK, LANES))
    return jnp.concatenate(parts, axis=1)


def matmul(left, right):
    return jnp.dot(left, right, preferred_element_type=f32)


def tiles_of(y):
    return y.reshape(PAIRS, HALF, LANES)


def norm_stats(sums, squares):
    average = group_sum(both_parities(sums)) / MEMBERS
    variance = group_sum(both_parities(squares)) / MEMBERS - average * average
    return average, lax.rsqrt(variance + EPS)


def strip_start(member, offset, strip):
    return pl.multiple_of((member ^ offset) * strip, strip)


def load_strips(member, strips, image):
    for offset, strip in enumerate(strips):
        rows = strip.shape[1]
        start = strip_start(member, offset, rows)
        for j in range(PAIRS):
            image[j, pl.ds(start, rows), :] = strip[0, :, j * LANES : (j + 1) * LANES].astype(f32)


def store_strips(member, image, strips):
    for offset, strip in enumerate(strips):
        rows = strip.shape[1]
        start = strip_start(member, offset, rows)
        for j in range(PAIRS):
            strip[0, :, j * LANES : (j + 1) * LANES] = image[j, pl.ds(start, rows), :].astype(strip.dtype)


def parity_rows(image, parity, j):
    return image[j, pl.ds(parity, HALF, stride=2), :]


def forward_kernel(count, *refs):
    member_ref = refs[0]
    strips = refs[1 : 1 + count]
    styles, biases, w_one, w_two, w_down, w_up = refs[1 + count : 7 + count]
    out = refs[7 + count : 7 + 2 * count]
    win_one, win_two, win_level, win_coarse, middle, down, stats = refs[7 + 2 * count : 14 + 2 * count]
    image, level = refs[14 + 2 * count :]
    member = member_ref[0]
    win_one, win_two, win_level, win_coarse = (ref.at[0] for ref in (win_one, win_two, win_level, win_coarse))
    middle, down = middle.at[0], down.at[0]

    load_strips(member, strips, image)

    def add_stats(j, carry):
        x = image[j]
        s, q = carry
        return s + x, q + x * x

    zero = jnp.zeros((H, LANES), f32)
    s, q = lax.fori_loop(0, PAIRS, add_stats, (zero, zero), unroll=4)
    average_one, inverse_one = norm_stats(total(s), total(q))
    gain_one = inverse_one * styles[0, 0:1, :]
    half_gain = 0.5 * gain_one[0:1]
    half_shift = 0.5 * (styles[0, 1:2, :] - average_one[0:1] * gain_one[0:1])

    def act_one(parity, j):
        h = parity_rows(image, parity, j) * half_gain + half_shift
        return h * jnp.tanh(h) + h

    build_windows(win_one, act_one)
    y = matmul(window_operand(win_one, range(4)), w_one[...])
    sums = jnp.zeros((1, LANES), f32)
    squares = jnp.zeros((1, LANES), f32)
    for a in range(2):
        v = y[:, a * LANES : (a + 1) * LANES] + biases[0:1, :]
        sums = sums + total(v)
        squares = squares + total(v * v)
        middle[a] = tiles_of(v)
    average_two, inverse_two = norm_stats(sums, squares)
    stats[0, 0:1, :] = average_one[0:1]
    stats[0, 1:2, :] = inverse_one[0:1]
    stats[0, 2:3, :] = average_two[0:1]
    stats[0, 3:4, :] = inverse_two[0:1]
    stats[0, 4:8, :] = jnp.zeros((4, LANES), f32)
    gain_two = inverse_two * styles[0, 2:3, :]
    half_gain_two = 0.5 * gain_two[0:1]
    half_shift_two = 0.5 * (styles[0, 3:4, :] - average_two[0:1] * gain_two[0:1])

    def act_two(parity, j):
        h = middle[parity, j] * half_gain_two + half_shift_two
        return h * jnp.tanh(h) + h

    build_windows(win_two, act_two)
    y = matmul(window_operand(win_two, range(4)), w_two[...])
    for a in range(2):
        v = y[:, a * LANES : (a + 1) * LANES] + biases[1:2, :]
        level[a] = tiles_of(v) + image[:, pl.ds(a, HALF, stride=2), :]

    build_windows(win_level, lambda parity, j: level[parity, j])
    operand = window_operand(win_level, range(4))
    y = matmul(operand[:, : 6 * LANES], w_down[...]) + biases[2:3, :]
    down[...] = tiles_of(y)

    low_lanes = lane_ids((HALF, LANES)) < C

    def write_coarse(j, cells):
        win_coarse[0, j] = row_before(cells).astype(bf16)
        win_coarse[1, j] = cells.astype(bf16)
        win_coarse[2, j] = row_after(cells).astype(bf16)

    def coarse_body(j, past):
        h = down[j] * 0.5
        coarse = h * jnp.tanh(h) + h
        write_coarse(j, jnp.where(low_lanes, past, coarse))
        return coarse

    past = lax.fori_loop(0, PAIRS, coarse_body, jnp.zeros((HALF, LANES), f32), unroll=4)
    write_coarse(PAIRS, jnp.where(low_lanes, past, 0.0))

    operand = window_operand(win_level, range(4))
    coarse_operand = window_operand(win_coarse, (0, 1, 1, 2))
    y = matmul(operand, w_up[: 16 * C, :]) + matmul(coarse_operand, w_up[16 * C :, :])
    for a in range(2):
        v = y[:, a * LANES : (a + 1) * LANES] + biases[3:4, :]
        image[:, pl.ds(a, HALF, stride=2), :] = tiles_of(v) + level[a]
    store_strips(member, image, out)


def slope_twice(h):
    t = jnp.tanh(h)
    return (1.0 + t) + h * (1.0 - t * t)


def backward_kernel(count, *refs):
    member_ref = refs[0]
    cot_strips = refs[1 : 1 + count]
    frame_strips = refs[1 + count : 1 + 2 * count]
    styles, stats, middle, down, w_up, w_down, w_two, w_one = refs[1 + 2 * count : 9 + 2 * count]
    out = refs[9 + 2 * count : 9 + 3 * count]
    tile_out, tile_level, tile_mid, coarse_pairs, pieces, bias_sums = refs[9 + 3 * count : 15 + 3 * count]
    image, level_grad, pre_grad, windows, coarse_below, row_sums = refs[15 + 3 * count :]
    member = member_ref[0]
    tile_out, tile_level, tile_mid, coarse_pairs = (ref.at[0] for ref in (tile_out, tile_level, tile_mid, coarse_pairs))
    middle, down = middle.at[0], down.at[0]
    low_lanes = lane_ids((HALF, LANES)) < C

    load_strips(member, cot_strips, image)

    def add_rows(j, s):
        return s + image[j]

    sums = lax.fori_loop(0, PAIRS, add_rows, jnp.zeros((H, LANES), f32), unroll=4)
    bias_up_sum = both_parities(total(sums))

    def out_tile(parity, j):
        x = parity_rows(image, parity, j)
        tile_out[parity, j] = x.astype(bf16)
        return x

    build_windows(windows, out_tile)
    y = matmul(window_operand(windows, range(4)), w_up[...])
    for a in range(2):
        level_grad[a] = tiles_of(y[:, (2 + a) * LANES : (3 + a) * LANES]) + image[:, pl.ds(a, HALF, stride=2), :]
    coarse = y[:, :LANES] + y[:, LANES : 2 * LANES]
    pre_grad[0] = tiles_of(coarse)

    def coarse_body(t, carry):
        after, sums = carry
        j = PAIRS - 1 - t
        g = pre_grad[0, j]
        g = g + swap_halves(g)
        h = down[j] * 0.5
        d = 0.5 * g * slope_twice(h)
        pair = jnp.where(low_lanes, d, after)
        coarse_pairs[j] = pair.astype(bf16)
        coarse_below[j] = row_after(pair).astype(bf16)
        return d, sums + d

    zero = jnp.zeros((HALF, LANES), f32)
    _, sums = lax.fori_loop(0, PAIRS, coarse_body, (zero, zero), unroll=4)
    bias_down_sum = jnp.broadcast_to(total(sums), (8, LANES))

    operand = jnp.concatenate(
        [coarse_pairs[...].reshape(BLOCK, LANES), coarse_below[...].reshape(BLOCK, LANES)], axis=1
    )
    y = matmul(operand, w_down[...])
    sums = jnp.zeros((1, LANES), f32)
    for a in range(2):
        v = y[:, a * LANES : (a + 1) * LANES] + level_grad[a].reshape(BLOCK, LANES)
        sums = sums + total(v)
        level_grad[a] = tiles_of(v)
    bias_two_sum = both_parities(sums)

    def level_tile(parity, j):
        x = level_grad[parity, j]
        tile_level[parity, j] = x.astype(bf16)
        return x

    build_windows(windows, level_tile)

    def norm_slopes(y, value, k):
        average, inverse = stats[0, 2 * k : 2 * k + 1, :], stats[0, 2 * k + 1 : 2 * k + 2, :]
        gain = inverse * styles[0, 2 * k : 2 * k + 1, :]
        half_gain = 0.5 * gain
        half_shift = 0.5 * (styles[0, 2 * k + 1 : 2 * k + 2, :] - average * gain)
        scale_sum = jnp.zeros((1, LANES), f32)
        shift_sum = jnp.zeros((1, LANES), f32)
        for a in range(2):
            v = value(a)
            g = 0.5 * y[:, a * LANES : (a + 1) * LANES] * slope_twice(v * half_gain + half_shift)
            pre_grad[a] = tiles_of(g)
            shift_sum = shift_sum + total(g)
            scale_sum = scale_sum + total(g * ((v - average) * inverse))
        scale_sum, shift_sum = both_parities(scale_sum), both_parities(shift_sum)
        factor = styles[0, 2 * k : 2 * k + 1, :]
        center = group_sum(factor * shift_sum) / MEMBERS
        tilt = group_sum(factor * scale_sum) / MEMBERS
        return scale_sum, shift_sum, gain, (inverse * center)[0:1], (inverse * tilt)[0:1], average, inverse

    y = matmul(window_operand(windows, range(4)), w_two[...])
    scale_two, shift_two, gain, center, tilt, average, inverse = norm_slopes(
        y, lambda a: middle[a].reshape(BLOCK, LANES), 1
    )
    tilt_slope = tilt * inverse
    constant = tilt_slope * average - center

    def mid_tile(parity, j):
        x = pre_grad[parity, j] * gain + (constant - middle[parity, j] * tilt_slope)
        tile_mid[parity, j] = x.astype(bf16)
        row_sums[...] += x
        return x

    row_sums[...] = jnp.zeros_like(row_sums)
    build_windows(windows, mid_tile)
    bias_one_sum = both_parities(total(row_sums[...]))

    load_strips(member, frame_strips, image)
    y = matmul(window_operand(windows, range(4)), w_one[...])
    scale_one, shift_one, gain_one, center_one, tilt_one, average_one, inverse_one = norm_slopes(
        y, lambda a: image[:, pl.ds(a, HALF, stride=2), :].reshape(BLOCK, LANES), 0
    )
    slope_one = tilt_one * inverse_one
    constant_one = slope_one * average_one - center_one

    def frame_body(j, carry):
        for parity in range(2):
            x = parity_rows(image, parity, j)
            g = pre_grad[parity, j] * gain_one + (constant_one - x * slope_one) + level_grad[parity, j]
            image[j, pl.ds(parity, HALF, stride=2), :] = g
        return carry

    lax.fori_loop(0, PAIRS, frame_body, 0, unroll=4)
    store_strips(member, image, out)
    for k, value in enumerate((scale_one, shift_one, scale_two, shift_two)):
        pieces[0, k : k + 1, :] = value[0:1]
    pieces[0, 4:8, :] = jnp.zeros((4, LANES), f32)
    for k, value in enumerate((bias_one_sum, bias_two_sum, bias_down_sum, bias_up_sum)):
        bias_sums[0, k : k + 1, :] = value[0:1]
    bias_sums[0, 4:8, :] = jnp.zeros((4, LANES), f32)


def outer(left, right):
    return lax.dot_general(left, right, (((0,), (0,)), ((), ())), preferred_element_type=f32)


def accumulate(wins, tiles, sums):
    win_one, win_two, win_level, win_coarse = wins
    tile_out, tile_level, tile_mid, coarse_pairs = tiles
    sum_one, sum_two, sum_down, sum_up = sums

    @pl.when(pl.program_id(0) == 0)
    def _():
        for ref in sums:
            ref[...] = jnp.zeros_like(ref)

    def blocks(tiles):
        return jnp.concatenate([tiles[0, a].reshape(BLOCK, LANES) for a in range(2)], axis=1)

    level_operand = window_operand(win_level.at[0], range(4))
    out_blocks = blocks(tile_out)
    sum_up[16 * C :, :] += outer(window_operand(win_coarse.at[0], (0, 1, 1, 2)), out_blocks)
    sum_up[: 16 * C, :] += outer(level_operand, out_blocks)
    sum_down[...] += outer(level_operand[:, : 6 * LANES], coarse_pairs[0].reshape(BLOCK, LANES))
    sum_two[...] += outer(window_operand(win_two.at[0], range(4)), blocks(tile_level))
    sum_one[...] += outer(window_operand(win_one.at[0], range(4)), blocks(tile_mid))


def fold(sums, base, p, q):
    halves = []
    for b in range(2):
        rows = [base + ((a + p) * 4 + b + q) * C for a in range(2)]
        halves.append(sums[rows[0] : rows[0] + C, :LANES] + sums[rows[1] : rows[1] + C, LANES:])
    return halves[0] + swap_halves(halves[1])


def weight_kernel(*refs):
    wins, tiles, grads, sums = refs[:4], refs[4:8], refs[8:12], refs[12:]
    g_one, g_two, g_down, g_up = grads
    sum_one, sum_two, sum_down, sum_up = sums
    accumulate(wins, tiles, sums)

    @pl.when(pl.program_id(0) == pl.num_programs(0) - 1)
    def _():
        for p in range(3):
            for q in range(3):
                at = (3 * p + q) * C
                g_one[at : at + C, :] = fold(sum_one, 0, p, q)[:, :C]
                g_two[at : at + C, :] = fold(sum_two, 0, p, q)[:, :C]
                g_up[2 * at : 2 * at + C, :] = fold(sum_up, 16 * C, p, q)[:, :C]
                g_up[2 * at + C : 2 * at + 2 * C, :] = fold(sum_up, 0, p, q)[:, :C]
                place = (p * 4 + q) * C
                g_down[at : at + C, :] = sum_down[place : place + C, :C]


PARTS = 16


def message_kernel(count, rows, *refs):
    where_ref, wins, tiles = refs[0], refs[1:5], refs[5:9]
    pieces, bias_sums = refs[9:11]
    outs = refs[11 : 11 + count]
    sums = refs[11 + count : 15 + count]
    g_pair, g_up, g_down, small = refs[15 + count :]
    sum_one, sum_two, sum_down, sum_up = sums
    accumulate(wins, tiles, sums)

    @pl.when(pl.program_id(0) == pl.num_programs(0) - 1)
    def _():
        low_lanes = lane_ids((C, LANES)) < C
        for p in range(3):
            for q in range(3):
                at = (3 * p + q) * C
                g_pair[at : at + C, :] = jnp.where(
                    low_lanes, fold(sum_one, 0, p, q), swap_halves(fold(sum_two, 0, p, q))
                )
                g_up[2 * at : 2 * at + C, :] = fold(sum_up, 16 * C, p, q)
                g_up[2 * at + C : 2 * at + 2 * C, :] = fold(sum_up, 0, p, q)
                place = (p * 4 + q) * C
                g_down[at : at + C, :] = sum_down[place : place + C, :]
        frames = pieces.shape[0]
        small[...] = jnp.zeros_like(small)
        total_bias = bias_sums[0, 0:4, :]
        for f in range(frames):
            small[4 * f : 4 * f + 4, :] = pieces[f, 0:4, :]
            if f > 0:
                total_bias = total_bias + bias_sums[f, 0:4, :]
        small[4 * frames : 4 * frames + 4, :] = total_bias
        exact = small[...]
        high = exact.astype(bf16).astype(f32)
        rest = exact - high
        mid = rest.astype(bf16).astype(f32)
        parts = (high, mid, rest - mid)
        low_lanes = lane_ids((rows, LANES)) < C
        nothing = jnp.zeros((rows - 3 * PARTS, LANES), f32)
        sent = jnp.concatenate([*parts, nothing], axis=0)
        kept = jnp.concatenate([exact, jnp.zeros((2 * PARTS, LANES), f32), nothing], axis=0)
        for offset in range(count):
            start = pl.multiple_of(seq_owner(where_ref[0], offset) * rows, 8)
            block = jnp.concatenate(
                [
                    g_pair[pl.ds(start, rows), :],
                    jnp.where(
                        low_lanes,
                        g_up[pl.ds(pl.multiple_of(2 * start, 8), rows), :],
                        swap_halves(g_up[pl.ds(pl.multiple_of(2 * start + rows, 8), rows), :]),
                    ),
                    jnp.where(low_lanes, g_down[pl.ds(start, rows), :], kept if offset == 0 else sent),
                ],
                axis=0,
            )
            outs[offset][...] = block.astype(outs[offset].dtype)


def reduce_kernel(count, rows, cells, frames, *refs):
    where_ref, own = refs[:2]
    messages = refs[2 : 1 + count]
    packs = refs[1 + count : 1 + 2 * count]
    act_table, noise_table, ada_one, ada_two, out, pieces_one, pieces_two, table = refs[1 + 2 * count :]
    place, member = where_ref[0], where_ref[1]
    taken = 4 * frames
    bias = jnp.zeros((4, LANES), f32)
    sums = own[...]
    lanes = lane_ids((1, LANES))
    low_lanes = lanes < C
    hot = []
    for offset in range(count):
        if offset == 0:
            small = sums[2 * rows : 2 * rows + PARTS]
        else:
            message = messages[offset - 1][...].astype(f32)
            sums = sums + message
            first = 2 * rows
            small = (
                message[first : first + PARTS]
                + message[first + PARTS : first + 2 * PARTS]
                + message[first + 2 * PARTS : first + 3 * PARTS]
            )
        turned = swap_halves(small)
        bias = bias + small[taken : taken + 4]
        ids = packs[offset][2 * rows + ID_ROW : 2 * rows + ID_ROW + 8, :].astype(f32)
        for f in range(frames):
            at = offset * frames + f
            for k, ref in ((0, pieces_one), (2, pieces_two)):
                ref[at : at + 1, :] = jnp.where(low_lanes, turned[4 * f + k : 4 * f + k + 1], small[4 * f + k + 1 : 4 * f + k + 2])
            mine = jnp.where(lane_ids(ids.shape) == C + member * frames + f, ids, 0.0)
            mine = jnp.sum(mine, axis=1, keepdims=True)
            action, noise, valid = mine[0:1], mine[1:2], mine[2:3]
            place_at = lanes.astype(f32)
            hot.append(jnp.where(place_at == action + ACT_ROW, valid, 0.0) + jnp.where(place_at == noise + NOISE_ROW, 1.0, 0.0))
    hot = jnp.concatenate(hot, axis=0)[:, :TABLE_ROWS]
    table[...] = jnp.zeros_like(table)
    table[ACT_ROW : ACT_ROW + NACT, :] = act_table[...].astype(f32)
    table[NOISE_ROW : NOISE_ROW + NLEV, :] = noise_table[...].astype(f32)
    embed = matmul(hot.astype(bf16), table[...].astype(bf16))

    def exact(left, right, dims):
        return lax.dot_general(left, right, (dims, ((), ())), precision=precise, preferred_element_type=f32)

    one, two = pieces_one[...], pieces_two[...]
    at = 3 * rows
    out[:at, :] = sums
    out[at : at + cells, :] = exact(embed, one, ((0,), (0,)))
    out[at + cells : at + 2 * cells, :] = exact(embed, two, ((0,), (0,)))
    embed_grad = exact(one, ada_one[...].astype(f32), ((1,), (1,))) + exact(two, ada_two[...].astype(f32), ((1,), (1,)))
    at = at + 2 * cells
    out[at : at + TABLE_ROWS, :] = jnp.zeros((TABLE_ROWS, LANES), f32)
    out[at : at + TABLE_ROWS, :cells] = exact(hot, embed_grad, ((0,), (0,)))
    at = at + TABLE_ROWS
    bias = jnp.concatenate([bias, jnp.zeros((4, LANES), f32)], axis=0)
    width = C // count
    out[at : at + 8, :] = pltpu.roll(bias, (C - place * width) % LANES, axis=1)


def finish_kernel(rows, cells, first, second, *outs):
    act_grad, noise_grad, ada_one, ada_two, g_one, g_two, g_down, g_up = outs[:8]
    bias_grads = outs[8:12]
    sums = first[...] + second[...]

    def turn(block):
        return jnp.concatenate([block, jnp.zeros((LANES - rows, LANES), f32)], axis=0).T[:, :rows]

    pair, halves, down = (turn(sums[k * rows : (k + 1) * rows]) for k in range(3))
    g_one[...] = pair[:C]
    g_two[...] = pair[C:]
    g_up[:, :rows] = halves[:C]
    g_up[:, rows:] = halves[C:]
    g_down[...] = down[:C]
    at = 3 * rows
    ada_one[...] = sums[at : at + cells]
    ada_two[...] = sums[at + cells : at + 2 * cells]
    at = at + 2 * cells
    act_grad[...] = sums[at + ACT_ROW : at + ACT_ROW + NACT, :cells]
    noise_grad[...] = sums[at + NOISE_ROW : at + NOISE_ROW + NLEV, :cells]
    at = at + TABLE_ROWS
    for k, ref in enumerate(bias_grads):
        ref[...] = sums[at + k : at + k + 1, : ref.shape[0]].reshape(ref.shape)


def write_operands(block, f_one, f_two, f_down, f_up, b_one, b_two, b_down, b_up):
    low_lanes = lane_ids((C, LANES)) < C
    zero = jnp.zeros((C, LANES), f32)

    def taps(name, base, step):
        plain, turned = {}, {}
        for p in range(3):
            for q in range(3):
                k = block(name, (3 * p + q) * step + base)
                plain[p, q] = k
                turned[p, q] = jnp.concatenate([k, k], axis=0).T[:C]
        return plain, turned

    def write_forward(ref, base, plain):
        for w in range(4):
            for p in range(3):
                tile = jnp.where(low_lanes, plain.get((p, w), zero), plain.get((p, w - 1), zero)).astype(bf16)
                for a in range(2):
                    at = base + ((a + p) * 4 + w) * C
                    ref[at : at + C, a * LANES : (a + 1) * LANES] = tile
            for a in range(2):
                for r in range(4):
                    if not 0 <= r - a < 3:
                        at = base + (r * 4 + w) * C
                        ref[at : at + C, a * LANES : (a + 1) * LANES] = zero.astype(bf16)

    def write_backward(ref, lane, turned):
        for w in range(4):
            for p in range(3):
                tile = jnp.where(low_lanes, turned.get((p, 2 - w), zero), turned.get((p, 3 - w), zero)).astype(bf16)
                for a in range(2):
                    at = ((a + 2 - p) * 4 + w) * C
                    ref[at : at + C, lane + a * LANES : lane + (a + 1) * LANES] = tile
            for a in range(2):
                for r in range(4):
                    if not 0 <= a + 2 - r < 3:
                        at = (r * 4 + w) * C
                        ref[at : at + C, lane + a * LANES : lane + (a + 1) * LANES] = zero.astype(bf16)

    for name, forward_ref, backward_ref in (("one", f_one, b_one), ("two", f_two, b_two)):
        plain, turned = taps(name, 0, C)
        write_forward(forward_ref, 0, plain)
        write_backward(backward_ref, 0, turned)
    plain, turned = taps("up", 0, 2 * C)
    write_forward(f_up, 16 * C, plain)
    write_backward(b_up, 0, turned)
    plain, turned = taps("up", C, 2 * C)
    write_forward(f_up, 0, plain)
    write_backward(b_up, 2 * LANES, turned)
    plain, turned = taps("down", 0, C)
    for p in range(3):
        for w in range(4):
            at = (p * 4 + w) * C
            f_down[at : at + C, :] = plain.get((p, w), zero).astype(bf16)
    for below in range(2):
        for right in range(2):
            at = (below * 2 + right) * C
            for a in range(2):
                p = {(0, 0): 1, (0, 1): 2, (1, 1): 0}.get((below, a))
                first, second = zero, zero
                if p is not None:
                    first = turned[p, 1] if right == 0 else zero
                    second = turned[p, 2] if right == 0 else turned[p, 0]
                b_down[at : at + C, a * LANES : (a + 1) * LANES] = jnp.where(low_lanes, first, second).astype(bf16)


def expand_kernel(conv_one, conv_two, down_kernel, up_kernel, *outs):
    kernels = {"one": conv_one, "two": conv_two, "down": down_kernel, "up": up_kernel}

    def block(name, row):
        k = kernels[name][row : row + C, :].astype(f32)
        return jnp.concatenate([k, k], axis=1)

    write_operands(block, *outs)


ACT_ROW, NOISE_ROW, TABLE_ROWS = 0, 24, 56
BIAS_ROW, ID_ROW = 56, 64


def pack_sizes(rows, cells):
    return 3 * rows, 3 * rows + 2 * cells, -(-(3 * rows + 2 * cells) // 16) * 16


def turned(values):
    wide = jnp.concatenate([values, jnp.zeros((C, LANES - values.shape[1]), f32)], axis=1)
    return jnp.concatenate([wide, jnp.zeros((C, LANES), f32)], axis=0).T[: values.shape[1]]


def pack_kernel(*refs):
    actions, noise_ids, valid, conv_one, conv_two, down_kernel, up_kernel, ada_one, ada_two = refs[:9]
    act_table, noise_table = refs[9:11]
    biases = refs[11:15]
    out, work = refs[15:]
    rows, cells = conv_one.shape[1], ada_one.shape[0]
    style_at, end, _ = pack_sizes(rows, cells)
    wide = lambda ref: ref[...].astype(f32)
    low_lanes = lane_ids((rows, LANES)) < C
    up = wide(up_kernel)
    work[...] = jnp.zeros_like(work)
    for at, low, high in (
        (0, turned(wide(conv_one)), turned(wide(conv_two))),
        (rows, turned(up[:, :rows]), turned(up[:, rows:])),
    ):
        work[at : at + rows, :] = jnp.where(low_lanes, low, swap_halves(high))
    work[2 * rows : 3 * rows, :] = turned(wide(down_kernel))
    extra = 2 * rows
    for at, ref in ((ACT_ROW, act_table), (NOISE_ROW, noise_table)):
        size = ref.shape
        work[extra + at : extra + at + size[0], C : C + size[1]] = wide(ref)
    for k, ref in enumerate(biases):
        at = extra + BIAS_ROW + k
        work[at : at + 1, C : C + ref.shape[0]] = wide(ref).reshape(1, ref.shape[0])
    lanes = lane_ids((1, LANES))
    for k, ref in enumerate((actions, noise_ids, valid)):
        line = jnp.zeros((1, LANES), jnp.int32)
        for f in range(ref.shape[0]):
            line = jnp.where(lanes == C + f, ref[f], line)
        at = extra + ID_ROW + k
        work[at : at + 1, C:] = line.astype(f32)[:, C:]
    work[style_at : style_at + cells, :] = wide(ada_one)
    work[style_at + cells : end, :] = wide(ada_two)
    out[...] = work[...].astype(bf16)


def seq_owner(place, offset):
    return place ^ offset


def prepare_kernel(count, rows, cells, *refs):
    where_ref, actions, noise_ids, valid = refs[:4]
    packs = refs[4 : 4 + count]
    outs = refs[4 + count : 12 + count]
    styles, biases = refs[12 + count : 14 + count]
    work_pair, work_up, work_down, work_one, work_two, work_table = refs[14 + count :]
    place, member, frames = where_ref[0], where_ref[1], styles.shape[0]
    style_at, _, _ = pack_sizes(rows, cells)
    bias_rows = jnp.zeros(SMALL, f32)
    for offset, ref in enumerate(packs):
        pack = ref[...].astype(f32)
        owner = seq_owner(place, offset)
        start = pl.multiple_of(owner * rows, 8)
        work_pair[pl.ds(start, rows), :] = pack[:rows]
        halves = pack[rows : 2 * rows]
        work_up[pl.ds(2 * start, rows), :] = halves
        work_up[pl.ds(pl.multiple_of(2 * start + rows, 8), rows), :] = swap_halves(halves)
        extra = pack[2 * rows : 3 * rows]
        work_down[pl.ds(start, rows), :] = extra
        work_one[offset * cells : (offset + 1) * cells, :] = pack[style_at : style_at + cells]
        work_two[offset * cells : (offset + 1) * cells, :] = pack[style_at + cells : style_at + 2 * cells]
        lane = (offset * cells) % LANES
        tables = pltpu.roll(extra[:TABLE_ROWS], (lane - C) % LANES, axis=1)
        kept = (lane_ids(tables.shape) >= lane) & (lane_ids(tables.shape) < lane + cells)
        column = offset * cells // LANES
        tables = jnp.where(kept, tables, 0.0)
        if lane == 0:
            work_table[column] = tables
        else:
            work_table[column] += tables
        slots = extra[BIAS_ROW : BIAS_ROW + 8]
        width = C // count
        slots = jnp.where((lane_ids(SMALL) >= C) & (lane_ids(SMALL) < C + width), slots, 0.0)
        bias_rows = bias_rows + pltpu.roll(slots, (owner * width + C) % LANES, axis=1)
    biases[...] = bias_rows + swap_halves(bias_rows)

    lanes = lane_ids((8, LANES))
    row_at = lax.broadcasted_iota(jnp.int32, (8, LANES), 0)
    hot = jnp.zeros((8, LANES), f32)
    for f in range(frames):
        at = member * frames + f
        here = jnp.where(lanes == actions[at] + ACT_ROW, valid[at], 0) + jnp.where(lanes == noise_ids[at] + NOISE_ROW, 1, 0)
        hot = jnp.where(row_at == f, here.astype(f32), hot)
    hot = hot[:, :TABLE_ROWS].astype(bf16)
    embed = jnp.concatenate([matmul(hot, work_table[k].astype(bf16)) for k in range(work_table.shape[0])], axis=1)
    low_lanes = lanes < C
    for k, work in enumerate((work_one, work_two)):
        style = jnp.dot(embed, work[...], precision=precise, preferred_element_type=f32)
        other = swap_halves(style)
        scale = 1.0 + jnp.where(low_lanes, style, other)
        shift = jnp.where(low_lanes, other, style)
        for f in range(frames):
            styles[f, 2 * k : 2 * k + 1, :] = scale[f : f + 1]
            styles[f, 2 * k + 1 : 2 * k + 2, :] = shift[f : f + 1]
    for f in range(frames):
        styles[f, 4:8, :] = jnp.zeros((4, LANES), f32)

    def block(name, row):
        work = {"one": work_pair, "two": work_pair, "down": work_down, "up": work_up}[name]
        k = work[row : row + C, :]
        low = lane_ids(k.shape) < C
        if name == "two":
            return jnp.where(low, swap_halves(k), k)
        return jnp.where(low, k, swap_halves(k))

    write_operands(block, *outs)


def shape(dims, kind):
    return jax.ShapeDtypeStruct(dims, kind)


def whole(dims):
    return pl.BlockSpec(dims, lambda f: (0,) * len(dims))


def per_frame(dims):
    return pl.BlockSpec((1,) + dims, lambda f: (f,) + (0,) * len(dims))


def strip_specs(count, strip):
    return [pl.BlockSpec((1, strip, W * C), lambda f: (f, 0, 0))] * count


SMALL = (8, LANES)
WINDOWS = (4, PAIRS + 1, HALF, LANES)
COARSE_WINDOWS = (3, PAIRS + 1, HALF, LANES)
TILES = (2, PAIRS, HALF, LANES)
COARSE = (PAIRS, HALF, LANES)
IMAGE = (PAIRS, H, LANES)
KEYS = 16 * C


def params():
    return pltpu.CompilerParams(vmem_limit_bytes=VMEM_LIMIT)


def cost(macs, moved):
    return pl.CostEstimate(flops=2 * macs, bytes_accessed=moved, transcendentals=0)


def expand(conv_one, conv_two, down_kernel, up_kernel):
    vmem = pl.BlockSpec(memory_space=pltpu.VMEM)
    return pl.pallas_call(
        expand_kernel,
        in_specs=[vmem] * 4,
        out_specs=[vmem] * 8,
        out_shape=[
            shape((KEYS, 2 * LANES), bf16),
            shape((KEYS, 2 * LANES), bf16),
            shape((6 * LANES, LANES), bf16),
            shape((2 * KEYS, 2 * LANES), bf16),
            shape((KEYS, 2 * LANES), bf16),
            shape((KEYS, 2 * LANES), bf16),
            shape((2 * LANES, 2 * LANES), bf16),
            shape((KEYS, 4 * LANES), bf16),
        ],
        compiler_params=params(),
        name="expand",
    )(conv_one, conv_two, down_kernel, up_kernel)


def forward(member, strips, styles, biases, w_one, w_two, w_down, w_up):
    count = len(strips)
    frames, strip, _ = strips[0].shape
    return pl.pallas_call(
        lambda *refs: forward_kernel(count, *refs),
        grid=(frames,),
        in_specs=[pl.BlockSpec(memory_space=pltpu.SMEM)]
        + strip_specs(count, strip)
        + [per_frame(SMALL), whole(SMALL)]
        + [whole(w.shape) for w in (w_one, w_two, w_down, w_up)],
        out_specs=strip_specs(count, strip)
        + [per_frame(d) for d in (WINDOWS, WINDOWS, WINDOWS, COARSE_WINDOWS, TILES, COARSE, SMALL)],
        out_shape=[shape((frames, strip, W * C), bf16)] * count
        + [
            shape((frames,) + WINDOWS, bf16),
            shape((frames,) + WINDOWS, bf16),
            shape((frames,) + WINDOWS, bf16),
            shape((frames,) + COARSE_WINDOWS, bf16),
            shape((frames,) + TILES, f32),
            shape((frames,) + COARSE, f32),
            shape((frames,) + SMALL, f32),
        ],
        scratch_shapes=[pltpu.VMEM(IMAGE, f32), pltpu.VMEM(TILES, f32)],
        compiler_params=params(),
        cost_estimate=cost(frames * BLOCK * KEYS * 2 * LANES * 5, frames * (14 << 20)),
        name="forward",
    )(member, *strips, styles, biases, w_one, w_two, w_down, w_up)


def backward(member, cot_strips, frame_strips, styles, stats, middle, down, w_up, w_down, w_two, w_one):
    count = len(cot_strips)
    frames, strip, _ = cot_strips[0].shape
    return pl.pallas_call(
        lambda *refs: backward_kernel(count, *refs),
        grid=(frames,),
        in_specs=[pl.BlockSpec(memory_space=pltpu.SMEM)]
        + strip_specs(2 * count, strip)
        + [per_frame(d) for d in (SMALL, SMALL, TILES, COARSE)]
        + [whole(w.shape) for w in (w_up, w_down, w_two, w_one)],
        out_specs=strip_specs(count, strip)
        + [per_frame(d) for d in (TILES, TILES, TILES, COARSE, SMALL, SMALL)],
        out_shape=[shape((frames, strip, W * C), bf16)] * count
        + [
            shape((frames,) + TILES, bf16),
            shape((frames,) + TILES, bf16),
            shape((frames,) + TILES, bf16),
            shape((frames,) + COARSE, bf16),
            shape((frames,) + SMALL, f32),
            shape((frames,) + SMALL, f32),
        ],
        scratch_shapes=[
            pltpu.VMEM(IMAGE, f32),
            pltpu.VMEM(TILES, f32),
            pltpu.VMEM(TILES, f32),
            pltpu.VMEM(WINDOWS, bf16),
            pltpu.VMEM(COARSE, bf16),
            pltpu.VMEM((HALF, LANES), f32),
        ],
        compiler_params=params(),
        cost_estimate=cost(frames * BLOCK * KEYS * 2 * LANES * 5, frames * (10 << 20)),
        name="backward",
    )(member, *cot_strips, *frame_strips, styles, stats, middle, down, w_up, w_down, w_two, w_one)


def weight_grads(win_one, win_two, win_level, win_coarse, tile_out, tile_level, tile_mid, coarse_pairs):
    frames = win_one.shape[0]
    return pl.pallas_call(
        weight_kernel,
        grid=(frames,),
        in_specs=[
            per_frame(d) for d in (WINDOWS, WINDOWS, WINDOWS, COARSE_WINDOWS, TILES, TILES, TILES, COARSE)
        ],
        out_specs=[whole((9 * C, C)), whole((9 * C, C)), whole((9 * C, C)), whole((18 * C, C))],
        out_shape=[shape((9 * C, C), f32)] * 3 + [shape((18 * C, C), f32)],
        scratch_shapes=[
            pltpu.VMEM((KEYS, 2 * LANES), f32),
            pltpu.VMEM((KEYS, 2 * LANES), f32),
            pltpu.VMEM((6 * LANES, LANES), f32),
            pltpu.VMEM((2 * KEYS, 2 * LANES), f32),
        ],
        compiler_params=params(),
        cost_estimate=cost(frames * BLOCK * KEYS * 2 * LANES * 5, frames * (6 << 20)),
        name="weights",
    )(win_one, win_two, win_level, win_coarse, tile_out, tile_level, tile_mid, coarse_pairs)


def in_vmem():
    return pl.BlockSpec(memory_space=pltpu.VMEM)


def in_smem():
    return pl.BlockSpec(memory_space=pltpu.SMEM)


def pack(actions, noise_ids, valid, conv_one, conv_two, down_kernel, up_kernel, ada_one, ada_two, act_table, noise_table, *biases):
    _, _, size = pack_sizes(conv_one.shape[0], ada_one.shape[0])
    kernels = [kernel.T for kernel in (conv_one, conv_two, down_kernel, up_kernel)]
    args = (*kernels, ada_one, ada_two, act_table, noise_table, *biases)
    return pl.pallas_call(
        pack_kernel,
        in_specs=[in_smem()] * 3 + [in_vmem()] * len(args),
        out_specs=in_vmem(),
        out_shape=shape((size, LANES), bf16),
        scratch_shapes=[pltpu.VMEM((size, LANES), f32)],
        compiler_params=params(),
        name="pack",
    )(actions, noise_ids, valid, *args)


OPERANDS = (
    (KEYS, 2 * LANES),
    (KEYS, 2 * LANES),
    (6 * LANES, LANES),
    (2 * KEYS, 2 * LANES),
    (KEYS, 2 * LANES),
    (KEYS, 2 * LANES),
    (2 * LANES, 2 * LANES),
    (KEYS, 4 * LANES),
)


def prepare(where, actions, noise_ids, valid, packs, rows, cells, frames):
    count = len(packs)
    return pl.pallas_call(
        lambda *refs: prepare_kernel(count, rows, cells, *refs),
        in_specs=[in_smem()] * 4 + [in_vmem()] * count,
        out_specs=[in_vmem()] * 10,
        out_shape=[shape(d, bf16) for d in OPERANDS] + [shape((frames,) + SMALL, f32), shape(SMALL, f32)],
        scratch_shapes=[
            pltpu.VMEM((9 * C, LANES), f32),
            pltpu.VMEM((18 * C, LANES), f32),
            pltpu.VMEM((9 * C, LANES), f32),
            pltpu.VMEM((count * cells, LANES), f32),
            pltpu.VMEM((count * cells, LANES), f32),
            pltpu.VMEM((count * cells // LANES, TABLE_ROWS, LANES), f32),
        ],
        compiler_params=params(),
        name="prepare",
    )(where, actions, noise_ids, valid, *packs)


def weight_messages(where, wins, tiles, pieces, bias_sums, count, rows):
    frames = pieces.shape[0]
    return pl.pallas_call(
        lambda *refs: message_kernel(count, rows, *refs),
        grid=(frames,),
        in_specs=[in_smem()]
        + [per_frame(d) for d in (WINDOWS, WINDOWS, WINDOWS, COARSE_WINDOWS, TILES, TILES, TILES, COARSE)]
        + [whole((frames,) + SMALL)] * 2,
        out_specs=[whole((3 * rows, LANES))] * count,
        out_shape=[shape((3 * rows, LANES), f32)] + [shape((3 * rows, LANES), bf16)] * (count - 1),
        scratch_shapes=[
            pltpu.VMEM((KEYS, 2 * LANES), f32),
            pltpu.VMEM((KEYS, 2 * LANES), f32),
            pltpu.VMEM((6 * LANES, LANES), f32),
            pltpu.VMEM((2 * KEYS, 2 * LANES), f32),
            pltpu.VMEM((9 * C, LANES), f32),
            pltpu.VMEM((18 * C, LANES), f32),
            pltpu.VMEM((9 * C, LANES), f32),
            pltpu.VMEM((PARTS, LANES), f32),
        ],
        compiler_params=params(),
        cost_estimate=cost(frames * BLOCK * KEYS * 2 * LANES * 5, frames * (6 << 20)),
        name="weights",
    )(where, *wins, *tiles, pieces, bias_sums)


def reduce_messages(where, own, messages, packs, act_table, noise_table, ada_one, ada_two, rows, cells, frames):
    count = len(packs)
    return pl.pallas_call(
        lambda *refs: reduce_kernel(count, rows, cells, frames, *refs),
        in_specs=[in_smem()] + [in_vmem()] * (2 * count + 4),
        out_specs=in_vmem(),
        out_shape=shape((3 * rows + 2 * cells + TABLE_ROWS + 8, LANES), f32),
        scratch_shapes=[
            pltpu.VMEM((count * frames, LANES), f32),
            pltpu.VMEM((count * frames, LANES), f32),
            pltpu.VMEM((TABLE_ROWS, cells), f32),
        ],
        compiler_params=params(),
        name="reduce",
    )(where, own, *messages, *packs, act_table, noise_table, ada_one, ada_two)


def finish(first, second, rows, cells, width):
    act_grad, noise_grad, one, two, *rest = pl.pallas_call(
        lambda *refs: finish_kernel(rows, cells, *refs),
        in_specs=[in_vmem()] * 2,
        out_specs=[in_vmem()] * 12,
        out_shape=[
            shape((NACT, cells), f32),
            shape((NLEV, cells), f32),
            shape((cells, LANES), f32),
            shape((cells, LANES), f32),
            shape((C, rows), f32),
            shape((C, rows), f32),
            shape((C, rows), f32),
            shape((C, 2 * rows), f32),
        ]
        + [shape((width,), f32)] * 4,
        compiler_params=params(),
        name="finish",
    )(first, second)
    return (act_grad, noise_grad, one, two, *[grad.T for grad in rest[:4]], *rest[4:])


def collect_kernel(member_ref, *refs):
    strips, out = refs[:-1], refs[-1]
    for offset, strip in enumerate(strips):
        out[member_ref[0] ^ offset, 0] = strip[0].astype(out.dtype)


def return_strips(strips):
    return tuple(trade(strip, offset) for offset, strip in enumerate(strips))


def collect_strips(member_box, strips, kind):
    count = len(strips)
    frames, rows, columns = strips[0].shape
    whole_strips = pl.pallas_call(
        collect_kernel,
        grid=(frames,),
        in_specs=[in_smem()] + [pl.BlockSpec((1, rows, columns), lambda f: (f, 0, 0))] * count,
        out_specs=pl.BlockSpec((count, 1, rows, columns), lambda f: (0, f, 0, 0)),
        out_shape=shape((count, frames, rows, columns), kind),
        compiler_params=params(),
        name="collect",
    )(member_box, *strips)
    return whole_strips.reshape(count * frames, rows, columns)


def twice(values):
    return jnp.concatenate([values, values], axis=-1)


def pad_small(rows):
    stacked = jnp.stack(rows, axis=-2)
    gaps = [(0, 0)] * (stacked.ndim - 2) + [(0, 8 - len(rows)), (0, 0)]
    return jnp.pad(stacked, gaps)


def trade(value, offset):
    if offset == 0:
        return value
    count = lax.axis_size("rows")
    return lax.ppermute(value, "rows", [(i, i ^ offset) for i in range(count)])


def spread_strips(array, member):
    count = lax.axis_size("rows")
    share = array.shape[0] // count
    return [
        trade(lax.dynamic_slice_in_dim(array, (member ^ offset) * share, share, axis=0), offset)
        for offset in range(count)
    ]


def seq_trade(value, offset):
    count = lax.axis_size("seq")
    return lax.ppermute(value, "seq", [(i, i ^ offset) for i in range(count)])


def layers(member_box, frame_strips, cot_strips, styles, bias_rows, operands):
    f_one, f_two, f_down, f_up, b_one, b_two, b_down, b_up = operands
    member = member_box[0]
    *out, win_one, win_two, win_level, win_coarse, middle, down, stats = forward(
        member_box, frame_strips, styles, bias_rows, f_one, f_two, f_down, f_up
    )
    out = return_strips(out)
    *grad_strips, tile_out, tile_level, tile_mid, coarse_pairs, pieces, bias_sums = backward(
        member_box, cot_strips, frame_strips, styles, stats, middle, down, b_up, b_down, b_two, b_one
    )
    grad_strips = return_strips(grad_strips)
    wins = (win_one, win_two, win_level, win_coarse)
    tiles = (tile_out, tile_level, tile_mid, coarse_pairs)
    pieces, out = lax.optimization_barrier((pieces, out))
    return out, grad_strips, wins, tiles, pieces, bias_sums


def local_direct(
    frames,
    cotangent,
    actions,
    noise_ids,
    valid,
    act_table,
    noise_table,
    ada_one,
    ada_two,
    conv_one,
    conv_two,
    down_kernel,
    up_kernel,
    bias_one,
    bias_two,
    bias_down,
    bias_up,
):
    member = lax.axis_index("rows").astype(jnp.int32)
    place = lax.axis_index("seq").astype(jnp.int32)
    count = lax.axis_size("seq")
    share = frames.shape[0] // lax.axis_size("rows")
    rows, cells, width = conv_one.shape[0], ada_one.shape[0], bias_one.shape[0]
    member_box = member.reshape(1)
    where = jnp.stack([place, member])
    packed = pack(
        actions,
        noise_ids,
        valid,
        conv_one,
        conv_two,
        down_kernel,
        up_kernel,
        ada_one,
        ada_two,
        act_table,
        noise_table,
        bias_one,
        bias_two,
        bias_down,
        bias_up,
    )
    packs = [packed] + [seq_trade(packed, offset) for offset in range(1, count)]
    frame_strips = spread_strips(frames, member)
    cot_strips = spread_strips(cotangent, member)
    *operands, styles, bias_rows = prepare(where, actions, noise_ids, valid, packs, rows, cells, share)
    out, grad_strips, wins, tiles, pieces, bias_sums = layers(
        member_box, frame_strips, cot_strips, styles, bias_rows, operands
    )
    own, *messages = weight_messages(where, wins, tiles, pieces, bias_sums, count, rows)
    messages, grad_strips = lax.optimization_barrier((messages, grad_strips))
    received = [seq_trade(messages[offset - 1], offset) for offset in range(1, count)]
    sums = reduce_messages(where, own, received, packs, act_table, noise_table, ada_one, ada_two, rows, cells, share)
    offset = 1
    while 2 * offset < lax.axis_size("rows"):
        sums = sums + trade(sums, offset)
        offset *= 2
    result = collect_strips(member_box, out, bf16)
    frames_grad = collect_strips(member_box, grad_strips, f32)
    return (result, frames_grad, *finish(sums, trade(sums, offset), rows, cells, width))


def local_general(
    frames,
    cotangent,
    actions,
    noise_ids,
    valid,
    act_table,
    noise_table,
    ada_one,
    ada_two,
    conv_one,
    conv_two,
    down_kernel,
    up_kernel,
    bias_one,
    bias_two,
    bias_down,
    bias_up,
):
    member = lax.axis_index("rows").astype(jnp.int32)
    share = frames.shape[0] // lax.axis_size("rows")
    member_box = member.reshape(1)

    def gathered(value, axis):
        return lax.all_gather(value, "seq", axis=axis, tiled=True)

    frame_strips = spread_strips(frames, member)
    cot_strips = spread_strips(cotangent, member)
    act_full = gathered(act_table, 1)
    noise_full = gathered(noise_table, 1)
    ada_full = gathered(jnp.concatenate([ada_one, ada_two], axis=1), 0).astype(f32)
    biases = gathered(jnp.stack([bias_one, bias_two, bias_down, bias_up]), 1).astype(f32)
    operands = expand(gathered(conv_one, 0), gathered(conv_two, 0), gathered(down_kernel, 0), gathered(up_kernel, 0))

    own = lambda ids: lax.dynamic_slice_in_dim(ids, member * share, share)
    own_actions, own_noise, own_valid = own(actions), own(noise_ids), own(valid)
    action_hot = (own_actions[:, None] == jnp.arange(NACT, dtype=jnp.int32)[None, :]).astype(f32) * own_valid[
        :, None
    ].astype(f32)
    noise_hot = (own_noise[:, None] == jnp.arange(NLEV, dtype=jnp.int32)[None, :]).astype(f32)
    embed = jnp.dot(action_hot, act_full.astype(f32), precision=precise) + jnp.dot(
        noise_hot, noise_full.astype(f32), precision=precise
    )
    style = jnp.dot(embed, ada_full, precision=precise)
    styles = pad_small(
        [
            twice(1.0 + style[:, :C]),
            twice(style[:, C : 2 * C]),
            twice(1.0 + style[:, 2 * C : 3 * C]),
            twice(style[:, 3 * C :]),
        ]
    )
    bias_rows = pad_small([twice(biases[k]) for k in range(4)])
    out, grad_strips, wins, tiles, pieces, bias_sums = layers(
        member_box, frame_strips, cot_strips, styles, bias_rows, operands
    )
    g_one, g_two, g_down, g_up = weight_grads(*wins, *tiles)
    result = collect_strips(member_box, out, bf16)
    frames_grad = collect_strips(member_box, grad_strips, f32)

    pieces_one = jnp.concatenate([pieces[:, 0, :C], pieces[:, 1, :C]], axis=1)
    pieces_two = jnp.concatenate([pieces[:, 2, :C], pieces[:, 3, :C]], axis=1)
    ada_one_grad = jnp.dot(embed.T, pieces_one, precision=precise)
    ada_two_grad = jnp.dot(embed.T, pieces_two, precision=precise)
    embed_grad = jnp.dot(jnp.concatenate([pieces_one, pieces_two], axis=1), ada_full.T, precision=precise)
    act_table_grad = jnp.dot(action_hot.T, embed_grad, precision=precise)
    noise_table_grad = jnp.dot(noise_hot.T, embed_grad, precision=precise)
    bias_total = jnp.sum(bias_sums, axis=0)[:4, :C]

    def shard(value, axis):
        return lax.psum_scatter(value, "seq", scatter_dimension=axis, tiled=True)

    shards = (
        shard(act_table_grad, 1),
        shard(noise_table_grad, 1),
        shard(ada_one_grad, 0),
        shard(ada_two_grad, 0),
        shard(g_one, 0),
        shard(g_two, 0),
        shard(g_down, 0),
        shard(g_up, 0),
        shard(bias_total[0], 0),
        shard(bias_total[1], 0),
        shard(bias_total[2], 0),
        shard(bias_total[3], 0),
    )
    return (result, frames_grad) + lax.psum(shards, "rows")


def fits_direct(mesh):
    count = mesh.shape["seq"]
    rows, cells = 9 * C // count, 256 // count
    return count in (2, 4, 8) and rows % 8 == 0 and rows >= ID_ROW + 8 and cells % 8 == 0 and mesh.shape["rows"] == 4


def solution(mesh):
    in_specs = (
        P("seq", "rows", None),
        P("seq", "rows", None),
        P("seq"),
        P("seq"),
        P("seq"),
        P(None, "seq"),
        P(None, "seq"),
        P("seq", None),
        P("seq", None),
        P("seq", None),
        P("seq", None),
        P("seq", None),
        P("seq", None),
        P("seq"),
        P("seq"),
        P("seq"),
        P("seq"),
    )
    out_specs = (
        P("seq", "rows", None),
        P("seq", "rows", None),
        P(None, "seq"),
        P(None, "seq"),
        P("seq", None),
        P("seq", None),
        P("seq", None),
        P("seq", None),
        P("seq", None),
        P("seq", None),
        P("seq"),
        P("seq"),
        P("seq"),
        P("seq"),
    )
    local = local_direct if fits_direct(mesh) else local_general
    return jax.shard_map(local, mesh=mesh, in_specs=in_specs, out_specs=out_specs, check_vma=False)
```

```python
import jax
import jax.numpy as jnp
from jax import lax
from jax.experimental import pallas as pl
from jax.experimental.pallas import tpu as pltpu
from jax.sharding import PartitionSpec as P

C = 64
NACT = 18
GROUPS = 32
NLEV = 32
H = 64
W = 64
PAIRS = W // 2
HALF = H // 2
LANES = 2 * C
BLOCK = PAIRS * HALF
MEMBERS = float(H * W * (C // GROUPS))
EPS = 1e-05

precise = lax.Precision.HIGHEST
f32 = jnp.float32
bf16 = jnp.bfloat16
VMEM_LIMIT = 24 * 2**20
VMEM_MOST = 60 * 2**20


def lane_ids(shape):
    return lax.broadcasted_iota(jnp.int32, shape, len(shape) - 1)


def swap_halves(x):
    return pltpu.roll(x, C, axis=x.ndim - 1)


def row_before(x):
    rows = lax.broadcasted_iota(jnp.int32, x.shape, 0)
    return jnp.where(rows == 0, 0.0, pltpu.roll(x, 1, axis=0))


def row_after(x):
    rows = lax.broadcasted_iota(jnp.int32, x.shape, 0)
    return jnp.where(rows == x.shape[0] - 1, 0.0, pltpu.roll(x, x.shape[0] - 1, axis=0))


def both_parities(x):
    x = jnp.broadcast_to(x, (8, LANES))
    return x + swap_halves(x)


def group_sum(x):
    even = lane_ids(x.shape) % 2 == 0
    return x + jnp.where(even, pltpu.roll(x, LANES - 1, axis=1), pltpu.roll(x, 1, axis=1))


def total(x):
    return jnp.sum(x, axis=0, keepdims=True)


def over_pairs(body, carry):
    for j in range(PAIRS):
        carry = body(j, carry)
    return carry


def build_windows(windows, tile):
    low_lanes = lane_ids((HALF, LANES)) < C
    zero = jnp.zeros((HALF, LANES), f32)

    def write(j, even, odd):
        windows[0, j] = row_before(odd).astype(bf16)
        windows[1, j] = even.astype(bf16)
        windows[2, j] = odd.astype(bf16)
        windows[3, j] = row_after(even).astype(bf16)

    def body(j, carry):
        even_past, odd_past = carry
        even = swap_halves(tile(0, j))
        odd = swap_halves(tile(1, j))
        write(j, jnp.where(low_lanes, even_past, even), jnp.where(low_lanes, odd_past, odd))
        return even, odd

    even, odd = over_pairs(body, (zero, zero))
    write(PAIRS, jnp.where(low_lanes, even, 0.0), jnp.where(low_lanes, odd, 0.0))


def window_operand(windows, slots):
    parts = []
    for slot in slots:
        for shift in (0, 1):
            parts.append(windows[slot, shift : shift + PAIRS].reshape(BLOCK, LANES))
    return jnp.concatenate(parts, axis=1)


def matmul(left, right):
    return jnp.dot(left, right, preferred_element_type=f32)


def tiles_of(y):
    return y.reshape(PAIRS, HALF, LANES)


def norm_stats(sums, squares):
    average = group_sum(both_parities(sums)) / MEMBERS
    variance = group_sum(both_parities(squares)) / MEMBERS - average * average
    return average, lax.rsqrt(variance + EPS)


def strip_start(member, offset, strip):
    return pl.multiple_of((member ^ offset) * strip, strip)


def load_strips(member, strips, f, image):
    for offset, strip in enumerate(strips):
        rows = strip.shape[1]
        start = strip_start(member, offset, rows)
        for j in range(PAIRS):
            image[j, pl.ds(start, rows), :] = strip[f, :, j * LANES : (j + 1) * LANES].astype(f32)


def store_strips(member, image, f, strips):
    for offset, strip in enumerate(strips):
        rows = strip.shape[1]
        start = strip_start(member, offset, rows)
        for j in range(PAIRS):
            strip[f, :, j * LANES : (j + 1) * LANES] = image[j, pl.ds(start, rows), :].astype(strip.dtype)


def parity_rows(image, parity, j):
    return image[j, pl.ds(parity, HALF, stride=2), :]


def staggered(steps):
    steps = list(steps)
    started = []
    while steps or started:
        if steps:
            started.append(steps.pop(0))
        for step in list(started):
            if next(step, "end") == "end":
                started.remove(step)


def forward_kernel(count, *refs):
    member_ref = refs[0]
    strips = refs[1 : 1 + count]
    styles, biases, w_one, w_two, w_down, w_up = refs[1 + count : 7 + count]
    out = refs[7 + count : 7 + 2 * count]
    outs = refs[7 + 2 * count : 14 + 2 * count]
    images, levels = refs[14 + 2 * count :]
    member = member_ref[0]
    low_lanes = lane_ids((HALF, LANES)) < C

    def frame(f):
        win_one, win_two, win_level, win_coarse, middle, down, stats = (ref.at[f] for ref in outs)
        image, level, style = images.at[f], levels.at[f], styles.at[f]
        load_strips(member, strips, f, image)

        def add_stats(j, carry):
            x = image[j]
            s, q = carry
            return s + x, q + x * x

        zero = jnp.zeros((H, LANES), f32)
        s, q = over_pairs(add_stats, (zero, zero))
        average_one, inverse_one = norm_stats(total(s), total(q))
        gain_one = inverse_one * style[0:1, :]
        half_gain = 0.5 * gain_one[0:1]
        half_shift = 0.5 * (style[1:2, :] - average_one[0:1] * gain_one[0:1])

        def act_one(parity, j):
            h = parity_rows(image, parity, j) * half_gain + half_shift
            return h * jnp.tanh(h) + h

        build_windows(win_one, act_one)
        yield
        y = matmul(window_operand(win_one, range(4)), w_one[...])
        sums = jnp.zeros((1, LANES), f32)
        squares = jnp.zeros((1, LANES), f32)
        for a in range(2):
            v = y[:, a * LANES : (a + 1) * LANES] + biases[0:1, :]
            sums = sums + total(v)
            squares = squares + total(v * v)
            middle[a] = tiles_of(v)
        yield
        average_two, inverse_two = norm_stats(sums, squares)
        stats[0:1, :] = average_one[0:1]
        stats[1:2, :] = inverse_one[0:1]
        stats[2:3, :] = average_two[0:1]
        stats[3:4, :] = inverse_two[0:1]
        stats[4:8, :] = jnp.zeros((4, LANES), f32)
        gain_two = inverse_two * style[2:3, :]
        half_gain_two = 0.5 * gain_two[0:1]
        half_shift_two = 0.5 * (style[3:4, :] - average_two[0:1] * gain_two[0:1])

        def act_two(parity, j):
            h = middle[parity, j] * half_gain_two + half_shift_two
            return h * jnp.tanh(h) + h

        build_windows(win_two, act_two)
        yield
        y = matmul(window_operand(win_two, range(4)), w_two[...])
        for a in range(2):
            v = y[:, a * LANES : (a + 1) * LANES] + biases[1:2, :]
            level[a] = tiles_of(v) + image[:, pl.ds(a, HALF, stride=2), :]
        yield
        build_windows(win_level, lambda parity, j: level[parity, j])
        yield
        operand = window_operand(win_level, range(4))
        y = matmul(operand[:, : 6 * LANES], w_down[...]) + biases[2:3, :]
        down[...] = tiles_of(y)
        yield

        def write_coarse(j, cells):
            win_coarse[0, j] = row_before(cells).astype(bf16)
            win_coarse[1, j] = cells.astype(bf16)
            win_coarse[2, j] = row_after(cells).astype(bf16)

        def coarse_body(j, past):
            h = down[j] * 0.5
            coarse = h * jnp.tanh(h) + h
            write_coarse(j, jnp.where(low_lanes, past, coarse))
            return coarse

        past = over_pairs(coarse_body, jnp.zeros((HALF, LANES), f32))
        write_coarse(PAIRS, jnp.where(low_lanes, past, 0.0))
        yield
        operand = window_operand(win_level, range(4))
        coarse_operand = window_operand(win_coarse, (0, 1, 1, 2))
        y = matmul(operand, w_up[: 16 * C, :]) + matmul(coarse_operand, w_up[16 * C :, :])
        for a in range(2):
            v = y[:, a * LANES : (a + 1) * LANES] + biases[3:4, :]
            image[:, pl.ds(a, HALF, stride=2), :] = tiles_of(v) + level[a]
        yield
        store_strips(member, image, f, out)

    staggered(frame(f) for f in range(styles.shape[0]))


def slope_twice(h):
    t = jnp.tanh(h)
    return (1.0 + t) + h * (1.0 - t * t)


def backward_kernel(count, *refs):
    member_ref = refs[0]
    cot_strips = refs[1 : 1 + count]
    frame_strips = refs[1 + count : 1 + 2 * count]
    styles, all_stats, all_middle, all_down, w_up, w_down, w_two, w_one = refs[1 + 2 * count : 9 + 2 * count]
    out = refs[9 + 2 * count : 9 + 3 * count]
    outs = refs[9 + 3 * count : 15 + 3 * count]
    scratch = refs[15 + 3 * count :]
    member = member_ref[0]
    low_lanes = lane_ids((HALF, LANES)) < C

    def frame(f):
        tile_out, tile_level, tile_mid, coarse_pairs, pieces, bias_sums = (ref.at[f] for ref in outs)
        image, level_grad, pre_grad, windows, coarse_below = (ref.at[f] for ref in scratch)
        style, stats, middle, down = (ref.at[f] for ref in (styles, all_stats, all_middle, all_down))
        load_strips(member, cot_strips, f, image)

        def add_rows(j, s):
            return s + image[j]

        sums = over_pairs(add_rows, jnp.zeros((H, LANES), f32))
        bias_up_sum = both_parities(total(sums))

        def out_tile(parity, j):
            x = parity_rows(image, parity, j)
            tile_out[parity, j] = x.astype(bf16)
            return x

        build_windows(windows, out_tile)
        yield
        y = matmul(window_operand(windows, range(4)), w_up[...])
        for a in range(2):
            level_grad[a] = tiles_of(y[:, (2 + a) * LANES : (3 + a) * LANES]) + image[:, pl.ds(a, HALF, stride=2), :]
        coarse = y[:, :LANES] + y[:, LANES : 2 * LANES]
        pre_grad[0] = tiles_of(coarse)
        yield

        def coarse_body(t, carry):
            after, sums = carry
            j = PAIRS - 1 - t
            g = pre_grad[0, j]
            g = g + swap_halves(g)
            h = down[j] * 0.5
            d = 0.5 * g * slope_twice(h)
            pair = jnp.where(low_lanes, d, after)
            coarse_pairs[j] = pair.astype(bf16)
            coarse_below[j] = row_after(pair).astype(bf16)
            return d, sums + d

        zero = jnp.zeros((HALF, LANES), f32)
        _, sums = over_pairs(coarse_body, (zero, zero))
        bias_down_sum = jnp.broadcast_to(total(sums), (8, LANES))
        load_strips(member, frame_strips, f, image)
        yield
        operand = jnp.concatenate(
            [coarse_pairs[...].reshape(BLOCK, LANES), coarse_below[...].reshape(BLOCK, LANES)], axis=1
        )
        y = matmul(operand, w_down[...])
        sums = jnp.zeros((1, LANES), f32)
        for a in range(2):
            v = y[:, a * LANES : (a + 1) * LANES] + level_grad[a].reshape(BLOCK, LANES)
            sums = sums + total(v)
            level_grad[a] = tiles_of(v)
        bias_two_sum = both_parities(sums)
        yield

        def level_tile(parity, j):
            x = level_grad[parity, j]
            tile_level[parity, j] = x.astype(bf16)
            return x

        build_windows(windows, level_tile)
        yield

        def norm_slopes(y, value, k):
            average, inverse = stats[2 * k : 2 * k + 1, :], stats[2 * k + 1 : 2 * k + 2, :]
            gain = inverse * style[2 * k : 2 * k + 1, :]
            half_gain = 0.5 * gain
            half_shift = 0.5 * (style[2 * k + 1 : 2 * k + 2, :] - average * gain)
            scale_sum = jnp.zeros((1, LANES), f32)
            shift_sum = jnp.zeros((1, LANES), f32)
            for a in range(2):
                v = value(a)
                g = 0.5 * y[:, a * LANES : (a + 1) * LANES] * slope_twice(v * half_gain + half_shift)
                pre_grad[a] = tiles_of(g)
                shift_sum = shift_sum + total(g)
                scale_sum = scale_sum + total(g * ((v - average) * inverse))
            scale_sum, shift_sum = both_parities(scale_sum), both_parities(shift_sum)
            factor = style[2 * k : 2 * k + 1, :]
            center = group_sum(factor * shift_sum) / MEMBERS
            tilt = group_sum(factor * scale_sum) / MEMBERS
            slope = (inverse * tilt)[0:1] * inverse
            return scale_sum, shift_sum, gain, slope, slope * average - (inverse * center)[0:1]

        y = matmul(window_operand(windows, range(4)), w_two[...])
        scale_two, shift_two, gain_two, slope_two, constant_two = norm_slopes(
            y, lambda a: middle[a].reshape(BLOCK, LANES), 1
        )
        yield
        row_sums = [zero]

        def mid_tile(parity, j):
            x = pre_grad[parity, j] * gain_two + (constant_two - middle[parity, j] * slope_two)
            tile_mid[parity, j] = x.astype(bf16)
            row_sums[0] = row_sums[0] + x
            return x

        build_windows(windows, mid_tile)
        bias_one_sum = both_parities(total(row_sums[0]))
        yield
        y = matmul(window_operand(windows, range(4)), w_one[...])
        scale_one, shift_one, gain_one, slope_one, constant_one = norm_slopes(
            y, lambda a: image[:, pl.ds(a, HALF, stride=2), :].reshape(BLOCK, LANES), 0
        )
        yield

        def frame_body(j, carry):
            for parity in range(2):
                x = parity_rows(image, parity, j)
                g = pre_grad[parity, j] * gain_one + (constant_one - x * slope_one) + level_grad[parity, j]
                image[j, pl.ds(parity, HALF, stride=2), :] = g
            return carry

        over_pairs(frame_body, 0)
        store_strips(member, image, f, out)
        for k, value in enumerate((scale_one, shift_one, scale_two, shift_two)):
            pieces[k : k + 1, :] = value[0:1]
        pieces[4:8, :] = jnp.zeros((4, LANES), f32)
        for k, value in enumerate((bias_one_sum, bias_two_sum, bias_down_sum, bias_up_sum)):
            bias_sums[k : k + 1, :] = value[0:1]
        bias_sums[4:8, :] = jnp.zeros((4, LANES), f32)

    staggered(frame(f) for f in range(styles.shape[0]))


def outer(left, right):
    return lax.dot_general(left, right, (((0,), (0,)), ((), ())), preferred_element_type=f32)


def accumulate(wins, tiles, sums):
    win_one, win_two, win_level, win_coarse = wins
    tile_out, tile_level, tile_mid, coarse_pairs = tiles
    sum_one, sum_two, sum_down, sum_up = sums

    @pl.when(pl.program_id(0) == 0)
    def _():
        for ref in sums:
            ref[...] = jnp.zeros_like(ref)

    def blocks(tiles):
        return jnp.concatenate([tiles[0, a].reshape(BLOCK, LANES) for a in range(2)], axis=1)

    level_operand = window_operand(win_level.at[0], range(4))
    out_blocks = blocks(tile_out)
    sum_up[16 * C :, :] += outer(window_operand(win_coarse.at[0], (0, 1, 1, 2)), out_blocks)
    sum_up[: 16 * C, :] += outer(level_operand, out_blocks)
    sum_down[...] += outer(level_operand[:, : 6 * LANES], coarse_pairs[0].reshape(BLOCK, LANES))
    sum_two[...] += outer(window_operand(win_two.at[0], range(4)), blocks(tile_level))
    sum_one[...] += outer(window_operand(win_one.at[0], range(4)), blocks(tile_mid))


def fold(sums, base, p, q):
    halves = []
    for b in range(2):
        rows = [base + ((a + p) * 4 + b + q) * C for a in range(2)]
        halves.append(sums[rows[0] : rows[0] + C, :LANES] + sums[rows[1] : rows[1] + C, LANES:])
    return halves[0] + swap_halves(halves[1])


def weight_kernel(*refs):
    wins, tiles, grads, sums = refs[:4], refs[4:8], refs[8:12], refs[12:]
    g_one, g_two, g_down, g_up = grads
    sum_one, sum_two, sum_down, sum_up = sums
    accumulate(wins, tiles, sums)

    @pl.when(pl.program_id(0) == pl.num_programs(0) - 1)
    def _():
        for p in range(3):
            for q in range(3):
                at = (3 * p + q) * C
                g_one[at : at + C, :] = fold(sum_one, 0, p, q)[:, :C]
                g_two[at : at + C, :] = fold(sum_two, 0, p, q)[:, :C]
                g_up[2 * at : 2 * at + C, :] = fold(sum_up, 16 * C, p, q)[:, :C]
                g_up[2 * at + C : 2 * at + 2 * C, :] = fold(sum_up, 0, p, q)[:, :C]
                place = (p * 4 + q) * C
                g_down[at : at + C, :] = sum_down[place : place + C, :C]


PARTS = 16


def message_kernel(count, rows, *refs):
    where_ref, wins, tiles = refs[0], refs[1:5], refs[5:9]
    pieces, bias_sums = refs[9:11]
    outs = refs[11 : 11 + count]
    sums = refs[11 + count : 15 + count]
    g_pair, g_up, g_down, small = refs[15 + count :]
    sum_one, sum_two, sum_down, sum_up = sums
    accumulate(wins, tiles, sums)

    @pl.when(pl.program_id(0) == pl.num_programs(0) - 1)
    def _():
        low_lanes = lane_ids((C, LANES)) < C
        for p in range(3):
            for q in range(3):
                at = (3 * p + q) * C
                g_pair[at : at + C, :] = jnp.where(
                    low_lanes, fold(sum_one, 0, p, q), swap_halves(fold(sum_two, 0, p, q))
                )
                g_up[2 * at : 2 * at + C, :] = fold(sum_up, 16 * C, p, q)
                g_up[2 * at + C : 2 * at + 2 * C, :] = fold(sum_up, 0, p, q)
                place = (p * 4 + q) * C
                g_down[at : at + C, :] = sum_down[place : place + C, :]
        frames = pieces.shape[0]
        small[...] = jnp.zeros_like(small)
        total_bias = bias_sums[0, 0:4, :]
        for f in range(frames):
            small[4 * f : 4 * f + 4, :] = pieces[f, 0:4, :]
            if f > 0:
                total_bias = total_bias + bias_sums[f, 0:4, :]
        small[4 * frames : 4 * frames + 4, :] = total_bias
        exact = small[...]
        high = exact.astype(bf16).astype(f32)
        rest = exact - high
        mid = rest.astype(bf16).astype(f32)
        parts = (high, mid, rest - mid)
        low_lanes = lane_ids((rows, LANES)) < C
        nothing = jnp.zeros((rows - 3 * PARTS, LANES), f32)
        sent = jnp.concatenate([*parts, nothing], axis=0)
        kept = jnp.concatenate([exact, jnp.zeros((2 * PARTS, LANES), f32), nothing], axis=0)
        for offset in range(count):
            start = pl.multiple_of(seq_owner(where_ref[0], offset) * rows, 8)
            block = jnp.concatenate(
                [
                    g_pair[pl.ds(start, rows), :],
                    jnp.where(
                        low_lanes,
                        g_up[pl.ds(pl.multiple_of(2 * start, 8), rows), :],
                        swap_halves(g_up[pl.ds(pl.multiple_of(2 * start + rows, 8), rows), :]),
                    ),
                    jnp.where(low_lanes, g_down[pl.ds(start, rows), :], kept if offset == 0 else sent),
                ],
                axis=0,
            )
            outs[offset][...] = block.astype(outs[offset].dtype)


def reduce_kernel(count, rows, cells, frames, *refs):
    where_ref, own = refs[:2]
    messages = refs[2 : 1 + count]
    packs = refs[1 + count : 1 + 2 * count]
    act_table, noise_table, ada_one, ada_two, out, pieces_one, pieces_two, table = refs[1 + 2 * count :]
    place, member = where_ref[0], where_ref[1]
    taken = 4 * frames
    bias = jnp.zeros((4, LANES), f32)
    sums = own[...]
    lanes = lane_ids((1, LANES))
    low_lanes = lanes < C
    hot = []
    for offset in range(count):
        if offset == 0:
            small = sums[2 * rows : 2 * rows + PARTS]
        else:
            message = messages[offset - 1][...].astype(f32)
            sums = sums + message
            first = 2 * rows
            small = (
                message[first : first + PARTS]
                + message[first + PARTS : first + 2 * PARTS]
                + message[first + 2 * PARTS : first + 3 * PARTS]
            )
        turned = swap_halves(small)
        bias = bias + small[taken : taken + 4]
        ids = packs[offset][2 * rows + ID_ROW : 2 * rows + ID_ROW + 8, :].astype(f32)
        for f in range(frames):
            at = offset * frames + f
            for k, ref in ((0, pieces_one), (2, pieces_two)):
                ref[at : at + 1, :] = jnp.where(low_lanes, turned[4 * f + k : 4 * f + k + 1], small[4 * f + k + 1 : 4 * f + k + 2])
            mine = jnp.where(lane_ids(ids.shape) == C + member * frames + f, ids, 0.0)
            mine = jnp.sum(mine, axis=1, keepdims=True)
            action, noise, valid = mine[0:1], mine[1:2], mine[2:3]
            place_at = lanes.astype(f32)
            hot.append(jnp.where(place_at == action + ACT_ROW, valid, 0.0) + jnp.where(place_at == noise + NOISE_ROW, 1.0, 0.0))
    hot = jnp.concatenate(hot, axis=0)[:, :TABLE_ROWS]
    table[...] = jnp.zeros_like(table)
    table[ACT_ROW : ACT_ROW + NACT, :] = act_table[...].astype(f32)
    table[NOISE_ROW : NOISE_ROW + NLEV, :] = noise_table[...].astype(f32)
    embed = matmul(hot.astype(bf16), table[...].astype(bf16))

    def exact(left, right, dims):
        return lax.dot_general(left, right, (dims, ((), ())), precision=precise, preferred_element_type=f32)

    one, two = pieces_one[...], pieces_two[...]
    at = 3 * rows
    out[:at, :] = sums
    out[at : at + cells, :] = exact(embed, one, ((0,), (0,)))
    out[at + cells : at + 2 * cells, :] = exact(embed, two, ((0,), (0,)))
    embed_grad = exact(one, ada_one[...].astype(f32), ((1,), (1,))) + exact(two, ada_two[...].astype(f32), ((1,), (1,)))
    at = at + 2 * cells
    out[at : at + TABLE_ROWS, :] = jnp.zeros((TABLE_ROWS, LANES), f32)
    out[at : at + TABLE_ROWS, :cells] = exact(hot, embed_grad, ((0,), (0,)))
    at = at + TABLE_ROWS
    bias = jnp.concatenate([bias, jnp.zeros((4, LANES), f32)], axis=0)
    width = C // count
    out[at : at + 8, :] = pltpu.roll(bias, (C - place * width) % LANES, axis=1)


def finish_kernel(rows, cells, first, second, *outs):
    act_grad, noise_grad, ada_one, ada_two, g_one, g_two, g_down, g_up = outs[:8]
    bias_grads = outs[8:12]
    sums = first[...] + second[...]

    def turn(block):
        return jnp.concatenate([block, jnp.zeros((LANES - rows, LANES), f32)], axis=0).T[:, :rows]

    pair, halves, down = (turn(sums[k * rows : (k + 1) * rows]) for k in range(3))
    g_one[...] = pair[:C]
    g_two[...] = pair[C:]
    g_up[:, :rows] = halves[:C]
    g_up[:, rows:] = halves[C:]
    g_down[...] = down[:C]
    at = 3 * rows
    ada_one[...] = sums[at : at + cells]
    ada_two[...] = sums[at + cells : at + 2 * cells]
    at = at + 2 * cells
    act_grad[...] = sums[at + ACT_ROW : at + ACT_ROW + NACT, :cells]
    noise_grad[...] = sums[at + NOISE_ROW : at + NOISE_ROW + NLEV, :cells]
    at = at + TABLE_ROWS
    for k, ref in enumerate(bias_grads):
        ref[...] = sums[at + k : at + k + 1, : ref.shape[0]].reshape(ref.shape)


def write_operands(block, f_one, f_two, f_down, f_up, b_one, b_two, b_down, b_up):
    low_lanes = lane_ids((C, LANES)) < C
    zero = jnp.zeros((C, LANES), f32)

    def taps(name, base, step):
        plain, turned = {}, {}
        for p in range(3):
            for q in range(3):
                k = block(name, (3 * p + q) * step + base)
                plain[p, q] = k
                turned[p, q] = jnp.concatenate([k, k], axis=0).T[:C]
        return plain, turned

    def write_forward(ref, base, plain):
        for w in range(4):
            for p in range(3):
                tile = jnp.where(low_lanes, plain.get((p, w), zero), plain.get((p, w - 1), zero)).astype(bf16)
                for a in range(2):
                    at = base + ((a + p) * 4 + w) * C
                    ref[at : at + C, a * LANES : (a + 1) * LANES] = tile
            for a in range(2):
                for r in range(4):
                    if not 0 <= r - a < 3:
                        at = base + (r * 4 + w) * C
                        ref[at : at + C, a * LANES : (a + 1) * LANES] = zero.astype(bf16)

    def write_backward(ref, lane, turned):
        for w in range(4):
            for p in range(3):
                tile = jnp.where(low_lanes, turned.get((p, 2 - w), zero), turned.get((p, 3 - w), zero)).astype(bf16)
                for a in range(2):
                    at = ((a + 2 - p) * 4 + w) * C
                    ref[at : at + C, lane + a * LANES : lane + (a + 1) * LANES] = tile
            for a in range(2):
                for r in range(4):
                    if not 0 <= a + 2 - r < 3:
                        at = (r * 4 + w) * C
                        ref[at : at + C, lane + a * LANES : lane + (a + 1) * LANES] = zero.astype(bf16)

    for name, forward_ref, backward_ref in (("one", f_one, b_one), ("two", f_two, b_two)):
        plain, turned = taps(name, 0, C)
        write_forward(forward_ref, 0, plain)
        write_backward(backward_ref, 0, turned)
    plain, turned = taps("up", 0, 2 * C)
    write_forward(f_up, 16 * C, plain)
    write_backward(b_up, 0, turned)
    plain, turned = taps("up", C, 2 * C)
    write_forward(f_up, 0, plain)
    write_backward(b_up, 2 * LANES, turned)
    plain, turned = taps("down", 0, C)
    for p in range(3):
        for w in range(4):
            at = (p * 4 + w) * C
            f_down[at : at + C, :] = plain.get((p, w), zero).astype(bf16)
    for below in range(2):
        for right in range(2):
            at = (below * 2 + right) * C
            for a in range(2):
                p = {(0, 0): 1, (0, 1): 2, (1, 1): 0}.get((below, a))
                first, second = zero, zero
                if p is not None:
                    first = turned[p, 1] if right == 0 else zero
                    second = turned[p, 2] if right == 0 else turned[p, 0]
                b_down[at : at + C, a * LANES : (a + 1) * LANES] = jnp.where(low_lanes, first, second).astype(bf16)


def expand_kernel(conv_one, conv_two, down_kernel, up_kernel, *outs):
    kernels = {"one": conv_one, "two": conv_two, "down": down_kernel, "up": up_kernel}

    def block(name, row):
        k = kernels[name][row : row + C, :].astype(f32)
        return jnp.concatenate([k, k], axis=1)

    write_operands(block, *outs)


ACT_ROW, NOISE_ROW, TABLE_ROWS = 0, 24, 56
BIAS_ROW, ID_ROW = 56, 64


def pack_sizes(rows, cells):
    return 3 * rows, 3 * rows + 2 * cells, -(-(3 * rows + 2 * cells) // 16) * 16


def turned(values):
    wide = jnp.concatenate([values, jnp.zeros((C, LANES - values.shape[1]), f32)], axis=1)
    return jnp.concatenate([wide, jnp.zeros((C, LANES), f32)], axis=0).T[: values.shape[1]]


def pack_kernel(*refs):
    actions, noise_ids, valid, conv_one, conv_two, down_kernel, up_kernel, ada_one, ada_two = refs[:9]
    act_table, noise_table = refs[9:11]
    biases = refs[11:15]
    out, work = refs[15:]
    rows, cells = conv_one.shape[1], ada_one.shape[0]
    style_at, end, _ = pack_sizes(rows, cells)
    wide = lambda ref: ref[...].astype(f32)
    low_lanes = lane_ids((rows, LANES)) < C
    up = wide(up_kernel)
    work[...] = jnp.zeros_like(work)
    for at, low, high in (
        (0, turned(wide(conv_one)), turned(wide(conv_two))),
        (rows, turned(up[:, :rows]), turned(up[:, rows:])),
    ):
        work[at : at + rows, :] = jnp.where(low_lanes, low, swap_halves(high))
    work[2 * rows : 3 * rows, :] = turned(wide(down_kernel))
    extra = 2 * rows
    for at, ref in ((ACT_ROW, act_table), (NOISE_ROW, noise_table)):
        size = ref.shape
        work[extra + at : extra + at + size[0], C : C + size[1]] = wide(ref)
    for k, ref in enumerate(biases):
        at = extra + BIAS_ROW + k
        work[at : at + 1, C : C + ref.shape[0]] = wide(ref).reshape(1, ref.shape[0])
    lanes = lane_ids((1, LANES))
    for k, ref in enumerate((actions, noise_ids, valid)):
        line = jnp.zeros((1, LANES), jnp.int32)
        for f in range(ref.shape[0]):
            line = jnp.where(lanes == C + f, ref[f], line)
        at = extra + ID_ROW + k
        work[at : at + 1, C:] = line.astype(f32)[:, C:]
    work[style_at : style_at + cells, :] = wide(ada_one)
    work[style_at + cells : end, :] = wide(ada_two)
    out[...] = work[...].astype(bf16)


def seq_owner(place, offset):
    return place ^ offset


def prepare_kernel(count, rows, cells, *refs):
    where_ref, actions, noise_ids, valid = refs[:4]
    packs = refs[4 : 4 + count]
    outs = refs[4 + count : 12 + count]
    styles, biases = refs[12 + count : 14 + count]
    work_pair, work_up, work_down, work_one, work_two, work_table = refs[14 + count :]
    place, member, frames = where_ref[0], where_ref[1], styles.shape[0]
    style_at, _, _ = pack_sizes(rows, cells)
    bias_rows = jnp.zeros(SMALL, f32)
    for offset, ref in enumerate(packs):
        pack = ref[...].astype(f32)
        owner = seq_owner(place, offset)
        start = pl.multiple_of(owner * rows, 8)
        work_pair[pl.ds(start, rows), :] = pack[:rows]
        halves = pack[rows : 2 * rows]
        work_up[pl.ds(2 * start, rows), :] = halves
        work_up[pl.ds(pl.multiple_of(2 * start + rows, 8), rows), :] = swap_halves(halves)
        extra = pack[2 * rows : 3 * rows]
        work_down[pl.ds(start, rows), :] = extra
        work_one[offset * cells : (offset + 1) * cells, :] = pack[style_at : style_at + cells]
        work_two[offset * cells : (offset + 1) * cells, :] = pack[style_at + cells : style_at + 2 * cells]
        lane = (offset * cells) % LANES
        tables = pltpu.roll(extra[:TABLE_ROWS], (lane - C) % LANES, axis=1)
        kept = (lane_ids(tables.shape) >= lane) & (lane_ids(tables.shape) < lane + cells)
        column = offset * cells // LANES
        tables = jnp.where(kept, tables, 0.0)
        if lane == 0:
            work_table[column] = tables
        else:
            work_table[column] += tables
        slots = extra[BIAS_ROW : BIAS_ROW + 8]
        width = C // count
        slots = jnp.where((lane_ids(SMALL) >= C) & (lane_ids(SMALL) < C + width), slots, 0.0)
        bias_rows = bias_rows + pltpu.roll(slots, (owner * width + C) % LANES, axis=1)
    biases[...] = bias_rows + swap_halves(bias_rows)

    lanes = lane_ids((8, LANES))
    row_at = lax.broadcasted_iota(jnp.int32, (8, LANES), 0)
    hot = jnp.zeros((8, LANES), f32)
    for f in range(frames):
        at = member * frames + f
        here = jnp.where(lanes == actions[at] + ACT_ROW, valid[at], 0) + jnp.where(lanes == noise_ids[at] + NOISE_ROW, 1, 0)
        hot = jnp.where(row_at == f, here.astype(f32), hot)
    hot = hot[:, :TABLE_ROWS].astype(bf16)
    embed = jnp.concatenate([matmul(hot, work_table[k].astype(bf16)) for k in range(work_table.shape[0])], axis=1)
    low_lanes = lanes < C
    for k, work in enumerate((work_one, work_two)):
        style = jnp.dot(embed, work[...], precision=precise, preferred_element_type=f32)
        other = swap_halves(style)
        scale = 1.0 + jnp.where(low_lanes, style, other)
        shift = jnp.where(low_lanes, other, style)
        for f in range(frames):
            styles[f, 2 * k : 2 * k + 1, :] = scale[f : f + 1]
            styles[f, 2 * k + 1 : 2 * k + 2, :] = shift[f : f + 1]
    for f in range(frames):
        styles[f, 4:8, :] = jnp.zeros((4, LANES), f32)

    def block(name, row):
        work = {"one": work_pair, "two": work_pair, "down": work_down, "up": work_up}[name]
        k = work[row : row + C, :]
        low = lane_ids(k.shape) < C
        if name == "two":
            return jnp.where(low, swap_halves(k), k)
        return jnp.where(low, k, swap_halves(k))

    write_operands(block, *outs)


def shape(dims, kind):
    return jax.ShapeDtypeStruct(dims, kind)


def whole(dims):
    return pl.BlockSpec(dims, lambda f: (0,) * len(dims))


def per_frame(dims):
    return pl.BlockSpec((1,) + dims, lambda f: (f,) + (0,) * len(dims))


def strip_specs(count, strip):
    return [pl.BlockSpec((1, strip, W * C), lambda f: (f, 0, 0))] * count


SMALL = (8, LANES)
WINDOWS = (4, PAIRS + 1, HALF, LANES)
COARSE_WINDOWS = (3, PAIRS + 1, HALF, LANES)
TILES = (2, PAIRS, HALF, LANES)
COARSE = (PAIRS, HALF, LANES)
IMAGE = (PAIRS, H, LANES)
KEYS = 16 * C


def in_vmem():
    return pl.BlockSpec(memory_space=pltpu.VMEM)


def in_smem():
    return pl.BlockSpec(memory_space=pltpu.SMEM)


def params(limit=VMEM_LIMIT):
    return pltpu.CompilerParams(vmem_limit_bytes=limit)


def cost(macs, moved):
    return pl.CostEstimate(flops=2 * macs, bytes_accessed=moved, transcendentals=0)


def expand(conv_one, conv_two, down_kernel, up_kernel):
    vmem = pl.BlockSpec(memory_space=pltpu.VMEM)
    return pl.pallas_call(
        expand_kernel,
        in_specs=[vmem] * 4,
        out_specs=[vmem] * 8,
        out_shape=[
            shape((KEYS, 2 * LANES), bf16),
            shape((KEYS, 2 * LANES), bf16),
            shape((6 * LANES, LANES), bf16),
            shape((2 * KEYS, 2 * LANES), bf16),
            shape((KEYS, 2 * LANES), bf16),
            shape((KEYS, 2 * LANES), bf16),
            shape((2 * LANES, 2 * LANES), bf16),
            shape((KEYS, 4 * LANES), bf16),
        ],
        compiler_params=params(),
        name="expand",
    )(conv_one, conv_two, down_kernel, up_kernel)


def forward(member, strips, styles, biases, w_one, w_two, w_down, w_up):
    count = len(strips)
    frames, strip, _ = strips[0].shape
    return pl.pallas_call(
        lambda *refs: forward_kernel(count, *refs),
        in_specs=[in_smem()] + [in_vmem()] * (count + 6),
        out_specs=[in_vmem()] * (count + 7),
        out_shape=[shape((frames, strip, W * C), bf16)] * count
        + [
            shape((frames,) + WINDOWS, bf16),
            shape((frames,) + WINDOWS, bf16),
            shape((frames,) + WINDOWS, bf16),
            shape((frames,) + COARSE_WINDOWS, bf16),
            shape((frames,) + TILES, f32),
            shape((frames,) + COARSE, f32),
            shape((frames,) + SMALL, f32),
        ],
        scratch_shapes=[pltpu.VMEM((frames,) + IMAGE, f32), pltpu.VMEM((frames,) + TILES, f32)],
        compiler_params=params(),
        cost_estimate=cost(frames * BLOCK * KEYS * 2 * LANES * 5, frames * (14 << 20)),
        name="forward",
    )(member, *strips, styles, biases, w_one, w_two, w_down, w_up)


def backward(member, cot_strips, frame_strips, styles, stats, middle, down, w_up, w_down, w_two, w_one):
    count = len(cot_strips)
    frames, strip, _ = cot_strips[0].shape
    return pl.pallas_call(
        lambda *refs: backward_kernel(count, *refs),
        in_specs=[in_smem()] + [in_vmem()] * (2 * count + 8),
        out_specs=[in_vmem()] * (count + 6),
        out_shape=[shape((frames, strip, W * C), bf16)] * count
        + [
            shape((frames,) + TILES, bf16),
            shape((frames,) + TILES, bf16),
            shape((frames,) + TILES, bf16),
            shape((frames,) + COARSE, bf16),
            shape((frames,) + SMALL, f32),
            shape((frames,) + SMALL, f32),
        ],
        scratch_shapes=[
            pltpu.VMEM((frames,) + IMAGE, f32),
            pltpu.VMEM((frames,) + TILES, f32),
            pltpu.VMEM((frames,) + TILES, f32),
            pltpu.VMEM((frames,) + WINDOWS, bf16),
            pltpu.VMEM((frames,) + COARSE, bf16),
        ],
        compiler_params=params(),
        cost_estimate=cost(frames * BLOCK * KEYS * 2 * LANES * 5, frames * (10 << 20)),
        name="backward",
    )(member, *cot_strips, *frame_strips, styles, stats, middle, down, w_up, w_down, w_two, w_one)


def weight_grads(win_one, win_two, win_level, win_coarse, tile_out, tile_level, tile_mid, coarse_pairs):
    frames = win_one.shape[0]
    return pl.pallas_call(
        weight_kernel,
        grid=(frames,),
        in_specs=[
            per_frame(d) for d in (WINDOWS, WINDOWS, WINDOWS, COARSE_WINDOWS, TILES, TILES, TILES, COARSE)
        ],
        out_specs=[whole((9 * C, C)), whole((9 * C, C)), whole((9 * C, C)), whole((18 * C, C))],
        out_shape=[shape((9 * C, C), f32)] * 3 + [shape((18 * C, C), f32)],
        scratch_shapes=[
            pltpu.VMEM((KEYS, 2 * LANES), f32),
            pltpu.VMEM((KEYS, 2 * LANES), f32),
            pltpu.VMEM((6 * LANES, LANES), f32),
            pltpu.VMEM((2 * KEYS, 2 * LANES), f32),
        ],
        compiler_params=params(),
        cost_estimate=cost(frames * BLOCK * KEYS * 2 * LANES * 5, frames * (6 << 20)),
        name="weights",
    )(win_one, win_two, win_level, win_coarse, tile_out, tile_level, tile_mid, coarse_pairs)


def pack(actions, noise_ids, valid, conv_one, conv_two, down_kernel, up_kernel, ada_one, ada_two, act_table, noise_table, *biases):
    _, _, size = pack_sizes(conv_one.shape[0], ada_one.shape[0])
    kernels = [kernel.T for kernel in (conv_one, conv_two, down_kernel, up_kernel)]
    args = (*kernels, ada_one, ada_two, act_table, noise_table, *biases)
    return pl.pallas_call(
        pack_kernel,
        in_specs=[in_smem()] * 3 + [in_vmem()] * len(args),
        out_specs=in_vmem(),
        out_shape=shape((size, LANES), bf16),
        scratch_shapes=[pltpu.VMEM((size, LANES), f32)],
        compiler_params=params(VMEM_MOST),
        name="pack",
    )(actions, noise_ids, valid, *args)


OPERANDS = (
    (KEYS, 2 * LANES),
    (KEYS, 2 * LANES),
    (6 * LANES, LANES),
    (2 * KEYS, 2 * LANES),
    (KEYS, 2 * LANES),
    (KEYS, 2 * LANES),
    (2 * LANES, 2 * LANES),
    (KEYS, 4 * LANES),
)


def prepare(where, actions, noise_ids, valid, packs, rows, cells, frames):
    count = len(packs)
    return pl.pallas_call(
        lambda *refs: prepare_kernel(count, rows, cells, *refs),
        in_specs=[in_smem()] * 4 + [in_vmem()] * count,
        out_specs=[in_vmem()] * 10,
        out_shape=[shape(d, bf16) for d in OPERANDS] + [shape((frames,) + SMALL, f32), shape(SMALL, f32)],
        scratch_shapes=[
            pltpu.VMEM((9 * C, LANES), f32),
            pltpu.VMEM((18 * C, LANES), f32),
            pltpu.VMEM((9 * C, LANES), f32),
            pltpu.VMEM((count * cells, LANES), f32),
            pltpu.VMEM((count * cells, LANES), f32),
            pltpu.VMEM((count * cells // LANES, TABLE_ROWS, LANES), f32),
        ],
        compiler_params=params(),
        name="prepare",
    )(where, actions, noise_ids, valid, *packs)


def weight_messages(where, wins, tiles, pieces, bias_sums, count, rows):
    frames = pieces.shape[0]
    return pl.pallas_call(
        lambda *refs: message_kernel(count, rows, *refs),
        grid=(frames,),
        in_specs=[in_smem()]
        + [per_frame(d) for d in (WINDOWS, WINDOWS, WINDOWS, COARSE_WINDOWS, TILES, TILES, TILES, COARSE)]
        + [whole((frames,) + SMALL)] * 2,
        out_specs=[whole((3 * rows, LANES))] * count,
        out_shape=[shape((3 * rows, LANES), f32)] + [shape((3 * rows, LANES), bf16)] * (count - 1),
        scratch_shapes=[
            pltpu.VMEM((KEYS, 2 * LANES), f32),
            pltpu.VMEM((KEYS, 2 * LANES), f32),
            pltpu.VMEM((6 * LANES, LANES), f32),
            pltpu.VMEM((2 * KEYS, 2 * LANES), f32),
            pltpu.VMEM((9 * C, LANES), f32),
            pltpu.VMEM((18 * C, LANES), f32),
            pltpu.VMEM((9 * C, LANES), f32),
            pltpu.VMEM((PARTS, LANES), f32),
        ],
        compiler_params=params(),
        cost_estimate=cost(frames * BLOCK * KEYS * 2 * LANES * 5, frames * (6 << 20)),
        name="weights",
    )(where, *wins, *tiles, pieces, bias_sums)


def reduce_messages(where, own, messages, packs, act_table, noise_table, ada_one, ada_two, rows, cells, frames):
    count = len(packs)
    return pl.pallas_call(
        lambda *refs: reduce_kernel(count, rows, cells, frames, *refs),
        in_specs=[in_smem()] + [in_vmem()] * (2 * count + 4),
        out_specs=in_vmem(),
        out_shape=shape((3 * rows + 2 * cells + TABLE_ROWS + 8, LANES), f32),
        scratch_shapes=[
            pltpu.VMEM((count * frames, LANES), f32),
            pltpu.VMEM((count * frames, LANES), f32),
            pltpu.VMEM((TABLE_ROWS, cells), f32),
        ],
        compiler_params=params(),
        name="reduce",
    )(where, own, *messages, *packs, act_table, noise_table, ada_one, ada_two)


def finish(first, second, rows, cells, width):
    act_grad, noise_grad, one, two, *rest = pl.pallas_call(
        lambda *refs: finish_kernel(rows, cells, *refs),
        in_specs=[in_vmem()] * 2,
        out_specs=[in_vmem()] * 12,
        out_shape=[
            shape((NACT, cells), f32),
            shape((NLEV, cells), f32),
            shape((cells, LANES), f32),
            shape((cells, LANES), f32),
            shape((C, rows), f32),
            shape((C, rows), f32),
            shape((C, rows), f32),
            shape((C, 2 * rows), f32),
        ]
        + [shape((width,), f32)] * 4,
        compiler_params=params(),
        name="finish",
    )(first, second)
    return (act_grad, noise_grad, one, two, *[grad.T for grad in rest[:4]], *rest[4:])


def collect_kernel(member_ref, *refs):
    strips, out = refs[:-1], refs[-1]
    for offset, strip in enumerate(strips):
        out[member_ref[0] ^ offset, 0] = strip[0].astype(out.dtype)


def return_strips(strips):
    return tuple(trade(strip, offset) for offset, strip in enumerate(strips))


def collect_strips(member_box, strips, kind):
    count = len(strips)
    frames, rows, columns = strips[0].shape
    whole_strips = pl.pallas_call(
        collect_kernel,
        grid=(frames,),
        in_specs=[in_smem()] + [pl.BlockSpec((1, rows, columns), lambda f: (f, 0, 0))] * count,
        out_specs=pl.BlockSpec((count, 1, rows, columns), lambda f: (0, f, 0, 0)),
        out_shape=shape((count, frames, rows, columns), kind),
        compiler_params=params(),
        name="collect",
    )(member_box, *strips)
    return whole_strips.reshape(count * frames, rows, columns)


def twice(values):
    return jnp.concatenate([values, values], axis=-1)


def pad_small(rows):
    stacked = jnp.stack(rows, axis=-2)
    gaps = [(0, 0)] * (stacked.ndim - 2) + [(0, 8 - len(rows)), (0, 0)]
    return jnp.pad(stacked, gaps)


def trade(value, offset):
    if offset == 0:
        return value
    count = lax.axis_size("rows")
    return lax.ppermute(value, "rows", [(i, i ^ offset) for i in range(count)])


def spread_strips(array, member):
    count = lax.axis_size("rows")
    share = array.shape[0] // count
    return [
        trade(lax.dynamic_slice_in_dim(array, (member ^ offset) * share, share, axis=0), offset)
        for offset in range(count)
    ]


def seq_trade(value, offset):
    count = lax.axis_size("seq")
    return lax.ppermute(value, "seq", [(i, i ^ offset) for i in range(count)])


def layers(member_box, frame_strips, cot_strips, styles, bias_rows, operands):
    f_one, f_two, f_down, f_up, b_one, b_two, b_down, b_up = operands
    member = member_box[0]
    *out, win_one, win_two, win_level, win_coarse, middle, down, stats = forward(
        member_box, frame_strips, styles, bias_rows, f_one, f_two, f_down, f_up
    )
    out = return_strips(out)
    *grad_strips, tile_out, tile_level, tile_mid, coarse_pairs, pieces, bias_sums = backward(
        member_box, cot_strips, frame_strips, styles, stats, middle, down, b_up, b_down, b_two, b_one
    )
    grad_strips = return_strips(grad_strips)
    wins = (win_one, win_two, win_level, win_coarse)
    tiles = (tile_out, tile_level, tile_mid, coarse_pairs)
    pieces, out = lax.optimization_barrier((pieces, out))
    return out, grad_strips, wins, tiles, pieces, bias_sums


def local_direct(
    frames,
    cotangent,
    actions,
    noise_ids,
    valid,
    act_table,
    noise_table,
    ada_one,
    ada_two,
    conv_one,
    conv_two,
    down_kernel,
    up_kernel,
    bias_one,
    bias_two,
    bias_down,
    bias_up,
):
    member = lax.axis_index("rows").astype(jnp.int32)
    place = lax.axis_index("seq").astype(jnp.int32)
    count = lax.axis_size("seq")
    share = frames.shape[0] // lax.axis_size("rows")
    rows, cells, width = conv_one.shape[0], ada_one.shape[0], bias_one.shape[0]
    member_box = member.reshape(1)
    where = jnp.stack([place, member])
    packed = pack(
        actions,
        noise_ids,
        valid,
        conv_one,
        conv_two,
        down_kernel,
        up_kernel,
        ada_one,
        ada_two,
        act_table,
        noise_table,
        bias_one,
        bias_two,
        bias_down,
        bias_up,
    )
    packs = [packed] + [seq_trade(packed, offset) for offset in range(1, count)]
    frame_strips = spread_strips(frames, member)
    cot_strips = spread_strips(cotangent, member)
    *operands, styles, bias_rows = prepare(where, actions, noise_ids, valid, packs, rows, cells, share)
    out, grad_strips, wins, tiles, pieces, bias_sums = layers(
        member_box, frame_strips, cot_strips, styles, bias_rows, operands
    )
    own, *messages = weight_messages(where, wins, tiles, pieces, bias_sums, count, rows)
    received = [seq_trade(messages[offset - 1], offset) for offset in range(1, count)]
    received, grad_strips = lax.optimization_barrier((received, grad_strips))
    sums = reduce_messages(where, own, received, packs, act_table, noise_table, ada_one, ada_two, rows, cells, share)
    offset = 1
    while 2 * offset < lax.axis_size("rows"):
        sums = sums + trade(sums, offset)
        offset *= 2
    result = collect_strips(member_box, out, bf16)
    frames_grad = collect_strips(member_box, grad_strips, f32)
    return (result, frames_grad, *finish(sums, trade(sums, offset), rows, cells, width))


def local_general(
    frames,
    cotangent,
    actions,
    noise_ids,
    valid,
    act_table,
    noise_table,
    ada_one,
    ada_two,
    conv_one,
    conv_two,
    down_kernel,
    up_kernel,
    bias_one,
    bias_two,
    bias_down,
    bias_up,
):
    member = lax.axis_index("rows").astype(jnp.int32)
    share = frames.shape[0] // lax.axis_size("rows")
    member_box = member.reshape(1)

    def gathered(value, axis):
        return lax.all_gather(value, "seq", axis=axis, tiled=True)

    frame_strips = spread_strips(frames, member)
    cot_strips = spread_strips(cotangent, member)
    act_full = gathered(act_table, 1)
    noise_full = gathered(noise_table, 1)
    ada_full = gathered(jnp.concatenate([ada_one, ada_two], axis=1), 0).astype(f32)
    biases = gathered(jnp.stack([bias_one, bias_two, bias_down, bias_up]), 1).astype(f32)
    operands = expand(gathered(conv_one, 0), gathered(conv_two, 0), gathered(down_kernel, 0), gathered(up_kernel, 0))

    own = lambda ids: lax.dynamic_slice_in_dim(ids, member * share, share)
    own_actions, own_noise, own_valid = own(actions), own(noise_ids), own(valid)
    action_hot = (own_actions[:, None] == jnp.arange(NACT, dtype=jnp.int32)[None, :]).astype(f32) * own_valid[
        :, None
    ].astype(f32)
    noise_hot = (own_noise[:, None] == jnp.arange(NLEV, dtype=jnp.int32)[None, :]).astype(f32)
    embed = jnp.dot(action_hot, act_full.astype(f32), precision=precise) + jnp.dot(
        noise_hot, noise_full.astype(f32), precision=precise
    )
    style = jnp.dot(embed, ada_full, precision=precise)
    styles = pad_small(
        [
            twice(1.0 + style[:, :C]),
            twice(style[:, C : 2 * C]),
            twice(1.0 + style[:, 2 * C : 3 * C]),
            twice(style[:, 3 * C :]),
        ]
    )
    bias_rows = pad_small([twice(biases[k]) for k in range(4)])
    out, grad_strips, wins, tiles, pieces, bias_sums = layers(
        member_box, frame_strips, cot_strips, styles, bias_rows, operands
    )
    g_one, g_two, g_down, g_up = weight_grads(*wins, *tiles)
    result = collect_strips(member_box, out, bf16)
    frames_grad = collect_strips(member_box, grad_strips, f32)

    pieces_one = jnp.concatenate([pieces[:, 0, :C], pieces[:, 1, :C]], axis=1)
    pieces_two = jnp.concatenate([pieces[:, 2, :C], pieces[:, 3, :C]], axis=1)
    ada_one_grad = jnp.dot(embed.T, pieces_one, precision=precise)
    ada_two_grad = jnp.dot(embed.T, pieces_two, precision=precise)
    embed_grad = jnp.dot(jnp.concatenate([pieces_one, pieces_two], axis=1), ada_full.T, precision=precise)
    act_table_grad = jnp.dot(action_hot.T, embed_grad, precision=precise)
    noise_table_grad = jnp.dot(noise_hot.T, embed_grad, precision=precise)
    bias_total = jnp.sum(bias_sums, axis=0)[:4, :C]

    def shard(value, axis):
        return lax.psum_scatter(value, "seq", scatter_dimension=axis, tiled=True)

    shards = (
        shard(act_table_grad, 1),
        shard(noise_table_grad, 1),
        shard(ada_one_grad, 0),
        shard(ada_two_grad, 0),
        shard(g_one, 0),
        shard(g_two, 0),
        shard(g_down, 0),
        shard(g_up, 0),
        shard(bias_total[0], 0),
        shard(bias_total[1], 0),
        shard(bias_total[2], 0),
        shard(bias_total[3], 0),
    )
    return (result, frames_grad) + lax.psum(shards, "rows")


def fits_direct(mesh):
    count = mesh.shape["seq"]
    rows, cells = 9 * C // count, 256 // count
    return count in (2, 4, 8) and rows % 8 == 0 and rows >= ID_ROW + 8 and cells % 8 == 0 and mesh.shape["rows"] == 4


def solution(mesh):
    in_specs = (
        P("seq", "rows", None),
        P("seq", "rows", None),
        P("seq"),
        P("seq"),
        P("seq"),
        P(None, "seq"),
        P(None, "seq"),
        P("seq", None),
        P("seq", None),
        P("seq", None),
        P("seq", None),
        P("seq", None),
        P("seq", None),
        P("seq"),
        P("seq"),
        P("seq"),
        P("seq"),
    )
    out_specs = (
        P("seq", "rows", None),
        P("seq", "rows", None),
        P(None, "seq"),
        P(None, "seq"),
        P("seq", None),
        P("seq", None),
        P("seq", None),
        P("seq", None),
        P("seq", None),
        P("seq", None),
        P("seq"),
        P("seq"),
        P("seq"),
        P("seq"),
    )
    local = local_direct if fits_direct(mesh) else local_general
    return jax.shard_map(local, mesh=mesh, in_specs=in_specs, out_specs=out_specs, check_vma=False)
```

```python
import jax
import jax.numpy as jnp
from jax import lax
from jax.experimental import pallas as pl
from jax.experimental.pallas import tpu as pltpu
from jax.sharding import PartitionSpec as P

C = 64
NACT = 18
GROUPS = 32
NLEV = 32
H = 64
W = 64
PAIRS = W // 2
HALF = H // 2
LANES = 2 * C
BLOCK = PAIRS * HALF
MEMBERS = float(H * W * (C // GROUPS))
EPS = 1e-05

precise = lax.Precision.HIGHEST
f32 = jnp.float32
bf16 = jnp.bfloat16
VMEM_LIMIT = 16 * 2**20
VMEM_MOST = 60 * 2**20


def lane_ids(shape):
    return lax.broadcasted_iota(jnp.int32, shape, len(shape) - 1)


def swap_halves(x):
    return pltpu.roll(x, C, axis=x.ndim - 1)


def row_before(x):
    rows = lax.broadcasted_iota(jnp.int32, x.shape, 0)
    return jnp.where(rows == 0, 0.0, pltpu.roll(x, 1, axis=0))


def row_after(x):
    rows = lax.broadcasted_iota(jnp.int32, x.shape, 0)
    return jnp.where(rows == x.shape[0] - 1, 0.0, pltpu.roll(x, x.shape[0] - 1, axis=0))


def both_parities(x):
    x = jnp.broadcast_to(x, (8, LANES))
    return x + swap_halves(x)


def group_sum(x):
    even = lane_ids(x.shape) % 2 == 0
    return x + jnp.where(even, pltpu.roll(x, LANES - 1, axis=1), pltpu.roll(x, 1, axis=1))


def total(x):
    return jnp.sum(x, axis=0, keepdims=True)


def over_pairs(body, carry):
    for j in range(PAIRS):
        carry = body(j, carry)
    return carry


def build_windows(windows, tile):
    low_lanes = lane_ids((HALF, LANES)) < C
    zero = jnp.zeros((HALF, LANES), f32)

    def write(j, even, odd):
        windows[0, j] = row_before(odd).astype(bf16)
        windows[1, j] = even.astype(bf16)
        windows[2, j] = odd.astype(bf16)
        windows[3, j] = row_after(even).astype(bf16)

    def body(j, carry):
        even_past, odd_past = carry
        even = swap_halves(tile(0, j))
        odd = swap_halves(tile(1, j))
        write(j, jnp.where(low_lanes, even_past, even), jnp.where(low_lanes, odd_past, odd))
        return even, odd

    even, odd = over_pairs(body, (zero, zero))
    write(PAIRS, jnp.where(low_lanes, even, 0.0), jnp.where(low_lanes, odd, 0.0))


def window_operand(windows, slots):
    parts = []
    for slot in slots:
        for shift in (0, 1):
            parts.append(windows[slot, shift : shift + PAIRS].reshape(BLOCK, LANES))
    return jnp.concatenate(parts, axis=1)


def matmul(left, right):
    return jnp.dot(left, right, preferred_element_type=f32)


def tiles_of(y):
    return y.reshape(PAIRS, HALF, LANES)


def norm_stats(sums, squares):
    average = group_sum(both_parities(sums)) / MEMBERS
    variance = group_sum(both_parities(squares)) / MEMBERS - average * average
    return average, lax.rsqrt(variance + EPS)


def strip_start(member, offset, strip):
    return pl.multiple_of((member ^ offset) * strip, strip)


def load_strips(member, strips, image):
    for offset, strip in enumerate(strips):
        rows = strip.shape[0]
        start = strip_start(member, offset, rows)
        for j in range(PAIRS):
            image[j, pl.ds(start, rows), :] = strip[:, j * LANES : (j + 1) * LANES].astype(f32)


def store_strips(member, image, f, strips):
    for offset, strip in enumerate(strips):
        rows = strip.shape[1]
        start = strip_start(member, offset, rows)
        for j in range(PAIRS):
            strip[f, :, j * LANES : (j + 1) * LANES] = image[j, pl.ds(start, rows), :].astype(strip.dtype)


def parity_rows(image, parity, j):
    return image[j, pl.ds(parity, HALF, stride=2), :]


def staggered(steps):
    steps = list(steps)
    started = []
    while steps or started:
        if steps:
            started.append(steps.pop(0))
        for step in list(started):
            if next(step, "end") == "end":
                started.remove(step)


def gather_frame(member, strips, image, stats):
    load_strips(member, strips, image)

    def add_stats(j, carry):
        x = image[j]
        s, q = carry
        return s + x, q + x * x

    zero = jnp.zeros((H, LANES), f32)
    s, q = over_pairs(add_stats, (zero, zero))
    average, inverse = norm_stats(total(s), total(q))
    stats[0:1, :] = average[0:1]
    stats[1:2, :] = inverse[0:1]
    stats[2:3, :] = both_parities(total(s))[0:1]
    stats[3:8, :] = jnp.zeros((5, LANES), f32)


def gather_kernel(member_ref, array, far, near, images, all_stats, own, sent):
    member = member_ref[0]
    frames = images.shape[0]
    copy = pltpu.make_async_copy(array.at[pl.ds(member * frames, frames)], own, sent)
    copy.start()
    first = member % 2 * frames
    copy.wait()
    for f in range(frames):
        strips = (own.at[f], near.at[f], far.at[first + f], near.at[frames + f])
        gather_frame(member, strips, images.at[f], all_stats.at[f])


def forward_kernel(count, *refs):
    member_ref, frame_images, frame_stats, styles, biases, w_one, w_two, w_down, w_up = refs[:9]
    out = refs[9 : 9 + count]
    outs = refs[9 + count : 16 + count]
    images, levels = refs[16 + count :]
    member = member_ref[0]
    low_lanes = lane_ids((HALF, LANES)) < C

    def frame(f):
        win_one, win_two, win_level, win_coarse, middle, down, stats = (ref.at[f] for ref in outs)
        frame_image, image, level, style = frame_images.at[f], images.at[f], levels.at[f], styles.at[f]
        average_one, inverse_one = frame_stats[f, 0:1, :], frame_stats[f, 1:2, :]
        gain_one = inverse_one * style[0:1, :]
        half_gain = 0.5 * gain_one
        half_shift = 0.5 * (style[1:2, :] - average_one * gain_one)

        def act_one(parity, j):
            h = parity_rows(frame_image, parity, j) * half_gain + half_shift
            return h * jnp.tanh(h) + h

        build_windows(win_one, act_one)
        yield
        y = matmul(window_operand(win_one, range(4)), w_one[...])
        sums = jnp.zeros((1, LANES), f32)
        squares = jnp.zeros((1, LANES), f32)
        for a in range(2):
            v = y[:, a * LANES : (a + 1) * LANES] + biases[0:1, :]
            sums = sums + total(v)
            squares = squares + total(v * v)
            middle[a] = tiles_of(v)
        yield
        average_two, inverse_two = norm_stats(sums, squares)
        stats[0:1, :] = average_one
        stats[1:2, :] = inverse_one
        stats[2:3, :] = average_two[0:1]
        stats[3:4, :] = inverse_two[0:1]
        stats[4:8, :] = jnp.zeros((4, LANES), f32)
        gain_two = inverse_two * style[2:3, :]
        half_gain_two = 0.5 * gain_two[0:1]
        half_shift_two = 0.5 * (style[3:4, :] - average_two[0:1] * gain_two[0:1])

        def act_two(parity, j):
            h = middle[parity, j] * half_gain_two + half_shift_two
            return h * jnp.tanh(h) + h

        build_windows(win_two, act_two)
        yield
        y = matmul(window_operand(win_two, range(4)), w_two[...])
        for a in range(2):
            v = y[:, a * LANES : (a + 1) * LANES] + biases[1:2, :]
            level[a] = tiles_of(v) + frame_image[:, pl.ds(a, HALF, stride=2), :]
        yield
        build_windows(win_level, lambda parity, j: level[parity, j])
        yield
        operand = window_operand(win_level, range(4))
        y = matmul(operand[:, : 6 * LANES], w_down[...]) + biases[2:3, :]
        down[...] = tiles_of(y)
        yield

        def write_coarse(j, cells):
            win_coarse[0, j] = row_before(cells).astype(bf16)
            win_coarse[1, j] = cells.astype(bf16)
            win_coarse[2, j] = row_after(cells).astype(bf16)

        def coarse_body(j, past):
            h = down[j] * 0.5
            coarse = h * jnp.tanh(h) + h
            write_coarse(j, jnp.where(low_lanes, past, coarse))
            return coarse

        past = over_pairs(coarse_body, jnp.zeros((HALF, LANES), f32))
        write_coarse(PAIRS, jnp.where(low_lanes, past, 0.0))
        yield
        operand = window_operand(win_level, range(4))
        coarse_operand = window_operand(win_coarse, (0, 1, 1, 2))
        y = matmul(operand, w_up[: 16 * C, :]) + matmul(coarse_operand, w_up[16 * C :, :])
        for a in range(2):
            v = y[:, a * LANES : (a + 1) * LANES] + biases[3:4, :]
            image[:, pl.ds(a, HALF, stride=2), :] = tiles_of(v) + level[a]
        yield
        store_strips(member, image, f, out)

    staggered(frame(f) for f in range(styles.shape[0]))


def slope_twice(h):
    t = jnp.tanh(h)
    return (1.0 + t) + h * (1.0 - t * t)


def backward_kernel(count, *refs):
    member_ref = refs[0]
    cot_images, cot_stats, frame_images, styles, all_stats, all_middle, all_down = refs[1:8]
    w_up, w_down, w_two, w_one = refs[8:12]
    out = refs[12 : 12 + count]
    outs = refs[12 + count : 18 + count]
    scratch = refs[18 + count :]
    member = member_ref[0]
    low_lanes = lane_ids((HALF, LANES)) < C

    def frame(f):
        tile_out, tile_level, tile_mid, coarse_pairs, pieces, bias_sums = (ref.at[f] for ref in outs)
        image, level_grad, pre_grad, windows, coarse_below = (ref.at[f] for ref in scratch)
        style, stats, middle, down, frame_image = (
            ref.at[f] for ref in (styles, all_stats, all_middle, all_down, frame_images)
        )
        cot_image = cot_images.at[f]

        def out_tile(parity, j):
            x = parity_rows(cot_image, parity, j)
            tile_out[parity, j] = x.astype(bf16)
            return x

        build_windows(windows, out_tile)
        yield
        y = matmul(window_operand(windows, range(4)), w_up[...])
        for a in range(2):
            level_grad[a] = (
                tiles_of(y[:, (2 + a) * LANES : (3 + a) * LANES]) + cot_image[:, pl.ds(a, HALF, stride=2), :]
            )
        coarse = y[:, :LANES] + y[:, LANES : 2 * LANES]
        pre_grad[0] = tiles_of(coarse)
        yield

        def coarse_body(t, carry):
            after, sums = carry
            j = PAIRS - 1 - t
            g = pre_grad[0, j]
            g = g + swap_halves(g)
            h = down[j] * 0.5
            d = 0.5 * g * slope_twice(h)
            pair = jnp.where(low_lanes, d, after)
            coarse_pairs[j] = pair.astype(bf16)
            coarse_below[j] = row_after(pair).astype(bf16)
            return d, sums + d

        zero = jnp.zeros((HALF, LANES), f32)
        _, sums = over_pairs(coarse_body, (zero, zero))
        bias_down_sum = jnp.broadcast_to(total(sums), (8, LANES))
        yield
        operand = jnp.concatenate(
            [coarse_pairs[...].reshape(BLOCK, LANES), coarse_below[...].reshape(BLOCK, LANES)], axis=1
        )
        y = matmul(operand, w_down[...])
        sums = jnp.zeros((1, LANES), f32)
        for a in range(2):
            v = y[:, a * LANES : (a + 1) * LANES] + level_grad[a].reshape(BLOCK, LANES)
            sums = sums + total(v)
            level_grad[a] = tiles_of(v)
        bias_two_sum = both_parities(sums)
        yield

        def level_tile(parity, j):
            x = level_grad[parity, j]
            tile_level[parity, j] = x.astype(bf16)
            return x

        build_windows(windows, level_tile)
        yield

        def norm_slopes(y, value, k):
            average, inverse = stats[2 * k : 2 * k + 1, :], stats[2 * k + 1 : 2 * k + 2, :]
            gain = inverse * style[2 * k : 2 * k + 1, :]
            half_gain = 0.5 * gain
            half_shift = 0.5 * (style[2 * k + 1 : 2 * k + 2, :] - average * gain)
            scale_sum = jnp.zeros((1, LANES), f32)
            shift_sum = jnp.zeros((1, LANES), f32)
            for a in range(2):
                v = value(a)
                g = 0.5 * y[:, a * LANES : (a + 1) * LANES] * slope_twice(v * half_gain + half_shift)
                pre_grad[a] = tiles_of(g)
                shift_sum = shift_sum + total(g)
                scale_sum = scale_sum + total(g * ((v - average) * inverse))
            scale_sum, shift_sum = both_parities(scale_sum), both_parities(shift_sum)
            factor = style[2 * k : 2 * k + 1, :]
            center = group_sum(factor * shift_sum) / MEMBERS
            tilt = group_sum(factor * scale_sum) / MEMBERS
            slope = (inverse * tilt)[0:1] * inverse
            return scale_sum, shift_sum, gain, slope, slope * average - (inverse * center)[0:1]

        y = matmul(window_operand(windows, range(4)), w_two[...])
        scale_two, shift_two, gain_two, slope_two, constant_two = norm_slopes(
            y, lambda a: middle[a].reshape(BLOCK, LANES), 1
        )
        yield
        row_sums = [zero]

        def mid_tile(parity, j):
            x = pre_grad[parity, j] * gain_two + (constant_two - middle[parity, j] * slope_two)
            tile_mid[parity, j] = x.astype(bf16)
            row_sums[0] = row_sums[0] + x
            return x

        build_windows(windows, mid_tile)
        bias_one_sum = both_parities(total(row_sums[0]))
        yield
        y = matmul(window_operand(windows, range(4)), w_one[...])
        scale_one, shift_one, gain_one, slope_one, constant_one = norm_slopes(
            y, lambda a: frame_image[:, pl.ds(a, HALF, stride=2), :].reshape(BLOCK, LANES), 0
        )
        yield

        def frame_body(j, carry):
            for parity in range(2):
                x = parity_rows(frame_image, parity, j)
                g = pre_grad[parity, j] * gain_one + (constant_one - x * slope_one) + level_grad[parity, j]
                image[j, pl.ds(parity, HALF, stride=2), :] = g
            return carry

        over_pairs(frame_body, 0)
        store_strips(member, image, f, out)
        for k, value in enumerate((scale_one, shift_one, scale_two, shift_two)):
            pieces[k : k + 1, :] = value[0:1]
        pieces[4:8, :] = jnp.zeros((4, LANES), f32)
        for k, value in enumerate((bias_one_sum, bias_two_sum, bias_down_sum, cot_stats[f, 2:3, :])):
            bias_sums[k : k + 1, :] = value[0:1]
        bias_sums[4:8, :] = jnp.zeros((4, LANES), f32)

    staggered(frame(f) for f in range(styles.shape[0]))


def outer(left, right):
    return lax.dot_general(left, right, (((0,), (0,)), ((), ())), preferred_element_type=f32)


def accumulate(wins, tiles, sums):
    win_one, win_two, win_level, win_coarse = wins
    tile_out, tile_level, tile_mid, coarse_pairs = tiles
    sum_one, sum_two, sum_down, sum_up = sums

    @pl.when(pl.program_id(0) == 0)
    def _():
        for ref in sums:
            ref[...] = jnp.zeros_like(ref)

    def blocks(tiles):
        return jnp.concatenate([tiles[0, a].reshape(BLOCK, LANES) for a in range(2)], axis=1)

    level_operand = window_operand(win_level.at[0], range(4))
    out_blocks = blocks(tile_out)
    sum_up[16 * C :, :] += outer(window_operand(win_coarse.at[0], (0, 1, 1, 2)), out_blocks)
    sum_up[: 16 * C, :] += outer(level_operand, out_blocks)
    sum_down[...] += outer(level_operand[:, : 6 * LANES], coarse_pairs[0].reshape(BLOCK, LANES))
    sum_two[...] += outer(window_operand(win_two.at[0], range(4)), blocks(tile_level))
    sum_one[...] += outer(window_operand(win_one.at[0], range(4)), blocks(tile_mid))


def fold(sums, base, p, q):
    halves = []
    for b in range(2):
        rows = [base + ((a + p) * 4 + b + q) * C for a in range(2)]
        halves.append(sums[rows[0] : rows[0] + C, :LANES] + sums[rows[1] : rows[1] + C, LANES:])
    return halves[0] + swap_halves(halves[1])


def weight_kernel(*refs):
    wins, tiles, grads, sums = refs[:4], refs[4:8], refs[8:12], refs[12:]
    g_one, g_two, g_down, g_up = grads
    sum_one, sum_two, sum_down, sum_up = sums
    accumulate(wins, tiles, sums)

    @pl.when(pl.program_id(0) == pl.num_programs(0) - 1)
    def _():
        for p in range(3):
            for q in range(3):
                at = (3 * p + q) * C
                g_one[at : at + C, :] = fold(sum_one, 0, p, q)[:, :C]
                g_two[at : at + C, :] = fold(sum_two, 0, p, q)[:, :C]
                g_up[2 * at : 2 * at + C, :] = fold(sum_up, 16 * C, p, q)[:, :C]
                g_up[2 * at + C : 2 * at + 2 * C, :] = fold(sum_up, 0, p, q)[:, :C]
                place = (p * 4 + q) * C
                g_down[at : at + C, :] = sum_down[place : place + C, :C]


PARTS = 16
FAR_HINT = 90
PAIR_PARTS = 24


def three_parts(exact):
    high = exact.astype(bf16).astype(f32)
    rest = exact - high
    mid = rest.astype(bf16).astype(f32)
    return jnp.concatenate([high, mid, rest - mid], axis=0)


def below(block, rows):
    if block.shape[0] == rows:
        return block
    return jnp.concatenate([block, jnp.zeros((rows - block.shape[0], LANES), f32)], axis=0)


def message_kernel(count, rows, *refs):
    where_ref, wins, tiles = refs[0], refs[1:5], refs[5:9]
    pieces, bias_sums, kept, small, theirs = refs[9:14]
    sums = refs[14:18]
    g_pair, g_up, g_down = refs[18:]
    sum_one, sum_two, sum_down, sum_up = sums
    accumulate(wins, tiles, sums)

    @pl.when(pl.program_id(0) == pl.num_programs(0) - 1)
    def _():
        low_lanes = lane_ids((C, LANES)) < C
        for p in range(3):
            for q in range(3):
                at = (3 * p + q) * C
                g_pair[at : at + C, :] = jnp.where(
                    low_lanes, fold(sum_one, 0, p, q), swap_halves(fold(sum_two, 0, p, q))
                )
                g_up[2 * at : 2 * at + C, :] = fold(sum_up, 16 * C, p, q)
                g_up[2 * at + C : 2 * at + 2 * C, :] = fold(sum_up, 0, p, q)
                place = (p * 4 + q) * C
                g_down[at : at + C, :] = sum_down[place : place + C, :]
        frames = pieces.shape[0]
        small[...] = jnp.zeros_like(small)
        total_bias = bias_sums[0, 0:4, :]
        for f in range(frames):
            small[4 * f : 4 * f + 4, :] = pieces[f, 0:4, :]
            if f > 0:
                total_bias = total_bias + bias_sums[f, 0:4, :]
        small[4 * frames : 4 * frames + 4, :] = total_bias
        sent = below(three_parts(small[...]), rows)
        low_lanes = lane_ids((rows, LANES)) < C
        half = count // 2
        for at in range(half):
            for ref, mine in ((kept, True), (theirs, False)):
                start = pl.multiple_of(seq_owner(where_ref[0], where_ref[1], half, at, mine) * rows, 8)
                blocks = (
                    g_pair[pl.ds(start, rows), :],
                    jnp.where(
                        low_lanes,
                        g_up[pl.ds(pl.multiple_of(2 * start, 8), rows), :],
                        swap_halves(g_up[pl.ds(pl.multiple_of(2 * start + rows, 8), rows), :]),
                    ),
                    jnp.where(low_lanes, g_down[pl.ds(start, rows), :], 0.0 if mine else sent),
                )
                ref[at * 3 * rows : (at + 1) * 3 * rows, :] = jnp.concatenate(blocks, axis=0).astype(ref.dtype)


def join_kernel(half, rows, frames, where_ref, kept, small, theirs, own, *messages):
    first = where_ref[1] % 2 == 0
    at = 2 * rows
    other = theirs[at : at + 3 * PARTS, :].astype(f32)
    other = other[:PARTS] + other[PARTS : 2 * PARTS] + other[2 * PARTS :]
    mine = small[...]
    n = 4 * frames
    exact = jnp.concatenate(
        [
            jnp.where(first, mine[:n], other[:n]),
            jnp.where(first, other[:n], mine[:n]),
            mine[n : n + 4] + other[n : n + 4],
            jnp.zeros((PAIR_PARTS - 2 * n - 4, LANES), f32),
        ],
        axis=0,
    )
    low_lanes = lane_ids((rows, LANES)) < C
    sent = below(three_parts(exact), rows)
    size = 3 * rows
    for k, message in enumerate(messages):
        block = kept[k * size : (k + 1) * size, :] + theirs[k * size : (k + 1) * size, :].astype(f32)
        message[:at, :] = block[:at].astype(bf16)
        message[at:, :] = jnp.where(low_lanes, block[at:], sent).astype(bf16)
        if k == 0:
            own[:at, :] = block[:at]
            own[at:, :] = jnp.where(low_lanes, block[at:], below(exact, rows))


def reduce_kernel(half, rows, cells, frames, *refs):
    where_ref, own = refs[:2]
    messages = refs[2 : 2 + half]
    hots, act_table, noise_table, ada_one, ada_two, out, pieces_one, pieces_two, table = refs[2 + half :]
    place, member = where_ref[0], where_ref[1]
    taken = 4 * frames
    bias = jnp.zeros((4, LANES), f32)
    sums = None
    lanes = lane_ids((1, LANES))
    low_lanes = lanes < C
    at = 2 * rows
    for k, ref in enumerate(messages):
        message = ref[...].astype(f32)
        if k == 0:
            message = jnp.where(member % 2 == 0, own[...], message)
        sums = message if sums is None else sums + message
        small = (
            message[at : at + PAIR_PARTS]
            + message[at + PAIR_PARTS : at + 2 * PAIR_PARTS]
            + message[at + 2 * PAIR_PARTS : at + 3 * PAIR_PARTS]
        )
        turned = swap_halves(small)
        bias = bias + small[taken : taken + 4]
        for f in range(frames):
            row = k * frames + f
            for kind, piece in ((0, pieces_one), (2, pieces_two)):
                low, high = 4 * f + kind, 4 * f + kind + 1
                piece[row : row + 1, :] = jnp.where(low_lanes, turned[low : low + 1], small[high : high + 1])
    hot = hots[:, :TABLE_ROWS]
    table[...] = jnp.zeros_like(table)
    table[ACT_ROW : ACT_ROW + NACT, :] = act_table[...].astype(f32)
    table[NOISE_ROW : NOISE_ROW + NLEV, :] = noise_table[...].astype(f32)
    embed = matmul(hot.astype(bf16), table[...].astype(bf16))

    def exact(left, right, dims):
        return lax.dot_general(left, right, (dims, ((), ())), precision=precise, preferred_element_type=f32)

    one, two = pieces_one[...], pieces_two[...]
    at = 3 * rows
    out[:at, :] = sums
    out[at : at + cells, :] = exact(embed, one, ((0,), (0,)))
    out[at + cells : at + 2 * cells, :] = exact(embed, two, ((0,), (0,)))
    embed_grad = exact(one, ada_one[...].astype(f32), ((1,), (1,))) + exact(two, ada_two[...].astype(f32), ((1,), (1,)))
    at = at + 2 * cells
    out[at : at + TABLE_ROWS, :] = jnp.zeros((TABLE_ROWS, LANES), f32)
    out[at : at + TABLE_ROWS, :cells] = exact(hot, embed_grad, ((0,), (0,)))
    at = at + TABLE_ROWS
    bias = jnp.concatenate([bias, jnp.zeros((4, LANES), f32)], axis=0)
    width = C // (2 * half)
    out[at : at + 8, :] = pltpu.roll(bias, (C - place * width) % LANES, axis=1)


def finish_kernel(rows, cells, first, second, *outs):
    act_grad, noise_grad, ada_one, ada_two, g_one, g_two, g_down, g_up = outs[:8]
    bias_grads = outs[8:12]
    sums = first[...] + second[...]

    def turn(block):
        return jnp.concatenate([block, jnp.zeros((LANES - rows, LANES), f32)], axis=0).T[:, :rows]

    pair, halves, down = (turn(sums[k * rows : (k + 1) * rows]) for k in range(3))
    g_one[...] = pair[:C]
    g_two[...] = pair[C:]
    g_up[:, :rows] = halves[:C]
    g_up[:, rows:] = halves[C:]
    g_down[...] = down[:C]
    at = 3 * rows
    ada_one[...] = sums[at : at + cells]
    ada_two[...] = sums[at + cells : at + 2 * cells]
    at = at + 2 * cells
    act_grad[...] = sums[at + ACT_ROW : at + ACT_ROW + NACT, :cells]
    noise_grad[...] = sums[at + NOISE_ROW : at + NOISE_ROW + NLEV, :cells]
    at = at + TABLE_ROWS
    for k, ref in enumerate(bias_grads):
        ref[...] = sums[at + k : at + k + 1, : ref.shape[0]].reshape(ref.shape)


def write_operands(block, f_one, f_two, f_down, f_up, b_one, b_two, b_down, b_up):
    low_lanes = lane_ids((C, LANES)) < C
    zero = jnp.zeros((C, LANES), f32)

    def taps(name, base, step):
        plain, turned = {}, {}
        for p in range(3):
            for q in range(3):
                k = block(name, (3 * p + q) * step + base)
                plain[p, q] = k
                turned[p, q] = jnp.concatenate([k, k], axis=0).T[:C]
        return plain, turned

    def write_forward(ref, base, plain):
        for w in range(4):
            for p in range(3):
                tile = jnp.where(low_lanes, plain.get((p, w), zero), plain.get((p, w - 1), zero)).astype(bf16)
                for a in range(2):
                    at = base + ((a + p) * 4 + w) * C
                    ref[at : at + C, a * LANES : (a + 1) * LANES] = tile
            for a in range(2):
                for r in range(4):
                    if not 0 <= r - a < 3:
                        at = base + (r * 4 + w) * C
                        ref[at : at + C, a * LANES : (a + 1) * LANES] = zero.astype(bf16)

    def write_backward(ref, lane, turned):
        for w in range(4):
            for p in range(3):
                tile = jnp.where(low_lanes, turned.get((p, 2 - w), zero), turned.get((p, 3 - w), zero)).astype(bf16)
                for a in range(2):
                    at = ((a + 2 - p) * 4 + w) * C
                    ref[at : at + C, lane + a * LANES : lane + (a + 1) * LANES] = tile
            for a in range(2):
                for r in range(4):
                    if not 0 <= a + 2 - r < 3:
                        at = (r * 4 + w) * C
                        ref[at : at + C, lane + a * LANES : lane + (a + 1) * LANES] = zero.astype(bf16)

    for name, forward_ref, backward_ref in (("one", f_one, b_one), ("two", f_two, b_two)):
        plain, turned = taps(name, 0, C)
        write_forward(forward_ref, 0, plain)
        write_backward(backward_ref, 0, turned)
    plain, turned = taps("up", 0, 2 * C)
    write_forward(f_up, 16 * C, plain)
    write_backward(b_up, 0, turned)
    plain, turned = taps("up", C, 2 * C)
    write_forward(f_up, 0, plain)
    write_backward(b_up, 2 * LANES, turned)
    plain, turned = taps("down", 0, C)
    for p in range(3):
        for w in range(4):
            at = (p * 4 + w) * C
            f_down[at : at + C, :] = plain.get((p, w), zero).astype(bf16)
    for below in range(2):
        for right in range(2):
            at = (below * 2 + right) * C
            for a in range(2):
                p = {(0, 0): 1, (0, 1): 2, (1, 1): 0}.get((below, a))
                first, second = zero, zero
                if p is not None:
                    first = turned[p, 1] if right == 0 else zero
                    second = turned[p, 2] if right == 0 else turned[p, 0]
                b_down[at : at + C, a * LANES : (a + 1) * LANES] = jnp.where(low_lanes, first, second).astype(bf16)


def expand_kernel(conv_one, conv_two, down_kernel, up_kernel, *outs):
    kernels = {"one": conv_one, "two": conv_two, "down": down_kernel, "up": up_kernel}

    def block(name, row):
        k = kernels[name][row : row + C, :].astype(f32)
        return jnp.concatenate([k, k], axis=1)

    write_operands(block, *outs)


ACT_ROW, NOISE_ROW, TABLE_ROWS = 0, 24, 56
BIAS_ROW, ID_ROW = 56, 64


def pack_sizes(rows, cells):
    return 3 * rows, 3 * rows + 2 * cells, -(-(3 * rows + 2 * cells) // 16) * 16


def turned(values):
    wide = jnp.concatenate([values, jnp.zeros((C, LANES - values.shape[1]), f32)], axis=1)
    return jnp.concatenate([wide, jnp.zeros((C, LANES), f32)], axis=0).T[: values.shape[1]]


def far_kernel(member_ref, array, out, sent):
    half = array.shape[0] // 2
    copy = pltpu.make_async_copy(array.at[pl.ds((1 - member_ref[0] // 2) * half, half)], out, sent)
    copy.start()
    copy.wait()


def near_kernel(member_ref, array, far, out, sent):
    share = out.shape[0] // 2
    other = member_ref[0] ^ 1
    copy = pltpu.make_async_copy(array.at[pl.ds(other * share, share)], out.at[pl.ds(0, share)], sent)
    copy.start()
    out[share:] = far[pl.ds(other % 2 * share, share)]
    copy.wait()


def pack_kernel(*refs):
    actions, noise_ids, valid, conv_one, conv_two, down_kernel, up_kernel, ada_one, ada_two = refs[:9]
    act_table, noise_table = refs[9:11]
    biases = refs[11:15]
    out, work = refs[15:]
    rows, cells = conv_one.shape[1], ada_one.shape[0]
    style_at, end, _ = pack_sizes(rows, cells)
    wide = lambda ref: ref[...].astype(f32)
    low_lanes = lane_ids((rows, LANES)) < C
    up = wide(up_kernel)
    work[...] = jnp.zeros_like(work)
    for at, low, high in (
        (0, turned(wide(conv_one)), turned(wide(conv_two))),
        (rows, turned(up[:, :rows]), turned(up[:, rows:])),
    ):
        work[at : at + rows, :] = jnp.where(low_lanes, low, swap_halves(high))
    work[2 * rows : 3 * rows, :] = turned(wide(down_kernel))
    extra = 2 * rows
    for at, ref in ((ACT_ROW, act_table), (NOISE_ROW, noise_table)):
        size = ref.shape
        work[extra + at : extra + at + size[0], C : C + size[1]] = wide(ref)
    for k, ref in enumerate(biases):
        at = extra + BIAS_ROW + k
        work[at : at + 1, C : C + ref.shape[0]] = wide(ref).reshape(1, ref.shape[0])
    lanes = lane_ids((1, LANES))
    for k, ref in enumerate((actions, noise_ids, valid)):
        line = jnp.zeros((1, LANES), jnp.int32)
        for f in range(ref.shape[0]):
            line = jnp.where(lanes == C + f, ref[f], line)
        at = extra + ID_ROW + k
        work[at : at + 1, C:] = line.astype(f32)[:, C:]
    work[style_at : style_at + cells, :] = wide(ada_one)
    work[style_at + cells : end, :] = wide(ada_two)
    out[...] = work[...].astype(bf16)


def seq_owner(place, member, half, at, mine=True):
    side = member % 2 if mine else 1 - member % 2
    even, odd = sides(2 * half)
    return place ^ (even[at] + side * (odd[at] - even[at]))


def sides(count):
    ones = lambda offset: bin(offset).count("1") % 2
    return tuple([offset for offset in range(count) if ones(offset) == side] for side in (0, 1))


def write_hots(hots, at, first, frames, ids):
    lanes = lane_ids((1, LANES)).astype(f32)
    for f in range(frames):
        mine = jnp.where(lane_ids(ids.shape) == C + first + f, ids, 0.0)
        mine = jnp.sum(mine, axis=1, keepdims=True)
        action, noise, valid = mine[0:1], mine[1:2], mine[2:3]
        hots[at + f : at + f + 1, :] = jnp.where(lanes == action + ACT_ROW, valid, 0.0) + jnp.where(
            lanes == noise + NOISE_ROW, 1.0, 0.0
        )


def prepare_kernel(count, rows, cells, *refs):
    where_ref, actions, noise_ids, valid, packed, mine, other = refs[:7]
    outs = refs[7:15]
    styles, biases, hots = refs[15:18]
    work_pair, work_up, work_down, work_one, work_two, work_table = refs[18:]
    place, member, frames = where_ref[0], where_ref[1], styles.shape[0]
    style_at, _, size = pack_sizes(rows, cells)
    bias_rows = jnp.zeros(SMALL, f32)
    half = count // 2
    for offset in range(count):
        ref = mine if offset < half else other
        at = offset % half
        pack = ref[at * size : (at + 1) * size, :].astype(f32)
        if at == 0:
            pack = jnp.where(member % 2 == offset // half, packed[...].astype(f32), pack)
        owner = seq_owner(place, member, half, at, offset < half)
        start = pl.multiple_of(owner * rows, 8)
        work_pair[pl.ds(start, rows), :] = pack[:rows]
        halves = pack[rows : 2 * rows]
        work_up[pl.ds(2 * start, rows), :] = halves
        work_up[pl.ds(pl.multiple_of(2 * start + rows, 8), rows), :] = swap_halves(halves)
        extra = pack[2 * rows : 3 * rows]
        work_down[pl.ds(start, rows), :] = extra
        work_one[offset * cells : (offset + 1) * cells, :] = pack[style_at : style_at + cells]
        work_two[offset * cells : (offset + 1) * cells, :] = pack[style_at + cells : style_at + 2 * cells]
        lane = (offset * cells) % LANES
        tables = pltpu.roll(extra[:TABLE_ROWS], (lane - C) % LANES, axis=1)
        kept = (lane_ids(tables.shape) >= lane) & (lane_ids(tables.shape) < lane + cells)
        column = offset * cells // LANES
        tables = jnp.where(kept, tables, 0.0)
        if lane == 0:
            work_table[column] = tables
        else:
            work_table[column] += tables
        slots = extra[BIAS_ROW : BIAS_ROW + 8]
        width = C // count
        slots = jnp.where((lane_ids(SMALL) >= C) & (lane_ids(SMALL) < C + width), slots, 0.0)
        bias_rows = bias_rows + pltpu.roll(slots, (owner * width + C) % LANES, axis=1)
        if offset < half:
            write_hots(hots, at * 2 * frames, member // 2 * 2 * frames, 2 * frames, extra[ID_ROW : ID_ROW + 8])
    biases[...] = bias_rows + swap_halves(bias_rows)

    lanes = lane_ids((8, LANES))
    row_at = lax.broadcasted_iota(jnp.int32, (8, LANES), 0)
    hot = jnp.zeros((8, LANES), f32)
    for f in range(frames):
        at = member * frames + f
        here = jnp.where(lanes == actions[at] + ACT_ROW, valid[at], 0) + jnp.where(lanes == noise_ids[at] + NOISE_ROW, 1, 0)
        hot = jnp.where(row_at == f, here.astype(f32), hot)
    hot = hot[:, :TABLE_ROWS].astype(bf16)
    embed = jnp.concatenate([matmul(hot, work_table[k].astype(bf16)) for k in range(work_table.shape[0])], axis=1)
    low_lanes = lanes < C
    for k, work in enumerate((work_one, work_two)):
        style = jnp.dot(embed, work[...], precision=precise, preferred_element_type=f32)
        other = swap_halves(style)
        scale = 1.0 + jnp.where(low_lanes, style, other)
        shift = jnp.where(low_lanes, other, style)
        for f in range(frames):
            styles[f, 2 * k : 2 * k + 1, :] = scale[f : f + 1]
            styles[f, 2 * k + 1 : 2 * k + 2, :] = shift[f : f + 1]
    for f in range(frames):
        styles[f, 4:8, :] = jnp.zeros((4, LANES), f32)

    def block(name, row):
        work = {"one": work_pair, "two": work_pair, "down": work_down, "up": work_up}[name]
        k = work[row : row + C, :]
        low = lane_ids(k.shape) < C
        if name == "two":
            return jnp.where(low, swap_halves(k), k)
        return jnp.where(low, k, swap_halves(k))

    write_operands(block, *outs)


def shape(dims, kind):
    return jax.ShapeDtypeStruct(dims, kind)


def whole(dims):
    return pl.BlockSpec(dims, lambda f: (0,) * len(dims))


def per_frame(dims):
    return pl.BlockSpec((1,) + dims, lambda f: (f,) + (0,) * len(dims))


def strip_specs(count, strip):
    return [pl.BlockSpec((1, strip, W * C), lambda f: (f, 0, 0))] * count


SMALL = (8, LANES)
WINDOWS = (4, PAIRS + 1, HALF, LANES)
COARSE_WINDOWS = (3, PAIRS + 1, HALF, LANES)
TILES = (2, PAIRS, HALF, LANES)
COARSE = (PAIRS, HALF, LANES)
IMAGE = (PAIRS, H, LANES)
KEYS = 16 * C


def in_vmem():
    return pl.BlockSpec(memory_space=pltpu.VMEM)


def in_smem():
    return pl.BlockSpec(memory_space=pltpu.SMEM)


def params(limit=VMEM_LIMIT):
    return pltpu.CompilerParams(vmem_limit_bytes=limit)


def cost(macs, moved):
    return pl.CostEstimate(flops=2 * macs, bytes_accessed=moved, transcendentals=0)


def expand(conv_one, conv_two, down_kernel, up_kernel):
    vmem = pl.BlockSpec(memory_space=pltpu.VMEM)
    return pl.pallas_call(
        expand_kernel,
        in_specs=[vmem] * 4,
        out_specs=[vmem] * 8,
        out_shape=[
            shape((KEYS, 2 * LANES), bf16),
            shape((KEYS, 2 * LANES), bf16),
            shape((6 * LANES, LANES), bf16),
            shape((2 * KEYS, 2 * LANES), bf16),
            shape((KEYS, 2 * LANES), bf16),
            shape((KEYS, 2 * LANES), bf16),
            shape((2 * LANES, 2 * LANES), bf16),
            shape((KEYS, 4 * LANES), bf16),
        ],
        compiler_params=params(),
        name="expand",
    )(conv_one, conv_two, down_kernel, up_kernel)


def gather_frames(member, array, far, hint=0):
    frames = array.shape[0] // lax.axis_size("rows")
    near = trade(cut_near(member, array, far, hint), 1)
    return pl.pallas_call(
        gather_kernel,
        in_specs=[in_smem(), in_place()] + [in_vmem()] * 2,
        out_specs=[in_vmem()] * 2,
        out_shape=[shape((frames,) + IMAGE, f32), shape((frames,) + SMALL, f32)],
        scratch_shapes=[pltpu.VMEM((frames,) + array.shape[1:], array.dtype), pltpu.SemaphoreType.DMA],
        compiler_params=params(),
        name="frames",
    )(member, array, far, near)


def forward(member, frame_images, frame_stats, styles, biases, w_one, w_two, w_down, w_up, count):
    frames = frame_images.shape[0]
    strip = H // count
    return pl.pallas_call(
        lambda *refs: forward_kernel(count, *refs),
        in_specs=[in_smem()] + [in_vmem()] * 8,
        out_specs=[in_vmem()] * (count + 7),
        out_shape=[shape((frames, strip, W * C), bf16)] * count
        + [
            shape((frames,) + WINDOWS, bf16),
            shape((frames,) + WINDOWS, bf16),
            shape((frames,) + WINDOWS, bf16),
            shape((frames,) + COARSE_WINDOWS, bf16),
            shape((frames,) + TILES, f32),
            shape((frames,) + COARSE, f32),
            shape((frames,) + SMALL, f32),
        ],
        scratch_shapes=[pltpu.VMEM((frames,) + IMAGE, f32), pltpu.VMEM((frames,) + TILES, f32)],
        compiler_params=params(),
        cost_estimate=cost(1 << 10, 1 << 10),
        name="forward",
    )(member, frame_images, frame_stats, styles, biases, w_one, w_two, w_down, w_up)


def backward(member, cot, frame_images, styles, stats, middle, down, w_up, w_down, w_two, w_one, count):
    frames = frame_images.shape[0]
    strip = H // count
    return pl.pallas_call(
        lambda *refs: backward_kernel(count, *refs),
        in_specs=[in_smem()] + [in_vmem()] * 11,
        out_specs=[in_vmem()] * (count + 6),
        out_shape=[shape((frames, strip, W * C), bf16)] * count
        + [
            shape((frames,) + TILES, bf16),
            shape((frames,) + TILES, bf16),
            shape((frames,) + TILES, bf16),
            shape((frames,) + COARSE, bf16),
            shape((frames,) + SMALL, f32),
            shape((frames,) + SMALL, f32),
        ],
        scratch_shapes=[
            pltpu.VMEM((frames,) + IMAGE, f32),
            pltpu.VMEM((frames,) + TILES, f32),
            pltpu.VMEM((frames,) + TILES, f32),
            pltpu.VMEM((frames,) + WINDOWS, bf16),
            pltpu.VMEM((frames,) + COARSE, bf16),
        ],
        compiler_params=params(),
        cost_estimate=cost(frames * BLOCK * KEYS * 2 * LANES * 5, frames * (10 << 20)),
        name="backward",
    )(member, *cot, frame_images, styles, stats, middle, down, w_up, w_down, w_two, w_one)


def weight_grads(win_one, win_two, win_level, win_coarse, tile_out, tile_level, tile_mid, coarse_pairs):
    frames = win_one.shape[0]
    return pl.pallas_call(
        weight_kernel,
        grid=(frames,),
        in_specs=[
            per_frame(d) for d in (WINDOWS, WINDOWS, WINDOWS, COARSE_WINDOWS, TILES, TILES, TILES, COARSE)
        ],
        out_specs=[whole((9 * C, C)), whole((9 * C, C)), whole((9 * C, C)), whole((18 * C, C))],
        out_shape=[shape((9 * C, C), f32)] * 3 + [shape((18 * C, C), f32)],
        scratch_shapes=[
            pltpu.VMEM((KEYS, 2 * LANES), f32),
            pltpu.VMEM((KEYS, 2 * LANES), f32),
            pltpu.VMEM((6 * LANES, LANES), f32),
            pltpu.VMEM((2 * KEYS, 2 * LANES), f32),
        ],
        compiler_params=params(),
        cost_estimate=cost(frames * BLOCK * KEYS * 2 * LANES * 5, frames * (6 << 20)),
        name="weights",
    )(win_one, win_two, win_level, win_coarse, tile_out, tile_level, tile_mid, coarse_pairs)


def in_place(space=pl.ANY):
    return pl.BlockSpec(memory_space=space)


def cut_far(member, array):
    array = pltpu.with_memory_space_constraint(array, pltpu.HBM)
    return pl.pallas_call(
        far_kernel,
        in_specs=[in_smem(), in_place(pltpu.HBM)],
        out_specs=in_vmem(),
        out_shape=shape((array.shape[0] // 2,) + array.shape[1:], array.dtype),
        scratch_shapes=[pltpu.SemaphoreType.DMA],
        compiler_params=params(),
        name="far",
    )(member, array)


def cut_near(member, array, far, hint):
    return pl.pallas_call(
        near_kernel,
        in_specs=[in_smem(), in_place(), in_vmem()],
        out_specs=in_vmem(),
        out_shape=shape(far.shape, array.dtype),
        scratch_shapes=[pltpu.SemaphoreType.DMA],
        compiler_params=params(),
        cost_estimate=cost(BLOCK * KEYS * 2 * LANES * hint, 1 << 20),
        name="near",
    )(member, array, far)


def pack(ids, kernels, ada_one, ada_two, act_table, noise_table, biases):
    _, _, size = pack_sizes(kernels[0].shape[0], ada_one.shape[0])
    args = (*[kernel.T for kernel in kernels], ada_one, ada_two, act_table, noise_table, *biases)
    return pl.pallas_call(
        pack_kernel,
        in_specs=[in_smem()] * 3 + [in_vmem()] * len(args),
        out_specs=in_vmem(),
        out_shape=shape((size, LANES), bf16),
        scratch_shapes=[pltpu.VMEM((size, LANES), f32)],
        compiler_params=params(VMEM_MOST),
        cost_estimate=cost(BLOCK * KEYS * 2 * LANES * 30, 1 << 20),
        name="pack",
    )(*ids, *args)


OPERANDS = (
    (KEYS, 2 * LANES),
    (KEYS, 2 * LANES),
    (6 * LANES, LANES),
    (2 * KEYS, 2 * LANES),
    (KEYS, 2 * LANES),
    (KEYS, 2 * LANES),
    (2 * LANES, 2 * LANES),
    (KEYS, 4 * LANES),
)


def prepare(where, ids, packed, mine, other, count, rows, cells, frames):
    return pl.pallas_call(
        lambda *refs: prepare_kernel(count, rows, cells, *refs),
        in_specs=[in_smem()] * 4 + [in_vmem()] * 3,
        out_specs=[in_vmem()] * 11,
        out_shape=[shape(d, bf16) for d in OPERANDS]
        + [shape((frames,) + SMALL, f32), shape(SMALL, f32), shape((count * frames, LANES), f32)],
        scratch_shapes=[
            pltpu.VMEM((9 * C, LANES), f32),
            pltpu.VMEM((18 * C, LANES), f32),
            pltpu.VMEM((9 * C, LANES), f32),
            pltpu.VMEM((count * cells, LANES), f32),
            pltpu.VMEM((count * cells, LANES), f32),
            pltpu.VMEM((count * cells // LANES, TABLE_ROWS, LANES), f32),
        ],
        compiler_params=params(),
        name="prepare",
    )(where, *ids, packed, mine, other)


def weight_messages(where, wins, tiles, pieces, bias_sums, count, rows):
    frames = pieces.shape[0]
    size = count // 2 * 3 * rows
    return pl.pallas_call(
        lambda *refs: message_kernel(count, rows, *refs),
        grid=(frames,),
        in_specs=[in_smem()]
        + [per_frame(d) for d in (WINDOWS, WINDOWS, WINDOWS, COARSE_WINDOWS, TILES, TILES, TILES, COARSE)]
        + [whole((frames,) + SMALL)] * 2,
        out_specs=[whole((size, LANES)), whole((PARTS, LANES)), whole((size, LANES))],
        out_shape=[shape((size, LANES), f32), shape((PARTS, LANES), f32), shape((size, LANES), bf16)],
        scratch_shapes=[
            pltpu.VMEM((KEYS, 2 * LANES), f32),
            pltpu.VMEM((KEYS, 2 * LANES), f32),
            pltpu.VMEM((6 * LANES, LANES), f32),
            pltpu.VMEM((2 * KEYS, 2 * LANES), f32),
            pltpu.VMEM((9 * C, LANES), f32),
            pltpu.VMEM((18 * C, LANES), f32),
            pltpu.VMEM((9 * C, LANES), f32),
        ],
        compiler_params=params(),
        cost_estimate=cost(frames * BLOCK * KEYS * 2 * LANES * 5, frames * (6 << 20)),
        name="weights",
    )(where, *wins, *tiles, pieces, bias_sums)


def join_messages(where, kept, small, theirs, half, rows, frames):
    return pl.pallas_call(
        lambda *refs: join_kernel(half, rows, frames, *refs),
        in_specs=[in_smem()] + [in_vmem()] * 3,
        out_specs=[in_vmem()] * (1 + half),
        out_shape=[shape((3 * rows, LANES), f32)] + [shape((3 * rows, LANES), bf16)] * half,
        compiler_params=params(),
        name="join",
    )(where, kept, small, theirs)


def reduce_messages(where, own, messages, hots, act_table, noise_table, ada_one, ada_two, rows, cells, frames):
    half = len(messages)
    return pl.pallas_call(
        lambda *refs: reduce_kernel(half, rows, cells, frames, *refs),
        in_specs=[in_smem()] + [in_vmem()] * (half + 6),
        out_specs=in_vmem(),
        out_shape=shape((3 * rows + 2 * cells + TABLE_ROWS + 8, LANES), f32),
        scratch_shapes=[
            pltpu.VMEM((half * frames, LANES), f32),
            pltpu.VMEM((half * frames, LANES), f32),
            pltpu.VMEM((TABLE_ROWS, cells), f32),
        ],
        compiler_params=params(),
        name="reduce",
    )(where, own, *messages, hots, act_table, noise_table, ada_one, ada_two)


def finish(first, second, rows, cells, width):
    act_grad, noise_grad, one, two, *rest = pl.pallas_call(
        lambda *refs: finish_kernel(rows, cells, *refs),
        in_specs=[in_vmem()] * 2,
        out_specs=[in_vmem()] * 12,
        out_shape=[
            shape((NACT, cells), f32),
            shape((NLEV, cells), f32),
            shape((cells, LANES), f32),
            shape((cells, LANES), f32),
            shape((C, rows), f32),
            shape((C, rows), f32),
            shape((C, rows), f32),
            shape((C, 2 * rows), f32),
        ]
        + [shape((width,), f32)] * 4,
        compiler_params=params(),
        name="finish",
    )(first, second)
    return (act_grad, noise_grad, one, two, *[grad.T for grad in rest[:4]], *rest[4:])


def collect_kernel(member_ref, *refs):
    strips, out = refs[:-1], refs[-1]
    for offset, strip in enumerate(strips):
        out[member_ref[0] ^ offset, 0] = strip[0].astype(out.dtype)


def trade_strips(strips):
    return tuple(trade(strip, offset) for offset, strip in enumerate(strips))


def collect_strips(member_box, strips, kind):
    count = len(strips)
    frames, rows, columns = strips[0].shape
    whole_strips = pl.pallas_call(
        collect_kernel,
        grid=(frames,),
        in_specs=[in_smem()] + [pl.BlockSpec((1, rows, columns), lambda f: (f, 0, 0))] * count,
        out_specs=pl.BlockSpec((count, 1, rows, columns), lambda f: (0, f, 0, 0)),
        out_shape=shape((count, frames, rows, columns), kind),
        compiler_params=params(),
        name="collect",
    )(member_box, *strips)
    return whole_strips.reshape(count * frames, rows, columns)


def twice(values):
    return jnp.concatenate([values, values], axis=-1)


def pad_small(rows):
    stacked = jnp.stack(rows, axis=-2)
    gaps = [(0, 0)] * (stacked.ndim - 2) + [(0, 8 - len(rows)), (0, 0)]
    return jnp.pad(stacked, gaps)


def trade(value, offset):
    if offset == 0:
        return value
    count = lax.axis_size("rows")
    return lax.ppermute(value, "rows", [(i, i ^ offset) for i in range(count)])


def half_trade(value, at):
    count, members = lax.axis_size("seq"), lax.axis_size("rows")
    pairs = []
    for place in range(count):
        for member in range(members):
            offset = sides(count)[member % 2][at]
            if offset:
                pairs.append((place * members + member, (place ^ offset) * members + member))
    return lax.ppermute(value, ("seq", "rows"), pairs)


def layers(member_box, frame_images, frame_stats, cotangent, cot_far, styles, bias_rows, operands):
    f_one, f_two, f_down, f_up, b_one, b_two, b_down, b_up = operands
    count = lax.axis_size("rows")
    *out, win_one, win_two, win_level, win_coarse, middle, down, stats = forward(
        member_box, frame_images, frame_stats, styles, bias_rows, f_one, f_two, f_down, f_up, count
    )
    out = trade_strips(out)
    down, cot_far = lax.optimization_barrier((down, cot_far))
    cot = gather_frames(member_box, cotangent, cot_far)
    *grad_strips, tile_out, tile_level, tile_mid, coarse_pairs, pieces, bias_sums = backward(
        member_box, cot, frame_images, styles, stats, middle, down, b_up, b_down, b_two, b_one, count
    )
    grad_strips = trade_strips(grad_strips)
    wins = (win_one, win_two, win_level, win_coarse)
    tiles = (tile_out, tile_level, tile_mid, coarse_pairs)
    return out, grad_strips, wins, tiles, pieces, bias_sums


def local_direct(
    frames,
    cotangent,
    actions,
    noise_ids,
    valid,
    act_table,
    noise_table,
    ada_one,
    ada_two,
    conv_one,
    conv_two,
    down_kernel,
    up_kernel,
    bias_one,
    bias_two,
    bias_down,
    bias_up,
):
    member = lax.axis_index("rows").astype(jnp.int32)
    place = lax.axis_index("seq").astype(jnp.int32)
    count = lax.axis_size("seq")
    share = frames.shape[0] // lax.axis_size("rows")
    rows, cells, width = conv_one.shape[0], ada_one.shape[0], bias_one.shape[0]
    half = count // 2
    member_box = member.reshape(1)
    where = jnp.stack([place, member])
    ids = (actions, noise_ids, valid)
    kernels = (conv_one, conv_two, down_kernel, up_kernel)
    biases = (bias_one, bias_two, bias_down, bias_up)
    far = trade(cut_far(member_box, frames), 2)
    packed = pack(ids, kernels, ada_one, ada_two, act_table, noise_table, biases)
    mine = jnp.concatenate([half_trade(packed, at) for at in range(half)], axis=0)
    other = trade(mine, 1)
    cot_far = trade(cut_far(member_box, cotangent), 2)
    frame_images, frame_stats = gather_frames(member_box, frames, far, FAR_HINT)
    *operands, styles, bias_rows, hots = prepare(where, ids, packed, mine, other, count, rows, cells, share)
    out, grad_strips, wins, tiles, pieces, bias_sums = layers(
        member_box, frame_images, frame_stats, cotangent, cot_far, styles, bias_rows, operands
    )
    kept, small, theirs = weight_messages(where, wins, tiles, pieces, bias_sums, count, rows)
    theirs, out = lax.optimization_barrier((theirs, out))
    own, *messages = join_messages(where, kept, small, trade(theirs, 1), half, rows, share)
    received = [half_trade(message, at) for at, message in enumerate(messages)]
    received, grad_strips = lax.optimization_barrier((received, grad_strips))
    sums = reduce_messages(
        where, own, received, hots, act_table, noise_table, ada_one, ada_two, rows, cells, 2 * share
    )
    offset = 1
    while 2 * offset < lax.axis_size("rows"):
        sums = sums + trade(sums, offset)
        offset *= 2
    result = collect_strips(member_box, out, bf16)
    frames_grad = collect_strips(member_box, grad_strips, f32)
    return (result, frames_grad, *finish(sums, trade(sums, offset), rows, cells, width))


def local_general(
    frames,
    cotangent,
    actions,
    noise_ids,
    valid,
    act_table,
    noise_table,
    ada_one,
    ada_two,
    conv_one,
    conv_two,
    down_kernel,
    up_kernel,
    bias_one,
    bias_two,
    bias_down,
    bias_up,
):
    member = lax.axis_index("rows").astype(jnp.int32)
    share = frames.shape[0] // lax.axis_size("rows")
    member_box = member.reshape(1)

    def gathered(value, axis):
        return lax.all_gather(value, "seq", axis=axis, tiled=True)

    cot_far = trade(cut_far(member_box, cotangent), 2)
    far = trade(cut_far(member_box, frames), 2)
    frame_images, frame_stats = gather_frames(member_box, frames, far)
    act_full = gathered(act_table, 1)
    noise_full = gathered(noise_table, 1)
    ada_full = gathered(jnp.concatenate([ada_one, ada_two], axis=1), 0).astype(f32)
    biases = gathered(jnp.stack([bias_one, bias_two, bias_down, bias_up]), 1).astype(f32)
    operands = expand(gathered(conv_one, 0), gathered(conv_two, 0), gathered(down_kernel, 0), gathered(up_kernel, 0))

    own = lambda ids: lax.dynamic_slice_in_dim(ids, member * share, share)
    own_actions, own_noise, own_valid = own(actions), own(noise_ids), own(valid)
    action_hot = (own_actions[:, None] == jnp.arange(NACT, dtype=jnp.int32)[None, :]).astype(f32) * own_valid[
        :, None
    ].astype(f32)
    noise_hot = (own_noise[:, None] == jnp.arange(NLEV, dtype=jnp.int32)[None, :]).astype(f32)
    embed = jnp.dot(action_hot, act_full.astype(f32), precision=precise) + jnp.dot(
        noise_hot, noise_full.astype(f32), precision=precise
    )
    style = jnp.dot(embed, ada_full, precision=precise)
    styles = pad_small(
        [
            twice(1.0 + style[:, :C]),
            twice(style[:, C : 2 * C]),
            twice(1.0 + style[:, 2 * C : 3 * C]),
            twice(style[:, 3 * C :]),
        ]
    )
    bias_rows = pad_small([twice(biases[k]) for k in range(4)])
    out, grad_strips, wins, tiles, pieces, bias_sums = layers(
        member_box, frame_images, frame_stats, cotangent, cot_far, styles, bias_rows, operands
    )
    g_one, g_two, g_down, g_up = weight_grads(*wins, *tiles)
    result = collect_strips(member_box, out, bf16)
    frames_grad = collect_strips(member_box, grad_strips, f32)

    pieces_one = jnp.concatenate([pieces[:, 0, :C], pieces[:, 1, :C]], axis=1)
    pieces_two = jnp.concatenate([pieces[:, 2, :C], pieces[:, 3, :C]], axis=1)
    ada_one_grad = jnp.dot(embed.T, pieces_one, precision=precise)
    ada_two_grad = jnp.dot(embed.T, pieces_two, precision=precise)
    embed_grad = jnp.dot(jnp.concatenate([pieces_one, pieces_two], axis=1), ada_full.T, precision=precise)
    act_table_grad = jnp.dot(action_hot.T, embed_grad, precision=precise)
    noise_table_grad = jnp.dot(noise_hot.T, embed_grad, precision=precise)
    bias_total = jnp.sum(bias_sums, axis=0)[:4, :C]

    def shard(value, axis):
        return lax.psum_scatter(value, "seq", scatter_dimension=axis, tiled=True)

    shards = (
        shard(act_table_grad, 1),
        shard(noise_table_grad, 1),
        shard(ada_one_grad, 0),
        shard(ada_two_grad, 0),
        shard(g_one, 0),
        shard(g_two, 0),
        shard(g_down, 0),
        shard(g_up, 0),
        shard(bias_total[0], 0),
        shard(bias_total[1], 0),
        shard(bias_total[2], 0),
        shard(bias_total[3], 0),
    )
    return (result, frames_grad) + lax.psum(shards, "rows")


def fits_direct(mesh):
    count = mesh.shape["seq"]
    rows, cells = 9 * C // count, 256 // count
    return count in (2, 4, 8) and rows % 8 == 0 and rows >= ID_ROW + 8 and cells % 8 == 0 and mesh.shape["rows"] == 4


def solution(mesh):
    in_specs = (
        P("seq", "rows", None),
        P("seq", "rows", None),
        P("seq"),
        P("seq"),
        P("seq"),
        P(None, "seq"),
        P(None, "seq"),
        P("seq", None),
        P("seq", None),
        P("seq", None),
        P("seq", None),
        P("seq", None),
        P("seq", None),
        P("seq"),
        P("seq"),
        P("seq"),
        P("seq"),
    )
    out_specs = (
        P("seq", "rows", None),
        P("seq", "rows", None),
        P(None, "seq"),
        P(None, "seq"),
        P("seq", None),
        P("seq", None),
        P("seq", None),
        P("seq", None),
        P("seq", None),
        P("seq", None),
        P("seq"),
        P("seq"),
        P("seq"),
        P("seq"),
    )
    local = local_direct if fits_direct(mesh) else local_general
    return jax.shard_map(local, mesh=mesh, in_specs=in_specs, out_specs=out_specs, check_vma=False)
```

```python
import jax
import jax.numpy as jnp
from jax import lax
from jax.experimental import pallas as pl
from jax.experimental.pallas import tpu as pltpu
from jax.sharding import PartitionSpec as P

C = 64
NACT = 18
GROUPS = 32
NLEV = 32
H = 64
W = 64
PAIRS = W // 2
HALF = H // 2
LANES = 2 * C
BLOCK = PAIRS * HALF
MEMBERS = float(H * W * (C // GROUPS))
EPS = 1e-05

precise = lax.Precision.HIGHEST
f32 = jnp.float32
bf16 = jnp.bfloat16
VMEM_LIMIT = 16 * 2**20
VMEM_MOST = 60 * 2**20


def lane_ids(shape):
    return lax.broadcasted_iota(jnp.int32, shape, len(shape) - 1)


def swap_halves(x):
    return pltpu.roll(x, C, axis=x.ndim - 1)


def row_before(x):
    rows = lax.broadcasted_iota(jnp.int32, x.shape, 0)
    return jnp.where(rows == 0, 0.0, pltpu.roll(x, 1, axis=0))


def row_after(x):
    rows = lax.broadcasted_iota(jnp.int32, x.shape, 0)
    return jnp.where(rows == x.shape[0] - 1, 0.0, pltpu.roll(x, x.shape[0] - 1, axis=0))


def both_parities(x):
    x = jnp.broadcast_to(x, (8, LANES))
    return x + swap_halves(x)


def group_sum(x):
    even = lane_ids(x.shape) % 2 == 0
    return x + jnp.where(even, pltpu.roll(x, LANES - 1, axis=1), pltpu.roll(x, 1, axis=1))


def total(x):
    return jnp.sum(x, axis=0, keepdims=True)


def over_pairs(body, carry):
    for j in range(PAIRS):
        carry = body(j, carry)
    return carry


def build_windows(windows, tile):
    low_lanes = lane_ids((HALF, LANES)) < C
    zero = jnp.zeros((HALF, LANES), f32)

    def write(j, even, odd):
        windows[0, j] = row_before(odd).astype(bf16)
        windows[1, j] = even.astype(bf16)
        windows[2, j] = odd.astype(bf16)
        windows[3, j] = row_after(even).astype(bf16)

    def body(j, carry):
        even_past, odd_past = carry
        even = swap_halves(tile(0, j))
        odd = swap_halves(tile(1, j))
        write(j, jnp.where(low_lanes, even_past, even), jnp.where(low_lanes, odd_past, odd))
        return even, odd

    even, odd = over_pairs(body, (zero, zero))
    write(PAIRS, jnp.where(low_lanes, even, 0.0), jnp.where(low_lanes, odd, 0.0))


def window_operand(windows, slots):
    parts = []
    for slot in slots:
        for shift in (0, 1):
            parts.append(windows[slot, shift : shift + PAIRS].reshape(BLOCK, LANES))
    return jnp.concatenate(parts, axis=1)


def matmul(left, right):
    return jnp.dot(left, right, preferred_element_type=f32)


def tiles_of(y):
    return y.reshape(PAIRS, HALF, LANES)


def norm_stats(sums, squares):
    average = group_sum(both_parities(sums)) / MEMBERS
    variance = group_sum(both_parities(squares)) / MEMBERS - average * average
    return average, lax.rsqrt(variance + EPS)


def strip_start(member, offset, strip):
    return pl.multiple_of((member ^ offset) * strip, strip)


def load_strips(member, strips, image):
    for offset, strip in enumerate(strips):
        rows = strip.shape[0]
        start = strip_start(member, offset, rows)
        for j in range(PAIRS):
            image[j, pl.ds(start, rows), :] = strip[:, j * LANES : (j + 1) * LANES].astype(f32)


def store_strips(member, image, f, strips):
    for offset, strip in enumerate(strips):
        rows = strip.shape[1]
        start = strip_start(member, offset, rows)
        for j in range(PAIRS):
            strip[f, :, j * LANES : (j + 1) * LANES] = image[j, pl.ds(start, rows), :].astype(strip.dtype)


def parity_rows(image, parity, j):
    return image[j, pl.ds(parity, HALF, stride=2), :]


def staggered(steps):
    steps = list(steps)
    started = []
    while steps or started:
        if steps:
            started.append(steps.pop(0))
        for step in list(started):
            if next(step, "end") == "end":
                started.remove(step)


def gather_frame(member, strips, image, stats):
    load_strips(member, strips, image)

    def add_stats(j, carry):
        x = image[j]
        s, q = carry
        return s + x, q + x * x

    zero = jnp.zeros((H, LANES), f32)
    s, q = over_pairs(add_stats, (zero, zero))
    average, inverse = norm_stats(total(s), total(q))
    stats[0:1, :] = average[0:1]
    stats[1:2, :] = inverse[0:1]
    stats[2:3, :] = both_parities(total(s))[0:1]
    stats[3:8, :] = jnp.zeros((5, LANES), f32)


def gather_kernel(member_ref, own, far, near, images, all_stats):
    member = member_ref[0]
    frames = images.shape[0]
    first = member % 2 * frames
    for f in range(frames):
        strips = (own.at[f], near.at[f], far.at[first + f], near.at[frames + f])
        gather_frame(member, strips, images.at[f], all_stats.at[f])


def forward_kernel(count, *refs):
    member_ref, frame_images, frame_stats, styles, biases, w_one, w_two, w_down, w_up = refs[:9]
    out = refs[9 : 9 + count]
    outs = refs[9 + count : 16 + count]
    images, levels = refs[16 + count :]
    member = member_ref[0]
    low_lanes = lane_ids((HALF, LANES)) < C

    def frame(f):
        win_one, win_two, win_level, win_coarse, middle, down, stats = (ref.at[f] for ref in outs)
        frame_image, image, level, style = frame_images.at[f], images.at[f], levels.at[f], styles.at[f]
        average_one, inverse_one = frame_stats[f, 0:1, :], frame_stats[f, 1:2, :]
        gain_one = inverse_one * style[0:1, :]
        half_gain = 0.5 * gain_one
        half_shift = 0.5 * (style[1:2, :] - average_one * gain_one)

        def act_one(parity, j):
            h = parity_rows(frame_image, parity, j) * half_gain + half_shift
            return h * jnp.tanh(h) + h

        build_windows(win_one, act_one)
        yield
        y = matmul(window_operand(win_one, range(4)), w_one[...])
        sums = jnp.zeros((1, LANES), f32)
        squares = jnp.zeros((1, LANES), f32)
        for a in range(2):
            v = y[:, a * LANES : (a + 1) * LANES] + biases[0:1, :]
            sums = sums + total(v)
            squares = squares + total(v * v)
            middle[a] = tiles_of(v)
        yield
        average_two, inverse_two = norm_stats(sums, squares)
        stats[0:1, :] = average_one
        stats[1:2, :] = inverse_one
        stats[2:3, :] = average_two[0:1]
        stats[3:4, :] = inverse_two[0:1]
        stats[4:8, :] = jnp.zeros((4, LANES), f32)
        gain_two = inverse_two * style[2:3, :]
        half_gain_two = 0.5 * gain_two[0:1]
        half_shift_two = 0.5 * (style[3:4, :] - average_two[0:1] * gain_two[0:1])

        def act_two(parity, j):
            h = middle[parity, j] * half_gain_two + half_shift_two
            return h * jnp.tanh(h) + h

        build_windows(win_two, act_two)
        yield
        y = matmul(window_operand(win_two, range(4)), w_two[...])
        for a in range(2):
            v = y[:, a * LANES : (a + 1) * LANES] + biases[1:2, :]
            level[a] = tiles_of(v) + frame_image[:, pl.ds(a, HALF, stride=2), :]
        yield
        build_windows(win_level, lambda parity, j: level[parity, j])
        yield
        operand = window_operand(win_level, range(4))
        y = matmul(operand[:, : 6 * LANES], w_down[...]) + biases[2:3, :]
        down[...] = tiles_of(y)
        yield

        def write_coarse(j, cells):
            win_coarse[0, j] = row_before(cells).astype(bf16)
            win_coarse[1, j] = cells.astype(bf16)
            win_coarse[2, j] = row_after(cells).astype(bf16)

        def coarse_body(j, past):
            h = down[j] * 0.5
            coarse = h * jnp.tanh(h) + h
            write_coarse(j, jnp.where(low_lanes, past, coarse))
            return coarse

        past = over_pairs(coarse_body, jnp.zeros((HALF, LANES), f32))
        write_coarse(PAIRS, jnp.where(low_lanes, past, 0.0))
        yield
        operand = window_operand(win_level, range(4))
        coarse_operand = window_operand(win_coarse, (0, 1, 1, 2))
        y = matmul(operand, w_up[: 16 * C, :]) + matmul(coarse_operand, w_up[16 * C :, :])
        for a in range(2):
            v = y[:, a * LANES : (a + 1) * LANES] + biases[3:4, :]
            image[:, pl.ds(a, HALF, stride=2), :] = tiles_of(v) + level[a]
        yield
        store_strips(member, image, f, out)

    staggered(frame(f) for f in range(styles.shape[0]))


def slope_twice(h):
    t = jnp.tanh(h)
    return (1.0 + t) + h * (1.0 - t * t)


def backward_kernel(count, *refs):
    member_ref = refs[0]
    cot_images, cot_stats, frame_images, styles, all_stats, all_middle, all_down = refs[1:8]
    w_up, w_down, w_two, w_one = refs[8:12]
    out = refs[12 : 12 + count]
    outs = refs[12 + count : 18 + count]
    scratch = refs[18 + count :]
    member = member_ref[0]
    low_lanes = lane_ids((HALF, LANES)) < C

    def frame(f):
        tile_out, tile_level, tile_mid, coarse_pairs, pieces, bias_sums = (ref.at[f] for ref in outs)
        image, level_grad, pre_grad, windows, coarse_below = (ref.at[f] for ref in scratch)
        style, stats, middle, down, frame_image = (
            ref.at[f] for ref in (styles, all_stats, all_middle, all_down, frame_images)
        )
        cot_image = cot_images.at[f]

        def out_tile(parity, j):
            x = parity_rows(cot_image, parity, j)
            tile_out[parity, j] = x.astype(bf16)
            return x

        build_windows(windows, out_tile)
        yield
        y = matmul(window_operand(windows, range(4)), w_up[...])
        for a in range(2):
            level_grad[a] = (
                tiles_of(y[:, (2 + a) * LANES : (3 + a) * LANES]) + cot_image[:, pl.ds(a, HALF, stride=2), :]
            )
        coarse = y[:, :LANES] + y[:, LANES : 2 * LANES]
        pre_grad[0] = tiles_of(coarse)
        yield

        def coarse_body(t, carry):
            after, sums = carry
            j = PAIRS - 1 - t
            g = pre_grad[0, j]
            g = g + swap_halves(g)
            h = down[j] * 0.5
            d = 0.5 * g * slope_twice(h)
            pair = jnp.where(low_lanes, d, after)
            coarse_pairs[j] = pair.astype(bf16)
            coarse_below[j] = row_after(pair).astype(bf16)
            return d, sums + d

        zero = jnp.zeros((HALF, LANES), f32)
        _, sums = over_pairs(coarse_body, (zero, zero))
        bias_down_sum = jnp.broadcast_to(total(sums), (8, LANES))
        yield
        operand = jnp.concatenate(
            [coarse_pairs[...].reshape(BLOCK, LANES), coarse_below[...].reshape(BLOCK, LANES)], axis=1
        )
        y = matmul(operand, w_down[...])
        sums = jnp.zeros((1, LANES), f32)
        for a in range(2):
            v = y[:, a * LANES : (a + 1) * LANES] + level_grad[a].reshape(BLOCK, LANES)
            sums = sums + total(v)
            level_grad[a] = tiles_of(v)
        bias_two_sum = both_parities(sums)
        yield

        def level_tile(parity, j):
            x = level_grad[parity, j]
            tile_level[parity, j] = x.astype(bf16)
            return x

        build_windows(windows, level_tile)
        yield

        def norm_slopes(y, value, k):
            average, inverse = stats[2 * k : 2 * k + 1, :], stats[2 * k + 1 : 2 * k + 2, :]
            gain = inverse * style[2 * k : 2 * k + 1, :]
            half_gain = 0.5 * gain
            half_shift = 0.5 * (style[2 * k + 1 : 2 * k + 2, :] - average * gain)
            scale_sum = jnp.zeros((1, LANES), f32)
            shift_sum = jnp.zeros((1, LANES), f32)
            for a in range(2):
                v = value(a)
                g = 0.5 * y[:, a * LANES : (a + 1) * LANES] * slope_twice(v * half_gain + half_shift)
                pre_grad[a] = tiles_of(g)
                shift_sum = shift_sum + total(g)
                scale_sum = scale_sum + total(g * ((v - average) * inverse))
            scale_sum, shift_sum = both_parities(scale_sum), both_parities(shift_sum)
            factor = style[2 * k : 2 * k + 1, :]
            center = group_sum(factor * shift_sum) / MEMBERS
            tilt = group_sum(factor * scale_sum) / MEMBERS
            slope = (inverse * tilt)[0:1] * inverse
            return scale_sum, shift_sum, gain, slope, slope * average - (inverse * center)[0:1]

        y = matmul(window_operand(windows, range(4)), w_two[...])
        scale_two, shift_two, gain_two, slope_two, constant_two = norm_slopes(
            y, lambda a: middle[a].reshape(BLOCK, LANES), 1
        )
        yield
        row_sums = [zero]

        def mid_tile(parity, j):
            x = pre_grad[parity, j] * gain_two + (constant_two - middle[parity, j] * slope_two)
            tile_mid[parity, j] = x.astype(bf16)
            row_sums[0] = row_sums[0] + x
            return x

        build_windows(windows, mid_tile)
        bias_one_sum = both_parities(total(row_sums[0]))
        yield
        y = matmul(window_operand(windows, range(4)), w_one[...])
        scale_one, shift_one, gain_one, slope_one, constant_one = norm_slopes(
            y, lambda a: frame_image[:, pl.ds(a, HALF, stride=2), :].reshape(BLOCK, LANES), 0
        )
        yield

        def frame_body(j, carry):
            for parity in range(2):
                x = parity_rows(frame_image, parity, j)
                g = pre_grad[parity, j] * gain_one + (constant_one - x * slope_one) + level_grad[parity, j]
                image[j, pl.ds(parity, HALF, stride=2), :] = g
            return carry

        over_pairs(frame_body, 0)
        store_strips(member, image, f, out)
        for k, value in enumerate((scale_one, shift_one, scale_two, shift_two)):
            pieces[k : k + 1, :] = value[0:1]
        pieces[4:8, :] = jnp.zeros((4, LANES), f32)
        for k, value in enumerate((bias_one_sum, bias_two_sum, bias_down_sum, cot_stats[f, 2:3, :])):
            bias_sums[k : k + 1, :] = value[0:1]
        bias_sums[4:8, :] = jnp.zeros((4, LANES), f32)

    staggered(frame(f) for f in range(styles.shape[0]))


def outer(left, right):
    return lax.dot_general(left, right, (((0,), (0,)), ((), ())), preferred_element_type=f32)


def accumulate(wins, tiles, sums):
    win_one, win_two, win_level, win_coarse = wins
    tile_out, tile_level, tile_mid, coarse_pairs = tiles
    sum_one, sum_two, sum_down, sum_up = sums
    cells = win_one.shape[0] * BLOCK

    def operand(windows, slots):
        parts = []
        for slot in slots:
            for shift in (0, 1):
                parts.append(windows[:, slot, shift : shift + PAIRS].reshape(cells, LANES))
        return jnp.concatenate(parts, axis=1)

    def blocks(tiles):
        return jnp.concatenate([tiles[:, a].reshape(cells, LANES) for a in range(2)], axis=1)

    out_blocks = blocks(tile_out)
    sum_up[16 * C :, :] = outer(operand(win_coarse, range(3)), out_blocks)
    sum_up[: 16 * C, :] = outer(operand(win_level, range(4)), out_blocks)
    sum_down[...] = outer(operand(win_level, range(3)), coarse_pairs[...].reshape(cells, LANES))
    sum_two[...] = outer(operand(win_two, range(4)), blocks(tile_level))
    sum_one[...] = outer(operand(win_one, range(4)), blocks(tile_mid))


def fold(sums, p, q):
    return fold_slots(sums, 0, p, q, range(4))


def fold_coarse(sums, p, q):
    return fold_slots(sums, 16 * C, p, q, (0, 1, 1, 2))


def fold_slots(sums, base, p, q, slots):
    halves = []
    for b in range(2):
        rows = [base + (slots[a + p] * 4 + b + q) * C for a in range(2)]
        halves.append(sums[rows[0] : rows[0] + C, :LANES] + sums[rows[1] : rows[1] + C, LANES:])
    return halves[0] + swap_halves(halves[1])


def weight_kernel(*refs):
    wins, tiles, grads, sums = refs[:4], refs[4:8], refs[8:12], refs[12:]
    g_one, g_two, g_down, g_up = grads
    sum_one, sum_two, sum_down, sum_up = sums
    accumulate(wins, tiles, sums)
    for p in range(3):
        for q in range(3):
            at = (3 * p + q) * C
            g_one[at : at + C, :] = fold(sum_one, p, q)[:, :C]
            g_two[at : at + C, :] = fold(sum_two, p, q)[:, :C]
            g_up[2 * at : 2 * at + C, :] = fold_coarse(sum_up, p, q)[:, :C]
            g_up[2 * at + C : 2 * at + 2 * C, :] = fold(sum_up, p, q)[:, :C]
            place = (p * 4 + q) * C
            g_down[at : at + C, :] = sum_down[place : place + C, :C]


PARTS = 16
FAR_HINTS = 0, 90
PAIR_PARTS = 24


def three_parts(exact):
    high = exact.astype(bf16).astype(f32)
    rest = exact - high
    mid = rest.astype(bf16).astype(f32)
    return jnp.concatenate([high, mid, rest - mid], axis=0)


def below(block, rows):
    if block.shape[0] == rows:
        return block
    return jnp.concatenate([block, jnp.zeros((rows - block.shape[0], LANES), f32)], axis=0)


def message_kernel(count, rows, *refs):
    where_ref, wins, tiles = refs[0], refs[1:5], refs[5:9]
    pieces, bias_sums, kept, small, theirs = refs[9:14]
    sums = refs[14:18]
    g_pair, g_up, g_down = refs[18:]
    sum_one, sum_two, sum_down, sum_up = sums
    accumulate(wins, tiles, sums)
    low_lanes = lane_ids((C, LANES)) < C
    for p in range(3):
        for q in range(3):
            at = (3 * p + q) * C
            g_pair[at : at + C, :] = jnp.where(
                low_lanes, fold(sum_one, p, q), swap_halves(fold(sum_two, p, q))
            )
            g_up[2 * at : 2 * at + C, :] = fold_coarse(sum_up, p, q)
            g_up[2 * at + C : 2 * at + 2 * C, :] = fold(sum_up, p, q)
            place = (p * 4 + q) * C
            g_down[at : at + C, :] = sum_down[place : place + C, :]
    frames = pieces.shape[0]
    small[...] = jnp.zeros_like(small)
    total_bias = bias_sums[0, 0:4, :]
    for f in range(frames):
        small[4 * f : 4 * f + 4, :] = pieces[f, 0:4, :]
        if f > 0:
            total_bias = total_bias + bias_sums[f, 0:4, :]
    small[4 * frames : 4 * frames + 4, :] = total_bias
    sent = below(three_parts(small[...]), rows)
    low_lanes = lane_ids((rows, LANES)) < C
    half = count // 2
    for at in range(half):
        for ref, mine in ((kept, True), (theirs, False)):
            start = pl.multiple_of(seq_owner(where_ref[0], where_ref[1], half, at, mine) * rows, 8)
            blocks = (
                g_pair[pl.ds(start, rows), :],
                jnp.where(
                    low_lanes,
                    g_up[pl.ds(pl.multiple_of(2 * start, 8), rows), :],
                    swap_halves(g_up[pl.ds(pl.multiple_of(2 * start + rows, 8), rows), :]),
                ),
                jnp.where(low_lanes, g_down[pl.ds(start, rows), :], 0.0 if mine else sent),
            )
            ref[at * 3 * rows : (at + 1) * 3 * rows, :] = jnp.concatenate(blocks, axis=0).astype(ref.dtype)


def join_kernel(half, rows, frames, where_ref, kept, small, theirs, own, *messages):
    first = where_ref[1] % 2 == 0
    at = 2 * rows
    other = theirs[at : at + 3 * PARTS, :].astype(f32)
    other = other[:PARTS] + other[PARTS : 2 * PARTS] + other[2 * PARTS :]
    mine = small[...]
    n = 4 * frames
    exact = jnp.concatenate(
        [
            jnp.where(first, mine[:n], other[:n]),
            jnp.where(first, other[:n], mine[:n]),
            mine[n : n + 4] + other[n : n + 4],
            jnp.zeros((PAIR_PARTS - 2 * n - 4, LANES), f32),
        ],
        axis=0,
    )
    low_lanes = lane_ids((rows, LANES)) < C
    sent = below(three_parts(exact), rows)
    size = 3 * rows
    for k, message in enumerate(messages):
        block = kept[k * size : (k + 1) * size, :] + theirs[k * size : (k + 1) * size, :].astype(f32)
        message[:at, :] = block[:at].astype(bf16)
        message[at:, :] = jnp.where(low_lanes, block[at:], sent).astype(bf16)
        if k == 0:
            own[:at, :] = block[:at]
            own[at:, :] = jnp.where(low_lanes, block[at:], below(exact, rows))


def reduce_kernel(half, rows, cells, frames, *refs):
    where_ref, own = refs[:2]
    messages = refs[2 : 2 + half]
    hots, act_table, noise_table, ada_one, ada_two, out, pieces_one, pieces_two, table, high_one, high_two = refs[2 + half :]
    place, member = where_ref[0], where_ref[1]
    taken = 4 * frames
    bias = jnp.zeros((4, LANES), f32)
    sums = None
    lanes = lane_ids((1, LANES))
    low_lanes = lanes < C
    at = 2 * rows
    for k, ref in enumerate(messages):
        message = ref[...].astype(f32)
        if k == 0:
            message = jnp.where(member % 2 == 0, own[...], message)
        sums = message if sums is None else sums + message
        small = (
            message[at : at + PAIR_PARTS]
            + message[at + PAIR_PARTS : at + 2 * PAIR_PARTS]
            + message[at + 2 * PAIR_PARTS : at + 3 * PAIR_PARTS]
        )
        turned = swap_halves(small)
        bias = bias + small[taken : taken + 4]
        for f in range(frames):
            row = k * frames + f
            for kind, piece in ((0, pieces_one), (2, pieces_two)):
                low, high = 4 * f + kind, 4 * f + kind + 1
                piece[row : row + 1, :] = jnp.where(low_lanes, turned[low : low + 1], small[high : high + 1])
    hot = hots[:, :TABLE_ROWS]
    table[...] = jnp.zeros_like(table)
    table[ACT_ROW : ACT_ROW + NACT, :] = act_table[...].astype(f32)
    table[NOISE_ROW : NOISE_ROW + NLEV, :] = noise_table[...].astype(f32)
    embed = matmul(hot.astype(bf16), table[...].astype(bf16))

    def exact(left, right, dims):
        return lax.dot_general(left, right, (dims, ((), ())), precision=precise, preferred_element_type=f32)

    one, two = pieces_one[...], pieces_two[...]
    for ref, ada in ((high_one, ada_one), (high_two, ada_two)):
        ref[...] = jnp.zeros_like(ref)
        ref[C : C + cells, :] = ada[...].astype(f32)
    embed_grad = exact(one, high_one[...], ((1,), (1,))) + exact(two, high_two[...], ((1,), (1,)))
    width = C // (2 * half)
    bias = pltpu.roll(jnp.concatenate([bias, bias], axis=0), (LANES - place * width) % LANES, axis=1)
    extra = below(jnp.concatenate([exact(hot, embed_grad, ((0,), (0,))), bias], axis=0), rows)
    at = 2 * rows
    out[:at, :] = sums[:at]
    out[at : at + rows, :] = jnp.where(lane_ids((rows, LANES)) < C, sums[at:], extra)
    at = at + rows
    out[at : at + cells, :] = exact(embed, one, ((0,), (0,)))
    out[at + cells : at + 2 * cells, :] = exact(embed, two, ((0,), (0,)))


def finish_kernel(rows, cells, first, second, *outs):
    act_grad, noise_grad, ada_one, ada_two, g_one, g_two, g_down, g_up = outs[:8]
    bias_grads = outs[8:12]
    sums = first[...].astype(f32) + second[...].astype(f32)

    def turn(block):
        return jnp.concatenate([block, jnp.zeros((LANES - rows, LANES), f32)], axis=0).T[:, :rows]

    pair, halves, down = (turn(sums[k * rows : (k + 1) * rows]) for k in range(3))
    g_one[...] = pair[:C]
    g_two[...] = pair[C:]
    g_up[:, :rows] = halves[:C]
    g_up[:, rows:] = halves[C:]
    g_down[...] = down[:C]
    at = 3 * rows
    ada_one[...] = sums[at : at + cells]
    ada_two[...] = sums[at + cells : at + 2 * cells]
    extra = swap_halves(sums[2 * rows : 3 * rows])
    act_grad[...] = extra[ACT_ROW : ACT_ROW + NACT, :cells]
    noise_grad[...] = extra[NOISE_ROW : NOISE_ROW + NLEV, :cells]
    for k, ref in enumerate(bias_grads):
        ref[...] = extra[BIAS_ROW + k : BIAS_ROW + k + 1, : ref.shape[0]].reshape(ref.shape)


def write_operands(block, turned_pairs, f_one, f_two, f_down, f_up, b_one, b_two, b_down, b_up):
    low_lanes = lane_ids((C, LANES)) < C
    zero = jnp.zeros((C, LANES), f32)

    pairs = {name: turned_pairs(name) for name in ("one", "two", "down", "up")}

    def taps(name, base, step):
        plain, turned = {}, {}
        for p in range(3):
            for q in range(3):
                at = (3 * p + q) * step + base
                plain[p, q] = block(name, at)
                pair = pairs[name][at // LANES]
                other = swap_halves(pair)
                turned[p, q] = jnp.where(low_lanes, pair, other) if at % LANES == 0 else jnp.where(low_lanes, other, pair)
        return plain, turned

    def write_forward(ref, base, plain):
        for w in range(4):
            for p in range(3):
                tile = jnp.where(low_lanes, plain.get((p, w), zero), plain.get((p, w - 1), zero)).astype(bf16)
                for a in range(2):
                    at = base + ((a + p) * 4 + w) * C
                    ref[at : at + C, a * LANES : (a + 1) * LANES] = tile
            for a in range(2):
                for r in range(4):
                    if not 0 <= r - a < 3:
                        at = base + (r * 4 + w) * C
                        ref[at : at + C, a * LANES : (a + 1) * LANES] = zero.astype(bf16)

    def write_backward(ref, lane, turned):
        for w in range(4):
            for p in range(3):
                tile = jnp.where(low_lanes, turned.get((p, 2 - w), zero), turned.get((p, 3 - w), zero)).astype(bf16)
                for a in range(2):
                    at = ((a + 2 - p) * 4 + w) * C
                    ref[at : at + C, lane + a * LANES : lane + (a + 1) * LANES] = tile
            for a in range(2):
                for r in range(4):
                    if not 0 <= a + 2 - r < 3:
                        at = (r * 4 + w) * C
                        ref[at : at + C, lane + a * LANES : lane + (a + 1) * LANES] = zero.astype(bf16)

    for name, forward_ref, backward_ref in (("one", f_one, b_one), ("two", f_two, b_two)):
        plain, turned = taps(name, 0, C)
        write_forward(forward_ref, 0, plain)
        write_backward(backward_ref, 0, turned)
    plain, turned = taps("up", 0, 2 * C)
    write_forward(f_up, 16 * C, plain)
    write_backward(b_up, 0, turned)
    plain, turned = taps("up", C, 2 * C)
    write_forward(f_up, 0, plain)
    write_backward(b_up, 2 * LANES, turned)
    plain, turned = taps("down", 0, C)
    for p in range(3):
        for w in range(4):
            at = (p * 4 + w) * C
            f_down[at : at + C, :] = plain.get((p, w), zero).astype(bf16)
    for below in range(2):
        for right in range(2):
            at = (below * 2 + right) * C
            for a in range(2):
                p = {(0, 0): 1, (0, 1): 2, (1, 1): 0}.get((below, a))
                first, second = zero, zero
                if p is not None:
                    first = turned[p, 1] if right == 0 else zero
                    second = turned[p, 2] if right == 0 else turned[p, 0]
                b_down[at : at + C, a * LANES : (a + 1) * LANES] = jnp.where(low_lanes, first, second).astype(bf16)


def expand_kernel(conv_one, conv_two, down_kernel, up_kernel, *outs):
    kernels = {"one": conv_one, "two": conv_two, "down": down_kernel, "up": up_kernel}

    def block(name, row):
        k = kernels[name][row : row + C, :].astype(f32)
        return jnp.concatenate([k, k], axis=1)

    def turned_pairs(name):
        found = []
        for at in range(0, kernels[name].shape[0], LANES):
            k = kernels[name][at : at + LANES, :].astype(f32)
            k = jnp.concatenate([k, jnp.zeros(k.shape, f32)], axis=1)
            if k.shape[0] < LANES:
                k = jnp.concatenate([k, jnp.zeros((LANES - k.shape[0], LANES), f32)], axis=0)
            found.append(k.T[:C])
        return found

    write_operands(block, turned_pairs, *outs)


ACT_ROW, NOISE_ROW, TABLE_ROWS = 0, 24, 56
BIAS_ROW, ID_ROW = 56, 64


def pack_sizes(rows, cells):
    return 3 * rows, 3 * rows + 2 * cells, -(-(3 * rows + 2 * cells) // 16) * 16


def turned(values):
    wide = jnp.concatenate([values, jnp.zeros((C, LANES - values.shape[1]), f32)], axis=1)
    return jnp.concatenate([wide, jnp.zeros((C, LANES), f32)], axis=0).T[: values.shape[1]]


def far_kernel(member_ref, array, out, own, other, sent):
    half, share = out.shape[0], own.shape[0]
    member = member_ref[0]
    copies = [
        pltpu.make_async_copy(array.at[pl.ds(first, ref.shape[0])], ref, sent.at[k])
        for k, (first, ref) in enumerate(
            (((1 - member // 2) * half, out), (member * share, own), ((member ^ 1) * share, other))
        )
    ]
    for copy in copies:
        copy.start()
    for copy in copies:
        copy.wait()


def share_kernel(member_ref, far, out):
    share = out.shape[0]
    out[...] = far[pl.ds((member_ref[0] ^ 1) % 2 * share, share)]


def near_kernel(other, shared, out):
    share = out.shape[0] // 2
    out[:share] = other[...]
    out[share:] = shared[...]


def pack_kernel(*refs):
    actions, noise_ids, valid, conv_one, conv_two, down_kernel, up_kernel, ada_one, ada_two = refs[:9]
    act_table, noise_table = refs[9:11]
    biases = refs[11:15]
    out, work = refs[15:]
    rows, cells = conv_one.shape[1], ada_one.shape[0]
    style_at, end, _ = pack_sizes(rows, cells)
    wide = lambda ref: ref[...].astype(f32)
    low_lanes = lane_ids((rows, LANES)) < C
    up = wide(up_kernel)
    work[...] = jnp.zeros_like(work)
    for at, low, high in (
        (0, turned(wide(conv_one)), turned(wide(conv_two))),
        (rows, turned(up[:, :rows]), turned(up[:, rows:])),
    ):
        work[at : at + rows, :] = jnp.where(low_lanes, low, swap_halves(high))
    work[2 * rows : 3 * rows, :] = turned(wide(down_kernel))
    extra = 2 * rows
    for at, ref in ((ACT_ROW, act_table), (NOISE_ROW, noise_table)):
        size = ref.shape
        work[extra + at : extra + at + size[0], C : C + size[1]] = wide(ref)
    for k, ref in enumerate(biases):
        at = extra + BIAS_ROW + k
        work[at : at + 1, C : C + ref.shape[0]] = wide(ref).reshape(1, ref.shape[0])
    lanes = lane_ids((1, LANES))
    for k, ref in enumerate((actions, noise_ids, valid)):
        line = jnp.zeros((1, LANES), jnp.int32)
        for f in range(ref.shape[0]):
            line = jnp.where(lanes == C + f, ref[f], line)
        at = extra + ID_ROW + k
        work[at : at + 1, C:] = line.astype(f32)[:, C:]
    work[style_at : style_at + cells, :] = wide(ada_one)
    work[style_at + cells : end, :] = wide(ada_two)
    out[...] = work[...].astype(bf16)


def seq_owner(place, member, half, at, mine=True):
    side = member % 2 if mine else 1 - member % 2
    even, odd = sides(2 * half)
    return place ^ (even[at] + side * (odd[at] - even[at]))


def sides(count):
    ones = lambda offset: bin(offset).count("1") % 2
    return tuple([offset for offset in range(count) if ones(offset) == side] for side in (0, 1))


def write_hots(hots, at, first, frames, ids):
    lanes = lane_ids((1, LANES)).astype(f32)
    for f in range(frames):
        mine = jnp.where(lane_ids(ids.shape) == C + first + f, ids, 0.0)
        mine = jnp.sum(mine, axis=1, keepdims=True)
        action, noise, valid = mine[0:1], mine[1:2], mine[2:3]
        hots[at + f : at + f + 1, :] = jnp.where(lanes == action + ACT_ROW, valid, 0.0) + jnp.where(
            lanes == noise + NOISE_ROW, 1.0, 0.0
        )


def prepare_kernel(count, rows, cells, *refs):
    where_ref, actions, noise_ids, valid, packed, mine, other = refs[:7]
    outs = refs[7:15]
    styles, biases, hots = refs[15:18]
    work_pair, work_up, work_down, work_one, work_two, work_table = refs[18:]
    place, member, frames = where_ref[0], where_ref[1], styles.shape[0]
    style_at, _, size = pack_sizes(rows, cells)
    bias_rows = jnp.zeros(SMALL, f32)
    half = count // 2
    for offset in range(count):
        ref = mine if offset < half else other
        at = offset % half
        pack = ref[at * size : (at + 1) * size, :].astype(f32)
        if at == 0:
            pack = jnp.where(member % 2 == offset // half, packed[...].astype(f32), pack)
        owner = seq_owner(place, member, half, at, offset < half)
        start = pl.multiple_of(owner * rows, 8)
        work_pair[pl.ds(start, rows), :] = pack[:rows]
        halves = pack[rows : 2 * rows]
        work_up[pl.ds(2 * start, rows), :] = halves
        work_up[pl.ds(pl.multiple_of(2 * start + rows, 8), rows), :] = swap_halves(halves)
        extra = pack[2 * rows : 3 * rows]
        work_down[pl.ds(start, rows), :] = extra
        work_one[offset * cells : (offset + 1) * cells, :] = pack[style_at : style_at + cells]
        work_two[offset * cells : (offset + 1) * cells, :] = pack[style_at + cells : style_at + 2 * cells]
        lane = (offset * cells) % LANES
        tables = pltpu.roll(extra[:TABLE_ROWS], (lane - C) % LANES, axis=1)
        kept = (lane_ids(tables.shape) >= lane) & (lane_ids(tables.shape) < lane + cells)
        column = offset * cells // LANES
        tables = jnp.where(kept, tables, 0.0)
        if lane == 0:
            work_table[column] = tables
        else:
            work_table[column] += tables
        slots = extra[BIAS_ROW : BIAS_ROW + 8]
        width = C // count
        slots = jnp.where((lane_ids(SMALL) >= C) & (lane_ids(SMALL) < C + width), slots, 0.0)
        bias_rows = bias_rows + pltpu.roll(slots, (owner * width + C) % LANES, axis=1)
        if offset < half:
            write_hots(hots, at * 2 * frames, member // 2 * 2 * frames, 2 * frames, extra[ID_ROW : ID_ROW + 8])
    biases[...] = bias_rows + swap_halves(bias_rows)

    lanes = lane_ids((8, LANES))
    row_at = lax.broadcasted_iota(jnp.int32, (8, LANES), 0)
    hot = jnp.zeros((8, LANES), f32)
    for f in range(frames):
        at = member * frames + f
        here = jnp.where(lanes == actions[at] + ACT_ROW, valid[at], 0) + jnp.where(lanes == noise_ids[at] + NOISE_ROW, 1, 0)
        hot = jnp.where(row_at == f, here.astype(f32), hot)
    hot = hot[:, :TABLE_ROWS].astype(bf16)
    embed = jnp.concatenate([matmul(hot, work_table[k].astype(bf16)) for k in range(work_table.shape[0])], axis=1)
    low_lanes = lanes < C
    for k, work in enumerate((work_one, work_two)):
        style = jnp.dot(embed, work[...], precision=precise, preferred_element_type=f32)
        other = swap_halves(style)
        scale = 1.0 + jnp.where(low_lanes, style, other)
        shift = jnp.where(low_lanes, other, style)
        for f in range(frames):
            styles[f, 2 * k : 2 * k + 1, :] = scale[f : f + 1]
            styles[f, 2 * k + 1 : 2 * k + 2, :] = shift[f : f + 1]
    for f in range(frames):
        styles[f, 4:8, :] = jnp.zeros((4, LANES), f32)

    def block(name, row):
        work = {"one": work_pair, "two": work_pair, "down": work_down, "up": work_up}[name]
        k = work[row : row + C, :]
        low = lane_ids(k.shape) < C
        if name == "two":
            return jnp.where(low, swap_halves(k), k)
        return jnp.where(low, k, swap_halves(k))

    both = {}

    def turned_pairs(name):
        work = {"one": work_pair, "two": work_pair, "down": work_down, "up": work_up}[name]
        if name not in both:
            found = []
            for at in range(0, work.shape[0], LANES):
                k = work[at : min(at + LANES, work.shape[0]), :]
                if k.shape[0] < LANES:
                    k = below(k, LANES)
                found.append(k.T)
            both["one" if name == "two" else name] = [k[:C] for k in found]
            both["two" if name == "one" else name] = [k[C:] for k in found] if name in ("one", "two") else both[name]
        return both[name]

    write_operands(block, turned_pairs, *outs)


def shape(dims, kind):
    return jax.ShapeDtypeStruct(dims, kind)


def whole(dims):
    return pl.BlockSpec(dims, lambda f: (0,) * len(dims))


def per_frame(dims):
    return pl.BlockSpec((1,) + dims, lambda f: (f,) + (0,) * len(dims))


def strip_specs(count, strip):
    return [pl.BlockSpec((1, strip, W * C), lambda f: (f, 0, 0))] * count


SMALL = (8, LANES)
WINDOWS = (4, PAIRS + 1, HALF, LANES)
COARSE_WINDOWS = (3, PAIRS + 1, HALF, LANES)
TILES = (2, PAIRS, HALF, LANES)
COARSE = (PAIRS, HALF, LANES)
IMAGE = (PAIRS, H, LANES)
KEYS = 16 * C


def in_vmem():
    return pl.BlockSpec(memory_space=pltpu.VMEM)


def in_smem():
    return pl.BlockSpec(memory_space=pltpu.SMEM)


def params(limit=VMEM_LIMIT):
    return pltpu.CompilerParams(vmem_limit_bytes=limit)


def cost(macs, moved):
    return pl.CostEstimate(flops=2 * macs, bytes_accessed=moved, transcendentals=0)


def expand(conv_one, conv_two, down_kernel, up_kernel):
    vmem = pl.BlockSpec(memory_space=pltpu.VMEM)
    return pl.pallas_call(
        expand_kernel,
        in_specs=[vmem] * 4,
        out_specs=[vmem] * 8,
        out_shape=[
            shape((KEYS, 2 * LANES), bf16),
            shape((KEYS, 2 * LANES), bf16),
            shape((6 * LANES, LANES), bf16),
            shape((2 * KEYS, 2 * LANES), bf16),
            shape((KEYS, 2 * LANES), bf16),
            shape((KEYS, 2 * LANES), bf16),
            shape((2 * LANES, 2 * LANES), bf16),
            shape((KEYS, 4 * LANES), bf16),
        ],
        compiler_params=params(),
        name="expand",
    )(conv_one, conv_two, down_kernel, up_kernel)


def fetch_far(member, array):
    far, own, other = cut_far(member, array, lax.axis_size("rows"))
    return trade(far, 2), own, other


def gather_frames(member, far, own, other, hints=(0, 0)):
    near = trade(cut_near(member, other, far, hints), 1)
    frames = own.shape[0]
    return pl.pallas_call(
        gather_kernel,
        in_specs=[in_smem()] + [in_vmem()] * 3,
        out_specs=[in_vmem()] * 2,
        out_shape=[shape((frames,) + IMAGE, f32), shape((frames,) + SMALL, f32)],
        compiler_params=params(),
        name="frames",
    )(member, own, far, near)


def forward(member, frame_images, frame_stats, styles, biases, w_one, w_two, w_down, w_up, count):
    frames = frame_images.shape[0]
    strip = H // count
    return pl.pallas_call(
        lambda *refs: forward_kernel(count, *refs),
        in_specs=[in_smem()] + [in_vmem()] * 8,
        out_specs=[in_vmem()] * (count + 7),
        out_shape=[shape((frames, strip, W * C), bf16)] * count
        + [
            shape((frames,) + WINDOWS, bf16),
            shape((frames,) + WINDOWS, bf16),
            shape((frames,) + WINDOWS, bf16),
            shape((frames,) + COARSE_WINDOWS, bf16),
            shape((frames,) + TILES, f32),
            shape((frames,) + COARSE, f32),
            shape((frames,) + SMALL, f32),
        ],
        scratch_shapes=[pltpu.VMEM((frames,) + IMAGE, f32), pltpu.VMEM((frames,) + TILES, f32)],
        compiler_params=params(),
        cost_estimate=cost(1 << 10, 1 << 10),
        name="forward",
    )(member, frame_images, frame_stats, styles, biases, w_one, w_two, w_down, w_up)


def backward(member, cot, frame_images, styles, stats, middle, down, w_up, w_down, w_two, w_one, count):
    frames = frame_images.shape[0]
    strip = H // count
    return pl.pallas_call(
        lambda *refs: backward_kernel(count, *refs),
        in_specs=[in_smem()] + [in_vmem()] * 11,
        out_specs=[in_vmem()] * (count + 6),
        out_shape=[shape((frames, strip, W * C), bf16)] * count
        + [
            shape((frames,) + TILES, bf16),
            shape((frames,) + TILES, bf16),
            shape((frames,) + TILES, bf16),
            shape((frames,) + COARSE, bf16),
            shape((frames,) + SMALL, f32),
            shape((frames,) + SMALL, f32),
        ],
        scratch_shapes=[
            pltpu.VMEM((frames,) + IMAGE, f32),
            pltpu.VMEM((frames,) + TILES, f32),
            pltpu.VMEM((frames,) + TILES, f32),
            pltpu.VMEM((frames,) + WINDOWS, bf16),
            pltpu.VMEM((frames,) + COARSE, bf16),
        ],
        compiler_params=params(),
        cost_estimate=cost(frames * BLOCK * KEYS * 2 * LANES * 5, frames * (10 << 20)),
        name="backward",
    )(member, *cot, frame_images, styles, stats, middle, down, w_up, w_down, w_two, w_one)


def sum_scratch():
    return [
        pltpu.VMEM((KEYS, 2 * LANES), f32),
        pltpu.VMEM((KEYS, 2 * LANES), f32),
        pltpu.VMEM((6 * LANES, LANES), f32),
        pltpu.VMEM((KEYS + 6 * LANES, 2 * LANES), f32),
    ]


def weight_grads(wins, tiles):
    return pl.pallas_call(
        weight_kernel,
        in_specs=[in_vmem()] * 8,
        out_specs=[in_vmem()] * 4,
        out_shape=[shape((9 * C, C), f32)] * 3 + [shape((18 * C, C), f32)],
        scratch_shapes=sum_scratch(),
        compiler_params=params(),
        name="weights",
    )(*wins, *tiles)


def in_place(space=pl.ANY):
    return pl.BlockSpec(memory_space=space)


def cut_far(member, array, count):
    half, share = ((array.shape[0] // n,) + array.shape[1:] for n in (2, count))
    array = pltpu.with_memory_space_constraint(array, pltpu.HBM)
    return pl.pallas_call(
        far_kernel,
        in_specs=[in_smem(), in_place(pltpu.HBM)],
        out_specs=[in_vmem()] * 3,
        out_shape=[shape(half, array.dtype), shape(share, array.dtype), shape(share, array.dtype)],
        scratch_shapes=[pltpu.SemaphoreType.DMA((3,))],
        compiler_params=params(),
        name="far",
    )(member, array)


def cut_near(member, other, far, hints):
    other = pltpu.with_memory_space_constraint(other, pltpu.VMEM)
    shared = pl.pallas_call(
        share_kernel,
        in_specs=[in_smem(), in_vmem()],
        out_specs=in_vmem(),
        out_shape=shape(other.shape, other.dtype),
        compiler_params=params(),
        cost_estimate=cost(BLOCK * KEYS * 2 * LANES * hints[0], 1 << 20),
        name="shared",
    )(member, far)
    return pl.pallas_call(
        near_kernel,
        in_specs=[in_vmem()] * 2,
        out_specs=in_vmem(),
        out_shape=shape(far.shape, other.dtype),
        compiler_params=params(),
        cost_estimate=cost(BLOCK * KEYS * 2 * LANES * hints[1], 1 << 20),
        name="near",
    )(other, shared)


def pack(ids, kernels, ada_one, ada_two, act_table, noise_table, biases):
    _, _, size = pack_sizes(kernels[0].shape[0], ada_one.shape[0])
    args = (*[kernel.T for kernel in kernels], ada_one, ada_two, act_table, noise_table, *biases)
    return pl.pallas_call(
        pack_kernel,
        in_specs=[in_smem()] * 3 + [in_vmem()] * len(args),
        out_specs=in_vmem(),
        out_shape=shape((size, LANES), bf16),
        scratch_shapes=[pltpu.VMEM((size, LANES), f32)],
        compiler_params=params(VMEM_MOST),
        cost_estimate=cost(BLOCK * KEYS * 2 * LANES * 30, 1 << 20),
        name="pack",
    )(*ids, *args)


OPERANDS = (
    (KEYS, 2 * LANES),
    (KEYS, 2 * LANES),
    (6 * LANES, LANES),
    (2 * KEYS, 2 * LANES),
    (KEYS, 2 * LANES),
    (KEYS, 2 * LANES),
    (2 * LANES, 2 * LANES),
    (KEYS, 4 * LANES),
)


def prepare(where, ids, packed, mine, other, count, rows, cells, frames):
    return pl.pallas_call(
        lambda *refs: prepare_kernel(count, rows, cells, *refs),
        in_specs=[in_smem()] * 4 + [in_vmem()] * 3,
        out_specs=[in_vmem()] * 11,
        out_shape=[shape(d, bf16) for d in OPERANDS]
        + [shape((frames,) + SMALL, f32), shape(SMALL, f32), shape((count * frames, LANES), f32)],
        scratch_shapes=[
            pltpu.VMEM((9 * C, LANES), f32),
            pltpu.VMEM((18 * C, LANES), f32),
            pltpu.VMEM((9 * C, LANES), f32),
            pltpu.VMEM((count * cells, LANES), f32),
            pltpu.VMEM((count * cells, LANES), f32),
            pltpu.VMEM((count * cells // LANES, TABLE_ROWS, LANES), f32),
        ],
        compiler_params=params(),
        name="prepare",
    )(where, *ids, packed, mine, other)


def weight_messages(where, wins, tiles, pieces, bias_sums, count, rows):
    frames = pieces.shape[0]
    size = count // 2 * 3 * rows
    return pl.pallas_call(
        lambda *refs: message_kernel(count, rows, *refs),
        in_specs=[in_smem()] + [in_vmem()] * 10,
        out_specs=[in_vmem()] * 3,
        out_shape=[shape((size, LANES), f32), shape((PARTS, LANES), f32), shape((size, LANES), bf16)],
        scratch_shapes=sum_scratch()
        + [pltpu.VMEM((9 * C, LANES), f32), pltpu.VMEM((18 * C, LANES), f32), pltpu.VMEM((9 * C, LANES), f32)],
        compiler_params=params(),
        cost_estimate=cost(frames * BLOCK * KEYS * 2 * LANES * 5, frames * (6 << 20)),
        name="weights",
    )(where, *wins, *tiles, pieces, bias_sums)


def join_messages(where, kept, small, theirs, half, rows, frames):
    return pl.pallas_call(
        lambda *refs: join_kernel(half, rows, frames, *refs),
        in_specs=[in_smem()] + [in_vmem()] * 3,
        out_specs=[in_vmem()] * (1 + half),
        out_shape=[shape((3 * rows, LANES), f32)] + [shape((3 * rows, LANES), bf16)] * half,
        compiler_params=params(),
        name="join",
    )(where, kept, small, theirs)


def reduce_messages(where, own, messages, hots, act_table, noise_table, ada_one, ada_two, rows, cells, frames):
    half = len(messages)
    return pl.pallas_call(
        lambda *refs: reduce_kernel(half, rows, cells, frames, *refs),
        in_specs=[in_smem()] + [in_vmem()] * (half + 6),
        out_specs=in_vmem(),
        out_shape=shape((3 * rows + 2 * cells, LANES), f32),
        scratch_shapes=[
            pltpu.VMEM((half * frames, LANES), f32),
            pltpu.VMEM((half * frames, LANES), f32),
            pltpu.VMEM((TABLE_ROWS, cells), f32),
            pltpu.VMEM((LANES, LANES), f32),
            pltpu.VMEM((LANES, LANES), f32),
        ],
        compiler_params=params(),
        name="reduce",
    )(where, own, *messages, hots, act_table, noise_table, ada_one, ada_two)


def finish(first, second, rows, cells, width):
    act_grad, noise_grad, one, two, *rest = pl.pallas_call(
        lambda *refs: finish_kernel(rows, cells, *refs),
        in_specs=[in_vmem()] * 2,
        out_specs=[in_vmem()] * 12,
        out_shape=[
            shape((NACT, cells), f32),
            shape((NLEV, cells), f32),
            shape((cells, LANES), f32),
            shape((cells, LANES), f32),
            shape((C, rows), f32),
            shape((C, rows), f32),
            shape((C, rows), f32),
            shape((C, 2 * rows), f32),
        ]
        + [shape((width,), f32)] * 4,
        compiler_params=params(),
        name="finish",
    )(first, second)
    return (act_grad, noise_grad, one, two, *[grad.T for grad in rest[:4]], *rest[4:])


def collect_kernel(member_ref, *refs):
    strips, out = refs[:-1], refs[-1]
    for offset, strip in enumerate(strips):
        out[member_ref[0] ^ offset, 0] = strip[0].astype(out.dtype)


def trade_strips(strips):
    return tuple(trade(strip, offset) for offset, strip in enumerate(strips))


def collect_strips(member_box, strips, kind):
    count = len(strips)
    frames, rows, columns = strips[0].shape
    whole_strips = pl.pallas_call(
        collect_kernel,
        grid=(frames,),
        in_specs=[in_smem()] + [pl.BlockSpec((1, rows, columns), lambda f: (f, 0, 0))] * count,
        out_specs=pl.BlockSpec((count, 1, rows, columns), lambda f: (0, f, 0, 0)),
        out_shape=shape((count, frames, rows, columns), kind),
        compiler_params=params(),
        name="collect",
    )(member_box, *strips)
    return whole_strips.reshape(count * frames, rows, columns)


def twice(values):
    return jnp.concatenate([values, values], axis=-1)


def pad_small(rows):
    stacked = jnp.stack(rows, axis=-2)
    gaps = [(0, 0)] * (stacked.ndim - 2) + [(0, 8 - len(rows)), (0, 0)]
    return jnp.pad(stacked, gaps)


def trade(value, offset):
    if offset == 0:
        return value
    count = lax.axis_size("rows")
    return lax.ppermute(value, "rows", [(i, i ^ offset) for i in range(count)])


def half_trade(value, at):
    count, members = lax.axis_size("seq"), lax.axis_size("rows")
    pairs = []
    for place in range(count):
        for member in range(members):
            offset = sides(count)[member % 2][at]
            if offset:
                pairs.append((place * members + member, (place ^ offset) * members + member))
    return lax.ppermute(value, ("seq", "rows"), pairs)


def layers(member_box, frame_images, frame_stats, cot_fetched, styles, bias_rows, operands):
    f_one, f_two, f_down, f_up, b_one, b_two, b_down, b_up = operands
    count = lax.axis_size("rows")
    *out, win_one, win_two, win_level, win_coarse, middle, down, stats = forward(
        member_box, frame_images, frame_stats, styles, bias_rows, f_one, f_two, f_down, f_up, count
    )
    out = trade_strips(out)
    down, cot_fetched = lax.optimization_barrier((down, cot_fetched))
    cot = gather_frames(member_box, *cot_fetched)
    *grad_strips, tile_out, tile_level, tile_mid, coarse_pairs, pieces, bias_sums = backward(
        member_box, cot, frame_images, styles, stats, middle, down, b_up, b_down, b_two, b_one, count
    )
    grad_strips = trade_strips(grad_strips)
    wins = (win_one, win_two, win_level, win_coarse)
    tiles = (tile_out, tile_level, tile_mid, coarse_pairs)
    return out, grad_strips, wins, tiles, pieces, bias_sums


def local_direct(
    frames,
    cotangent,
    actions,
    noise_ids,
    valid,
    act_table,
    noise_table,
    ada_one,
    ada_two,
    conv_one,
    conv_two,
    down_kernel,
    up_kernel,
    bias_one,
    bias_two,
    bias_down,
    bias_up,
):
    member = lax.axis_index("rows").astype(jnp.int32)
    place = lax.axis_index("seq").astype(jnp.int32)
    count = lax.axis_size("seq")
    share = frames.shape[0] // lax.axis_size("rows")
    rows, cells, width = conv_one.shape[0], ada_one.shape[0], bias_one.shape[0]
    half = count // 2
    member_box = member.reshape(1)
    where = jnp.stack([place, member])
    ids = (actions, noise_ids, valid)
    kernels = (conv_one, conv_two, down_kernel, up_kernel)
    biases = (bias_one, bias_two, bias_down, bias_up)
    fetched = fetch_far(member_box, frames)
    packed = pack(ids, kernels, ada_one, ada_two, act_table, noise_table, biases)
    mine = jnp.concatenate([half_trade(packed, at) for at in range(half)], axis=0)
    other = trade(mine, 1)
    cot_fetched = fetch_far(member_box, cotangent)
    frame_images, frame_stats = gather_frames(member_box, *fetched, FAR_HINTS)
    *operands, styles, bias_rows, hots = prepare(where, ids, packed, mine, other, count, rows, cells, share)
    out, grad_strips, wins, tiles, pieces, bias_sums = layers(
        member_box, frame_images, frame_stats, cot_fetched, styles, bias_rows, operands
    )
    kept, small, theirs = weight_messages(where, wins, tiles, pieces, bias_sums, count, rows)
    theirs, out = lax.optimization_barrier((theirs, out))
    own, *messages = join_messages(where, kept, small, trade(theirs, 1), half, rows, share)
    received = [half_trade(message, at) for at, message in enumerate(messages)]
    received, grad_strips = lax.optimization_barrier((received, grad_strips))
    sums = reduce_messages(
        where, own, received, hots, act_table, noise_table, ada_one, ada_two, rows, cells, 2 * share
    )
    offset = 1
    while 2 * offset < lax.axis_size("rows"):
        sums = sums + trade(sums, offset)
        offset *= 2
    result = collect_strips(member_box, out, bf16)
    frames_grad = collect_strips(member_box, grad_strips, f32)
    sums = sums.astype(bf16)
    return (result, frames_grad, *finish(sums, trade(sums, offset), rows, cells, width))


def local_general(
    frames,
    cotangent,
    actions,
    noise_ids,
    valid,
    act_table,
    noise_table,
    ada_one,
    ada_two,
    conv_one,
    conv_two,
    down_kernel,
    up_kernel,
    bias_one,
    bias_two,
    bias_down,
    bias_up,
):
    member = lax.axis_index("rows").astype(jnp.int32)
    share = frames.shape[0] // lax.axis_size("rows")
    member_box = member.reshape(1)

    def gathered(value, axis):
        return lax.all_gather(value, "seq", axis=axis, tiled=True)

    cot_fetched = fetch_far(member_box, cotangent)
    frame_images, frame_stats = gather_frames(member_box, *fetch_far(member_box, frames))
    act_full = gathered(act_table, 1)
    noise_full = gathered(noise_table, 1)
    ada_full = gathered(jnp.concatenate([ada_one, ada_two], axis=1), 0).astype(f32)
    biases = gathered(jnp.stack([bias_one, bias_two, bias_down, bias_up]), 1).astype(f32)
    operands = expand(gathered(conv_one, 0), gathered(conv_two, 0), gathered(down_kernel, 0), gathered(up_kernel, 0))

    own = lambda ids: lax.dynamic_slice_in_dim(ids, member * share, share)
    own_actions, own_noise, own_valid = own(actions), own(noise_ids), own(valid)
    action_hot = (own_actions[:, None] == jnp.arange(NACT, dtype=jnp.int32)[None, :]).astype(f32) * own_valid[
        :, None
    ].astype(f32)
    noise_hot = (own_noise[:, None] == jnp.arange(NLEV, dtype=jnp.int32)[None, :]).astype(f32)
    embed = jnp.dot(action_hot, act_full.astype(f32), precision=precise) + jnp.dot(
        noise_hot, noise_full.astype(f32), precision=precise
    )
    style = jnp.dot(embed, ada_full, precision=precise)
    styles = pad_small(
        [
            twice(1.0 + style[:, :C]),
            twice(style[:, C : 2 * C]),
            twice(1.0 + style[:, 2 * C : 3 * C]),
            twice(style[:, 3 * C :]),
        ]
    )
    bias_rows = pad_small([twice(biases[k]) for k in range(4)])
    out, grad_strips, wins, tiles, pieces, bias_sums = layers(
        member_box, frame_images, frame_stats, cot_fetched, styles, bias_rows, operands
    )
    g_one, g_two, g_down, g_up = weight_grads(wins, tiles)
    result = collect_strips(member_box, out, bf16)
    frames_grad = collect_strips(member_box, grad_strips, f32)

    pieces_one = jnp.concatenate([pieces[:, 0, :C], pieces[:, 1, :C]], axis=1)
    pieces_two = jnp.concatenate([pieces[:, 2, :C], pieces[:, 3, :C]], axis=1)
    ada_one_grad = jnp.dot(embed.T, pieces_one, precision=precise)
    ada_two_grad = jnp.dot(embed.T, pieces_two, precision=precise)
    embed_grad = jnp.dot(jnp.concatenate([pieces_one, pieces_two], axis=1), ada_full.T, precision=precise)
    act_table_grad = jnp.dot(action_hot.T, embed_grad, precision=precise)
    noise_table_grad = jnp.dot(noise_hot.T, embed_grad, precision=precise)
    bias_total = jnp.sum(bias_sums, axis=0)[:4, :C]

    def shard(value, axis):
        return lax.psum_scatter(value, "seq", scatter_dimension=axis, tiled=True)

    shards = (
        shard(act_table_grad, 1),
        shard(noise_table_grad, 1),
        shard(ada_one_grad, 0),
        shard(ada_two_grad, 0),
        shard(g_one, 0),
        shard(g_two, 0),
        shard(g_down, 0),
        shard(g_up, 0),
        shard(bias_total[0], 0),
        shard(bias_total[1], 0),
        shard(bias_total[2], 0),
        shard(bias_total[3], 0),
    )
    return (result, frames_grad) + lax.psum(shards, "rows")


def fits_direct(mesh):
    count = mesh.shape["seq"]
    rows, cells = 9 * C // count, 256 // count
    return count in (2, 4, 8) and rows % 8 == 0 and rows >= ID_ROW + 8 and cells % 8 == 0 and mesh.shape["rows"] == 4


def solution(mesh):
    in_specs = (
        P("seq", "rows", None),
        P("seq", "rows", None),
        P("seq"),
        P("seq"),
        P("seq"),
        P(None, "seq"),
        P(None, "seq"),
        P("seq", None),
        P("seq", None),
        P("seq", None),
        P("seq", None),
        P("seq", None),
        P("seq", None),
        P("seq"),
        P("seq"),
        P("seq"),
        P("seq"),
    )
    out_specs = (
        P("seq", "rows", None),
        P("seq", "rows", None),
        P(None, "seq"),
        P(None, "seq"),
        P("seq", None),
        P("seq", None),
        P("seq", None),
        P("seq", None),
        P("seq", None),
        P("seq", None),
        P("seq"),
        P("seq"),
        P("seq"),
        P("seq"),
    )
    local = local_direct if fits_direct(mesh) else local_general
    return jax.shard_map(local, mesh=mesh, in_specs=in_specs, out_specs=out_specs, check_vma=False)
```

```python
import jax
import jax.numpy as jnp
from jax import lax
from jax.experimental import pallas as pl
from jax.experimental.pallas import tpu as pltpu
from jax.sharding import PartitionSpec as P

C = 64
NACT = 18
GROUPS = 32
NLEV = 32
H = 64
W = 64
PAIRS = W // 2
HALF = H // 2
LANES = 2 * C
BLOCK = PAIRS * HALF
MEMBERS = float(H * W * (C // GROUPS))
EPS = 1e-05

precise = lax.Precision.HIGHEST
f32 = jnp.float32
bf16 = jnp.bfloat16
VMEM_LIMIT = 16 * 2**20
VMEM_MOST = 60 * 2**20


def lane_ids(shape):
    return lax.broadcasted_iota(jnp.int32, shape, len(shape) - 1)


def swap_halves(x):
    return pltpu.roll(x, C, axis=x.ndim - 1)


def row_before(x):
    rows = lax.broadcasted_iota(jnp.int32, x.shape, 0)
    return jnp.where(rows == 0, 0.0, pltpu.roll(x, 1, axis=0))


def row_after(x):
    rows = lax.broadcasted_iota(jnp.int32, x.shape, 0)
    return jnp.where(rows == x.shape[0] - 1, 0.0, pltpu.roll(x, x.shape[0] - 1, axis=0))


def both_parities(x):
    x = jnp.broadcast_to(x, (8, LANES))
    return x + swap_halves(x)


def group_sum(x):
    even = lane_ids(x.shape) % 2 == 0
    return x + jnp.where(even, pltpu.roll(x, LANES - 1, axis=1), pltpu.roll(x, 1, axis=1))


def total(x):
    return jnp.sum(x, axis=0, keepdims=True)


def over_pairs(body, carry):
    for j in range(PAIRS):
        carry = body(j, carry)
    return carry


def build_windows(windows, tile):
    low_lanes = lane_ids((HALF, LANES)) < C
    zero = jnp.zeros((HALF, LANES), f32)

    def write(j, even, odd):
        windows[0, j] = row_before(odd).astype(bf16)
        windows[1, j] = even.astype(bf16)
        windows[2, j] = odd.astype(bf16)
        windows[3, j] = row_after(even).astype(bf16)

    def body(j, carry):
        even_past, odd_past = carry
        even = swap_halves(tile(0, j))
        odd = swap_halves(tile(1, j))
        write(j, jnp.where(low_lanes, even_past, even), jnp.where(low_lanes, odd_past, odd))
        return even, odd

    even, odd = over_pairs(body, (zero, zero))
    write(PAIRS, jnp.where(low_lanes, even, 0.0), jnp.where(low_lanes, odd, 0.0))


def window_operand(windows, slots):
    parts = []
    for slot in slots:
        for shift in (0, 1):
            parts.append(windows[slot, shift : shift + PAIRS].reshape(BLOCK, LANES))
    return jnp.concatenate(parts, axis=1)


def matmul(left, right):
    return jnp.dot(left, right, preferred_element_type=f32)


def tiles_of(y):
    return y.reshape(PAIRS, HALF, LANES)


def norm_stats(sums, squares):
    average = group_sum(both_parities(sums)) / MEMBERS
    variance = group_sum(both_parities(squares)) / MEMBERS - average * average
    return average, lax.rsqrt(variance + EPS)


def strip_start(member, offset, strip):
    return pl.multiple_of((member ^ offset) * strip, strip)


def load_strips(member, strips, image):
    for offset, strip in enumerate(strips):
        rows = strip.shape[0]
        start = strip_start(member, offset, rows)
        for j in range(PAIRS):
            image[j, pl.ds(start, rows), :] = strip[:, j * LANES : (j + 1) * LANES].astype(f32)


def store_strips(member, image, f, strips):
    for offset, strip in enumerate(strips):
        rows = strip.shape[1]
        start = strip_start(member, offset, rows)
        for j in range(PAIRS):
            strip[f, :, j * LANES : (j + 1) * LANES] = image[j, pl.ds(start, rows), :].astype(strip.dtype)


def parity_rows(image, parity, j):
    return image[j, pl.ds(parity, HALF, stride=2), :]


def staggered(steps):
    steps = list(steps)
    started = []
    while steps or started:
        if steps:
            started.append(steps.pop(0))
        for step in list(started):
            if next(step, "end") == "end":
                started.remove(step)


def gather_frame(member, strips, image, stats):
    load_strips(member, strips, image)

    def add_stats(j, carry):
        x = image[j]
        s, q = carry
        return s + x, q + x * x

    zero = jnp.zeros((H, LANES), f32)
    s, q = over_pairs(add_stats, (zero, zero))
    average, inverse = norm_stats(total(s), total(q))
    stats[0:1, :] = average[0:1]
    stats[1:2, :] = inverse[0:1]
    stats[2:3, :] = both_parities(total(s))[0:1]
    stats[3:8, :] = jnp.zeros((5, LANES), f32)


def gather_kernel(member_ref, own, far, near, images, all_stats):
    member = member_ref[0]
    frames = images.shape[0]
    first = member % 2 * frames
    for f in range(frames):
        strips = (own.at[f], near.at[f], far.at[first + f], near.at[frames + f])
        gather_frame(member, strips, images.at[f], all_stats.at[f])


def forward_kernel(count, *refs):
    member_ref, frame_images, frame_stats, styles, biases, work_pair, work_up, work_down = refs[:8]
    out = refs[8 : 8 + count]
    outs = refs[8 + count : 15 + count]
    turned_operands = refs[15 + count : 19 + count]
    images, levels, w_one, w_two, w_down, w_up = refs[19 + count :]
    member = member_ref[0]
    works = {"one": work_pair, "two": work_pair, "down": work_down, "up": work_up}
    found = {}

    def block(name, row):
        k = works[name][row : row + C, :]
        low = lane_ids(k.shape) < C
        if name == "two":
            return jnp.where(low, swap_halves(k), k)
        return jnp.where(low, k, swap_halves(k))

    def turned_pairs(name):
        work = works[name]
        key = "one" if name == "two" else name
        if key not in found:
            blocks = [work[at : min(at + LANES, work.shape[0]), :] for at in range(0, work.shape[0], LANES)]
            found[key] = [below(block, LANES).T for block in blocks]
        return [k[C:] if name == "two" else k[:C] for k in found[key]]

    def operands():
        yield from write_forward_operands(block, w_one, w_two, w_down, w_up)
        yield from write_backward_operands(turned_pairs, *turned_operands)

    low_lanes = lane_ids((HALF, LANES)) < C

    def frame(f):
        win_one, win_two, win_level, win_coarse, middle, down, stats = (ref.at[f] for ref in outs)
        frame_image, image, level, style = frame_images.at[f], images.at[f], levels.at[f], styles.at[f]
        average_one, inverse_one = frame_stats[f, 0:1, :], frame_stats[f, 1:2, :]
        gain_one = inverse_one * style[0:1, :]
        half_gain = 0.5 * gain_one
        half_shift = 0.5 * (style[1:2, :] - average_one * gain_one)

        def act_one(parity, j):
            h = parity_rows(frame_image, parity, j) * half_gain + half_shift
            return h * jnp.tanh(h) + h

        build_windows(win_one, act_one)
        yield
        y = matmul(window_operand(win_one, range(4)), w_one[...])
        sums = jnp.zeros((1, LANES), f32)
        squares = jnp.zeros((1, LANES), f32)
        for a in range(2):
            v = y[:, a * LANES : (a + 1) * LANES] + biases[0:1, :]
            sums = sums + total(v)
            squares = squares + total(v * v)
            middle[a] = tiles_of(v)
        yield
        average_two, inverse_two = norm_stats(sums, squares)
        stats[0:1, :] = average_one
        stats[1:2, :] = inverse_one
        stats[2:3, :] = average_two[0:1]
        stats[3:4, :] = inverse_two[0:1]
        stats[4:8, :] = jnp.zeros((4, LANES), f32)
        gain_two = inverse_two * style[2:3, :]
        half_gain_two = 0.5 * gain_two[0:1]
        half_shift_two = 0.5 * (style[3:4, :] - average_two[0:1] * gain_two[0:1])

        def act_two(parity, j):
            h = middle[parity, j] * half_gain_two + half_shift_two
            return h * jnp.tanh(h) + h

        build_windows(win_two, act_two)
        yield
        y = matmul(window_operand(win_two, range(4)), w_two[...])
        for a in range(2):
            v = y[:, a * LANES : (a + 1) * LANES] + biases[1:2, :]
            level[a] = tiles_of(v) + frame_image[:, pl.ds(a, HALF, stride=2), :]
        yield
        build_windows(win_level, lambda parity, j: level[parity, j])
        yield
        operand = window_operand(win_level, range(4))
        y = matmul(operand[:, : 6 * LANES], w_down[...]) + biases[2:3, :]
        down[...] = tiles_of(y)
        yield

        def write_coarse(j, cells):
            win_coarse[0, j] = row_before(cells).astype(bf16)
            win_coarse[1, j] = cells.astype(bf16)
            win_coarse[2, j] = row_after(cells).astype(bf16)

        def coarse_body(j, past):
            h = down[j] * 0.5
            coarse = h * jnp.tanh(h) + h
            write_coarse(j, jnp.where(low_lanes, past, coarse))
            return coarse

        past = over_pairs(coarse_body, jnp.zeros((HALF, LANES), f32))
        write_coarse(PAIRS, jnp.where(low_lanes, past, 0.0))
        yield
        operand = window_operand(win_level, range(4))
        coarse_operand = window_operand(win_coarse, (0, 1, 1, 2))
        y = matmul(operand, w_up[: 16 * C, :]) + matmul(coarse_operand, w_up[16 * C :, :])
        for a in range(2):
            v = y[:, a * LANES : (a + 1) * LANES] + biases[3:4, :]
            image[:, pl.ds(a, HALF, stride=2), :] = tiles_of(v) + level[a]
        yield
        store_strips(member, image, f, out)

    staggered([operands()] + [frame(f) for f in range(styles.shape[0])])


def slope_twice(h):
    t = jnp.tanh(h)
    return (1.0 + t) + h * (1.0 - t * t)


def backward_kernel(count, *refs):
    member_ref = refs[0]
    cot_images, cot_stats, frame_images, styles, all_stats, all_middle, all_down = refs[1:8]
    w_up, w_down, w_two, w_one = refs[8:12]
    out = refs[12 : 12 + count]
    outs = refs[12 + count : 18 + count]
    scratch = refs[18 + count :]
    member = member_ref[0]
    low_lanes = lane_ids((HALF, LANES)) < C

    def frame(f):
        tile_out, tile_level, tile_mid, coarse_pairs, pieces, bias_sums = (ref.at[f] for ref in outs)
        image, level_grad, pre_grad, windows, coarse_below = (ref.at[f] for ref in scratch)
        style, stats, middle, down, frame_image = (
            ref.at[f] for ref in (styles, all_stats, all_middle, all_down, frame_images)
        )
        cot_image = cot_images.at[f]

        def out_tile(parity, j):
            x = parity_rows(cot_image, parity, j)
            tile_out[parity, j] = x.astype(bf16)
            return x

        build_windows(windows, out_tile)
        yield
        y = matmul(window_operand(windows, range(4)), w_up[...])
        for a in range(2):
            level_grad[a] = (
                tiles_of(y[:, (2 + a) * LANES : (3 + a) * LANES]) + cot_image[:, pl.ds(a, HALF, stride=2), :]
            )
        coarse = y[:, :LANES] + y[:, LANES : 2 * LANES]
        pre_grad[0] = tiles_of(coarse)
        yield

        def coarse_body(t, carry):
            after, sums = carry
            j = PAIRS - 1 - t
            g = pre_grad[0, j]
            g = g + swap_halves(g)
            h = down[j] * 0.5
            d = 0.5 * g * slope_twice(h)
            pair = jnp.where(low_lanes, d, after)
            coarse_pairs[j] = pair.astype(bf16)
            coarse_below[j] = row_after(pair).astype(bf16)
            return d, sums + d

        zero = jnp.zeros((HALF, LANES), f32)
        _, sums = over_pairs(coarse_body, (zero, zero))
        bias_down_sum = jnp.broadcast_to(total(sums), (8, LANES))
        operand = jnp.concatenate(
            [coarse_pairs[...].reshape(BLOCK, LANES), coarse_below[...].reshape(BLOCK, LANES)], axis=1
        )
        y = matmul(operand, w_down[...])
        sums = jnp.zeros((1, LANES), f32)
        for a in range(2):
            v = y[:, a * LANES : (a + 1) * LANES] + level_grad[a].reshape(BLOCK, LANES)
            sums = sums + total(v)
            level_grad[a] = tiles_of(v)
        bias_two_sum = both_parities(sums)

        def level_tile(parity, j):
            x = level_grad[parity, j]
            tile_level[parity, j] = x.astype(bf16)
            return x

        build_windows(windows, level_tile)
        yield

        def norm_slopes(y, value, k):
            average, inverse = stats[2 * k : 2 * k + 1, :], stats[2 * k + 1 : 2 * k + 2, :]
            gain = inverse * style[2 * k : 2 * k + 1, :]
            half_gain = 0.5 * gain
            half_shift = 0.5 * (style[2 * k + 1 : 2 * k + 2, :] - average * gain)
            scale_sum = jnp.zeros((1, LANES), f32)
            shift_sum = jnp.zeros((1, LANES), f32)
            for a in range(2):
                v = value(a)
                g = 0.5 * y[:, a * LANES : (a + 1) * LANES] * slope_twice(v * half_gain + half_shift)
                pre_grad[a] = tiles_of(g)
                shift_sum = shift_sum + total(g)
                scale_sum = scale_sum + total(g * ((v - average) * inverse))
            scale_sum, shift_sum = both_parities(scale_sum), both_parities(shift_sum)
            factor = style[2 * k : 2 * k + 1, :]
            center = group_sum(factor * shift_sum) / MEMBERS
            tilt = group_sum(factor * scale_sum) / MEMBERS
            slope = (inverse * tilt)[0:1] * inverse
            return scale_sum, shift_sum, gain, slope, slope * average - (inverse * center)[0:1]

        y = matmul(window_operand(windows, range(4)), w_two[...])
        scale_two, shift_two, gain_two, slope_two, constant_two = norm_slopes(
            y, lambda a: middle[a].reshape(BLOCK, LANES), 1
        )
        yield
        row_sums = [zero]

        def mid_tile(parity, j):
            x = pre_grad[parity, j] * gain_two + (constant_two - middle[parity, j] * slope_two)
            tile_mid[parity, j] = x.astype(bf16)
            row_sums[0] = row_sums[0] + x
            return x

        build_windows(windows, mid_tile)
        bias_one_sum = both_parities(total(row_sums[0]))
        yield
        y = matmul(window_operand(windows, range(4)), w_one[...])
        scale_one, shift_one, gain_one, slope_one, constant_one = norm_slopes(
            y, lambda a: frame_image[:, pl.ds(a, HALF, stride=2), :].reshape(BLOCK, LANES), 0
        )
        yield

        def frame_body(j, carry):
            for parity in range(2):
                x = parity_rows(frame_image, parity, j)
                g = pre_grad[parity, j] * gain_one + (constant_one - x * slope_one) + level_grad[parity, j]
                image[j, pl.ds(parity, HALF, stride=2), :] = g
            return carry

        over_pairs(frame_body, 0)
        store_strips(member, image, f, out)
        for k, value in enumerate((scale_one, shift_one, scale_two, shift_two)):
            pieces[k : k + 1, :] = value[0:1]
        pieces[4:8, :] = jnp.zeros((4, LANES), f32)
        for k, value in enumerate((bias_one_sum, bias_two_sum, bias_down_sum, cot_stats[f, 2:3, :])):
            bias_sums[k : k + 1, :] = value[0:1]
        bias_sums[4:8, :] = jnp.zeros((4, LANES), f32)

    staggered(frame(f) for f in range(styles.shape[0]))


def outer(left, right):
    return lax.dot_general(left, right, (((0,), (0,)), ((), ())), preferred_element_type=f32)


def accumulate(wins, tiles, sums):
    win_one, win_two, win_level, win_coarse = wins
    tile_out, tile_level, tile_mid, coarse_pairs = tiles
    sum_one, sum_two, sum_down, sum_up = sums
    cells = win_one.shape[0] * BLOCK

    def operand(windows, slots):
        parts = []
        for slot in slots:
            for shift in (0, 1):
                parts.append(windows[:, slot, shift : shift + PAIRS].reshape(cells, LANES))
        return jnp.concatenate(parts, axis=1)

    def blocks(tiles):
        return jnp.concatenate([tiles[:, a].reshape(cells, LANES) for a in range(2)], axis=1)

    out_blocks = blocks(tile_out)
    sum_up[16 * C :, :] = outer(operand(win_coarse, range(3)), out_blocks)
    sum_up[: 16 * C, :] = outer(operand(win_level, range(4)), out_blocks)
    sum_down[...] = outer(operand(win_level, range(3)), coarse_pairs[...].reshape(cells, LANES))
    sum_two[...] = outer(operand(win_two, range(4)), blocks(tile_level))
    sum_one[...] = outer(operand(win_one, range(4)), blocks(tile_mid))


def fold(sums, p, q):
    return fold_slots(sums, 0, p, q, range(4))


def fold_coarse(sums, p, q):
    return fold_slots(sums, 16 * C, p, q, (0, 1, 1, 2))


def fold_slots(sums, base, p, q, slots):
    halves = []
    for b in range(2):
        rows = [base + (slots[a + p] * 4 + b + q) * C for a in range(2)]
        halves.append(sums[rows[0] : rows[0] + C, :LANES] + sums[rows[1] : rows[1] + C, LANES:])
    return halves[0] + swap_halves(halves[1])


def weight_kernel(*refs):
    wins, tiles, grads, sums = refs[:4], refs[4:8], refs[8:12], refs[12:]
    g_one, g_two, g_down, g_up = grads
    sum_one, sum_two, sum_down, sum_up = sums
    accumulate(wins, tiles, sums)
    for p in range(3):
        for q in range(3):
            at = (3 * p + q) * C
            g_one[at : at + C, :] = fold(sum_one, p, q)[:, :C]
            g_two[at : at + C, :] = fold(sum_two, p, q)[:, :C]
            g_up[2 * at : 2 * at + C, :] = fold_coarse(sum_up, p, q)[:, :C]
            g_up[2 * at + C : 2 * at + 2 * C, :] = fold(sum_up, p, q)[:, :C]
            place = (p * 4 + q) * C
            g_down[at : at + C, :] = sum_down[place : place + C, :C]


PARTS = 16
FAR_HINT = 90
PAIR_PARTS = 24


def three_parts(exact):
    high = exact.astype(bf16).astype(f32)
    rest = exact - high
    mid = rest.astype(bf16).astype(f32)
    return jnp.concatenate([high, mid, rest - mid], axis=0)


def below(block, rows):
    if block.shape[0] == rows:
        return block
    return jnp.concatenate([block, jnp.zeros((rows - block.shape[0], LANES), f32)], axis=0)


def message_kernel(count, rows, *refs):
    where_ref, wins, tiles = refs[0], refs[1:5], refs[5:9]
    pieces, bias_sums, ids, kept, small, theirs, hots = refs[9:16]
    sums = refs[16:20]
    g_pair, g_up, g_down = refs[20:]
    sum_one, sum_two, sum_down, sum_up = sums
    taken = 2 * pieces.shape[0]
    for at in range(ids.shape[0]):
        write_hots(hots, at * taken, where_ref[1] // 2 * taken, taken, ids[at])
    accumulate(wins, tiles, sums)
    low_lanes = lane_ids((C, LANES)) < C
    for p in range(3):
        for q in range(3):
            at = (3 * p + q) * C
            g_pair[at : at + C, :] = jnp.where(
                low_lanes, fold(sum_one, p, q), swap_halves(fold(sum_two, p, q))
            )
            g_up[2 * at : 2 * at + C, :] = fold_coarse(sum_up, p, q)
            g_up[2 * at + C : 2 * at + 2 * C, :] = fold(sum_up, p, q)
            place = (p * 4 + q) * C
            g_down[at : at + C, :] = sum_down[place : place + C, :]
    frames = pieces.shape[0]
    small[...] = jnp.zeros_like(small)
    total_bias = bias_sums[0, 0:4, :]
    for f in range(frames):
        small[4 * f : 4 * f + 4, :] = pieces[f, 0:4, :]
        if f > 0:
            total_bias = total_bias + bias_sums[f, 0:4, :]
    small[4 * frames : 4 * frames + 4, :] = total_bias
    sent = below(three_parts(small[...]), rows)
    low_lanes = lane_ids((rows, LANES)) < C
    half = count // 2
    for at in range(half):
        for ref, mine in ((kept, True), (theirs, False)):
            start = pl.multiple_of(seq_owner(where_ref[0], where_ref[1], half, at, mine) * rows, 8)
            blocks = (
                g_pair[pl.ds(start, rows), :],
                jnp.where(
                    low_lanes,
                    g_up[pl.ds(pl.multiple_of(2 * start, 8), rows), :],
                    swap_halves(g_up[pl.ds(pl.multiple_of(2 * start + rows, 8), rows), :]),
                ),
                jnp.where(low_lanes, g_down[pl.ds(start, rows), :], 0.0 if mine else sent),
            )
            ref[at * 3 * rows : (at + 1) * 3 * rows, :] = jnp.concatenate(blocks, axis=0).astype(ref.dtype)


def join_kernel(half, rows, frames, where_ref, kept, small, theirs, own, *messages):
    first = where_ref[1] % 2 == 0
    at = 2 * rows
    other = theirs[at : at + 3 * PARTS, :].astype(f32)
    other = other[:PARTS] + other[PARTS : 2 * PARTS] + other[2 * PARTS :]
    mine = small[...]
    n = 4 * frames
    exact = jnp.concatenate(
        [
            jnp.where(first, mine[:n], other[:n]),
            jnp.where(first, other[:n], mine[:n]),
            mine[n : n + 4] + other[n : n + 4],
            jnp.zeros((PAIR_PARTS - 2 * n - 4, LANES), f32),
        ],
        axis=0,
    )
    low_lanes = lane_ids((rows, LANES)) < C
    sent = below(three_parts(exact), rows)
    size = 3 * rows
    for k, message in enumerate(messages):
        block = kept[k * size : (k + 1) * size, :] + theirs[k * size : (k + 1) * size, :].astype(f32)
        message[:at, :] = block[:at].astype(bf16)
        message[at:, :] = jnp.where(low_lanes, block[at:], sent).astype(bf16)
        if k == half - 1:
            own[:at, :] = block[:at]
            own[at:, :] = jnp.where(low_lanes, block[at:], below(exact, rows))


def reduce_kernel(half, rows, cells, frames, *refs):
    where_ref, own = refs[:2]
    messages = refs[2 : 2 + half]
    hots, act_table, noise_table, ada_one, ada_two, out, pieces_one, pieces_two, table, high_one, high_two = refs[2 + half :]
    place, member = where_ref[0], where_ref[1]
    taken = 4 * frames
    bias = jnp.zeros((4, LANES), f32)
    sums = None
    lanes = lane_ids((1, LANES))
    low_lanes = lanes < C
    at = 2 * rows
    for k, ref in enumerate(messages):
        message = ref[...].astype(f32)
        if k == half - 1:
            message = jnp.where(member % 2 == 0, own[...], message)
        sums = message if sums is None else sums + message
        small = (
            message[at : at + PAIR_PARTS]
            + message[at + PAIR_PARTS : at + 2 * PAIR_PARTS]
            + message[at + 2 * PAIR_PARTS : at + 3 * PAIR_PARTS]
        )
        turned = swap_halves(small)
        bias = bias + small[taken : taken + 4]
        for f in range(frames):
            row = k * frames + f
            for kind, piece in ((0, pieces_one), (2, pieces_two)):
                low, high = 4 * f + kind, 4 * f + kind + 1
                piece[row : row + 1, :] = jnp.where(low_lanes, turned[low : low + 1], small[high : high + 1])
    hot = hots[:, :TABLE_ROWS]
    table[...] = jnp.zeros_like(table)
    table[ACT_ROW : ACT_ROW + NACT, :] = act_table[...].astype(f32)
    table[NOISE_ROW : NOISE_ROW + NLEV, :] = noise_table[...].astype(f32)
    embed = matmul(hot.astype(bf16), table[...].astype(bf16))

    def exact(left, right, dims):
        return lax.dot_general(left, right, (dims, ((), ())), precision=precise, preferred_element_type=f32)

    one, two = pieces_one[...], pieces_two[...]
    for ref, ada in ((high_one, ada_one), (high_two, ada_two)):
        ref[...] = jnp.zeros_like(ref)
        ref[C : C + cells, :] = ada[...].astype(f32)
    embed_grad = exact(one, high_one[...], ((1,), (1,))) + exact(two, high_two[...], ((1,), (1,)))
    width = C // (2 * half)
    bias = pltpu.roll(jnp.concatenate([bias, bias], axis=0), (LANES - place * width) % LANES, axis=1)
    extra = below(jnp.concatenate([exact(hot, embed_grad, ((0,), (0,))), bias], axis=0), rows)
    at = 2 * rows
    blocks = (
        sums[:at],
        jnp.where(lane_ids((rows, LANES)) < C, sums[at:], extra),
        exact(embed, one, ((0,), (0,))),
        exact(embed, two, ((0,), (0,))),
    )
    out[...] = jnp.concatenate(blocks, axis=0).astype(out.dtype)


def finish_kernel(rows, cells, count, *refs):
    parts, outs = [ref[...].astype(f32) for ref in refs[:count]], refs[count:]
    act_grad, noise_grad, ada_one, ada_two, g_one, g_two, g_down, g_up = outs[:8]
    bias_grads = outs[8:12]
    while len(parts) > 1:
        parts = [parts[k] + parts[k + 1] for k in range(0, len(parts), 2)]
    sums = parts[0]

    def turn(block):
        return jnp.concatenate([block, jnp.zeros((LANES - rows, LANES), f32)], axis=0).T[:, :rows]

    pair, halves, down = (turn(sums[k * rows : (k + 1) * rows]) for k in range(3))
    g_one[...] = pair[:C]
    g_two[...] = pair[C:]
    g_up[:, :rows] = halves[:C]
    g_up[:, rows:] = halves[C:]
    g_down[...] = down[:C]
    at = 3 * rows
    ada_one[...] = sums[at : at + cells]
    ada_two[...] = sums[at + cells : at + 2 * cells]
    extra = swap_halves(sums[2 * rows : 3 * rows])
    act_grad[...] = extra[ACT_ROW : ACT_ROW + NACT, :cells]
    noise_grad[...] = extra[NOISE_ROW : NOISE_ROW + NLEV, :cells]
    for k, ref in enumerate(bias_grads):
        ref[...] = extra[BIAS_ROW + k : BIAS_ROW + k + 1, : ref.shape[0]].reshape(ref.shape)


def write_forward_operands(block, f_one, f_two, f_down, f_up):
    low_lanes = lane_ids((C, LANES)) < C
    zero = jnp.zeros((C, LANES), f32)

    def taps(name, base, step):
        return {(p, q): block(name, (3 * p + q) * step + base) for p in range(3) for q in range(3)}

    def write(ref, base, found):
        for w in range(4):
            for p in range(3):
                tile = jnp.where(low_lanes, found.get((p, w), zero), found.get((p, w - 1), zero)).astype(bf16)
                for a in range(2):
                    at = base + ((a + p) * 4 + w) * C
                    ref[at : at + C, a * LANES : (a + 1) * LANES] = tile
            for a in range(2):
                for r in range(4):
                    if not 0 <= r - a < 3:
                        at = base + (r * 4 + w) * C
                        ref[at : at + C, a * LANES : (a + 1) * LANES] = zero.astype(bf16)

    write(f_one, 0, taps("one", 0, C))
    yield
    write(f_two, 0, taps("two", 0, C))
    yield
    found = taps("down", 0, C)
    for p in range(3):
        for w in range(4):
            at = (p * 4 + w) * C
            f_down[at : at + C, :] = found.get((p, w), zero).astype(bf16)
    yield
    write(f_up, 0, taps("up", C, 2 * C))
    yield
    write(f_up, 16 * C, taps("up", 0, 2 * C))
    yield


def write_backward_operands(turned_pairs, b_one, b_two, b_down, b_up):
    low_lanes = lane_ids((C, LANES)) < C
    zero = jnp.zeros((C, LANES), f32)
    def taps(pairs, base, step):
        found = {}
        for p in range(3):
            for q in range(3):
                at = (3 * p + q) * step + base
                pair = pairs[at // LANES]
                other = swap_halves(pair)
                low, high = (pair, other) if at % LANES == 0 else (other, pair)
                found[p, q] = jnp.where(low_lanes, low, high)
        return found

    def write(ref, lane, found):
        for w in range(4):
            for p in range(3):
                tile = jnp.where(low_lanes, found.get((p, 2 - w), zero), found.get((p, 3 - w), zero)).astype(bf16)
                for a in range(2):
                    at = ((a + 2 - p) * 4 + w) * C
                    ref[at : at + C, lane + a * LANES : lane + (a + 1) * LANES] = tile
            for a in range(2):
                for r in range(4):
                    if not 0 <= a + 2 - r < 3:
                        at = (r * 4 + w) * C
                        ref[at : at + C, lane + a * LANES : lane + (a + 1) * LANES] = zero.astype(bf16)

    one, two = turned_pairs("one"), turned_pairs("two")
    write(b_one, 0, taps(one, 0, C))
    yield
    write(b_two, 0, taps(two, 0, C))
    yield
    pairs = turned_pairs("up")
    write(b_up, 0, taps(pairs, 0, 2 * C))
    yield
    write(b_up, 2 * LANES, taps(pairs, C, 2 * C))
    yield
    found = taps(turned_pairs("down"), 0, C)
    for under in range(2):
        for right in range(2):
            at = (under * 2 + right) * C
            for a in range(2):
                p = {(0, 0): 1, (0, 1): 2, (1, 1): 0}.get((under, a))
                first, second = zero, zero
                if p is not None:
                    first = found[p, 1] if right == 0 else zero
                    second = found[p, 2] if right == 0 else found[p, 0]
                b_down[at : at + C, a * LANES : (a + 1) * LANES] = jnp.where(low_lanes, first, second).astype(bf16)


ACT_ROW, NOISE_ROW, TABLE_ROWS = 0, 24, 56
BIAS_ROW, ID_ROW = 56, 64


def pack_sizes(rows, cells):
    return 3 * rows, 3 * rows + 2 * cells, -(-(3 * rows + 2 * cells) // 16) * 16


def turned(values):
    wide = jnp.concatenate([values, jnp.zeros((C, LANES - values.shape[1]), f32)], axis=1)
    return jnp.concatenate([wide, jnp.zeros((C, LANES), f32)], axis=0).T[: values.shape[1]]


def far_kernel(member_ref, array, out, own, other, sent):
    half, share = out.shape[0], own.shape[0]
    member = member_ref[0]
    copies = [
        pltpu.make_async_copy(array.at[pl.ds(first, ref.shape[0])], ref, sent.at[k])
        for k, (first, ref) in enumerate(
            (((1 - member // 2) * half, out), (member * share, own), ((member ^ 1) * share, other))
        )
    ]
    for copy in copies:
        copy.start()
    for copy in copies:
        copy.wait()


def share_kernel(member_ref, far, out):
    share = out.shape[0]
    out[...] = far[pl.ds((member_ref[0] ^ 1) % 2 * share, share)]


def mark_kernel(far, out):
    out[...] = far[0, :8, :LANES].astype(f32)


def near_kernel(other, shared, mark, out):
    share = out.shape[0] // 2
    out[:share] = other[...]
    out[share:] = shared[...]


def pack_kernel(*refs):
    actions, noise_ids, valid, conv_one, conv_two, down_kernel, up_kernel, ada_one, ada_two = refs[:9]
    act_table, noise_table = refs[9:11]
    biases = refs[11:15]
    out, work = refs[15:]
    rows, cells = conv_one.shape[1], ada_one.shape[0]
    style_at, end, _ = pack_sizes(rows, cells)
    wide = lambda ref: ref[...].astype(f32)
    low_lanes = lane_ids((rows, LANES)) < C
    up = wide(up_kernel)
    work[...] = jnp.zeros_like(work)
    for at, low, high in (
        (0, turned(wide(conv_one)), turned(wide(conv_two))),
        (rows, turned(up[:, :rows]), turned(up[:, rows:])),
    ):
        work[at : at + rows, :] = jnp.where(low_lanes, low, swap_halves(high))
    work[2 * rows : 3 * rows, :] = turned(wide(down_kernel))
    extra = 2 * rows
    for at, ref in ((ACT_ROW, act_table), (NOISE_ROW, noise_table)):
        size = ref.shape
        work[extra + at : extra + at + size[0], C : C + size[1]] = wide(ref)
    for k, ref in enumerate(biases):
        at = extra + BIAS_ROW + k
        work[at : at + 1, C : C + ref.shape[0]] = wide(ref).reshape(1, ref.shape[0])
    lanes = lane_ids((1, LANES))
    for k, ref in enumerate((actions, noise_ids, valid)):
        line = jnp.zeros((1, LANES), jnp.int32)
        for f in range(ref.shape[0]):
            line = jnp.where(lanes == C + f, ref[f], line)
        at = extra + ID_ROW + k
        work[at : at + 1, C:] = line.astype(f32)[:, C:]
    work[style_at : style_at + cells, :] = wide(ada_one)
    work[style_at + cells : end, :] = wide(ada_two)
    out[...] = work[...].astype(bf16)


def seq_owner(place, member, half, at, mine=True):
    side = member % 2 if mine else 1 - member % 2
    even, odd = sides(2 * half)
    return place ^ (even[at] + side * (odd[at] - even[at]))


def sides(count):
    ones = lambda offset: bin(offset).count("1") % 2
    return tuple([offset for offset in reversed(range(count)) if ones(offset) == side] for side in (0, 1))


def write_hots(hots, at, first, frames, ids):
    lanes = lane_ids((1, LANES)).astype(f32)
    for f in range(frames):
        mine = jnp.where(lane_ids(ids.shape) == C + first + f, ids, 0.0)
        mine = jnp.sum(mine, axis=1, keepdims=True)
        action, noise, valid = mine[0:1], mine[1:2], mine[2:3]
        hots[at + f : at + f + 1, :] = jnp.where(lanes == action + ACT_ROW, valid, 0.0) + jnp.where(
            lanes == noise + NOISE_ROW, 1.0, 0.0
        )


def prepare_kernel(count, rows, cells, *refs):
    where_ref, actions, noise_ids, valid, packed, mine, other = refs[:7]
    styles, biases, ids, work_pair, work_up, work_down, work_one, work_two, work_table = refs[7:]
    place, member, frames = where_ref[0], where_ref[1], styles.shape[0]
    style_at, _, size = pack_sizes(rows, cells)
    bias_rows = jnp.zeros(SMALL, f32)
    half = count // 2
    for offset in range(count):
        ref = mine if offset < half else other
        at = offset % half
        pack = ref[at * size : (at + 1) * size, :].astype(f32)
        if at == half - 1:
            pack = jnp.where(member % 2 == offset // half, packed[...].astype(f32), pack)
        owner = seq_owner(place, member, half, at, offset < half)
        start = pl.multiple_of(owner * rows, 8)
        work_pair[pl.ds(start, rows), :] = pack[:rows]
        halves = pack[rows : 2 * rows]
        work_up[pl.ds(2 * start, rows), :] = halves
        work_up[pl.ds(pl.multiple_of(2 * start + rows, 8), rows), :] = swap_halves(halves)
        extra = pack[2 * rows : 3 * rows]
        work_down[pl.ds(start, rows), :] = extra
        work_one[offset * cells : (offset + 1) * cells, :] = pack[style_at : style_at + cells]
        work_two[offset * cells : (offset + 1) * cells, :] = pack[style_at + cells : style_at + 2 * cells]
        lane = (offset * cells) % LANES
        tables = pltpu.roll(extra[:TABLE_ROWS], (lane - C) % LANES, axis=1)
        kept = (lane_ids(tables.shape) >= lane) & (lane_ids(tables.shape) < lane + cells)
        column = offset * cells // LANES
        tables = jnp.where(kept, tables, 0.0)
        if lane == 0:
            work_table[column] = tables
        else:
            work_table[column] += tables
        slots = extra[BIAS_ROW : BIAS_ROW + 8]
        width = C // count
        slots = jnp.where((lane_ids(SMALL) >= C) & (lane_ids(SMALL) < C + width), slots, 0.0)
        bias_rows = bias_rows + pltpu.roll(slots, (owner * width + C) % LANES, axis=1)
        if offset < half:
            ids[at] = extra[ID_ROW : ID_ROW + 8]
    biases[...] = bias_rows + swap_halves(bias_rows)

    lanes = lane_ids((8, LANES))
    row_at = lax.broadcasted_iota(jnp.int32, (8, LANES), 0)
    hot = jnp.zeros((8, LANES), f32)
    for f in range(frames):
        at = member * frames + f
        here = jnp.where(lanes == actions[at] + ACT_ROW, valid[at], 0) + jnp.where(lanes == noise_ids[at] + NOISE_ROW, 1, 0)
        hot = jnp.where(row_at == f, here.astype(f32), hot)
    hot = hot[:, :TABLE_ROWS].astype(bf16)
    embed = jnp.concatenate([matmul(hot, work_table[k].astype(bf16)) for k in range(work_table.shape[0])], axis=1)
    low_lanes = lanes < C
    for k, work in enumerate((work_one, work_two)):
        style = jnp.dot(embed, work[...], precision=precise, preferred_element_type=f32)
        other = swap_halves(style)
        scale = 1.0 + jnp.where(low_lanes, style, other)
        shift = jnp.where(low_lanes, other, style)
        for f in range(frames):
            styles[f, 2 * k : 2 * k + 1, :] = scale[f : f + 1]
            styles[f, 2 * k + 1 : 2 * k + 2, :] = shift[f : f + 1]
    for f in range(frames):
        styles[f, 4:8, :] = jnp.zeros((4, LANES), f32)


def shape(dims, kind):
    return jax.ShapeDtypeStruct(dims, kind)


def whole(dims):
    return pl.BlockSpec(dims, lambda f: (0,) * len(dims))


def per_frame(dims):
    return pl.BlockSpec((1,) + dims, lambda f: (f,) + (0,) * len(dims))


def strip_specs(count, strip):
    return [pl.BlockSpec((1, strip, W * C), lambda f: (f, 0, 0))] * count


SMALL = (8, LANES)
WINDOWS = (4, PAIRS + 1, HALF, LANES)
COARSE_WINDOWS = (3, PAIRS + 1, HALF, LANES)
TILES = (2, PAIRS, HALF, LANES)
COARSE = (PAIRS, HALF, LANES)
IMAGE = (PAIRS, H, LANES)
KEYS = 16 * C


def in_vmem():
    return pl.BlockSpec(memory_space=pltpu.VMEM)


def in_smem():
    return pl.BlockSpec(memory_space=pltpu.SMEM)


def params(limit=VMEM_LIMIT):
    return pltpu.CompilerParams(vmem_limit_bytes=limit)


def cost(macs, moved):
    return pl.CostEstimate(flops=2 * macs, bytes_accessed=moved, transcendentals=0)


def fetch_far(member, array):
    far, own, other = cut_far(member, array, lax.axis_size("rows"))
    return trade(far, 2), own, other


def gather_frames(member, far, own, other, hint=0):
    near = trade(cut_near(member, other, far, hint), 1)
    frames = own.shape[0]
    return pl.pallas_call(
        gather_kernel,
        in_specs=[in_smem()] + [in_vmem()] * 3,
        out_specs=[in_vmem()] * 2,
        out_shape=[shape((frames,) + IMAGE, f32), shape((frames,) + SMALL, f32)],
        compiler_params=params(),
        name="frames",
    )(member, own, far, near)


def forward(member, frame_images, frame_stats, styles, biases, works, count):
    frames = frame_images.shape[0]
    strip = H // count
    return pl.pallas_call(
        lambda *refs: forward_kernel(count, *refs),
        in_specs=[in_smem()] + [in_vmem()] * 7,
        out_specs=[in_vmem()] * (count + 11),
        out_shape=[shape((frames, strip, W * C), bf16)] * count
        + [
            shape((frames,) + WINDOWS, bf16),
            shape((frames,) + WINDOWS, bf16),
            shape((frames,) + WINDOWS, bf16),
            shape((frames,) + COARSE_WINDOWS, bf16),
            shape((frames,) + TILES, f32),
            shape((frames,) + COARSE, f32),
            shape((frames,) + SMALL, f32),
        ]
        + [shape(dims, bf16) for dims in OPERANDS[4:]],
        scratch_shapes=[pltpu.VMEM((frames,) + IMAGE, f32), pltpu.VMEM((frames,) + TILES, f32)]
        + [pltpu.VMEM(dims, bf16) for dims in OPERANDS[:4]],
        compiler_params=params(),
        cost_estimate=cost(1 << 10, 1 << 10),
        name="forward",
    )(member, frame_images, frame_stats, styles, biases, *works)


def backward(member, cot, frame_images, styles, stats, middle, down, w_up, w_down, w_two, w_one, count):
    frames = frame_images.shape[0]
    strip = H // count
    return pl.pallas_call(
        lambda *refs: backward_kernel(count, *refs),
        in_specs=[in_smem()] + [in_vmem()] * 11,
        out_specs=[in_vmem()] * (count + 6),
        out_shape=[shape((frames, strip, W * C), bf16)] * count
        + [
            shape((frames,) + TILES, bf16),
            shape((frames,) + TILES, bf16),
            shape((frames,) + TILES, bf16),
            shape((frames,) + COARSE, bf16),
            shape((frames,) + SMALL, f32),
            shape((frames,) + SMALL, f32),
        ],
        scratch_shapes=[
            pltpu.VMEM((frames,) + IMAGE, f32),
            pltpu.VMEM((frames,) + TILES, f32),
            pltpu.VMEM((frames,) + TILES, f32),
            pltpu.VMEM((frames,) + WINDOWS, bf16),
            pltpu.VMEM((frames,) + COARSE, bf16),
        ],
        compiler_params=params(),
        cost_estimate=cost(frames * BLOCK * KEYS * 2 * LANES * 5, frames * (10 << 20)),
        name="backward",
    )(member, *cot, frame_images, styles, stats, middle, down, w_up, w_down, w_two, w_one)


def sum_scratch():
    return [
        pltpu.VMEM((KEYS, 2 * LANES), f32),
        pltpu.VMEM((KEYS, 2 * LANES), f32),
        pltpu.VMEM((6 * LANES, LANES), f32),
        pltpu.VMEM((KEYS + 6 * LANES, 2 * LANES), f32),
    ]


def weight_grads(wins, tiles):
    return pl.pallas_call(
        weight_kernel,
        in_specs=[in_vmem()] * 8,
        out_specs=[in_vmem()] * 4,
        out_shape=[shape((9 * C, C), f32)] * 3 + [shape((18 * C, C), f32)],
        scratch_shapes=sum_scratch(),
        compiler_params=params(),
        name="weights",
    )(*wins, *tiles)


def in_place(space=pl.ANY):
    return pl.BlockSpec(memory_space=space)


def cut_far(member, array, count):
    half, share = ((array.shape[0] // n,) + array.shape[1:] for n in (2, count))
    array = pltpu.with_memory_space_constraint(array, pltpu.HBM)
    return pl.pallas_call(
        far_kernel,
        in_specs=[in_smem(), in_place(pltpu.HBM)],
        out_specs=[in_vmem()] * 3,
        out_shape=[pltpu.VMEM(dims, array.dtype) for dims in (half, share, share)],
        scratch_shapes=[pltpu.SemaphoreType.DMA((3,))],
        compiler_params=params(),
        name="far",
    )(member, array)


def cut_near(member, other, far, hint):
    shared = pl.pallas_call(
        share_kernel,
        in_specs=[in_smem(), in_vmem()],
        out_specs=in_vmem(),
        out_shape=shape(other.shape, other.dtype),
        compiler_params=params(),
        name="shared",
    )(member, far)
    mark = pl.pallas_call(
        mark_kernel,
        in_specs=[in_vmem()],
        out_specs=in_vmem(),
        out_shape=shape(SMALL, f32),
        compiler_params=params(),
        cost_estimate=cost(BLOCK * KEYS * 2 * LANES * hint, 1 << 20),
        name="mark",
    )(far)
    return pl.pallas_call(
        near_kernel,
        in_specs=[in_vmem()] * 3,
        out_specs=in_vmem(),
        out_shape=shape(far.shape, other.dtype),
        compiler_params=params(),
        name="near",
    )(other, shared, mark)


def pack(ids, kernels, ada_one, ada_two, act_table, noise_table, biases):
    _, _, size = pack_sizes(kernels[0].shape[0], ada_one.shape[0])
    args = (*[kernel.T for kernel in kernels], ada_one, ada_two, act_table, noise_table, *biases)
    return pl.pallas_call(
        pack_kernel,
        in_specs=[in_smem()] * 3 + [in_vmem()] * len(args),
        out_specs=in_vmem(),
        out_shape=shape((size, LANES), bf16),
        scratch_shapes=[pltpu.VMEM((size, LANES), f32)],
        compiler_params=params(VMEM_MOST),
        cost_estimate=cost(BLOCK * KEYS * 2 * LANES * 30, 1 << 20),
        name="pack",
    )(*ids, *args)


OPERANDS = (
    (KEYS, 2 * LANES),
    (KEYS, 2 * LANES),
    (6 * LANES, LANES),
    (2 * KEYS, 2 * LANES),
    (KEYS, 2 * LANES),
    (KEYS, 2 * LANES),
    (2 * LANES, 2 * LANES),
    (KEYS, 4 * LANES),
)


def prepare(where, ids, packed, mine, other, count, rows, cells, frames):
    found = pl.pallas_call(
        lambda *refs: prepare_kernel(count, rows, cells, *refs),
        in_specs=[in_smem()] * 4 + [in_vmem()] * 3,
        out_specs=[in_vmem()] * 6,
        out_shape=[shape((frames,) + SMALL, f32), shape(SMALL, f32), shape((count // 2,) + SMALL, f32)]
        + [shape((n * C, LANES), f32) for n in (9, 18, 9)],
        scratch_shapes=[
            pltpu.VMEM((count * cells, LANES), f32),
            pltpu.VMEM((count * cells, LANES), f32),
            pltpu.VMEM((count * cells // LANES, TABLE_ROWS, LANES), f32),
        ],
        compiler_params=params(),
        name="prepare",
    )(where, *ids, packed, mine, other)
    return found[0], found[1], found[2], found[3:]


def weight_messages(where, wins, tiles, pieces, bias_sums, ids, count, rows):
    frames = pieces.shape[0]
    size = count // 2 * 3 * rows
    return pl.pallas_call(
        lambda *refs: message_kernel(count, rows, *refs),
        in_specs=[in_smem()] + [in_vmem()] * 11,
        out_specs=[in_vmem()] * 4,
        out_shape=[
            shape((size, LANES), f32),
            shape((PARTS, LANES), f32),
            shape((size, LANES), bf16),
            shape((count * frames, LANES), f32),
        ],
        scratch_shapes=sum_scratch()
        + [pltpu.VMEM((9 * C, LANES), f32), pltpu.VMEM((18 * C, LANES), f32), pltpu.VMEM((9 * C, LANES), f32)],
        compiler_params=params(),
        cost_estimate=cost(frames * BLOCK * KEYS * 2 * LANES * 5, frames * (6 << 20)),
        name="weights",
    )(where, *wins, *tiles, pieces, bias_sums, ids)


def join_messages(where, kept, small, theirs, half, rows, frames):
    return pl.pallas_call(
        lambda *refs: join_kernel(half, rows, frames, *refs),
        in_specs=[in_smem()] + [in_vmem()] * 3,
        out_specs=[in_vmem()] * (1 + half),
        out_shape=[shape((3 * rows, LANES), f32)] + [shape((3 * rows, LANES), bf16)] * half,
        compiler_params=params(),
        name="join",
    )(where, kept, small, theirs)


def reduce_messages(where, own, messages, hots, act_table, noise_table, ada_one, ada_two, rows, cells, frames):
    half = len(messages)
    return pl.pallas_call(
        lambda *refs: reduce_kernel(half, rows, cells, frames, *refs),
        in_specs=[in_smem()] + [in_vmem()] * (half + 6),
        out_specs=in_vmem(),
        out_shape=shape((3 * rows + 2 * cells, LANES), bf16),
        scratch_shapes=[
            pltpu.VMEM((half * frames, LANES), f32),
            pltpu.VMEM((half * frames, LANES), f32),
            pltpu.VMEM((TABLE_ROWS, cells), f32),
            pltpu.VMEM((LANES, LANES), f32),
            pltpu.VMEM((LANES, LANES), f32),
        ],
        compiler_params=params(),
        name="reduce",
    )(where, own, *messages, hots, act_table, noise_table, ada_one, ada_two)


def finish(parts, rows, cells, width):
    act_grad, noise_grad, one, two, *rest = pl.pallas_call(
        lambda *refs: finish_kernel(rows, cells, len(parts), *refs),
        in_specs=[in_vmem()] * len(parts),
        out_specs=[in_vmem()] * 12,
        out_shape=[
            shape((NACT, cells), f32),
            shape((NLEV, cells), f32),
            shape((cells, LANES), f32),
            shape((cells, LANES), f32),
            shape((C, rows), f32),
            shape((C, rows), f32),
            shape((C, rows), f32),
            shape((C, 2 * rows), f32),
        ]
        + [shape((width,), f32)] * 4,
        compiler_params=params(),
        name="finish",
    )(*parts)
    return (act_grad, noise_grad, one, two, *[grad.T for grad in rest[:4]], *rest[4:])


def collect_kernel(member_ref, *refs):
    strips, out = refs[:-1], refs[-1]
    for offset, strip in enumerate(strips):
        out[member_ref[0] ^ offset, 0] = strip[0].astype(out.dtype)


def trade_strips(strips):
    return tuple(trade(strip, offset) for offset, strip in enumerate(strips))


def collect_strips(member_box, strips, kind):
    count = len(strips)
    frames, rows, columns = strips[0].shape
    whole_strips = pl.pallas_call(
        collect_kernel,
        grid=(frames,),
        in_specs=[in_smem()] + [pl.BlockSpec((1, rows, columns), lambda f: (f, 0, 0))] * count,
        out_specs=pl.BlockSpec((count, 1, rows, columns), lambda f: (0, f, 0, 0)),
        out_shape=shape((count, frames, rows, columns), kind),
        compiler_params=params(),
        name="collect",
    )(member_box, *strips)
    return whole_strips.reshape(count * frames, rows, columns)


def twice(values):
    return jnp.concatenate([values, values], axis=-1)


def pad_small(rows):
    stacked = jnp.stack(rows, axis=-2)
    gaps = [(0, 0)] * (stacked.ndim - 2) + [(0, 8 - len(rows)), (0, 0)]
    return jnp.pad(stacked, gaps)


def trade(value, offset):
    if offset == 0:
        return value
    count = lax.axis_size("rows")
    return lax.ppermute(value, "rows", [(i, i ^ offset) for i in range(count)])


def half_trade(value, at):
    count, members = lax.axis_size("seq"), lax.axis_size("rows")
    pairs = []
    for place in range(count):
        for member in range(members):
            offset = sides(count)[member % 2][at]
            if offset:
                pairs.append((place * members + member, (place ^ offset) * members + member))
    return lax.ppermute(value, ("seq", "rows"), pairs)


def layers(member_box, frame_images, frame_stats, cot_fetched, styles, bias_rows, works):
    count = lax.axis_size("rows")
    *out, win_one, win_two, win_level, win_coarse, middle, down, stats, b_one, b_two, b_down, b_up = forward(
        member_box, frame_images, frame_stats, styles, bias_rows, works, count
    )
    out = trade_strips(out)
    down, cot_fetched = lax.optimization_barrier((down, cot_fetched))
    cot = gather_frames(member_box, *cot_fetched)
    *grad_strips, tile_out, tile_level, tile_mid, coarse_pairs, pieces, bias_sums = backward(
        member_box, cot, frame_images, styles, stats, middle, down, b_up, b_down, b_two, b_one, count
    )
    grad_strips = trade_strips(grad_strips)
    wins = (win_one, win_two, win_level, win_coarse)
    tiles = (tile_out, tile_level, tile_mid, coarse_pairs)
    return out, grad_strips, wins, tiles, pieces, bias_sums


def local_direct(
    frames,
    cotangent,
    actions,
    noise_ids,
    valid,
    act_table,
    noise_table,
    ada_one,
    ada_two,
    conv_one,
    conv_two,
    down_kernel,
    up_kernel,
    bias_one,
    bias_two,
    bias_down,
    bias_up,
):
    member = lax.axis_index("rows").astype(jnp.int32)
    place = lax.axis_index("seq").astype(jnp.int32)
    count = lax.axis_size("seq")
    share = frames.shape[0] // lax.axis_size("rows")
    rows, cells, width = conv_one.shape[0], ada_one.shape[0], bias_one.shape[0]
    half = count // 2
    member_box = member.reshape(1)
    where = jnp.stack([place, member])
    ids = (actions, noise_ids, valid)
    kernels = (conv_one, conv_two, down_kernel, up_kernel)
    biases = (bias_one, bias_two, bias_down, bias_up)
    fetched = fetch_far(member_box, frames)
    packed = pack(ids, kernels, ada_one, ada_two, act_table, noise_table, biases)
    mine = jnp.concatenate([half_trade(packed, at) for at in range(half)], axis=0)
    other = trade(mine, 1)
    cot_fetched = fetch_far(member_box, cotangent)
    frame_images, frame_stats = gather_frames(member_box, *fetched, FAR_HINT)
    styles, bias_rows, group_ids, works = prepare(where, ids, packed, mine, other, count, rows, cells, share)
    out, grad_strips, wins, tiles, pieces, bias_sums = layers(
        member_box, frame_images, frame_stats, cot_fetched, styles, bias_rows, works
    )
    kept, small, theirs, hots = weight_messages(where, wins, tiles, pieces, bias_sums, group_ids, count, rows)
    theirs, out = lax.optimization_barrier((theirs, out))
    own, *messages = join_messages(where, kept, small, trade(theirs, 1), half, rows, share)
    received = [half_trade(message, at) for at, message in enumerate(messages)]
    result = collect_strips(member_box, out, bf16)
    frames_grad = collect_strips(member_box, grad_strips, f32)
    received, result, frames_grad = lax.optimization_barrier((received, result, frames_grad))
    sums = reduce_messages(
        where, own, received, hots, act_table, noise_table, ada_one, ada_two, rows, cells, 2 * share
    )
    parts = [trade(sums, offset) for offset in range(lax.axis_size("rows"))]
    return (result, frames_grad, *finish(parts, rows, cells, width))


def local_general(
    frames,
    cotangent,
    actions,
    noise_ids,
    valid,
    act_table,
    noise_table,
    ada_one,
    ada_two,
    conv_one,
    conv_two,
    down_kernel,
    up_kernel,
    bias_one,
    bias_two,
    bias_down,
    bias_up,
):
    member = lax.axis_index("rows").astype(jnp.int32)
    share = frames.shape[0] // lax.axis_size("rows")
    member_box = member.reshape(1)

    def gathered(value, axis):
        return lax.all_gather(value, "seq", axis=axis, tiled=True)

    cot_fetched = fetch_far(member_box, cotangent)
    frame_images, frame_stats = gather_frames(member_box, *fetch_far(member_box, frames))
    act_full = gathered(act_table, 1)
    noise_full = gathered(noise_table, 1)
    ada_full = gathered(jnp.concatenate([ada_one, ada_two], axis=1), 0).astype(f32)
    biases = gathered(jnp.stack([bias_one, bias_two, bias_down, bias_up]), 1).astype(f32)
    wide = lambda kernel: gathered(kernel, 0).astype(f32)
    works = (
        jnp.concatenate([wide(conv_one), wide(conv_two)], axis=1),
        twice(wide(up_kernel)),
        twice(wide(down_kernel)),
    )

    own = lambda ids: lax.dynamic_slice_in_dim(ids, member * share, share)
    own_actions, own_noise, own_valid = own(actions), own(noise_ids), own(valid)
    action_hot = (own_actions[:, None] == jnp.arange(NACT, dtype=jnp.int32)[None, :]).astype(f32) * own_valid[
        :, None
    ].astype(f32)
    noise_hot = (own_noise[:, None] == jnp.arange(NLEV, dtype=jnp.int32)[None, :]).astype(f32)
    embed = jnp.dot(action_hot, act_full.astype(f32), precision=precise) + jnp.dot(
        noise_hot, noise_full.astype(f32), precision=precise
    )
    style = jnp.dot(embed, ada_full, precision=precise)
    styles = pad_small(
        [
            twice(1.0 + style[:, :C]),
            twice(style[:, C : 2 * C]),
            twice(1.0 + style[:, 2 * C : 3 * C]),
            twice(style[:, 3 * C :]),
        ]
    )
    bias_rows = pad_small([twice(biases[k]) for k in range(4)])
    out, grad_strips, wins, tiles, pieces, bias_sums = layers(
        member_box, frame_images, frame_stats, cot_fetched, styles, bias_rows, works
    )
    g_one, g_two, g_down, g_up = weight_grads(wins, tiles)
    result = collect_strips(member_box, out, bf16)
    frames_grad = collect_strips(member_box, grad_strips, f32)

    pieces_one = jnp.concatenate([pieces[:, 0, :C], pieces[:, 1, :C]], axis=1)
    pieces_two = jnp.concatenate([pieces[:, 2, :C], pieces[:, 3, :C]], axis=1)
    ada_one_grad = jnp.dot(embed.T, pieces_one, precision=precise)
    ada_two_grad = jnp.dot(embed.T, pieces_two, precision=precise)
    embed_grad = jnp.dot(jnp.concatenate([pieces_one, pieces_two], axis=1), ada_full.T, precision=precise)
    act_table_grad = jnp.dot(action_hot.T, embed_grad, precision=precise)
    noise_table_grad = jnp.dot(noise_hot.T, embed_grad, precision=precise)
    bias_total = jnp.sum(bias_sums, axis=0)[:4, :C]

    def shard(value, axis):
        return lax.psum_scatter(value, "seq", scatter_dimension=axis, tiled=True)

    shards = (
        shard(act_table_grad, 1),
        shard(noise_table_grad, 1),
        shard(ada_one_grad, 0),
        shard(ada_two_grad, 0),
        shard(g_one, 0),
        shard(g_two, 0),
        shard(g_down, 0),
        shard(g_up, 0),
        shard(bias_total[0], 0),
        shard(bias_total[1], 0),
        shard(bias_total[2], 0),
        shard(bias_total[3], 0),
    )
    return (result, frames_grad) + lax.psum(shards, "rows")


def fits_direct(mesh):
    count = mesh.shape["seq"]
    rows, cells = 9 * C // count, 256 // count
    return count in (2, 4, 8) and rows % 8 == 0 and rows >= ID_ROW + 8 and cells % 8 == 0 and mesh.shape["rows"] == 4


def solution(mesh):
    in_specs = (
        P("seq", "rows", None),
        P("seq", "rows", None),
        P("seq"),
        P("seq"),
        P("seq"),
        P(None, "seq"),
        P(None, "seq"),
        P("seq", None),
        P("seq", None),
        P("seq", None),
        P("seq", None),
        P("seq", None),
        P("seq", None),
        P("seq"),
        P("seq"),
        P("seq"),
        P("seq"),
    )
    out_specs = (
        P("seq", "rows", None),
        P("seq", "rows", None),
        P(None, "seq"),
        P(None, "seq"),
        P("seq", None),
        P("seq", None),
        P("seq", None),
        P("seq", None),
        P("seq", None),
        P("seq", None),
        P("seq"),
        P("seq"),
        P("seq"),
        P("seq"),
    )
    local = local_direct if fits_direct(mesh) else local_general
    return jax.shard_map(local, mesh=mesh, in_specs=in_specs, out_specs=out_specs, check_vma=False)
```

```python
import jax
import jax.numpy as jnp
from jax import lax
from jax.experimental import pallas as pl
from jax.experimental.pallas import tpu as pltpu
from jax.sharding import PartitionSpec as P

C = 64
NACT = 18
GROUPS = 32
NLEV = 32
H = 64
W = 64
PAIRS = W // 2
HALF = H // 2
LANES = 2 * C
BLOCK = PAIRS * HALF
MEMBERS = float(H * W * (C // GROUPS))
EPS = 1e-05

precise = lax.Precision.HIGHEST
f32 = jnp.float32
bf16 = jnp.bfloat16
VMEM_LIMIT = 16 * 2**20
VMEM_MOST = 60 * 2**20


def lane_ids(shape):
    return lax.broadcasted_iota(jnp.int32, shape, len(shape) - 1)


def swap_halves(x):
    return pltpu.roll(x, C, axis=x.ndim - 1)


def row_before(x):
    rows = lax.broadcasted_iota(jnp.int32, x.shape, 0)
    return jnp.where(rows == 0, 0.0, pltpu.roll(x, 1, axis=0))


def row_after(x):
    rows = lax.broadcasted_iota(jnp.int32, x.shape, 0)
    return jnp.where(rows == x.shape[0] - 1, 0.0, pltpu.roll(x, x.shape[0] - 1, axis=0))


def both_parities(x):
    x = jnp.broadcast_to(x, (8, LANES))
    return x + swap_halves(x)


def group_sum(x):
    even = lane_ids(x.shape) % 2 == 0
    return x + jnp.where(even, pltpu.roll(x, LANES - 1, axis=1), pltpu.roll(x, 1, axis=1))


def total(x):
    return jnp.sum(x, axis=0, keepdims=True)


def over_pairs(body, carry):
    for j in range(PAIRS):
        carry = body(j, carry)
    return carry


def build_windows(windows, tile):
    low_lanes = lane_ids((HALF, LANES)) < C
    zero = jnp.zeros((HALF, LANES), f32)

    def write(j, even, odd):
        windows[0, j] = row_before(odd).astype(bf16)
        windows[1, j] = even.astype(bf16)
        windows[2, j] = odd.astype(bf16)
        windows[3, j] = row_after(even).astype(bf16)

    def body(j, carry):
        even_past, odd_past = carry
        even = swap_halves(tile(0, j))
        odd = swap_halves(tile(1, j))
        write(j, jnp.where(low_lanes, even_past, even), jnp.where(low_lanes, odd_past, odd))
        return even, odd

    even, odd = over_pairs(body, (zero, zero))
    write(PAIRS, jnp.where(low_lanes, even, 0.0), jnp.where(low_lanes, odd, 0.0))


def window_operand(windows, slots):
    parts = []
    for slot in slots:
        for shift in (0, 1):
            parts.append(windows[slot, shift : shift + PAIRS].reshape(BLOCK, LANES))
    return jnp.concatenate(parts, axis=1)


def matmul(left, right):
    return jnp.dot(left, right, preferred_element_type=f32)


def tiles_of(y):
    return y.reshape(PAIRS, HALF, LANES)


def norm_stats(sums, squares):
    average = group_sum(both_parities(sums)) / MEMBERS
    variance = group_sum(both_parities(squares)) / MEMBERS - average * average
    return average, lax.rsqrt(jnp.maximum(variance, 0.0) + EPS)


def strip_start(member, offset, strip):
    return pl.multiple_of((member ^ offset) * strip, strip)


def load_strips(member, strips, image):
    for offset, strip in enumerate(strips):
        rows = strip.shape[0]
        start = strip_start(member, offset, rows)
        for j in range(PAIRS):
            image[j, pl.ds(start, rows), :] = strip[:, j * LANES : (j + 1) * LANES].astype(f32)


def store_strips(member, image, f, strips):
    for offset, strip in enumerate(strips):
        rows = strip.shape[1]
        start = strip_start(member, offset, rows)
        for j in range(PAIRS):
            strip[f, :, j * LANES : (j + 1) * LANES] = image[j, pl.ds(start, rows), :].astype(strip.dtype)


def parity_rows(image, parity, j):
    return image[j, pl.ds(parity, HALF, stride=2), :]


def staggered(steps):
    steps = list(steps)
    started = []
    while steps or started:
        if steps:
            started.append(steps.pop(0))
        for step in list(started):
            if next(step, "end") == "end":
                started.remove(step)


def gather_frame(member, strips, image, stats):
    load_strips(member, strips, image)

    def add_stats(j, carry):
        x = image[j]
        s, q = carry
        return s + x, q + x * x

    zero = jnp.zeros((H, LANES), f32)
    s, q = over_pairs(add_stats, (zero, zero))
    average, inverse = norm_stats(total(s), total(q))
    stats[0:1, :] = average[0:1]
    stats[1:2, :] = inverse[0:1]
    stats[2:3, :] = both_parities(total(s))[0:1]
    stats[3:8, :] = jnp.zeros((5, LANES), f32)


def gather_kernel(member_ref, own, far, near, images, all_stats):
    member = member_ref[0]
    frames = images.shape[0]
    first = member % 2 * frames
    for f in range(frames):
        strips = (own.at[f], near.at[f], far.at[first + f], near.at[frames + f])
        gather_frame(member, strips, images.at[f], all_stats.at[f])


def forward_kernel(count, *refs):
    member_ref, frame_images, frame_stats, styles, biases, work_pair, work_up, work_down = refs[:8]
    out = refs[8 : 8 + count]
    outs = refs[8 + count : 15 + count]
    turned_operands = refs[15 + count : 19 + count]
    images, levels, w_one, w_two, w_down, w_up = refs[19 + count :]
    member = member_ref[0]
    works = {"one": work_pair, "two": work_pair, "down": work_down, "up": work_up}
    found = {}

    def block(name, row):
        k = works[name][row : row + C, :]
        low = lane_ids(k.shape) < C
        if name == "two":
            return jnp.where(low, swap_halves(k), k)
        return jnp.where(low, k, swap_halves(k))

    def turned_pairs(name):
        work = works[name]
        key = "one" if name == "two" else name
        if key not in found:
            blocks = [work[at : min(at + LANES, work.shape[0]), :] for at in range(0, work.shape[0], LANES)]
            found[key] = [below(block, LANES).T for block in blocks]
        return [k[C:] if name == "two" else k[:C] for k in found[key]]

    def operands():
        yield from write_forward_operands(block, w_one, w_two, w_down, w_up)
        yield from write_backward_operands(turned_pairs, *turned_operands)

    low_lanes = lane_ids((HALF, LANES)) < C

    def frame(f):
        win_one, win_two, win_level, win_coarse, middle, down, stats = (ref.at[f] for ref in outs)
        frame_image, image, level, style = frame_images.at[f], images.at[f], levels.at[f], styles.at[f]
        average_one, inverse_one = frame_stats[f, 0:1, :], frame_stats[f, 1:2, :]
        gain_one = inverse_one * style[0:1, :]
        half_gain = 0.5 * gain_one
        half_shift = 0.5 * (style[1:2, :] - average_one * gain_one)

        def act_one(parity, j):
            h = parity_rows(frame_image, parity, j) * half_gain + half_shift
            return h * jnp.tanh(h) + h

        build_windows(win_one, act_one)
        yield
        y = matmul(window_operand(win_one, range(4)), w_one[...])
        sums = jnp.zeros((1, LANES), f32)
        squares = jnp.zeros((1, LANES), f32)
        for a in range(2):
            v = y[:, a * LANES : (a + 1) * LANES] + biases[0:1, :]
            sums = sums + total(v)
            squares = squares + total(v * v)
            middle[a] = tiles_of(v)
        yield
        average_two, inverse_two = norm_stats(sums, squares)
        stats[0:1, :] = average_one
        stats[1:2, :] = inverse_one
        stats[2:3, :] = average_two[0:1]
        stats[3:4, :] = inverse_two[0:1]
        stats[4:8, :] = jnp.zeros((4, LANES), f32)
        gain_two = inverse_two * style[2:3, :]
        half_gain_two = 0.5 * gain_two[0:1]
        half_shift_two = 0.5 * (style[3:4, :] - average_two[0:1] * gain_two[0:1])

        def act_two(parity, j):
            h = middle[parity, j] * half_gain_two + half_shift_two
            return h * jnp.tanh(h) + h

        build_windows(win_two, act_two)
        yield
        y = matmul(window_operand(win_two, range(4)), w_two[...])
        for a in range(2):
            v = y[:, a * LANES : (a + 1) * LANES] + biases[1:2, :]
            level[a] = tiles_of(v) + frame_image[:, pl.ds(a, HALF, stride=2), :]
        yield
        build_windows(win_level, lambda parity, j: level[parity, j])
        yield
        operand = window_operand(win_level, range(4))
        y = matmul(operand[:, : 6 * LANES], w_down[...]) + biases[2:3, :]
        down[...] = tiles_of(y)
        yield

        def write_coarse(j, cells):
            win_coarse[0, j] = row_before(cells).astype(bf16)
            win_coarse[1, j] = cells.astype(bf16)
            win_coarse[2, j] = row_after(cells).astype(bf16)

        def coarse_body(j, past):
            h = down[j] * 0.5
            coarse = h * jnp.tanh(h) + h
            write_coarse(j, jnp.where(low_lanes, past, coarse))
            return coarse

        past = over_pairs(coarse_body, jnp.zeros((HALF, LANES), f32))
        write_coarse(PAIRS, jnp.where(low_lanes, past, 0.0))
        yield
        operand = window_operand(win_level, range(4))
        coarse_operand = window_operand(win_coarse, (0, 1, 1, 2))
        y = matmul(operand, w_up[: 16 * C, :]) + matmul(coarse_operand, w_up[16 * C :, :])
        for a in range(2):
            v = y[:, a * LANES : (a + 1) * LANES] + biases[3:4, :]
            image[:, pl.ds(a, HALF, stride=2), :] = tiles_of(v) + level[a]
        yield
        store_strips(member, image, f, out)

    staggered([operands()] + [frame(f) for f in range(styles.shape[0])])


def slope_twice(h):
    t = jnp.tanh(h)
    return (1.0 + t) + h * (1.0 - t * t)


def backward_kernel(count, *refs):
    member_ref = refs[0]
    cot_images, cot_stats, frame_images, styles, all_stats, all_middle, all_down = refs[1:8]
    w_up, w_down, w_two, w_one = refs[8:12]
    out = refs[12 : 12 + count]
    outs = refs[12 + count : 18 + count]
    scratch = refs[18 + count :]
    member = member_ref[0]
    low_lanes = lane_ids((HALF, LANES)) < C

    def frame(f):
        tile_out, tile_level, tile_mid, coarse_pairs, pieces, bias_sums = (ref.at[f] for ref in outs)
        image, level_grad, pre_grad, windows, coarse_below = (ref.at[f] for ref in scratch)
        style, stats, middle, down, frame_image = (
            ref.at[f] for ref in (styles, all_stats, all_middle, all_down, frame_images)
        )
        cot_image = cot_images.at[f]

        def out_tile(parity, j):
            x = parity_rows(cot_image, parity, j)
            tile_out[parity, j] = x.astype(bf16)
            return x

        build_windows(windows, out_tile)
        yield
        y = matmul(window_operand(windows, range(4)), w_up[...])
        for a in range(2):
            level_grad[a] = (
                tiles_of(y[:, (2 + a) * LANES : (3 + a) * LANES]) + cot_image[:, pl.ds(a, HALF, stride=2), :]
            )
        coarse = y[:, :LANES] + y[:, LANES : 2 * LANES]
        pre_grad[0] = tiles_of(coarse)
        yield

        def coarse_body(t, carry):
            after, sums = carry
            j = PAIRS - 1 - t
            g = pre_grad[0, j]
            g = g + swap_halves(g)
            h = down[j] * 0.5
            d = g * slope_twice(h)
            pair = jnp.where(low_lanes, d, after)
            coarse_pairs[j] = pair.astype(bf16)
            coarse_below[j] = row_after(pair).astype(bf16)
            return d, sums + d

        zero = jnp.zeros((HALF, LANES), f32)
        _, sums = over_pairs(coarse_body, (zero, zero))
        bias_down_sum = jnp.broadcast_to(total(sums), (8, LANES))
        operand = jnp.concatenate(
            [coarse_pairs[...].reshape(BLOCK, LANES), coarse_below[...].reshape(BLOCK, LANES)], axis=1
        )
        y = matmul(operand, w_down[...])
        sums = jnp.zeros((1, LANES), f32)
        for a in range(2):
            v = y[:, a * LANES : (a + 1) * LANES] + level_grad[a].reshape(BLOCK, LANES)
            sums = sums + total(v)
            level_grad[a] = tiles_of(v)
        bias_two_sum = both_parities(sums)

        def level_tile(parity, j):
            x = level_grad[parity, j]
            tile_level[parity, j] = x.astype(bf16)
            return x

        build_windows(windows, level_tile)
        yield

        def norm_slopes(y, value, k):
            average, inverse = stats[2 * k : 2 * k + 1, :], stats[2 * k + 1 : 2 * k + 2, :]
            gain = inverse * style[2 * k : 2 * k + 1, :]
            half_gain = 0.5 * gain
            half_shift = 0.5 * (style[2 * k + 1 : 2 * k + 2, :] - average * gain)
            scale_sum = jnp.zeros((1, LANES), f32)
            shift_sum = jnp.zeros((1, LANES), f32)
            for a in range(2):
                v = value(a)
                g = y[:, a * LANES : (a + 1) * LANES] * slope_twice(v * half_gain + half_shift)
                pre_grad[a] = tiles_of(g)
                shift_sum = shift_sum + total(g)
                scale_sum = scale_sum + total(g * ((v - average) * inverse))
            scale_sum, shift_sum = both_parities(scale_sum), both_parities(shift_sum)
            factor = style[2 * k : 2 * k + 1, :]
            center = group_sum(factor * shift_sum) / MEMBERS
            tilt = group_sum(factor * scale_sum) / MEMBERS
            slope = (inverse * tilt)[0:1] * inverse
            return scale_sum, shift_sum, gain, slope, slope * average - (inverse * center)[0:1]

        y = matmul(window_operand(windows, range(4)), w_two[...])
        scale_two, shift_two, gain_two, slope_two, constant_two = norm_slopes(
            y, lambda a: middle[a].reshape(BLOCK, LANES), 1
        )
        yield
        row_sums = [zero]

        def mid_tile(parity, j):
            x = pre_grad[parity, j] * gain_two + (constant_two - middle[parity, j] * slope_two)
            tile_mid[parity, j] = x.astype(bf16)
            row_sums[0] = row_sums[0] + x
            return x

        build_windows(windows, mid_tile)
        bias_one_sum = both_parities(total(row_sums[0]))
        yield
        y = matmul(window_operand(windows, range(4)), w_one[...])
        scale_one, shift_one, gain_one, slope_one, constant_one = norm_slopes(
            y, lambda a: frame_image[:, pl.ds(a, HALF, stride=2), :].reshape(BLOCK, LANES), 0
        )
        yield

        def frame_body(j, carry):
            for parity in range(2):
                x = parity_rows(frame_image, parity, j)
                g = pre_grad[parity, j] * gain_one + (constant_one - x * slope_one) + level_grad[parity, j]
                image[j, pl.ds(parity, HALF, stride=2), :] = g
            return carry

        over_pairs(frame_body, 0)
        store_strips(member, image, f, out)
        for k, value in enumerate((scale_one, shift_one, scale_two, shift_two)):
            pieces[k : k + 1, :] = value[0:1]
        pieces[4:8, :] = jnp.zeros((4, LANES), f32)
        for k, value in enumerate((bias_one_sum, bias_two_sum, bias_down_sum, cot_stats[f, 2:3, :])):
            bias_sums[k : k + 1, :] = value[0:1]
        bias_sums[4:8, :] = jnp.zeros((4, LANES), f32)

    staggered(frame(f) for f in range(styles.shape[0]))


def outer(left, right):
    return lax.dot_general(left, right, (((0,), (0,)), ((), ())), preferred_element_type=f32)


def accumulate(wins, tiles, sums, folds):
    win_one, win_two, win_level, win_coarse = wins
    tile_out, tile_level, tile_mid, coarse_pairs = tiles
    sum_one, sum_two, sum_down, sum_up = sums
    cells = win_one.shape[0] * BLOCK

    def operand(windows, slots):
        parts = []
        for slot in slots:
            for shift in (0, 1):
                parts.append(windows[:, slot, shift : shift + PAIRS].reshape(cells, LANES))
        return jnp.concatenate(parts, axis=1)

    def blocks(tiles):
        return jnp.concatenate([tiles[:, a].reshape(cells, LANES) for a in range(2)], axis=1)

    out_blocks = blocks(tile_out)
    sum_up[16 * C :, :] = outer(operand(win_coarse, range(3)), out_blocks)
    sum_up[: 16 * C, :] = outer(operand(win_level, range(4)), out_blocks)
    sum_down[...] = outer(operand(win_level, range(3)), coarse_pairs[...].reshape(cells, LANES))
    sum_two[...] = outer(operand(win_two, range(4)), blocks(tile_level))
    folds[0]()
    sum_one[...] = outer(operand(win_one, range(4)), blocks(tile_mid))
    folds[1]()
    folds[2]()


def taps():
    return [(p, q, (3 * p + q) * C) for p in range(3) for q in range(3)]


def fold(sums, p, q):
    return fold_slots(sums, 0, p, q, range(4))


def fold_coarse(sums, p, q):
    return fold_slots(sums, 16 * C, p, q, (0, 1, 1, 2))


def fold_slots(sums, base, p, q, slots):
    halves = []
    for b in range(2):
        rows = [base + (slots[a + p] * 4 + b + q) * C for a in range(2)]
        halves.append(sums[rows[0] : rows[0] + C, :LANES] + sums[rows[1] : rows[1] + C, LANES:])
    return halves[0] + swap_halves(halves[1])


def weight_kernel(*refs):
    wins, tiles, grads, sums = refs[:4], refs[4:8], refs[8:12], refs[12:]
    g_one, g_two, g_down, g_up = grads
    sum_one, sum_two, sum_down, sum_up = sums

    def fold_up():
        for p, q, at in taps():
            g_up[2 * at : 2 * at + C, :] = fold_coarse(sum_up, p, q)[:, :C]
            g_up[2 * at + C : 2 * at + 2 * C, :] = fold(sum_up, p, q)[:, :C]
            place = (p * 4 + q) * C
            g_down[at : at + C, :] = sum_down[place : place + C, :C]

    def fold_two():
        for p, q, at in taps():
            g_two[at : at + C, :] = fold(sum_two, p, q)[:, :C]

    def fold_one():
        for p, q, at in taps():
            g_one[at : at + C, :] = fold(sum_one, p, q)[:, :C]

    accumulate(wins, tiles, sums, (fold_up, fold_two, fold_one))


PARTS = 16
FAR_HINT = 90
PAIR_PARTS = 24


def three_parts(exact):
    high = exact.astype(bf16).astype(f32)
    rest = exact - high
    mid = rest.astype(bf16).astype(f32)
    return jnp.concatenate([high, mid, rest - mid], axis=0)


def below(block, rows):
    if block.shape[0] == rows:
        return block
    return jnp.concatenate([block, jnp.zeros((rows - block.shape[0], LANES), f32)], axis=0)


def message_kernel(count, rows, *refs):
    where_ref, wins, tiles = refs[0], refs[1:5], refs[5:9]
    pieces, bias_sums, ids, kept, small, theirs, hots = refs[9:16]
    sums = refs[16:20]
    g_pair, g_up, g_down = refs[20:]
    sum_one, sum_two, sum_down, sum_up = sums
    taken = 2 * pieces.shape[0]
    for at in range(ids.shape[0]):
        write_hots(hots, at * taken, where_ref[1] // 2 * taken, taken, ids[at])
    low_lanes = lane_ids((C, LANES)) < C

    def fold_up():
        for p, q, at in taps():
            g_up[2 * at : 2 * at + C, :] = fold_coarse(sum_up, p, q)
            g_up[2 * at + C : 2 * at + 2 * C, :] = fold(sum_up, p, q)
            place = (p * 4 + q) * C
            g_down[at : at + C, :] = sum_down[place : place + C, :]

    def fold_two():
        for p, q, at in taps():
            g_pair[at : at + C, :] = swap_halves(fold(sum_two, p, q))

    def fold_one():
        for p, q, at in taps():
            g_pair[at : at + C, :] = jnp.where(low_lanes, fold(sum_one, p, q), g_pair[at : at + C, :])

    accumulate(wins, tiles, sums, (fold_up, fold_two, fold_one))
    frames = pieces.shape[0]
    small[...] = jnp.zeros_like(small)
    total_bias = bias_sums[0, 0:4, :]
    for f in range(frames):
        small[4 * f : 4 * f + 4, :] = pieces[f, 0:4, :]
        if f > 0:
            total_bias = total_bias + bias_sums[f, 0:4, :]
    small[4 * frames : 4 * frames + 4, :] = total_bias
    sent = below(three_parts(small[...]), rows)
    low_lanes = lane_ids((rows, LANES)) < C
    half = count // 2
    for at in range(half):
        for ref, mine in ((kept, True), (theirs, False)):
            start = pl.multiple_of(seq_owner(where_ref[0], where_ref[1], half, at, mine) * rows, 8)
            blocks = (
                g_pair[pl.ds(start, rows), :],
                jnp.where(
                    low_lanes,
                    g_up[pl.ds(pl.multiple_of(2 * start, 8), rows), :],
                    swap_halves(g_up[pl.ds(pl.multiple_of(2 * start + rows, 8), rows), :]),
                ),
                jnp.where(low_lanes, g_down[pl.ds(start, rows), :], 0.0 if mine else sent),
            )
            ref[at * 3 * rows : (at + 1) * 3 * rows, :] = jnp.concatenate(blocks, axis=0).astype(ref.dtype)


def join_kernel(half, rows, frames, where_ref, kept, small, theirs, own, *messages):
    first = where_ref[1] % 2 == 0
    at = 2 * rows
    other = theirs[at : at + 3 * PARTS, :].astype(f32)
    other = other[:PARTS] + other[PARTS : 2 * PARTS] + other[2 * PARTS :]
    mine = small[...]
    n = 4 * frames
    exact = jnp.concatenate(
        [
            jnp.where(first, mine[:n], other[:n]),
            jnp.where(first, other[:n], mine[:n]),
            mine[n : n + 4] + other[n : n + 4],
            jnp.zeros((PAIR_PARTS - 2 * n - 4, LANES), f32),
        ],
        axis=0,
    )
    low_lanes = lane_ids((rows, LANES)) < C
    sent = below(three_parts(exact), rows)
    size = 3 * rows
    for k, message in enumerate(messages):
        block = kept[k * size : (k + 1) * size, :] + theirs[k * size : (k + 1) * size, :].astype(f32)
        message[:at, :] = block[:at].astype(bf16)
        message[at:, :] = jnp.where(low_lanes, block[at:], sent).astype(bf16)
        if k == half - 1:
            own[:at, :] = block[:at]
            own[at:, :] = jnp.where(low_lanes, block[at:], below(exact, rows))


def reduce_kernel(half, rows, cells, frames, *refs):
    where_ref, own = refs[:2]
    messages = refs[2 : 2 + half]
    hots, act_table, noise_table, ada_one, ada_two, out, pieces_one, pieces_two, table, high_one, high_two = refs[2 + half :]
    place, member = where_ref[0], where_ref[1]
    taken = 4 * frames
    bias = jnp.zeros((4, LANES), f32)
    sums = None
    lanes = lane_ids((1, LANES))
    low_lanes = lanes < C
    at = 2 * rows
    for k, ref in enumerate(messages):
        message = ref[...].astype(f32)
        if k == half - 1:
            message = jnp.where(member % 2 == 0, own[...], message)
        sums = message if sums is None else sums + message
        small = (
            message[at : at + PAIR_PARTS]
            + message[at + PAIR_PARTS : at + 2 * PAIR_PARTS]
            + message[at + 2 * PAIR_PARTS : at + 3 * PAIR_PARTS]
        )
        turned = swap_halves(small)
        bias = bias + small[taken : taken + 4]
        for f in range(frames):
            row = k * frames + f
            for kind, piece in ((0, pieces_one), (2, pieces_two)):
                low, high = 4 * f + kind, 4 * f + kind + 1
                piece[row : row + 1, :] = jnp.where(low_lanes, turned[low : low + 1], small[high : high + 1])
    hot = hots[:, :TABLE_ROWS]
    table[...] = jnp.zeros_like(table)
    table[ACT_ROW : ACT_ROW + NACT, :] = act_table[...].astype(f32)
    table[NOISE_ROW : NOISE_ROW + NLEV, :] = noise_table[...].astype(f32)
    embed = matmul(hot.astype(bf16), table[...].astype(bf16))

    def exact(left, right, dims):
        return lax.dot_general(left, right, (dims, ((), ())), precision=precise, preferred_element_type=f32)

    one, two = pieces_one[...], pieces_two[...]
    for ref, ada in ((high_one, ada_one), (high_two, ada_two)):
        ref[...] = jnp.zeros_like(ref)
        ref[C : C + cells, :] = ada[...].astype(f32)
    pieces = jnp.concatenate([one, two], axis=1)
    embed_grad = exact(pieces, jnp.concatenate([high_one[...], high_two[...]], axis=1), ((1,), (1,)))
    ada_grads = exact(embed, pieces, ((0,), (0,)))
    width = C // (2 * half)
    bias = pltpu.roll(jnp.concatenate([bias, bias], axis=0), (LANES - place * width) % LANES, axis=1)
    extra = below(jnp.concatenate([exact(hot, embed_grad, ((0,), (0,))), bias], axis=0), rows)
    at = 2 * rows
    blocks = (
        sums[:at],
        jnp.where(lane_ids((rows, LANES)) < C, sums[at:], extra),
        ada_grads[:, :LANES],
        ada_grads[:, LANES:],
    )
    out[...] = jnp.concatenate(blocks, axis=0).astype(out.dtype)


def finish_kernel(rows, cells, count, *refs):
    parts, outs = [ref[...].astype(f32) for ref in refs[:count]], refs[count:]
    act_grad, noise_grad, ada_one, ada_two, g_one, g_two, g_down, g_up = outs[:8]
    bias_grads = outs[8:12]
    while len(parts) > 1:
        parts = [parts[k] + parts[k + 1] for k in range(0, len(parts), 2)]
    sums = parts[0]

    def turn(block):
        return jnp.concatenate([block, jnp.zeros((LANES - rows, LANES), f32)], axis=0).T[:, :rows]

    pair, halves, down = (turn(sums[k * rows : (k + 1) * rows]) for k in range(3))
    g_one[...] = pair[:C]
    g_two[...] = pair[C:]
    g_up[:, :rows] = halves[:C]
    g_up[:, rows:] = halves[C:]
    g_down[...] = down[:C]
    at = 3 * rows
    ada_one[...] = sums[at : at + cells]
    ada_two[...] = sums[at + cells : at + 2 * cells]
    extra = swap_halves(sums[2 * rows : 3 * rows])
    act_grad[...] = extra[ACT_ROW : ACT_ROW + NACT, :cells]
    noise_grad[...] = extra[NOISE_ROW : NOISE_ROW + NLEV, :cells]
    for k, ref in enumerate(bias_grads):
        ref[...] = extra[BIAS_ROW + k : BIAS_ROW + k + 1, : ref.shape[0]].reshape(ref.shape)


def write_forward_operands(block, f_one, f_two, f_down, f_up):
    low_lanes = lane_ids((C, LANES)) < C
    zero = jnp.zeros((C, LANES), f32)

    def taps(name, base, step):
        return {(p, q): block(name, (3 * p + q) * step + base) for p in range(3) for q in range(3)}

    def write(ref, base, found):
        for w in range(4):
            for p in range(3):
                tile = jnp.where(low_lanes, found.get((p, w), zero), found.get((p, w - 1), zero)).astype(bf16)
                for a in range(2):
                    at = base + ((a + p) * 4 + w) * C
                    ref[at : at + C, a * LANES : (a + 1) * LANES] = tile
            for a in range(2):
                for r in range(4):
                    if not 0 <= r - a < 3:
                        at = base + (r * 4 + w) * C
                        ref[at : at + C, a * LANES : (a + 1) * LANES] = zero.astype(bf16)

    write(f_one, 0, taps("one", 0, C))
    yield
    write(f_two, 0, taps("two", 0, C))
    yield
    found = taps("down", 0, C)
    for p in range(3):
        for w in range(4):
            at = (p * 4 + w) * C
            f_down[at : at + C, :] = found.get((p, w), zero).astype(bf16)
    yield
    write(f_up, 0, taps("up", C, 2 * C))
    yield
    write(f_up, 16 * C, taps("up", 0, 2 * C))
    yield


def write_backward_operands(turned_pairs, b_one, b_two, b_down, b_up):
    low_lanes = lane_ids((C, LANES)) < C
    zero = jnp.zeros((C, LANES), f32)
    def taps(pairs, base, step, scale=1.0):
        found = {}
        for p in range(3):
            for q in range(3):
                at = (3 * p + q) * step + base
                pair = pairs[at // LANES]
                other = swap_halves(pair)
                low, high = (pair, other) if at % LANES == 0 else (other, pair)
                found[p, q] = jnp.where(low_lanes, low, high) * scale
        return found

    def write(ref, lane, found):
        for w in range(4):
            for p in range(3):
                tile = jnp.where(low_lanes, found.get((p, 2 - w), zero), found.get((p, 3 - w), zero)).astype(bf16)
                for a in range(2):
                    at = ((a + 2 - p) * 4 + w) * C
                    ref[at : at + C, lane + a * LANES : lane + (a + 1) * LANES] = tile
            for a in range(2):
                for r in range(4):
                    if not 0 <= a + 2 - r < 3:
                        at = (r * 4 + w) * C
                        ref[at : at + C, lane + a * LANES : lane + (a + 1) * LANES] = zero.astype(bf16)

    one, two = turned_pairs("one"), turned_pairs("two")
    write(b_one, 0, taps(one, 0, C, 0.5))
    yield
    write(b_two, 0, taps(two, 0, C, 0.5))
    yield
    pairs = turned_pairs("up")
    write(b_up, 0, taps(pairs, 0, 2 * C, 0.5))
    yield
    write(b_up, 2 * LANES, taps(pairs, C, 2 * C))
    yield
    found = taps(turned_pairs("down"), 0, C)
    for under in range(2):
        for right in range(2):
            at = (under * 2 + right) * C
            for a in range(2):
                p = {(0, 0): 1, (0, 1): 2, (1, 1): 0}.get((under, a))
                first, second = zero, zero
                if p is not None:
                    first = found[p, 1] if right == 0 else zero
                    second = found[p, 2] if right == 0 else found[p, 0]
                b_down[at : at + C, a * LANES : (a + 1) * LANES] = jnp.where(low_lanes, first, second).astype(bf16)


ACT_ROW, NOISE_ROW, TABLE_ROWS = 0, 24, 56
BIAS_ROW, ID_ROW = 56, 64


def pack_sizes(rows, cells):
    return 3 * rows, 3 * rows + 2 * cells, -(-(3 * rows + 2 * cells) // 16) * 16


def turned(values):
    wide = jnp.concatenate([values, jnp.zeros((C, LANES - values.shape[1]), f32)], axis=1)
    return jnp.concatenate([wide, jnp.zeros((C, LANES), f32)], axis=0).T[: values.shape[1]]


def copy_all(pairs, sent):
    copies = [pltpu.make_async_copy(source, target, sent.at[k]) for k, (source, target) in enumerate(pairs)]
    for copy in copies:
        copy.start()
    for copy in copies:
        copy.wait()


def far_part(member, array, out):
    half = out.shape[0]
    return array.at[pl.ds((1 - member // 2) * half, half)], out


def strip_parts(member, array, own, other):
    share = own.shape[0]
    return [
        (array.at[pl.ds(member * share, share)], own),
        (array.at[pl.ds((member ^ 1) * share, share)], other),
    ]


def far_kernel(member_ref, array, out, sent):
    copy_all([far_part(member_ref[0], array, out)], sent)


def cut_kernel(member_ref, frames, cotangent, own, other, far, cot_own, cot_other, sent):
    member = member_ref[0]
    pairs = strip_parts(member, frames, own, other) + strip_parts(member, cotangent, cot_own, cot_other)
    copy_all([far_part(member, cotangent, far)] + pairs, sent)


def share_kernel(member_ref, far, out):
    share = out.shape[0]
    out[...] = far[pl.ds((member_ref[0] ^ 1) % 2 * share, share)]


def mark_kernel(far, out):
    out[...] = far[0, :8, :LANES].astype(f32)


def near_kernel(other, shared, mark, out):
    share = out.shape[0] // 2
    out[:share] = other[...]
    out[share:] = shared[...]


def pack_kernel(*refs):
    actions, noise_ids, valid, conv_one, conv_two, down_kernel, up_kernel, ada_one, ada_two = refs[:9]
    act_table, noise_table = refs[9:11]
    biases = refs[11:15]
    out, work = refs[15:]
    rows, cells = conv_one.shape[1], ada_one.shape[0]
    style_at, end, _ = pack_sizes(rows, cells)
    wide = lambda ref: ref[...].astype(f32)
    low_lanes = lane_ids((rows, LANES)) < C
    up = wide(up_kernel)
    work[...] = jnp.zeros_like(work)
    for at, low, high in (
        (0, turned(wide(conv_one)), turned(wide(conv_two))),
        (rows, turned(up[:, :rows]), turned(up[:, rows:])),
    ):
        work[at : at + rows, :] = jnp.where(low_lanes, low, swap_halves(high))
    work[2 * rows : 3 * rows, :] = turned(wide(down_kernel))
    extra = 2 * rows
    for at, ref in ((ACT_ROW, act_table), (NOISE_ROW, noise_table)):
        size = ref.shape
        work[extra + at : extra + at + size[0], C : C + size[1]] = wide(ref)
    for k, ref in enumerate(biases):
        at = extra + BIAS_ROW + k
        work[at : at + 1, C : C + ref.shape[0]] = wide(ref).reshape(1, ref.shape[0])
    lanes = lane_ids((1, LANES))
    for k, ref in enumerate((actions, noise_ids, valid)):
        line = jnp.zeros((1, LANES), jnp.int32)
        for f in range(ref.shape[0]):
            line = jnp.where(lanes == C + f, ref[f], line)
        at = extra + ID_ROW + k
        work[at : at + 1, C:] = line.astype(f32)[:, C:]
    work[style_at : style_at + cells, :] = wide(ada_one)
    work[style_at + cells : end, :] = wide(ada_two)
    out[...] = work[...].astype(bf16)


def seq_owner(place, member, half, at, mine=True):
    side = member % 2 if mine else 1 - member % 2
    even, odd = sides(2 * half)
    return place ^ (even[at] + side * (odd[at] - even[at]))


def sides(count):
    ones = lambda offset: bin(offset).count("1") % 2
    return tuple([offset for offset in reversed(range(count)) if ones(offset) == side] for side in (0, 1))


def write_hots(hots, at, first, frames, ids):
    lanes = lane_ids((1, LANES)).astype(f32)
    for f in range(frames):
        mine = jnp.where(lane_ids(ids.shape) == C + first + f, ids, 0.0)
        mine = jnp.sum(mine, axis=1, keepdims=True)
        action, noise, valid = mine[0:1], mine[1:2], mine[2:3]
        hots[at + f : at + f + 1, :] = jnp.where(lanes == action + ACT_ROW, valid, 0.0) + jnp.where(
            lanes == noise + NOISE_ROW, 1.0, 0.0
        )


def prepare_kernel(count, rows, cells, *refs):
    where_ref, packed, mine, other = refs[:4]
    styles, biases, ids, work_pair, work_up, work_down, work_one, work_two, work_table, hots = refs[4:]
    place, member, frames = where_ref[0], where_ref[1], styles.shape[0]
    style_at, _, size = pack_sizes(rows, cells)
    bias_rows = jnp.zeros(SMALL, f32)
    half = count // 2
    for offset in range(count):
        ref = mine if offset < half else other
        at = offset % half
        pack = ref[at * size : (at + 1) * size, :].astype(f32)
        if at == half - 1:
            pack = jnp.where(member % 2 == offset // half, packed[...].astype(f32), pack)
        owner = seq_owner(place, member, half, at, offset < half)
        start = pl.multiple_of(owner * rows, 8)
        work_pair[pl.ds(start, rows), :] = pack[:rows]
        halves = pack[rows : 2 * rows]
        work_up[pl.ds(2 * start, rows), :] = halves
        work_up[pl.ds(pl.multiple_of(2 * start + rows, 8), rows), :] = swap_halves(halves)
        extra = pack[2 * rows : 3 * rows]
        work_down[pl.ds(start, rows), :] = extra
        work_one[offset * cells : (offset + 1) * cells, :] = pack[style_at : style_at + cells]
        work_two[offset * cells : (offset + 1) * cells, :] = pack[style_at + cells : style_at + 2 * cells]
        lane = (offset * cells) % LANES
        tables = pltpu.roll(extra[:TABLE_ROWS], (lane - C) % LANES, axis=1)
        kept = (lane_ids(tables.shape) >= lane) & (lane_ids(tables.shape) < lane + cells)
        column = offset * cells // LANES
        tables = jnp.where(kept, tables, 0.0)
        if lane == 0:
            work_table[column] = tables
        else:
            work_table[column] += tables
        slots = extra[BIAS_ROW : BIAS_ROW + 8]
        width = C // count
        slots = jnp.where((lane_ids(SMALL) >= C) & (lane_ids(SMALL) < C + width), slots, 0.0)
        bias_rows = bias_rows + pltpu.roll(slots, (owner * width + C) % LANES, axis=1)
        if offset < half:
            ids[at] = extra[ID_ROW : ID_ROW + 8]
    biases[...] = bias_rows + swap_halves(bias_rows)

    at = 2 * rows + ID_ROW
    hots[...] = jnp.zeros_like(hots)
    write_hots(hots, 0, member * frames, frames, packed[at : at + 8, :].astype(f32))
    hot = hots[:, :TABLE_ROWS].astype(bf16)
    embed = jnp.concatenate([matmul(hot, work_table[k].astype(bf16)) for k in range(work_table.shape[0])], axis=1)
    low_lanes = lane_ids(SMALL) < C
    for k, work in enumerate((work_one, work_two)):
        style = jnp.dot(embed, work[...], precision=precise, preferred_element_type=f32)
        other = swap_halves(style)
        scale = 1.0 + jnp.where(low_lanes, style, other)
        shift = jnp.where(low_lanes, other, style)
        for f in range(frames):
            styles[f, 2 * k : 2 * k + 1, :] = scale[f : f + 1]
            styles[f, 2 * k + 1 : 2 * k + 2, :] = shift[f : f + 1]
    for f in range(frames):
        styles[f, 4:8, :] = jnp.zeros((4, LANES), f32)


def shape(dims, kind):
    return jax.ShapeDtypeStruct(dims, kind)


def whole(dims):
    return pl.BlockSpec(dims, lambda f: (0,) * len(dims))


def per_frame(dims):
    return pl.BlockSpec((1,) + dims, lambda f: (f,) + (0,) * len(dims))


def strip_specs(count, strip):
    return [pl.BlockSpec((1, strip, W * C), lambda f: (f, 0, 0))] * count


SMALL = (8, LANES)
WINDOWS = (4, PAIRS + 1, HALF, LANES)
COARSE_WINDOWS = (3, PAIRS + 1, HALF, LANES)
TILES = (2, PAIRS, HALF, LANES)
COARSE = (PAIRS, HALF, LANES)
IMAGE = (PAIRS, H, LANES)
KEYS = 16 * C


def in_vmem():
    return pl.BlockSpec(memory_space=pltpu.VMEM)


def in_smem():
    return pl.BlockSpec(memory_space=pltpu.SMEM)


def params(limit=VMEM_LIMIT):
    return pltpu.CompilerParams(vmem_limit_bytes=limit)


def cost(macs, moved):
    return pl.CostEstimate(flops=2 * macs, bytes_accessed=moved, transcendentals=0)


def gather_frames(member, far, own, other, hint=0):
    near = trade(cut_near(member, other, far, hint), 1)
    frames = own.shape[0]
    return pl.pallas_call(
        gather_kernel,
        in_specs=[in_smem()] + [in_vmem()] * 3,
        out_specs=[in_vmem()] * 2,
        out_shape=[shape((frames,) + IMAGE, f32), shape((frames,) + SMALL, f32)],
        compiler_params=params(),
        name="frames",
    )(member, own, far, near)


def forward(member, frame_images, frame_stats, styles, biases, works, count):
    frames = frame_images.shape[0]
    strip = H // count
    return pl.pallas_call(
        lambda *refs: forward_kernel(count, *refs),
        in_specs=[in_smem()] + [in_vmem()] * 7,
        out_specs=[in_vmem()] * (count + 11),
        out_shape=[shape((frames, strip, W * C), bf16)] * count
        + [
            shape((frames,) + WINDOWS, bf16),
            shape((frames,) + WINDOWS, bf16),
            shape((frames,) + WINDOWS, bf16),
            shape((frames,) + COARSE_WINDOWS, bf16),
            shape((frames,) + TILES, f32),
            shape((frames,) + COARSE, f32),
            shape((frames,) + SMALL, f32),
        ]
        + [shape(dims, bf16) for dims in OPERANDS[4:]],
        scratch_shapes=[pltpu.VMEM((frames,) + IMAGE, f32), pltpu.VMEM((frames,) + TILES, f32)]
        + [pltpu.VMEM(dims, bf16) for dims in OPERANDS[:4]],
        compiler_params=params(),
        cost_estimate=cost(1 << 10, 1 << 10),
        name="forward",
    )(member, frame_images, frame_stats, styles, biases, *works)


def backward(member, cot, frame_images, styles, stats, middle, down, w_up, w_down, w_two, w_one, count):
    frames = frame_images.shape[0]
    strip = H // count
    return pl.pallas_call(
        lambda *refs: backward_kernel(count, *refs),
        in_specs=[in_smem()] + [in_vmem()] * 11,
        out_specs=[in_vmem()] * (count + 6),
        out_shape=[shape((frames, strip, W * C), bf16)] * count
        + [
            shape((frames,) + TILES, bf16),
            shape((frames,) + TILES, bf16),
            shape((frames,) + TILES, bf16),
            shape((frames,) + COARSE, bf16),
            shape((frames,) + SMALL, f32),
            shape((frames,) + SMALL, f32),
        ],
        scratch_shapes=[
            pltpu.VMEM((frames,) + IMAGE, f32),
            pltpu.VMEM((frames,) + TILES, f32),
            pltpu.VMEM((frames,) + TILES, f32),
            pltpu.VMEM((frames,) + WINDOWS, bf16),
            pltpu.VMEM((frames,) + COARSE, bf16),
        ],
        compiler_params=params(),
        cost_estimate=cost(frames * BLOCK * KEYS * 2 * LANES * 5, frames * (10 << 20)),
        name="backward",
    )(member, *cot, frame_images, styles, stats, middle, down, w_up, w_down, w_two, w_one)


def sum_scratch():
    return [
        pltpu.VMEM((KEYS, 2 * LANES), f32),
        pltpu.VMEM((KEYS, 2 * LANES), f32),
        pltpu.VMEM((6 * LANES, LANES), f32),
        pltpu.VMEM((KEYS + 6 * LANES, 2 * LANES), f32),
    ]


def weight_grads(wins, tiles):
    return pl.pallas_call(
        weight_kernel,
        in_specs=[in_vmem()] * 8,
        out_specs=[in_vmem()] * 4,
        out_shape=[shape((9 * C, C), f32)] * 3 + [shape((18 * C, C), f32)],
        scratch_shapes=sum_scratch(),
        compiler_params=params(),
        name="weights",
    )(*wins, *tiles)


def in_place(space=pl.ANY):
    return pl.BlockSpec(memory_space=space)


def cut_far(member, array):
    array = pltpu.with_memory_space_constraint(array, pltpu.HBM)
    return pl.pallas_call(
        far_kernel,
        in_specs=[in_smem(), in_place(pltpu.HBM)],
        out_specs=in_vmem(),
        out_shape=pltpu.VMEM((array.shape[0] // 2,) + array.shape[1:], array.dtype),
        scratch_shapes=[pltpu.SemaphoreType.DMA((1,))],
        compiler_params=params(),
        name="far",
    )(member, array)


def cut_others(member, frames, cotangent, count):
    half, share = ((frames.shape[0] // n,) + frames.shape[1:] for n in (2, count))
    frames, cotangent = (pltpu.with_memory_space_constraint(array, pltpu.HBM) for array in (frames, cotangent))
    return pl.pallas_call(
        cut_kernel,
        in_specs=[in_smem()] + [in_place(pltpu.HBM)] * 2,
        out_specs=[in_vmem()] * 5,
        out_shape=[pltpu.VMEM(dims, frames.dtype) for dims in (share, share, half, share, share)],
        scratch_shapes=[pltpu.SemaphoreType.DMA((5,))],
        compiler_params=params(),
        name="cut",
    )(member, frames, cotangent)


def cut_near(member, other, far, hint):
    shared = pl.pallas_call(
        share_kernel,
        in_specs=[in_smem(), in_vmem()],
        out_specs=in_vmem(),
        out_shape=shape(other.shape, other.dtype),
        compiler_params=params(),
        name="shared",
    )(member, far)
    mark = pl.pallas_call(
        mark_kernel,
        in_specs=[in_vmem()],
        out_specs=in_vmem(),
        out_shape=shape(SMALL, f32),
        compiler_params=params(),
        cost_estimate=cost(BLOCK * KEYS * 2 * LANES * hint, 1 << 20),
        name="mark",
    )(far)
    return pl.pallas_call(
        near_kernel,
        in_specs=[in_vmem()] * 3,
        out_specs=in_vmem(),
        out_shape=shape(far.shape, other.dtype),
        compiler_params=params(),
        name="near",
    )(other, shared, mark)


def pack(ids, kernels, ada_one, ada_two, act_table, noise_table, biases):
    _, _, size = pack_sizes(kernels[0].shape[0], ada_one.shape[0])
    args = (*[kernel.T for kernel in kernels], ada_one, ada_two, act_table, noise_table, *biases)
    return pl.pallas_call(
        pack_kernel,
        in_specs=[in_smem()] * 3 + [in_vmem()] * len(args),
        out_specs=in_vmem(),
        out_shape=shape((size, LANES), bf16),
        scratch_shapes=[pltpu.VMEM((size, LANES), f32)],
        compiler_params=params(VMEM_MOST),
        cost_estimate=cost(BLOCK * KEYS * 2 * LANES * 30, 1 << 20),
        name="pack",
    )(*ids, *args)


OPERANDS = (
    (KEYS, 2 * LANES),
    (KEYS, 2 * LANES),
    (6 * LANES, LANES),
    (2 * KEYS, 2 * LANES),
    (KEYS, 2 * LANES),
    (KEYS, 2 * LANES),
    (2 * LANES, 2 * LANES),
    (KEYS, 4 * LANES),
)


def prepare(where, packed, mine, other, count, rows, cells, frames):
    found = pl.pallas_call(
        lambda *refs: prepare_kernel(count, rows, cells, *refs),
        in_specs=[in_smem()] + [in_vmem()] * 3,
        out_specs=[in_vmem()] * 6,
        out_shape=[shape((frames,) + SMALL, f32), shape(SMALL, f32), shape((count // 2,) + SMALL, f32)]
        + [shape((n * C, LANES), f32) for n in (9, 18, 9)],
        scratch_shapes=[
            pltpu.VMEM((count * cells, LANES), f32),
            pltpu.VMEM((count * cells, LANES), f32),
            pltpu.VMEM((count * cells // LANES, TABLE_ROWS, LANES), f32),
            pltpu.VMEM(SMALL, f32),
        ],
        compiler_params=params(),
        name="prepare",
    )(where, packed, mine, other)
    return found[0], found[1], found[2], found[3:]


def weight_messages(where, wins, tiles, pieces, bias_sums, ids, count, rows):
    frames = pieces.shape[0]
    size = count // 2 * 3 * rows
    return pl.pallas_call(
        lambda *refs: message_kernel(count, rows, *refs),
        in_specs=[in_smem()] + [in_vmem()] * 11,
        out_specs=[in_vmem()] * 4,
        out_shape=[
            shape((size, LANES), f32),
            shape((PARTS, LANES), f32),
            shape((size, LANES), bf16),
            shape((count * frames, LANES), f32),
        ],
        scratch_shapes=sum_scratch()
        + [pltpu.VMEM((9 * C, LANES), f32), pltpu.VMEM((18 * C, LANES), f32), pltpu.VMEM((9 * C, LANES), f32)],
        compiler_params=params(),
        cost_estimate=cost(frames * BLOCK * KEYS * 2 * LANES * 5, frames * (6 << 20)),
        name="weights",
    )(where, *wins, *tiles, pieces, bias_sums, ids)


def join_messages(where, kept, small, theirs, half, rows, frames):
    return pl.pallas_call(
        lambda *refs: join_kernel(half, rows, frames, *refs),
        in_specs=[in_smem()] + [in_vmem()] * 3,
        out_specs=[in_vmem()] * (1 + half),
        out_shape=[shape((3 * rows, LANES), f32)] + [shape((3 * rows, LANES), bf16)] * half,
        compiler_params=params(),
        name="join",
    )(where, kept, small, theirs)


def reduce_messages(where, own, messages, hots, act_table, noise_table, ada_one, ada_two, rows, cells, frames):
    half = len(messages)
    return pl.pallas_call(
        lambda *refs: reduce_kernel(half, rows, cells, frames, *refs),
        in_specs=[in_smem()] + [in_vmem()] * (half + 6),
        out_specs=in_vmem(),
        out_shape=shape((3 * rows + 2 * cells, LANES), bf16),
        scratch_shapes=[
            pltpu.VMEM((half * frames, LANES), f32),
            pltpu.VMEM((half * frames, LANES), f32),
            pltpu.VMEM((TABLE_ROWS, cells), f32),
            pltpu.VMEM((LANES, LANES), f32),
            pltpu.VMEM((LANES, LANES), f32),
        ],
        compiler_params=params(),
        name="reduce",
    )(where, own, *messages, hots, act_table, noise_table, ada_one, ada_two)


def finish(parts, rows, cells, width):
    act_grad, noise_grad, one, two, *rest = pl.pallas_call(
        lambda *refs: finish_kernel(rows, cells, len(parts), *refs),
        in_specs=[in_vmem()] * len(parts),
        out_specs=[in_vmem()] * 12,
        out_shape=[
            shape((NACT, cells), f32),
            shape((NLEV, cells), f32),
            shape((cells, LANES), f32),
            shape((cells, LANES), f32),
            shape((C, rows), f32),
            shape((C, rows), f32),
            shape((C, rows), f32),
            shape((C, 2 * rows), f32),
        ]
        + [shape((width,), f32)] * 4,
        compiler_params=params(),
        name="finish",
    )(*parts)
    return (act_grad, noise_grad, one, two, *[grad.T for grad in rest[:4]], *rest[4:])


def collect_kernel(member_ref, *refs):
    strips, out = refs[:-1], refs[-1]
    for offset, strip in enumerate(strips):
        out[member_ref[0] ^ offset, 0] = strip[0].astype(out.dtype)


def trade_strips(strips):
    return tuple(trade(strip, offset) for offset, strip in enumerate(strips))


def collect_strips(member_box, strips, kind):
    count = len(strips)
    frames, rows, columns = strips[0].shape
    whole_strips = pl.pallas_call(
        collect_kernel,
        grid=(frames,),
        in_specs=[in_smem()] + [pl.BlockSpec((1, rows, columns), lambda f: (f, 0, 0))] * count,
        out_specs=pl.BlockSpec((count, 1, rows, columns), lambda f: (0, f, 0, 0)),
        out_shape=shape((count, frames, rows, columns), kind),
        compiler_params=params(),
        name="collect",
    )(member_box, *strips)
    return whole_strips.reshape(count * frames, rows, columns)


def twice(values):
    return jnp.concatenate([values, values], axis=-1)


def pad_small(rows):
    stacked = jnp.stack(rows, axis=-2)
    gaps = [(0, 0)] * (stacked.ndim - 2) + [(0, 8 - len(rows)), (0, 0)]
    return jnp.pad(stacked, gaps)


def trade(value, offset):
    if offset == 0:
        return value
    count = lax.axis_size("rows")
    return lax.ppermute(value, "rows", [(i, i ^ offset) for i in range(count)])


def half_trade(value, at):
    count, members = lax.axis_size("seq"), lax.axis_size("rows")
    pairs = []
    for place in range(count):
        for member in range(members):
            offset = sides(count)[member % 2][at]
            if offset:
                pairs.append((place * members + member, (place ^ offset) * members + member))
    return lax.ppermute(value, ("seq", "rows"), pairs)


def layers(member_box, frame_images, frame_stats, cot_fetched, styles, bias_rows, works):
    count = lax.axis_size("rows")
    *out, win_one, win_two, win_level, win_coarse, middle, down, stats, b_one, b_two, b_down, b_up = forward(
        member_box, frame_images, frame_stats, styles, bias_rows, works, count
    )
    out = trade_strips(out)
    down, cot_fetched = lax.optimization_barrier((down, cot_fetched))
    cot = gather_frames(member_box, *cot_fetched)
    *grad_strips, tile_out, tile_level, tile_mid, coarse_pairs, pieces, bias_sums = backward(
        member_box, cot, frame_images, styles, stats, middle, down, b_up, b_down, b_two, b_one, count
    )
    grad_strips = trade_strips(grad_strips)
    wins = (win_one, win_two, win_level, win_coarse)
    tiles = (tile_out, tile_level, tile_mid, coarse_pairs)
    return out, grad_strips, wins, tiles, pieces, bias_sums


def local_direct(
    frames,
    cotangent,
    actions,
    noise_ids,
    valid,
    act_table,
    noise_table,
    ada_one,
    ada_two,
    conv_one,
    conv_two,
    down_kernel,
    up_kernel,
    bias_one,
    bias_two,
    bias_down,
    bias_up,
):
    member = lax.axis_index("rows").astype(jnp.int32)
    place = lax.axis_index("seq").astype(jnp.int32)
    count = lax.axis_size("seq")
    share = frames.shape[0] // lax.axis_size("rows")
    rows, cells, width = conv_one.shape[0], ada_one.shape[0], bias_one.shape[0]
    half = count // 2
    member_box = member.reshape(1)
    where = jnp.stack([place, member])
    ids = (actions, noise_ids, valid)
    kernels = (conv_one, conv_two, down_kernel, up_kernel)
    biases = (bias_one, bias_two, bias_down, bias_up)
    far = trade(cut_far(member_box, frames), 2)
    packed = pack(ids, kernels, ada_one, ada_two, act_table, noise_table, biases)
    mine = jnp.concatenate([half_trade(packed, at) for at in range(half)], axis=0)
    other = trade(mine, 1)
    own, near, cot_far, *cot_rest = cut_others(member_box, frames, cotangent, lax.axis_size("rows"))
    cot_fetched = (trade(cot_far, 2), *cot_rest)
    frame_images, frame_stats = gather_frames(member_box, far, own, near, FAR_HINT)
    styles, bias_rows, group_ids, works = prepare(where, packed, mine, other, count, rows, cells, share)
    out, grad_strips, wins, tiles, pieces, bias_sums = layers(
        member_box, frame_images, frame_stats, cot_fetched, styles, bias_rows, works
    )
    kept, small, theirs, hots = weight_messages(where, wins, tiles, pieces, bias_sums, group_ids, count, rows)
    theirs, out = lax.optimization_barrier((theirs, out))
    own, *messages = join_messages(where, kept, small, trade(theirs, 1), half, rows, share)
    received = [half_trade(message, at) for at, message in enumerate(messages)]
    result = collect_strips(member_box, out, bf16)
    frames_grad = collect_strips(member_box, grad_strips, f32)
    received, result, frames_grad = lax.optimization_barrier((received, result, frames_grad))
    sums = reduce_messages(
        where, own, received, hots, act_table, noise_table, ada_one, ada_two, rows, cells, 2 * share
    )
    pair = (sums.astype(f32) + trade(sums, 1).astype(f32)).astype(bf16)
    parts = [pair, trade(pair, 2)]
    return (result, frames_grad, *finish(parts, rows, cells, width))


def local_general(
    frames,
    cotangent,
    actions,
    noise_ids,
    valid,
    act_table,
    noise_table,
    ada_one,
    ada_two,
    conv_one,
    conv_two,
    down_kernel,
    up_kernel,
    bias_one,
    bias_two,
    bias_down,
    bias_up,
):
    member = lax.axis_index("rows").astype(jnp.int32)
    share = frames.shape[0] // lax.axis_size("rows")
    member_box = member.reshape(1)

    def gathered(value, axis):
        return lax.all_gather(value, "seq", axis=axis, tiled=True)

    far = trade(cut_far(member_box, frames), 2)
    own, near, cot_far, *cot_rest = cut_others(member_box, frames, cotangent, lax.axis_size("rows"))
    cot_fetched = (trade(cot_far, 2), *cot_rest)
    frame_images, frame_stats = gather_frames(member_box, far, own, near)
    act_full = gathered(act_table, 1)
    noise_full = gathered(noise_table, 1)
    ada_full = gathered(jnp.concatenate([ada_one, ada_two], axis=1), 0).astype(f32)
    biases = gathered(jnp.stack([bias_one, bias_two, bias_down, bias_up]), 1).astype(f32)
    wide = lambda kernel: gathered(kernel, 0).astype(f32)
    works = (
        jnp.concatenate([wide(conv_one), wide(conv_two)], axis=1),
        twice(wide(up_kernel)),
        twice(wide(down_kernel)),
    )

    own = lambda ids: lax.dynamic_slice_in_dim(ids, member * share, share)
    own_actions, own_noise, own_valid = own(actions), own(noise_ids), own(valid)
    action_hot = (own_actions[:, None] == jnp.arange(NACT, dtype=jnp.int32)[None, :]).astype(f32) * own_valid[
        :, None
    ].astype(f32)
    noise_hot = (own_noise[:, None] == jnp.arange(NLEV, dtype=jnp.int32)[None, :]).astype(f32)
    embed = jnp.dot(action_hot, act_full.astype(f32), precision=precise) + jnp.dot(
        noise_hot, noise_full.astype(f32), precision=precise
    )
    style = jnp.dot(embed, ada_full, precision=precise)
    styles = pad_small(
        [
            twice(1.0 + style[:, :C]),
            twice(style[:, C : 2 * C]),
            twice(1.0 + style[:, 2 * C : 3 * C]),
            twice(style[:, 3 * C :]),
        ]
    )
    bias_rows = pad_small([twice(biases[k]) for k in range(4)])
    out, grad_strips, wins, tiles, pieces, bias_sums = layers(
        member_box, frame_images, frame_stats, cot_fetched, styles, bias_rows, works
    )
    g_one, g_two, g_down, g_up = weight_grads(wins, tiles)
    result = collect_strips(member_box, out, bf16)
    frames_grad = collect_strips(member_box, grad_strips, f32)

    pieces_one = jnp.concatenate([pieces[:, 0, :C], pieces[:, 1, :C]], axis=1)
    pieces_two = jnp.concatenate([pieces[:, 2, :C], pieces[:, 3, :C]], axis=1)
    ada_one_grad = jnp.dot(embed.T, pieces_one, precision=precise)
    ada_two_grad = jnp.dot(embed.T, pieces_two, precision=precise)
    embed_grad = jnp.dot(jnp.concatenate([pieces_one, pieces_two], axis=1), ada_full.T, precision=precise)
    act_table_grad = jnp.dot(action_hot.T, embed_grad, precision=precise)
    noise_table_grad = jnp.dot(noise_hot.T, embed_grad, precision=precise)
    bias_total = jnp.sum(bias_sums, axis=0)[:4, :C]

    def shard(value, axis):
        return lax.psum_scatter(value, "seq", scatter_dimension=axis, tiled=True)

    shards = (
        shard(act_table_grad, 1),
        shard(noise_table_grad, 1),
        shard(ada_one_grad, 0),
        shard(ada_two_grad, 0),
        shard(g_one, 0),
        shard(g_two, 0),
        shard(g_down, 0),
        shard(g_up, 0),
        shard(bias_total[0], 0),
        shard(bias_total[1], 0),
        shard(bias_total[2], 0),
        shard(bias_total[3], 0),
    )
    return (result, frames_grad) + lax.psum(shards, "rows")


def fits_direct(mesh):
    count = mesh.shape["seq"]
    rows, cells = 9 * C // count, 256 // count
    return count in (2, 4, 8) and rows % 8 == 0 and rows >= ID_ROW + 8 and cells % 8 == 0 and mesh.shape["rows"] == 4


def solution(mesh):
    in_specs = (
        P("seq", "rows", None),
        P("seq", "rows", None),
        P("seq"),
        P("seq"),
        P("seq"),
        P(None, "seq"),
        P(None, "seq"),
        P("seq", None),
        P("seq", None),
        P("seq", None),
        P("seq", None),
        P("seq", None),
        P("seq", None),
        P("seq"),
        P("seq"),
        P("seq"),
        P("seq"),
    )
    out_specs = (
        P("seq", "rows", None),
        P("seq", "rows", None),
        P(None, "seq"),
        P(None, "seq"),
        P("seq", None),
        P("seq", None),
        P("seq", None),
        P("seq", None),
        P("seq", None),
        P("seq", None),
        P("seq"),
        P("seq"),
        P("seq"),
        P("seq"),
    )
    local = local_direct if fits_direct(mesh) else local_general
    return jax.shard_map(local, mesh=mesh, in_specs=in_specs, out_specs=out_specs, check_vma=False)
```

```python
import jax
import jax.numpy as jnp
from jax import lax
from jax.experimental import pallas as pl
from jax.experimental.pallas import tpu as pltpu
from jax.sharding import PartitionSpec as P

C = 64
NACT = 18
GROUPS = 32
NLEV = 32
H = 64
W = 64
PAIRS = W // 2
HALF = H // 2
LANES = 2 * C
BLOCK = PAIRS * HALF
MEMBERS = float(H * W * (C // GROUPS))
EPS = 1e-05

precise = lax.Precision.HIGHEST
f32 = jnp.float32
bf16 = jnp.bfloat16
VMEM_LIMIT = 16 * 2**20
VMEM_MOST = 60 * 2**20


def lane_ids(shape):
    return lax.broadcasted_iota(jnp.int32, shape, len(shape) - 1)


def swap_halves(x):
    return pltpu.roll(x, C, axis=x.ndim - 1)


def row_before(x):
    rows = lax.broadcasted_iota(jnp.int32, x.shape, 0)
    return jnp.where(rows == 0, 0.0, pltpu.roll(x, 1, axis=0))


def row_after(x):
    rows = lax.broadcasted_iota(jnp.int32, x.shape, 0)
    return jnp.where(rows == x.shape[0] - 1, 0.0, pltpu.roll(x, x.shape[0] - 1, axis=0))


def both_parities(x):
    x = jnp.broadcast_to(x, (8, LANES))
    return x + swap_halves(x)


def group_sum(x):
    even = lane_ids(x.shape) % 2 == 0
    return x + jnp.where(even, pltpu.roll(x, LANES - 1, axis=1), pltpu.roll(x, 1, axis=1))


def total(x):
    return jnp.sum(x, axis=0, keepdims=True)


def over_pairs(body, carry):
    for j in range(PAIRS):
        carry = body(j, carry)
    return carry


def build_windows(windows, tile):
    low_lanes = lane_ids((HALF, LANES)) < C
    zero = jnp.zeros((HALF, LANES), f32)

    def write(j, even, odd):
        windows[0, j] = row_before(odd).astype(bf16)
        windows[1, j] = even.astype(bf16)
        windows[2, j] = odd.astype(bf16)
        windows[3, j] = row_after(even).astype(bf16)

    def body(j, carry):
        even_past, odd_past = carry
        even = swap_halves(tile(0, j))
        odd = swap_halves(tile(1, j))
        write(j, jnp.where(low_lanes, even_past, even), jnp.where(low_lanes, odd_past, odd))
        return even, odd

    even, odd = over_pairs(body, (zero, zero))
    write(PAIRS, jnp.where(low_lanes, even, 0.0), jnp.where(low_lanes, odd, 0.0))


def window_operand(windows, slots):
    parts = []
    for slot in slots:
        for shift in (0, 1):
            parts.append(windows[slot, shift : shift + PAIRS].reshape(BLOCK, LANES))
    return jnp.concatenate(parts, axis=1)


def matmul(left, right):
    return jnp.dot(left, right, preferred_element_type=f32)


def tiles_of(y):
    return y.reshape(PAIRS, HALF, LANES)


def norm_stats(sums, squares):
    average = group_sum(both_parities(sums)) / MEMBERS
    variance = group_sum(both_parities(squares)) / MEMBERS - average * average
    return average, lax.rsqrt(jnp.maximum(variance, 0.0) + EPS)


def strip_start(member, offset, strip):
    return pl.multiple_of((member ^ offset) * strip, strip)


def load_strips(member, strips, image):
    for offset, strip in enumerate(strips):
        rows = strip.shape[0]
        start = strip_start(member, offset, rows)
        for j in range(PAIRS):
            image[j, pl.ds(start, rows), :] = strip[:, j * LANES : (j + 1) * LANES].astype(f32)


def store_strips(member, image, f, strips, pairs=range(PAIRS)):
    for offset, strip in enumerate(strips):
        rows = strip.shape[1]
        start = strip_start(member, offset, rows)
        for j in pairs:
            strip[f, :, j * LANES : (j + 1) * LANES] = image[j, pl.ds(start, rows), :].astype(strip.dtype)


def parity_rows(image, parity, j):
    return image[j, pl.ds(parity, HALF, stride=2), :]


def staggered(steps):
    steps = list(steps)
    started = []
    while steps or started:
        if steps:
            started.append(steps.pop(0))
        for step in list(started):
            if next(step, "end") == "end":
                started.remove(step)


def gather_frame(member, strips, image, stats):
    load_strips(member, strips, image)

    def add_stats(j, carry):
        x = image[j]
        s, q = carry
        return s + x, q + x * x

    zero = jnp.zeros((H, LANES), f32)
    s, q = over_pairs(add_stats, (zero, zero))
    average, inverse = norm_stats(total(s), total(q))
    stats[0:1, :] = average[0:1]
    stats[1:2, :] = inverse[0:1]
    stats[2:3, :] = both_parities(total(s))[0:1]
    stats[3:8, :] = jnp.zeros((5, LANES), f32)


def gather_kernel(member_ref, own, far, near, images, all_stats):
    member = member_ref[0]
    frames = images.shape[0]
    first = member % 2 * frames
    for f in range(frames):
        strips = (own.at[f], near.at[f], far.at[first + f], near.at[frames + f])
        gather_frame(member, strips, images.at[f], all_stats.at[f])


def forward_kernel(count, *refs):
    member_ref, frame_images, frame_stats, styles, biases, work_pair, work_up, work_down = refs[:8]
    out = refs[8 : 8 + count]
    outs = refs[8 + count : 15 + count]
    turned_operands = refs[15 + count : 19 + count]
    images, levels, w_one, w_two, w_down, w_up = refs[19 + count :]
    member = member_ref[0]
    works = {"one": work_pair, "two": work_pair, "down": work_down, "up": work_up}
    found = {}

    def block(name, row):
        k = works[name][row : row + C, :]
        low = lane_ids(k.shape) < C
        if name == "two":
            return jnp.where(low, swap_halves(k), k)
        return jnp.where(low, k, swap_halves(k))

    def turned_pairs(name):
        work = works[name]
        key = "one" if name == "two" else name
        if key not in found:
            blocks = [work[at : min(at + LANES, work.shape[0]), :] for at in range(0, work.shape[0], LANES)]
            found[key] = [below(block, LANES).T for block in blocks]
        return [k[C:] if name == "two" else k[:C] for k in found[key]]

    def operands():
        yield from write_forward_operands(block, w_one, w_two, w_down, w_up)
        yield from write_backward_operands(turned_pairs, *turned_operands)

    low_lanes = lane_ids((HALF, LANES)) < C

    def frame(f):
        win_one, win_two, win_level, win_coarse, middle, down, stats = (ref.at[f] for ref in outs)
        frame_image, image, level, style = frame_images.at[f], images.at[f], levels.at[f], styles.at[f]
        average_one, inverse_one = frame_stats[f, 0:1, :], frame_stats[f, 1:2, :]
        gain_one = inverse_one * style[0:1, :]
        half_gain = 0.5 * gain_one
        half_shift = 0.5 * (style[1:2, :] - average_one * gain_one)

        def act_one(parity, j):
            h = parity_rows(frame_image, parity, j) * half_gain + half_shift
            return h * jnp.tanh(h) + h

        build_windows(win_one, act_one)
        yield
        y = matmul(window_operand(win_one, range(4)), w_one[...])
        sums = jnp.zeros((1, LANES), f32)
        squares = jnp.zeros((1, LANES), f32)
        for a in range(2):
            v = y[:, a * LANES : (a + 1) * LANES] + biases[0:1, :]
            sums = sums + total(v)
            squares = squares + total(v * v)
            middle[a] = tiles_of(v)
        yield
        average_two, inverse_two = norm_stats(sums, squares)
        stats[0:1, :] = average_one
        stats[1:2, :] = inverse_one
        stats[2:3, :] = average_two[0:1]
        stats[3:4, :] = inverse_two[0:1]
        stats[4:8, :] = jnp.zeros((4, LANES), f32)
        gain_two = inverse_two * style[2:3, :]
        half_gain_two = 0.5 * gain_two[0:1]
        half_shift_two = 0.5 * (style[3:4, :] - average_two[0:1] * gain_two[0:1])

        def act_two(parity, j):
            h = middle[parity, j] * half_gain_two + half_shift_two
            return h * jnp.tanh(h) + h

        build_windows(win_two, act_two)
        yield
        y = matmul(window_operand(win_two, range(4)), w_two[...])
        for a in range(2):
            v = y[:, a * LANES : (a + 1) * LANES] + biases[1:2, :]
            level[a] = tiles_of(v) + frame_image[:, pl.ds(a, HALF, stride=2), :]
        yield
        build_windows(win_level, lambda parity, j: level[parity, j])
        yield
        operand = window_operand(win_level, range(4))
        y = matmul(operand[:, : 6 * LANES], w_down[...]) + biases[2:3, :]
        down[...] = tiles_of(y)
        yield

        def write_coarse(j, cells):
            win_coarse[0, j] = row_before(cells).astype(bf16)
            win_coarse[1, j] = cells.astype(bf16)
            win_coarse[2, j] = row_after(cells).astype(bf16)

        def coarse_body(j, past):
            h = down[j] * 0.5
            coarse = h * jnp.tanh(h) + h
            write_coarse(j, jnp.where(low_lanes, past, coarse))
            return coarse

        past = over_pairs(coarse_body, jnp.zeros((HALF, LANES), f32))
        write_coarse(PAIRS, jnp.where(low_lanes, past, 0.0))
        yield
        operand = window_operand(win_level, range(4))
        coarse_operand = window_operand(win_coarse, (0, 1, 1, 2))
        y = matmul(operand, w_up[: 16 * C, :]) + matmul(coarse_operand, w_up[16 * C :, :])
        for a in range(2):
            v = y[:, a * LANES : (a + 1) * LANES] + biases[3:4, :]
            image[:, pl.ds(a, HALF, stride=2), :] = tiles_of(v) + level[a]
        yield
        store_strips(member, image, f, out)

    staggered([operands()] + [frame(f) for f in range(styles.shape[0])])


def slope_twice(h):
    t = jnp.tanh(h)
    return (1.0 + t) + h * (1.0 - t * t)


def backward_kernel(count, *refs):
    member_ref = refs[0]
    cot_images, cot_stats, frame_images, styles, all_stats, all_middle, all_down = refs[1:8]
    w_up, w_down, w_two, w_one = refs[8:12]
    out = refs[12 : 12 + count]
    outs = refs[12 + count : 18 + count]
    scratch = refs[18 + count :]
    member = member_ref[0]
    low_lanes = lane_ids((HALF, LANES)) < C

    def frame(f):
        tile_out, tile_level, tile_mid, coarse_pairs, pieces, bias_sums = (ref.at[f] for ref in outs)
        image, level_grad, pre_grad, windows, coarse_below = (ref.at[f] for ref in scratch)
        style, stats, middle, down, frame_image = (
            ref.at[f] for ref in (styles, all_stats, all_middle, all_down, frame_images)
        )
        cot_image = cot_images.at[f]

        def out_tile(parity, j):
            x = parity_rows(cot_image, parity, j)
            tile_out[parity, j] = x.astype(bf16)
            return x

        build_windows(windows, out_tile)
        yield
        y = matmul(window_operand(windows, range(4)), w_up[...])
        for a in range(2):
            level_grad[a] = (
                tiles_of(y[:, (2 + a) * LANES : (3 + a) * LANES]) + cot_image[:, pl.ds(a, HALF, stride=2), :]
            )
        coarse = y[:, :LANES] + y[:, LANES : 2 * LANES]
        pre_grad[0] = tiles_of(coarse)
        yield

        def coarse_body(t, carry):
            after, sums = carry
            j = PAIRS - 1 - t
            g = pre_grad[0, j]
            g = g + swap_halves(g)
            h = down[j] * 0.5
            d = g * slope_twice(h)
            pair = jnp.where(low_lanes, d, after)
            coarse_pairs[j] = pair.astype(bf16)
            coarse_below[j] = row_after(pair).astype(bf16)
            return d, sums + d

        zero = jnp.zeros((HALF, LANES), f32)
        _, sums = over_pairs(coarse_body, (zero, zero))
        bias_down_sum = jnp.broadcast_to(total(sums), (8, LANES))
        operand = jnp.concatenate(
            [coarse_pairs[...].reshape(BLOCK, LANES), coarse_below[...].reshape(BLOCK, LANES)], axis=1
        )
        y = matmul(operand, w_down[...])
        sums = jnp.zeros((1, LANES), f32)
        for a in range(2):
            v = y[:, a * LANES : (a + 1) * LANES] + level_grad[a].reshape(BLOCK, LANES)
            sums = sums + total(v)
            level_grad[a] = tiles_of(v)
        bias_two_sum = both_parities(sums)

        def level_tile(parity, j):
            x = level_grad[parity, j]
            tile_level[parity, j] = x.astype(bf16)
            return x

        build_windows(windows, level_tile)
        yield

        def norm_slopes(y, value, k):
            average, inverse = stats[2 * k : 2 * k + 1, :], stats[2 * k + 1 : 2 * k + 2, :]
            gain = inverse * style[2 * k : 2 * k + 1, :]
            half_gain = 0.5 * gain
            half_shift = 0.5 * (style[2 * k + 1 : 2 * k + 2, :] - average * gain)
            scale_sum = jnp.zeros((1, LANES), f32)
            shift_sum = jnp.zeros((1, LANES), f32)
            for a in range(2):
                v = value(a)
                g = y[:, a * LANES : (a + 1) * LANES] * slope_twice(v * half_gain + half_shift)
                pre_grad[a] = tiles_of(g)
                shift_sum = shift_sum + total(g)
                scale_sum = scale_sum + total(g * ((v - average) * inverse))
            scale_sum, shift_sum = both_parities(scale_sum), both_parities(shift_sum)
            factor = style[2 * k : 2 * k + 1, :]
            center = group_sum(factor * shift_sum) / MEMBERS
            tilt = group_sum(factor * scale_sum) / MEMBERS
            slope = (inverse * tilt)[0:1] * inverse
            return scale_sum, shift_sum, gain, slope, slope * average - (inverse * center)[0:1]

        y = matmul(window_operand(windows, range(4)), w_two[...])
        scale_two, shift_two, gain_two, slope_two, constant_two = norm_slopes(
            y, lambda a: middle[a].reshape(BLOCK, LANES), 1
        )
        yield
        row_sums = [zero]

        def mid_tile(parity, j):
            x = pre_grad[parity, j] * gain_two + (constant_two - middle[parity, j] * slope_two)
            tile_mid[parity, j] = x.astype(bf16)
            row_sums[0] = row_sums[0] + x
            return x

        build_windows(windows, mid_tile)
        bias_one_sum = both_parities(total(row_sums[0]))
        yield
        y = matmul(window_operand(windows, range(4)), w_one[...])
        scale_one, shift_one, gain_one, slope_one, constant_one = norm_slopes(
            y, lambda a: frame_image[:, pl.ds(a, HALF, stride=2), :].reshape(BLOCK, LANES), 0
        )
        yield

        def frame_body(j, carry):
            for parity in range(2):
                x = parity_rows(frame_image, parity, j)
                g = pre_grad[parity, j] * gain_one + (constant_one - x * slope_one) + level_grad[parity, j]
                image[j, pl.ds(parity, HALF, stride=2), :] = g
            store_strips(member, image, f, out, (j,))
            return carry

        over_pairs(frame_body, 0)
        for k, value in enumerate((scale_one, shift_one, scale_two, shift_two)):
            pieces[k : k + 1, :] = value[0:1]
        pieces[4:8, :] = jnp.zeros((4, LANES), f32)
        for k, value in enumerate((bias_one_sum, bias_two_sum, bias_down_sum, cot_stats[f, 2:3, :])):
            bias_sums[k : k + 1, :] = value[0:1]
        bias_sums[4:8, :] = jnp.zeros((4, LANES), f32)

    staggered(frame(f) for f in range(styles.shape[0]))


def outer(left, right):
    return lax.dot_general(left, right, (((0,), (0,)), ((), ())), preferred_element_type=f32)


def accumulate(wins, tiles, sums, folds):
    win_one, win_two, win_level, win_coarse = wins
    tile_out, tile_level, tile_mid, coarse_pairs = tiles
    sum_one, sum_two, sum_down, sum_up = sums
    cells = win_one.shape[0] * BLOCK

    def operand(windows, slots):
        parts = []
        for slot in slots:
            for shift in (0, 1):
                parts.append(windows[:, slot, shift : shift + PAIRS].reshape(cells, LANES))
        return jnp.concatenate(parts, axis=1)

    def blocks(tiles):
        return jnp.concatenate([tiles[:, a].reshape(cells, LANES) for a in range(2)], axis=1)

    out_blocks = blocks(tile_out)
    sum_up[16 * C :, :] = outer(operand(win_coarse, range(3)), out_blocks)
    sum_up[: 16 * C, :] = outer(operand(win_level, range(4)), out_blocks)
    sum_down[...] = outer(operand(win_level, range(3)), coarse_pairs[...].reshape(cells, LANES))
    sum_two[...] = outer(operand(win_two, range(4)), blocks(tile_level))
    folds[0]()
    sum_one[...] = outer(operand(win_one, range(4)), blocks(tile_mid))
    folds[1]()
    folds[2]()


def taps():
    return [(p, q, (3 * p + q) * C) for p in range(3) for q in range(3)]


def fold(sums, p, q):
    return fold_slots(sums, 0, p, q, range(4))


def fold_coarse(sums, p, q):
    return fold_slots(sums, 16 * C, p, q, (0, 1, 1, 2))


def fold_slots(sums, base, p, q, slots):
    halves = []
    for b in range(2):
        rows = [base + (slots[a + p] * 4 + b + q) * C for a in range(2)]
        halves.append(sums[rows[0] : rows[0] + C, :LANES] + sums[rows[1] : rows[1] + C, LANES:])
    return halves[0] + swap_halves(halves[1])


def weight_kernel(*refs):
    wins, tiles, grads, sums = refs[:4], refs[4:8], refs[8:12], refs[12:]
    g_one, g_two, g_down, g_up = grads
    sum_one, sum_two, sum_down, sum_up = sums

    def fold_up():
        for p, q, at in taps():
            g_up[2 * at : 2 * at + C, :] = fold_coarse(sum_up, p, q)[:, :C]
            g_up[2 * at + C : 2 * at + 2 * C, :] = fold(sum_up, p, q)[:, :C]
            place = (p * 4 + q) * C
            g_down[at : at + C, :] = sum_down[place : place + C, :C]

    def fold_two():
        for p, q, at in taps():
            g_two[at : at + C, :] = fold(sum_two, p, q)[:, :C]

    def fold_one():
        for p, q, at in taps():
            g_one[at : at + C, :] = fold(sum_one, p, q)[:, :C]

    accumulate(wins, tiles, sums, (fold_up, fold_two, fold_one))


PARTS = 16
FAR_HINT = 90
PAIR_PARTS = 24


def three_parts(exact):
    high = exact.astype(bf16).astype(f32)
    rest = exact - high
    mid = rest.astype(bf16).astype(f32)
    return jnp.concatenate([high, mid, rest - mid], axis=0)


def below(block, rows):
    if block.shape[0] == rows:
        return block
    return jnp.concatenate([block, jnp.zeros((rows - block.shape[0], LANES), f32)], axis=0)


def message_kernel(count, rows, *refs):
    where_ref, wins, tiles = refs[0], refs[1:5], refs[5:9]
    pieces, bias_sums, ids, kept, small, theirs, hots = refs[9:16]
    sums = refs[16:20]
    g_pair, g_up, g_down = refs[20:]
    sum_one, sum_two, sum_down, sum_up = sums
    taken = 2 * pieces.shape[0]
    for at in range(ids.shape[0]):
        write_hots(hots, at * taken, where_ref[1] // 2 * taken, taken, ids[at])
    low_lanes = lane_ids((C, LANES)) < C

    def fold_up():
        for p, q, at in taps():
            g_up[2 * at : 2 * at + C, :] = fold_coarse(sum_up, p, q)
            g_up[2 * at + C : 2 * at + 2 * C, :] = fold(sum_up, p, q)
            place = (p * 4 + q) * C
            g_down[at : at + C, :] = sum_down[place : place + C, :]

    def fold_two():
        for p, q, at in taps():
            g_pair[at : at + C, :] = swap_halves(fold(sum_two, p, q))

    def fold_one():
        for p, q, at in taps():
            g_pair[at : at + C, :] = jnp.where(low_lanes, fold(sum_one, p, q), g_pair[at : at + C, :])

    accumulate(wins, tiles, sums, (fold_up, fold_two, fold_one))
    frames = pieces.shape[0]
    small[...] = jnp.zeros_like(small)
    total_bias = bias_sums[0, 0:4, :]
    for f in range(frames):
        small[4 * f : 4 * f + 4, :] = pieces[f, 0:4, :]
        if f > 0:
            total_bias = total_bias + bias_sums[f, 0:4, :]
    small[4 * frames : 4 * frames + 4, :] = total_bias
    sent = below(three_parts(small[...]), rows)
    low_lanes = lane_ids((rows, LANES)) < C
    half = count // 2
    for at in range(half):
        for ref, mine in ((kept, True), (theirs, False)):
            start = pl.multiple_of(seq_owner(where_ref[0], where_ref[1], half, at, mine) * rows, 8)
            blocks = (
                g_pair[pl.ds(start, rows), :],
                jnp.where(
                    low_lanes,
                    g_up[pl.ds(pl.multiple_of(2 * start, 8), rows), :],
                    swap_halves(g_up[pl.ds(pl.multiple_of(2 * start + rows, 8), rows), :]),
                ),
                jnp.where(low_lanes, g_down[pl.ds(start, rows), :], 0.0 if mine else sent),
            )
            ref[at * 3 * rows : (at + 1) * 3 * rows, :] = jnp.concatenate(blocks, axis=0).astype(ref.dtype)


def join_kernel(half, rows, frames, where_ref, kept, small, theirs, own, *messages):
    first = where_ref[1] % 2 == 0
    at = 2 * rows
    other = theirs[at : at + 3 * PARTS, :].astype(f32)
    other = other[:PARTS] + other[PARTS : 2 * PARTS] + other[2 * PARTS :]
    mine = small[...]
    n = 4 * frames
    exact = jnp.concatenate(
        [
            jnp.where(first, mine[:n], other[:n]),
            jnp.where(first, other[:n], mine[:n]),
            mine[n : n + 4] + other[n : n + 4],
            jnp.zeros((PAIR_PARTS - 2 * n - 4, LANES), f32),
        ],
        axis=0,
    )
    low_lanes = lane_ids((rows, LANES)) < C
    sent = below(three_parts(exact), rows)
    size = 3 * rows
    for k, message in enumerate(messages):
        block = kept[k * size : (k + 1) * size, :] + theirs[k * size : (k + 1) * size, :].astype(f32)
        message[:at, :] = block[:at].astype(bf16)
        message[at:, :] = jnp.where(low_lanes, block[at:], sent).astype(bf16)
        if k == half - 1:
            own[:at, :] = block[:at]
            own[at:, :] = jnp.where(low_lanes, block[at:], below(exact, rows))


def reduce_kernel(half, rows, cells, frames, *refs):
    where_ref, own = refs[:2]
    messages = refs[2 : 2 + half]
    hots, act_table, noise_table, ada_one, ada_two, out, pieces_one, pieces_two, table, high_one, high_two = refs[2 + half :]
    place, member = where_ref[0], where_ref[1]
    taken = 4 * frames
    bias = jnp.zeros((4, LANES), f32)
    sums = None
    lanes = lane_ids((1, LANES))
    low_lanes = lanes < C
    at = 2 * rows
    for k, ref in enumerate(messages):
        message = ref[...].astype(f32)
        if k == half - 1:
            message = jnp.where(member % 2 == 0, own[...], message)
        sums = message if sums is None else sums + message
        small = (
            message[at : at + PAIR_PARTS]
            + message[at + PAIR_PARTS : at + 2 * PAIR_PARTS]
            + message[at + 2 * PAIR_PARTS : at + 3 * PAIR_PARTS]
        )
        turned = swap_halves(small)
        bias = bias + small[taken : taken + 4]
        for f in range(frames):
            row = k * frames + f
            for kind, piece in ((0, pieces_one), (2, pieces_two)):
                low, high = 4 * f + kind, 4 * f + kind + 1
                piece[row : row + 1, :] = jnp.where(low_lanes, turned[low : low + 1], small[high : high + 1])
    hot = hots[:, :TABLE_ROWS]
    table[...] = jnp.zeros_like(table)
    table[ACT_ROW : ACT_ROW + NACT, :] = act_table[...].astype(f32)
    table[NOISE_ROW : NOISE_ROW + NLEV, :] = noise_table[...].astype(f32)
    embed = matmul(hot.astype(bf16), table[...].astype(bf16))

    def exact(left, right, dims):
        return lax.dot_general(left, right, (dims, ((), ())), precision=precise, preferred_element_type=f32)

    one, two = pieces_one[...], pieces_two[...]
    for ref, ada in ((high_one, ada_one), (high_two, ada_two)):
        ref[...] = jnp.zeros_like(ref)
        ref[C : C + cells, :] = ada[...].astype(f32)
    pieces = jnp.concatenate([one, two], axis=1)
    embed_grad = exact(pieces, jnp.concatenate([high_one[...], high_two[...]], axis=1), ((1,), (1,)))
    ada_grads = exact(embed, pieces, ((0,), (0,)))
    width = C // (2 * half)
    bias = pltpu.roll(jnp.concatenate([bias, bias], axis=0), (LANES - place * width) % LANES, axis=1)
    extra = below(jnp.concatenate([exact(hot, embed_grad, ((0,), (0,))), bias], axis=0), rows)
    at = 2 * rows
    blocks = (
        sums[:at],
        jnp.where(lane_ids((rows, LANES)) < C, sums[at:], extra),
        ada_grads[:, :LANES],
        ada_grads[:, LANES:],
    )
    out[...] = jnp.concatenate(blocks, axis=0).astype(out.dtype)


def finish_kernel(rows, cells, count, *refs):
    parts, outs = [ref[...].astype(f32) for ref in refs[:count]], refs[count:]
    act_grad, noise_grad, ada_one, ada_two, g_one, g_two, g_down, g_up = outs[:8]
    bias_grads = outs[8:12]
    while len(parts) > 1:
        parts = [parts[k] + parts[k + 1] for k in range(0, len(parts), 2)]
    sums = parts[0]

    def turn(block):
        return jnp.concatenate([block, jnp.zeros((LANES - rows, LANES), f32)], axis=0).T[:, :rows]

    pair, halves, down = (turn(sums[k * rows : (k + 1) * rows]) for k in range(3))
    g_one[...] = pair[:C]
    g_two[...] = pair[C:]
    g_up[:, :rows] = halves[:C]
    g_up[:, rows:] = halves[C:]
    g_down[...] = down[:C]
    at = 3 * rows
    ada_one[...] = sums[at : at + cells]
    ada_two[...] = sums[at + cells : at + 2 * cells]
    extra = swap_halves(sums[2 * rows : 3 * rows])
    act_grad[...] = extra[ACT_ROW : ACT_ROW + NACT, :cells]
    noise_grad[...] = extra[NOISE_ROW : NOISE_ROW + NLEV, :cells]
    for k, ref in enumerate(bias_grads):
        ref[...] = extra[BIAS_ROW + k : BIAS_ROW + k + 1, : ref.shape[0]].reshape(ref.shape)


def write_forward_operands(block, f_one, f_two, f_down, f_up):
    low_lanes = lane_ids((C, LANES)) < C
    zero = jnp.zeros((C, LANES), f32)

    def taps(name, base, step):
        return {(p, q): block(name, (3 * p + q) * step + base) for p in range(3) for q in range(3)}

    def write(ref, base, found):
        for w in range(4):
            for p in range(3):
                tile = jnp.where(low_lanes, found.get((p, w), zero), found.get((p, w - 1), zero)).astype(bf16)
                for a in range(2):
                    at = base + ((a + p) * 4 + w) * C
                    ref[at : at + C, a * LANES : (a + 1) * LANES] = tile
            for a in range(2):
                for r in range(4):
                    if not 0 <= r - a < 3:
                        at = base + (r * 4 + w) * C
                        ref[at : at + C, a * LANES : (a + 1) * LANES] = zero.astype(bf16)

    write(f_one, 0, taps("one", 0, C))
    yield
    write(f_two, 0, taps("two", 0, C))
    yield
    found = taps("down", 0, C)
    for p in range(3):
        for w in range(4):
            at = (p * 4 + w) * C
            f_down[at : at + C, :] = found.get((p, w), zero).astype(bf16)
    yield
    write(f_up, 0, taps("up", C, 2 * C))
    yield
    write(f_up, 16 * C, taps("up", 0, 2 * C))
    yield


def write_backward_operands(turned_pairs, b_one, b_two, b_down, b_up):
    low_lanes = lane_ids((C, LANES)) < C
    zero = jnp.zeros((C, LANES), f32)
    def taps(pairs, base, step, scale=1.0):
        found = {}
        for p in range(3):
            for q in range(3):
                at = (3 * p + q) * step + base
                pair = pairs[at // LANES]
                other = swap_halves(pair)
                low, high = (pair, other) if at % LANES == 0 else (other, pair)
                found[p, q] = jnp.where(low_lanes, low, high) * scale
        return found

    def write(ref, lane, found):
        for w in range(4):
            for p in range(3):
                tile = jnp.where(low_lanes, found.get((p, 2 - w), zero), found.get((p, 3 - w), zero)).astype(bf16)
                for a in range(2):
                    at = ((a + 2 - p) * 4 + w) * C
                    ref[at : at + C, lane + a * LANES : lane + (a + 1) * LANES] = tile
            for a in range(2):
                for r in range(4):
                    if not 0 <= a + 2 - r < 3:
                        at = (r * 4 + w) * C
                        ref[at : at + C, lane + a * LANES : lane + (a + 1) * LANES] = zero.astype(bf16)

    one, two = turned_pairs("one"), turned_pairs("two")
    write(b_one, 0, taps(one, 0, C, 0.5))
    yield
    write(b_two, 0, taps(two, 0, C, 0.5))
    yield
    pairs = turned_pairs("up")
    write(b_up, 0, taps(pairs, 0, 2 * C, 0.5))
    yield
    write(b_up, 2 * LANES, taps(pairs, C, 2 * C))
    yield
    found = taps(turned_pairs("down"), 0, C)
    for under in range(2):
        for right in range(2):
            at = (under * 2 + right) * C
            for a in range(2):
                p = {(0, 0): 1, (0, 1): 2, (1, 1): 0}.get((under, a))
                first, second = zero, zero
                if p is not None:
                    first = found[p, 1] if right == 0 else zero
                    second = found[p, 2] if right == 0 else found[p, 0]
                b_down[at : at + C, a * LANES : (a + 1) * LANES] = jnp.where(low_lanes, first, second).astype(bf16)


ACT_ROW, NOISE_ROW, TABLE_ROWS = 0, 24, 56
BIAS_ROW, ID_ROW = 56, 64


def pack_sizes(rows, cells):
    return 3 * rows, 3 * rows + 2 * cells, -(-(3 * rows + 2 * cells) // 16) * 16


def turned(values):
    wide = jnp.concatenate([values, jnp.zeros((C, LANES - values.shape[1]), f32)], axis=1)
    return jnp.concatenate([wide, jnp.zeros((C, LANES), f32)], axis=0).T[: values.shape[1]]


def copy_all(pairs, sent):
    copies = [pltpu.make_async_copy(source, target, sent.at[k]) for k, (source, target) in enumerate(pairs)]
    for copy in copies:
        copy.start()
    for copy in copies:
        copy.wait()


def far_part(member, array, out):
    half = out.shape[0]
    return array.at[pl.ds((1 - member // 2) * half, half)], out


def strip_parts(member, array, own, other):
    share = own.shape[0]
    return [
        (array.at[pl.ds(member * share, share)], own),
        (array.at[pl.ds((member ^ 1) * share, share)], other),
    ]


def far_kernel(member_ref, array, out, sent):
    copy_all([far_part(member_ref[0], array, out)], sent)


def cut_kernel(member_ref, frames, cotangent, own, other, far, cot_own, cot_other, sent):
    member = member_ref[0]
    pairs = strip_parts(member, frames, own, other) + strip_parts(member, cotangent, cot_own, cot_other)
    copy_all([far_part(member, cotangent, far)] + pairs, sent)


def share_kernel(member_ref, far, out):
    share = out.shape[0]
    out[...] = far[pl.ds((member_ref[0] ^ 1) % 2 * share, share)]


def mark_kernel(far, out):
    out[...] = far[0, :8, :LANES].astype(f32)


def near_kernel(other, shared, mark, out):
    share = out.shape[0] // 2
    out[:share] = other[...]
    out[share:] = shared[...]


def pack_kernel(*refs):
    actions, noise_ids, valid, conv_one, conv_two, down_kernel, up_kernel, ada_one, ada_two = refs[:9]
    act_table, noise_table = refs[9:11]
    biases = refs[11:15]
    out, work = refs[15:]
    rows, cells = conv_one.shape[1], ada_one.shape[0]
    style_at, end, _ = pack_sizes(rows, cells)
    wide = lambda ref: ref[...].astype(f32)
    low_lanes = lane_ids((rows, LANES)) < C
    up = wide(up_kernel)
    work[...] = jnp.zeros_like(work)
    for at, low, high in (
        (0, turned(wide(conv_one)), turned(wide(conv_two))),
        (rows, turned(up[:, :rows]), turned(up[:, rows:])),
    ):
        work[at : at + rows, :] = jnp.where(low_lanes, low, swap_halves(high))
    work[2 * rows : 3 * rows, :] = turned(wide(down_kernel))
    extra = 2 * rows
    for at, ref in ((ACT_ROW, act_table), (NOISE_ROW, noise_table)):
        size = ref.shape
        work[extra + at : extra + at + size[0], C : C + size[1]] = wide(ref)
    for k, ref in enumerate(biases):
        at = extra + BIAS_ROW + k
        work[at : at + 1, C : C + ref.shape[0]] = wide(ref).reshape(1, ref.shape[0])
    lanes = lane_ids((1, LANES))
    for k, ref in enumerate((actions, noise_ids, valid)):
        line = jnp.zeros((1, LANES), jnp.int32)
        for f in range(ref.shape[0]):
            line = jnp.where(lanes == C + f, ref[f], line)
        at = extra + ID_ROW + k
        work[at : at + 1, C:] = line.astype(f32)[:, C:]
    work[style_at : style_at + cells, :] = wide(ada_one)
    work[style_at + cells : end, :] = wide(ada_two)
    out[...] = work[...].astype(bf16)


def seq_owner(place, member, half, at, mine=True):
    side = member % 2 if mine else 1 - member % 2
    even, odd = sides(2 * half)
    return place ^ (even[at] + side * (odd[at] - even[at]))


def sides(count):
    ones = lambda offset: bin(offset).count("1") % 2
    return tuple([offset for offset in reversed(range(count)) if ones(offset) == side] for side in (0, 1))


def write_hots(hots, at, first, frames, ids):
    lanes = lane_ids((1, LANES)).astype(f32)
    for f in range(frames):
        mine = jnp.where(lane_ids(ids.shape) == C + first + f, ids, 0.0)
        mine = jnp.sum(mine, axis=1, keepdims=True)
        action, noise, valid = mine[0:1], mine[1:2], mine[2:3]
        hots[at + f : at + f + 1, :] = jnp.where(lanes == action + ACT_ROW, valid, 0.0) + jnp.where(
            lanes == noise + NOISE_ROW, 1.0, 0.0
        )


def prepare_kernel(count, rows, cells, *refs):
    where_ref, packed, mine, other = refs[:4]
    styles, biases, ids, work_pair, work_up, work_down, work_one, work_two, work_table, hots = refs[4:]
    place, member, frames = where_ref[0], where_ref[1], styles.shape[0]
    style_at, _, size = pack_sizes(rows, cells)
    bias_rows = jnp.zeros(SMALL, f32)
    half = count // 2
    for offset in range(count):
        ref = mine if offset < half else other
        at = offset % half
        pack = ref[at * size : (at + 1) * size, :].astype(f32)
        if at == half - 1:
            pack = jnp.where(member % 2 == offset // half, packed[...].astype(f32), pack)
        owner = seq_owner(place, member, half, at, offset < half)
        start = pl.multiple_of(owner * rows, 8)
        work_pair[pl.ds(start, rows), :] = pack[:rows]
        halves = pack[rows : 2 * rows]
        work_up[pl.ds(2 * start, rows), :] = halves
        work_up[pl.ds(pl.multiple_of(2 * start + rows, 8), rows), :] = swap_halves(halves)
        extra = pack[2 * rows : 3 * rows]
        work_down[pl.ds(start, rows), :] = extra
        work_one[offset * cells : (offset + 1) * cells, :] = pack[style_at : style_at + cells]
        work_two[offset * cells : (offset + 1) * cells, :] = pack[style_at + cells : style_at + 2 * cells]
        lane = (offset * cells) % LANES
        tables = pltpu.roll(extra[:TABLE_ROWS], (lane - C) % LANES, axis=1)
        kept = (lane_ids(tables.shape) >= lane) & (lane_ids(tables.shape) < lane + cells)
        column = offset * cells // LANES
        tables = jnp.where(kept, tables, 0.0)
        if lane == 0:
            work_table[column] = tables
        else:
            work_table[column] += tables
        slots = extra[BIAS_ROW : BIAS_ROW + 8]
        width = C // count
        slots = jnp.where((lane_ids(SMALL) >= C) & (lane_ids(SMALL) < C + width), slots, 0.0)
        bias_rows = bias_rows + pltpu.roll(slots, (owner * width + C) % LANES, axis=1)
        if offset < half:
            ids[at] = extra[ID_ROW : ID_ROW + 8]
    biases[...] = bias_rows + swap_halves(bias_rows)

    at = 2 * rows + ID_ROW
    hots[...] = jnp.zeros_like(hots)
    write_hots(hots, 0, member * frames, frames, packed[at : at + 8, :].astype(f32))
    hot = hots[:, :TABLE_ROWS].astype(bf16)
    embed = jnp.concatenate([matmul(hot, work_table[k].astype(bf16)) for k in range(work_table.shape[0])], axis=1)
    low_lanes = lane_ids(SMALL) < C
    for k, work in enumerate((work_one, work_two)):
        style = jnp.dot(embed, work[...], precision=precise, preferred_element_type=f32)
        other = swap_halves(style)
        scale = 1.0 + jnp.where(low_lanes, style, other)
        shift = jnp.where(low_lanes, other, style)
        for f in range(frames):
            styles[f, 2 * k : 2 * k + 1, :] = scale[f : f + 1]
            styles[f, 2 * k + 1 : 2 * k + 2, :] = shift[f : f + 1]
    for f in range(frames):
        styles[f, 4:8, :] = jnp.zeros((4, LANES), f32)


def shape(dims, kind):
    return jax.ShapeDtypeStruct(dims, kind)


def whole(dims):
    return pl.BlockSpec(dims, lambda f: (0,) * len(dims))


def per_frame(dims):
    return pl.BlockSpec((1,) + dims, lambda f: (f,) + (0,) * len(dims))


def strip_specs(count, strip):
    return [pl.BlockSpec((1, strip, W * C), lambda f: (f, 0, 0))] * count


SMALL = (8, LANES)
WINDOWS = (4, PAIRS + 1, HALF, LANES)
COARSE_WINDOWS = (3, PAIRS + 1, HALF, LANES)
TILES = (2, PAIRS, HALF, LANES)
COARSE = (PAIRS, HALF, LANES)
IMAGE = (PAIRS, H, LANES)
KEYS = 16 * C


def in_vmem():
    return pl.BlockSpec(memory_space=pltpu.VMEM)


def in_smem():
    return pl.BlockSpec(memory_space=pltpu.SMEM)


def params(limit=VMEM_LIMIT):
    return pltpu.CompilerParams(vmem_limit_bytes=limit)


def cost(macs, moved):
    return pl.CostEstimate(flops=2 * macs, bytes_accessed=moved, transcendentals=0)


def gather_frames(member, far, own, other, hint=0):
    near = trade(cut_near(member, other, far, hint), 1)
    frames = own.shape[0]
    return pl.pallas_call(
        gather_kernel,
        in_specs=[in_smem()] + [in_vmem()] * 3,
        out_specs=[in_vmem()] * 2,
        out_shape=[shape((frames,) + IMAGE, f32), shape((frames,) + SMALL, f32)],
        compiler_params=params(),
        name="frames",
    )(member, own, far, near)


def forward(member, frame_images, frame_stats, styles, biases, works, count):
    frames = frame_images.shape[0]
    strip = H // count
    return pl.pallas_call(
        lambda *refs: forward_kernel(count, *refs),
        in_specs=[in_smem()] + [in_vmem()] * 7,
        out_specs=[in_vmem()] * (count + 11),
        out_shape=[shape((frames, strip, W * C), bf16)] * count
        + [
            shape((frames,) + WINDOWS, bf16),
            shape((frames,) + WINDOWS, bf16),
            shape((frames,) + WINDOWS, bf16),
            shape((frames,) + COARSE_WINDOWS, bf16),
            shape((frames,) + TILES, f32),
            shape((frames,) + COARSE, f32),
            shape((frames,) + SMALL, f32),
        ]
        + [shape(dims, bf16) for dims in OPERANDS[4:]],
        scratch_shapes=[pltpu.VMEM((frames,) + IMAGE, f32), pltpu.VMEM((frames,) + TILES, f32)]
        + [pltpu.VMEM(dims, bf16) for dims in OPERANDS[:4]],
        compiler_params=params(),
        cost_estimate=cost(1 << 10, 1 << 10),
        name="forward",
    )(member, frame_images, frame_stats, styles, biases, *works)


def backward(member, cot, frame_images, styles, stats, middle, down, w_up, w_down, w_two, w_one, count):
    frames = frame_images.shape[0]
    strip = H // count
    return pl.pallas_call(
        lambda *refs: backward_kernel(count, *refs),
        in_specs=[in_smem()] + [in_vmem()] * 11,
        out_specs=[in_vmem()] * (count + 6),
        out_shape=[shape((frames, strip, W * C), bf16)] * count
        + [
            shape((frames,) + TILES, bf16),
            shape((frames,) + TILES, bf16),
            shape((frames,) + TILES, bf16),
            shape((frames,) + COARSE, bf16),
            shape((frames,) + SMALL, f32),
            shape((frames,) + SMALL, f32),
        ],
        scratch_shapes=[
            pltpu.VMEM((frames,) + IMAGE, f32),
            pltpu.VMEM((frames,) + TILES, f32),
            pltpu.VMEM((frames,) + TILES, f32),
            pltpu.VMEM((frames,) + WINDOWS, bf16),
            pltpu.VMEM((frames,) + COARSE, bf16),
        ],
        compiler_params=params(),
        cost_estimate=cost(frames * BLOCK * KEYS * 2 * LANES * 5, frames * (10 << 20)),
        name="backward",
    )(member, *cot, frame_images, styles, stats, middle, down, w_up, w_down, w_two, w_one)


def sum_scratch():
    return [
        pltpu.VMEM((KEYS, 2 * LANES), f32),
        pltpu.VMEM((KEYS, 2 * LANES), f32),
        pltpu.VMEM((6 * LANES, LANES), f32),
        pltpu.VMEM((KEYS + 6 * LANES, 2 * LANES), f32),
    ]


def weight_grads(wins, tiles):
    return pl.pallas_call(
        weight_kernel,
        in_specs=[in_vmem()] * 8,
        out_specs=[in_vmem()] * 4,
        out_shape=[shape((9 * C, C), f32)] * 3 + [shape((18 * C, C), f32)],
        scratch_shapes=sum_scratch(),
        compiler_params=params(),
        name="weights",
    )(*wins, *tiles)


def in_place(space=pl.ANY):
    return pl.BlockSpec(memory_space=space)


def cut_far(member, array):
    array = pltpu.with_memory_space_constraint(array, pltpu.HBM)
    return pl.pallas_call(
        far_kernel,
        in_specs=[in_smem(), in_place(pltpu.HBM)],
        out_specs=in_vmem(),
        out_shape=pltpu.VMEM((array.shape[0] // 2,) + array.shape[1:], array.dtype),
        scratch_shapes=[pltpu.SemaphoreType.DMA((1,))],
        compiler_params=params(),
        name="far",
    )(member, array)


def cut_others(member, frames, cotangent, count):
    half, share = ((frames.shape[0] // n,) + frames.shape[1:] for n in (2, count))
    frames, cotangent = (pltpu.with_memory_space_constraint(array, pltpu.HBM) for array in (frames, cotangent))
    return pl.pallas_call(
        cut_kernel,
        in_specs=[in_smem()] + [in_place(pltpu.HBM)] * 2,
        out_specs=[in_vmem()] * 5,
        out_shape=[pltpu.VMEM(dims, frames.dtype) for dims in (share, share, half, share, share)],
        scratch_shapes=[pltpu.SemaphoreType.DMA((5,))],
        compiler_params=params(),
        name="cut",
    )(member, frames, cotangent)


def cut_near(member, other, far, hint):
    shared = pl.pallas_call(
        share_kernel,
        in_specs=[in_smem(), in_vmem()],
        out_specs=in_vmem(),
        out_shape=shape(other.shape, other.dtype),
        compiler_params=params(),
        name="shared",
    )(member, far)
    mark = pl.pallas_call(
        mark_kernel,
        in_specs=[in_vmem()],
        out_specs=in_vmem(),
        out_shape=shape(SMALL, f32),
        compiler_params=params(),
        cost_estimate=cost(BLOCK * KEYS * 2 * LANES * hint, 1 << 20),
        name="mark",
    )(far)
    return pl.pallas_call(
        near_kernel,
        in_specs=[in_vmem()] * 3,
        out_specs=in_vmem(),
        out_shape=shape(far.shape, other.dtype),
        compiler_params=params(),
        name="near",
    )(other, shared, mark)


def pack(ids, kernels, ada_one, ada_two, act_table, noise_table, biases):
    _, _, size = pack_sizes(kernels[0].shape[0], ada_one.shape[0])
    args = (*[kernel.T for kernel in kernels], ada_one, ada_two, act_table, noise_table, *biases)
    return pl.pallas_call(
        pack_kernel,
        in_specs=[in_smem()] * 3 + [in_vmem()] * len(args),
        out_specs=in_vmem(),
        out_shape=shape((size, LANES), bf16),
        scratch_shapes=[pltpu.VMEM((size, LANES), f32)],
        compiler_params=params(VMEM_MOST),
        cost_estimate=cost(BLOCK * KEYS * 2 * LANES * 30, 1 << 20),
        name="pack",
    )(*ids, *args)


OPERANDS = (
    (KEYS, 2 * LANES),
    (KEYS, 2 * LANES),
    (6 * LANES, LANES),
    (2 * KEYS, 2 * LANES),
    (KEYS, 2 * LANES),
    (KEYS, 2 * LANES),
    (2 * LANES, 2 * LANES),
    (KEYS, 4 * LANES),
)


def prepare(where, packed, mine, other, count, rows, cells, frames):
    found = pl.pallas_call(
        lambda *refs: prepare_kernel(count, rows, cells, *refs),
        in_specs=[in_smem()] + [in_vmem()] * 3,
        out_specs=[in_vmem()] * 6,
        out_shape=[shape((frames,) + SMALL, f32), shape(SMALL, f32), shape((count // 2,) + SMALL, f32)]
        + [shape((n * C, LANES), f32) for n in (9, 18, 9)],
        scratch_shapes=[
            pltpu.VMEM((count * cells, LANES), f32),
            pltpu.VMEM((count * cells, LANES), f32),
            pltpu.VMEM((count * cells // LANES, TABLE_ROWS, LANES), f32),
            pltpu.VMEM(SMALL, f32),
        ],
        compiler_params=params(),
        name="prepare",
    )(where, packed, mine, other)
    return found[0], found[1], found[2], found[3:]


def weight_messages(where, wins, tiles, pieces, bias_sums, ids, count, rows):
    frames = pieces.shape[0]
    size = count // 2 * 3 * rows
    return pl.pallas_call(
        lambda *refs: message_kernel(count, rows, *refs),
        in_specs=[in_smem()] + [in_vmem()] * 11,
        out_specs=[in_vmem()] * 4,
        out_shape=[
            shape((size, LANES), f32),
            shape((PARTS, LANES), f32),
            shape((size, LANES), bf16),
            shape((count * frames, LANES), f32),
        ],
        scratch_shapes=sum_scratch()
        + [pltpu.VMEM((9 * C, LANES), f32), pltpu.VMEM((18 * C, LANES), f32), pltpu.VMEM((9 * C, LANES), f32)],
        compiler_params=params(),
        cost_estimate=cost(frames * BLOCK * KEYS * 2 * LANES * 5, frames * (6 << 20)),
        name="weights",
    )(where, *wins, *tiles, pieces, bias_sums, ids)


def join_messages(where, kept, small, theirs, half, rows, frames):
    return pl.pallas_call(
        lambda *refs: join_kernel(half, rows, frames, *refs),
        in_specs=[in_smem()] + [in_vmem()] * 3,
        out_specs=[in_vmem()] * (1 + half),
        out_shape=[shape((3 * rows, LANES), f32)] + [shape((3 * rows, LANES), bf16)] * half,
        compiler_params=params(),
        name="join",
    )(where, kept, small, theirs)


def reduce_messages(where, own, messages, hots, act_table, noise_table, ada_one, ada_two, rows, cells, frames):
    half = len(messages)
    return pl.pallas_call(
        lambda *refs: reduce_kernel(half, rows, cells, frames, *refs),
        in_specs=[in_smem()] + [in_vmem()] * (half + 6),
        out_specs=in_vmem(),
        out_shape=shape((3 * rows + 2 * cells, LANES), bf16),
        scratch_shapes=[
            pltpu.VMEM((half * frames, LANES), f32),
            pltpu.VMEM((half * frames, LANES), f32),
            pltpu.VMEM((TABLE_ROWS, cells), f32),
            pltpu.VMEM((LANES, LANES), f32),
            pltpu.VMEM((LANES, LANES), f32),
        ],
        compiler_params=params(),
        name="reduce",
    )(where, own, *messages, hots, act_table, noise_table, ada_one, ada_two)


def finish(parts, rows, cells, width):
    act_grad, noise_grad, one, two, *rest = pl.pallas_call(
        lambda *refs: finish_kernel(rows, cells, len(parts), *refs),
        in_specs=[in_vmem()] * len(parts),
        out_specs=[in_vmem()] * 12,
        out_shape=[
            shape((NACT, cells), f32),
            shape((NLEV, cells), f32),
            shape((cells, LANES), f32),
            shape((cells, LANES), f32),
            shape((C, rows), f32),
            shape((C, rows), f32),
            shape((C, rows), f32),
            shape((C, 2 * rows), f32),
        ]
        + [shape((width,), f32)] * 4,
        compiler_params=params(),
        name="finish",
    )(*parts)
    return (act_grad, noise_grad, one, two, *[grad.T for grad in rest[:4]], *rest[4:])


def collect_kernel(member_ref, *refs):
    strips, out = refs[:-1], refs[-1]
    for offset, strip in enumerate(strips):
        out[member_ref[0] ^ offset, 0] = strip[0].astype(out.dtype)


def trade_strips(strips):
    return tuple(trade(strip, offset) for offset, strip in enumerate(strips))


def collect_strips(member_box, strips, kind):
    count = len(strips)
    frames, rows, columns = strips[0].shape
    whole_strips = pl.pallas_call(
        collect_kernel,
        grid=(frames,),
        in_specs=[in_smem()] + [pl.BlockSpec((1, rows, columns), lambda f: (f, 0, 0))] * count,
        out_specs=pl.BlockSpec((count, 1, rows, columns), lambda f: (0, f, 0, 0)),
        out_shape=shape((count, frames, rows, columns), kind),
        compiler_params=params(),
        name="collect",
    )(member_box, *strips)
    return whole_strips.reshape(count * frames, rows, columns)


def twice(values):
    return jnp.concatenate([values, values], axis=-1)


def pad_small(rows):
    stacked = jnp.stack(rows, axis=-2)
    gaps = [(0, 0)] * (stacked.ndim - 2) + [(0, 8 - len(rows)), (0, 0)]
    return jnp.pad(stacked, gaps)


def trade(value, offset):
    if offset == 0:
        return value
    count = lax.axis_size("rows")
    return lax.ppermute(value, "rows", [(i, i ^ offset) for i in range(count)])


def half_trade(value, at):
    count, members = lax.axis_size("seq"), lax.axis_size("rows")
    pairs = []
    for place in range(count):
        for member in range(members):
            offset = sides(count)[member % 2][at]
            if offset:
                pairs.append((place * members + member, (place ^ offset) * members + member))
    return lax.ppermute(value, ("seq", "rows"), pairs)


def layers(member_box, frame_images, frame_stats, cot_fetched, styles, bias_rows, works):
    count = lax.axis_size("rows")
    *out, win_one, win_two, win_level, win_coarse, middle, down, stats, b_one, b_two, b_down, b_up = forward(
        member_box, frame_images, frame_stats, styles, bias_rows, works, count
    )
    out = trade_strips(out)
    down, cot_fetched = lax.optimization_barrier((down, cot_fetched))
    cot = gather_frames(member_box, *cot_fetched)
    *grad_strips, tile_out, tile_level, tile_mid, coarse_pairs, pieces, bias_sums = backward(
        member_box, cot, frame_images, styles, stats, middle, down, b_up, b_down, b_two, b_one, count
    )
    grad_strips = trade_strips(grad_strips)
    wins = (win_one, win_two, win_level, win_coarse)
    tiles = (tile_out, tile_level, tile_mid, coarse_pairs)
    return out, grad_strips, wins, tiles, pieces, bias_sums


def local_direct(
    frames,
    cotangent,
    actions,
    noise_ids,
    valid,
    act_table,
    noise_table,
    ada_one,
    ada_two,
    conv_one,
    conv_two,
    down_kernel,
    up_kernel,
    bias_one,
    bias_two,
    bias_down,
    bias_up,
):
    member = lax.axis_index("rows").astype(jnp.int32)
    place = lax.axis_index("seq").astype(jnp.int32)
    count = lax.axis_size("seq")
    share = frames.shape[0] // lax.axis_size("rows")
    rows, cells, width = conv_one.shape[0], ada_one.shape[0], bias_one.shape[0]
    half = count // 2
    member_box = member.reshape(1)
    where = jnp.stack([place, member])
    ids = (actions, noise_ids, valid)
    kernels = (conv_one, conv_two, down_kernel, up_kernel)
    biases = (bias_one, bias_two, bias_down, bias_up)
    far = trade(cut_far(member_box, frames), 2)
    packed = pack(ids, kernels, ada_one, ada_two, act_table, noise_table, biases)
    mine = jnp.concatenate([half_trade(packed, at) for at in range(half)], axis=0)
    other = trade(mine, 1)
    own, near, cot_far, *cot_rest = cut_others(member_box, frames, cotangent, lax.axis_size("rows"))
    cot_fetched = (trade(cot_far, 2), *cot_rest)
    frame_images, frame_stats = gather_frames(member_box, far, own, near, FAR_HINT)
    styles, bias_rows, group_ids, works = prepare(where, packed, mine, other, count, rows, cells, share)
    out, grad_strips, wins, tiles, pieces, bias_sums = layers(
        member_box, frame_images, frame_stats, cot_fetched, styles, bias_rows, works
    )
    kept, small, theirs, hots = weight_messages(where, wins, tiles, pieces, bias_sums, group_ids, count, rows)
    theirs, out = lax.optimization_barrier((theirs, out))
    own, *messages = join_messages(where, kept, small, trade(theirs, 1), half, rows, share)
    received = [half_trade(message, at) for at, message in enumerate(messages)]
    result = collect_strips(member_box, out, bf16)
    frames_grad = collect_strips(member_box, grad_strips, f32)
    received, result, frames_grad = lax.optimization_barrier((received, result, frames_grad))
    sums = reduce_messages(
        where, own, received, hots, act_table, noise_table, ada_one, ada_two, rows, cells, 2 * share
    )
    pair = (sums.astype(f32) + trade(sums, 1).astype(f32)).astype(bf16)
    parts = [pair, trade(pair, 2)]
    return (result, frames_grad, *finish(parts, rows, cells, width))


def local_general(
    frames,
    cotangent,
    actions,
    noise_ids,
    valid,
    act_table,
    noise_table,
    ada_one,
    ada_two,
    conv_one,
    conv_two,
    down_kernel,
    up_kernel,
    bias_one,
    bias_two,
    bias_down,
    bias_up,
):
    member = lax.axis_index("rows").astype(jnp.int32)
    share = frames.shape[0] // lax.axis_size("rows")
    member_box = member.reshape(1)

    def gathered(value, axis):
        return lax.all_gather(value, "seq", axis=axis, tiled=True)

    far = trade(cut_far(member_box, frames), 2)
    own, near, cot_far, *cot_rest = cut_others(member_box, frames, cotangent, lax.axis_size("rows"))
    cot_fetched = (trade(cot_far, 2), *cot_rest)
    frame_images, frame_stats = gather_frames(member_box, far, own, near)
    act_full = gathered(act_table, 1)
    noise_full = gathered(noise_table, 1)
    ada_full = gathered(jnp.concatenate([ada_one, ada_two], axis=1), 0).astype(f32)
    biases = gathered(jnp.stack([bias_one, bias_two, bias_down, bias_up]), 1).astype(f32)
    wide = lambda kernel: gathered(kernel, 0).astype(f32)
    works = (
        jnp.concatenate([wide(conv_one), wide(conv_two)], axis=1),
        twice(wide(up_kernel)),
        twice(wide(down_kernel)),
    )

    own = lambda ids: lax.dynamic_slice_in_dim(ids, member * share, share)
    own_actions, own_noise, own_valid = own(actions), own(noise_ids), own(valid)
    action_hot = (own_actions[:, None] == jnp.arange(NACT, dtype=jnp.int32)[None, :]).astype(f32) * own_valid[
        :, None
    ].astype(f32)
    noise_hot = (own_noise[:, None] == jnp.arange(NLEV, dtype=jnp.int32)[None, :]).astype(f32)
    embed = jnp.dot(action_hot, act_full.astype(f32), precision=precise) + jnp.dot(
        noise_hot, noise_full.astype(f32), precision=precise
    )
    style = jnp.dot(embed, ada_full, precision=precise)
    styles = pad_small(
        [
            twice(1.0 + style[:, :C]),
            twice(style[:, C : 2 * C]),
            twice(1.0 + style[:, 2 * C : 3 * C]),
            twice(style[:, 3 * C :]),
        ]
    )
    bias_rows = pad_small([twice(biases[k]) for k in range(4)])
    out, grad_strips, wins, tiles, pieces, bias_sums = layers(
        member_box, frame_images, frame_stats, cot_fetched, styles, bias_rows, works
    )
    g_one, g_two, g_down, g_up = weight_grads(wins, tiles)
    result = collect_strips(member_box, out, bf16)
    frames_grad = collect_strips(member_box, grad_strips, f32)

    pieces_one = jnp.concatenate([pieces[:, 0, :C], pieces[:, 1, :C]], axis=1)
    pieces_two = jnp.concatenate([pieces[:, 2, :C], pieces[:, 3, :C]], axis=1)
    ada_one_grad = jnp.dot(embed.T, pieces_one, precision=precise)
    ada_two_grad = jnp.dot(embed.T, pieces_two, precision=precise)
    embed_grad = jnp.dot(jnp.concatenate([pieces_one, pieces_two], axis=1), ada_full.T, precision=precise)
    act_table_grad = jnp.dot(action_hot.T, embed_grad, precision=precise)
    noise_table_grad = jnp.dot(noise_hot.T, embed_grad, precision=precise)
    bias_total = jnp.sum(bias_sums, axis=0)[:4, :C]

    def shard(value, axis):
        return lax.psum_scatter(value, "seq", scatter_dimension=axis, tiled=True)

    shards = (
        shard(act_table_grad, 1),
        shard(noise_table_grad, 1),
        shard(ada_one_grad, 0),
        shard(ada_two_grad, 0),
        shard(g_one, 0),
        shard(g_two, 0),
        shard(g_down, 0),
        shard(g_up, 0),
        shard(bias_total[0], 0),
        shard(bias_total[1], 0),
        shard(bias_total[2], 0),
        shard(bias_total[3], 0),
    )
    return (result, frames_grad) + lax.psum(shards, "rows")


def fits_direct(mesh):
    count = mesh.shape["seq"]
    rows, cells = 9 * C // count, 256 // count
    return count in (2, 4, 8) and rows % 8 == 0 and rows >= ID_ROW + 8 and cells % 8 == 0 and mesh.shape["rows"] == 4


def solution(mesh):
    in_specs = (
        P("seq", "rows", None),
        P("seq", "rows", None),
        P("seq"),
        P("seq"),
        P("seq"),
        P(None, "seq"),
        P(None, "seq"),
        P("seq", None),
        P("seq", None),
        P("seq", None),
        P("seq", None),
        P("seq", None),
        P("seq", None),
        P("seq"),
        P("seq"),
        P("seq"),
        P("seq"),
    )
    out_specs = (
        P("seq", "rows", None),
        P("seq", "rows", None),
        P(None, "seq"),
        P(None, "seq"),
        P("seq", None),
        P("seq", None),
        P("seq", None),
        P("seq", None),
        P("seq", None),
        P("seq", None),
        P("seq"),
        P("seq"),
        P("seq"),
        P("seq"),
    )
    local = local_direct if fits_direct(mesh) else local_general
    return jax.shard_map(local, mesh=mesh, in_specs=in_specs, out_specs=out_specs, check_vma=False)
```

```python
import jax
import jax.numpy as jnp
from jax import lax
from jax.experimental import pallas as pl
from jax.experimental.pallas import tpu as pltpu
from jax.sharding import PartitionSpec as P

C = 64
NACT = 18
GROUPS = 32
NLEV = 32
H = 64
W = 64
PAIRS = W // 2
HALF = H // 2
LANES = 2 * C
BLOCK = PAIRS * HALF
MEMBERS = float(H * W * (C // GROUPS))
EPS = 1e-05

precise = lax.Precision.HIGHEST
f32 = jnp.float32
bf16 = jnp.bfloat16
VMEM_LIMIT = 16 * 2**20
VMEM_MOST = 60 * 2**20


def lane_ids(shape):
    return lax.broadcasted_iota(jnp.int32, shape, len(shape) - 1)


def swap_halves(x):
    return pltpu.roll(x, C, axis=x.ndim - 1)


def row_before(x):
    rows = lax.broadcasted_iota(jnp.int32, x.shape, 0)
    return jnp.where(rows == 0, 0.0, pltpu.roll(x, 1, axis=0))


def row_after(x):
    rows = lax.broadcasted_iota(jnp.int32, x.shape, 0)
    return jnp.where(rows == x.shape[0] - 1, 0.0, pltpu.roll(x, x.shape[0] - 1, axis=0))


def both_parities(x):
    x = jnp.broadcast_to(x, (8, LANES))
    return x + swap_halves(x)


def group_sum(x):
    even = lane_ids(x.shape) % 2 == 0
    return x + jnp.where(even, pltpu.roll(x, LANES - 1, axis=1), pltpu.roll(x, 1, axis=1))


def total(x):
    return jnp.sum(x, axis=0, keepdims=True)


def over_pairs(body, carry):
    for j in range(PAIRS):
        carry = body(j, carry)
    return carry


def build_windows(windows, tile):
    low_lanes = lane_ids((HALF, LANES)) < C
    zero = jnp.zeros((HALF, LANES), f32)

    def write(j, even, odd):
        windows[0, j] = row_before(odd).astype(bf16)
        windows[1, j] = even.astype(bf16)
        windows[2, j] = odd.astype(bf16)
        windows[3, j] = row_after(even).astype(bf16)

    def body(j, carry):
        even_past, odd_past = carry
        even = swap_halves(tile(0, j))
        odd = swap_halves(tile(1, j))
        write(j, jnp.where(low_lanes, even_past, even), jnp.where(low_lanes, odd_past, odd))
        return even, odd

    even, odd = over_pairs(body, (zero, zero))
    write(PAIRS, jnp.where(low_lanes, even, 0.0), jnp.where(low_lanes, odd, 0.0))


def window_operand(windows, slots):
    parts = []
    for slot in slots:
        for shift in (0, 1):
            parts.append(windows[slot, shift : shift + PAIRS].reshape(BLOCK, LANES))
    return jnp.concatenate(parts, axis=1)


def matmul(left, right):
    return jnp.dot(left, right, preferred_element_type=f32)


def tiles_of(y):
    return y.reshape(PAIRS, HALF, LANES)


def norm_stats(sums, squares):
    average = group_sum(both_parities(sums)) / MEMBERS
    variance = group_sum(both_parities(squares)) / MEMBERS - average * average
    return average, lax.rsqrt(jnp.maximum(variance, 0.0) + EPS)


def strip_start(member, offset, strip):
    return pl.multiple_of((member ^ offset) * strip, strip)


def load_strips(member, strips, image):
    for offset, strip in enumerate(strips):
        rows = strip.shape[0]
        start = strip_start(member, offset, rows)
        for j in range(PAIRS):
            image[j, pl.ds(start, rows), :] = strip[:, j * LANES : (j + 1) * LANES].astype(f32)


def store_strips(member, image, f, strips, pairs=range(PAIRS)):
    for offset, strip in enumerate(strips):
        rows = strip.shape[1]
        start = strip_start(member, offset, rows)
        for j in pairs:
            strip[f, :, j * LANES : (j + 1) * LANES] = image[j, pl.ds(start, rows), :].astype(strip.dtype)


def parity_rows(image, parity, j):
    return image[j, pl.ds(parity, HALF, stride=2), :]


def staggered(steps):
    steps = list(steps)
    started = []
    while steps or started:
        if steps:
            started.append(steps.pop(0))
        for step in list(started):
            if next(step, "end") == "end":
                started.remove(step)


def gather_frame(member, strips, image, stats):
    load_strips(member, strips, image)

    def add_stats(j, carry):
        x = image[j]
        s, q = carry
        return s + x, q + x * x

    zero = jnp.zeros((H, LANES), f32)
    s, q = over_pairs(add_stats, (zero, zero))
    average, inverse = norm_stats(total(s), total(q))
    stats[0:1, :] = average[0:1]
    stats[1:2, :] = inverse[0:1]
    stats[2:3, :] = both_parities(total(s))[0:1]
    stats[3:8, :] = jnp.zeros((5, LANES), f32)


def gather_kernel(member_ref, own, far, near, images, all_stats):
    member = member_ref[0]
    frames = images.shape[0]
    first = member % 2 * frames
    for f in range(frames):
        strips = (own.at[f], near.at[f], far.at[first + f], near.at[frames + f])
        gather_frame(member, strips, images.at[f], all_stats.at[f])


def forward_kernel(count, *refs):
    member_ref, frame_images, frame_stats, styles, biases, work_pair, work_up, work_down = refs[:8]
    out = refs[8 : 8 + count]
    outs = refs[8 + count : 15 + count]
    turned_operands = refs[15 + count : 19 + count]
    images, levels, w_one, w_two, w_down, w_up = refs[19 + count :]
    member = member_ref[0]
    works = {"one": work_pair, "two": work_pair, "down": work_down, "up": work_up}
    found = {}

    def block(name, row):
        k = works[name][row : row + C, :]
        low = lane_ids(k.shape) < C
        if name == "two":
            return jnp.where(low, swap_halves(k), k)
        return jnp.where(low, k, swap_halves(k))

    def turned_pairs(name):
        work = works[name]
        key = "one" if name == "two" else name
        if key not in found:
            blocks = [work[at : min(at + LANES, work.shape[0]), :] for at in range(0, work.shape[0], LANES)]
            found[key] = [below(block, LANES).T for block in blocks]
        return [k[C:] if name == "two" else k[:C] for k in found[key]]

    def operands():
        yield from write_forward_operands(block, w_one, w_two, w_down, w_up)
        yield from write_backward_operands(turned_pairs, *turned_operands)

    low_lanes = lane_ids((HALF, LANES)) < C

    def frame(f):
        win_one, win_two, win_level, win_coarse, middle, down, stats = (ref.at[f] for ref in outs)
        frame_image, image, level, style = frame_images.at[f], images.at[f], levels.at[f], styles.at[f]
        average_one, inverse_one = frame_stats[f, 0:1, :], frame_stats[f, 1:2, :]
        gain_one = inverse_one * style[0:1, :]
        half_gain = 0.5 * gain_one
        half_shift = 0.5 * (style[1:2, :] - average_one * gain_one)

        def act_one(parity, j):
            h = parity_rows(frame_image, parity, j) * half_gain + half_shift
            return h * jnp.tanh(h) + h

        build_windows(win_one, act_one)
        yield
        y = matmul(window_operand(win_one, range(4)), w_one[...])
        sums = jnp.zeros((1, LANES), f32)
        squares = jnp.zeros((1, LANES), f32)
        for a in range(2):
            v = y[:, a * LANES : (a + 1) * LANES] + biases[0:1, :]
            sums = sums + total(v)
            squares = squares + total(v * v)
            middle[a] = tiles_of(v)
        yield
        average_two, inverse_two = norm_stats(sums, squares)
        stats[0:1, :] = average_one
        stats[1:2, :] = inverse_one
        stats[2:3, :] = average_two[0:1]
        stats[3:4, :] = inverse_two[0:1]
        stats[4:8, :] = jnp.zeros((4, LANES), f32)
        gain_two = inverse_two * style[2:3, :]
        half_gain_two = 0.5 * gain_two[0:1]
        half_shift_two = 0.5 * (style[3:4, :] - average_two[0:1] * gain_two[0:1])

        def act_two(parity, j):
            h = middle[parity, j] * half_gain_two + half_shift_two
            return h * jnp.tanh(h) + h

        build_windows(win_two, act_two)
        yield
        y = matmul(window_operand(win_two, range(4)), w_two[...])
        for a in range(2):
            v = y[:, a * LANES : (a + 1) * LANES] + biases[1:2, :]
            level[a] = tiles_of(v) + frame_image[:, pl.ds(a, HALF, stride=2), :]
        yield
        build_windows(win_level, lambda parity, j: level[parity, j])
        yield
        operand = window_operand(win_level, range(4))
        y = matmul(operand[:, : 6 * LANES], w_down[...]) + biases[2:3, :]
        down[...] = tiles_of(y)
        yield

        def write_coarse(j, cells):
            win_coarse[0, j] = row_before(cells).astype(bf16)
            win_coarse[1, j] = cells.astype(bf16)
            win_coarse[2, j] = row_after(cells).astype(bf16)

        def coarse_body(j, past):
            h = down[j] * 0.5
            coarse = h * jnp.tanh(h) + h
            write_coarse(j, jnp.where(low_lanes, past, coarse))
            return coarse

        past = over_pairs(coarse_body, jnp.zeros((HALF, LANES), f32))
        write_coarse(PAIRS, jnp.where(low_lanes, past, 0.0))
        yield
        operand = window_operand(win_level, range(4))
        coarse_operand = window_operand(win_coarse, (0, 1, 1, 2))
        y = matmul(operand, w_up[: 16 * C, :]) + matmul(coarse_operand, w_up[16 * C :, :])
        for a in range(2):
            v = y[:, a * LANES : (a + 1) * LANES] + biases[3:4, :]
            image[:, pl.ds(a, HALF, stride=2), :] = tiles_of(v) + level[a]
        yield
        store_strips(member, image, f, out)

    staggered([operands()] + [frame(f) for f in range(styles.shape[0])])


def slope_twice(h):
    t = jnp.tanh(h)
    return (1.0 + t) + h * (1.0 - t * t)


def backward_kernel(count, *refs):
    member_ref = refs[0]
    cot_images, cot_stats, frame_images, styles, all_stats, all_middle, all_down = refs[1:8]
    w_up, w_down, w_two, w_one = refs[8:12]
    out = refs[12 : 12 + count]
    outs = refs[12 + count : 18 + count]
    scratch = refs[18 + count :]
    member = member_ref[0]
    low_lanes = lane_ids((HALF, LANES)) < C

    def frame(f):
        tile_out, tile_level, tile_mid, coarse_pairs, pieces, bias_sums = (ref.at[f] for ref in outs)
        image, level_grad, pre_grad, windows, coarse_below = (ref.at[f] for ref in scratch)
        style, stats, middle, down, frame_image = (
            ref.at[f] for ref in (styles, all_stats, all_middle, all_down, frame_images)
        )
        cot_image = cot_images.at[f]

        def out_tile(parity, j):
            x = parity_rows(cot_image, parity, j)
            tile_out[parity, j] = x.astype(bf16)
            return x

        build_windows(windows, out_tile)
        yield
        y = matmul(window_operand(windows, range(4)), w_up[...])
        for a in range(2):
            level_grad[a] = (
                tiles_of(y[:, (2 + a) * LANES : (3 + a) * LANES]) + cot_image[:, pl.ds(a, HALF, stride=2), :]
            )
        coarse = y[:, :LANES] + y[:, LANES : 2 * LANES]
        pre_grad[0] = tiles_of(coarse)
        yield

        def coarse_body(t, carry):
            after, sums = carry
            j = PAIRS - 1 - t
            g = pre_grad[0, j]
            g = g + swap_halves(g)
            h = down[j] * 0.5
            d = g * slope_twice(h)
            pair = jnp.where(low_lanes, d, after)
            coarse_pairs[j] = pair.astype(bf16)
            coarse_below[j] = row_after(pair).astype(bf16)
            return d, sums + d

        zero = jnp.zeros((HALF, LANES), f32)
        _, sums = over_pairs(coarse_body, (zero, zero))
        bias_down_sum = jnp.broadcast_to(total(sums), (8, LANES))
        operand = jnp.concatenate(
            [coarse_pairs[...].reshape(BLOCK, LANES), coarse_below[...].reshape(BLOCK, LANES)], axis=1
        )
        y = matmul(operand, w_down[...])
        sums = jnp.zeros((1, LANES), f32)
        for a in range(2):
            v = y[:, a * LANES : (a + 1) * LANES] + level_grad[a].reshape(BLOCK, LANES)
            sums = sums + total(v)
            level_grad[a] = tiles_of(v)
        bias_two_sum = both_parities(sums)

        def level_tile(parity, j):
            x = level_grad[parity, j]
            tile_level[parity, j] = x.astype(bf16)
            return x

        build_windows(windows, level_tile)
        yield

        def norm_slopes(y, value, k):
            average, inverse = stats[2 * k : 2 * k + 1, :], stats[2 * k + 1 : 2 * k + 2, :]
            gain = inverse * style[2 * k : 2 * k + 1, :]
            half_gain = 0.5 * gain
            half_shift = 0.5 * style[2 * k + 1 : 2 * k + 2, :]
            scale_sum = jnp.zeros((1, LANES), f32)
            shift_sum = jnp.zeros((1, LANES), f32)
            for a in range(2):
                v = value(a) - average
                g = y[:, a * LANES : (a + 1) * LANES] * slope_twice(v * half_gain + half_shift)
                pre_grad[a] = tiles_of(g)
                shift_sum = shift_sum + total(g)
                scale_sum = scale_sum + total(g * v)
            scale_sum, shift_sum = both_parities(scale_sum * inverse), both_parities(shift_sum)
            factor = style[2 * k : 2 * k + 1, :]
            center = group_sum(factor * shift_sum) / MEMBERS
            tilt = group_sum(factor * scale_sum) / MEMBERS
            slope = (inverse * tilt)[0:1] * inverse
            return scale_sum, shift_sum, gain, slope, slope * average - (inverse * center)[0:1]

        y = matmul(window_operand(windows, range(4)), w_two[...])
        scale_two, shift_two, gain_two, slope_two, constant_two = norm_slopes(
            y, lambda a: middle[a].reshape(BLOCK, LANES), 1
        )
        yield
        row_sums = [zero]

        def mid_tile(parity, j):
            x = pre_grad[parity, j] * gain_two + (constant_two - middle[parity, j] * slope_two)
            tile_mid[parity, j] = x.astype(bf16)
            row_sums[0] = row_sums[0] + x
            return x

        build_windows(windows, mid_tile)
        bias_one_sum = both_parities(total(row_sums[0]))
        yield
        y = matmul(window_operand(windows, range(4)), w_one[...])
        scale_one, shift_one, gain_one, slope_one, constant_one = norm_slopes(
            y, lambda a: frame_image[:, pl.ds(a, HALF, stride=2), :].reshape(BLOCK, LANES), 0
        )
        yield

        def frame_body(j, carry):
            for parity in range(2):
                x = parity_rows(frame_image, parity, j)
                g = pre_grad[parity, j] * gain_one + (constant_one - x * slope_one) + level_grad[parity, j]
                image[j, pl.ds(parity, HALF, stride=2), :] = g
            store_strips(member, image, f, out, (j,))
            return carry

        over_pairs(frame_body, 0)
        for k, value in enumerate((scale_one, shift_one, scale_two, shift_two)):
            pieces[k : k + 1, :] = value[0:1]
        pieces[4:8, :] = jnp.zeros((4, LANES), f32)
        for k, value in enumerate((bias_one_sum, bias_two_sum, bias_down_sum, cot_stats[f, 2:3, :])):
            bias_sums[k : k + 1, :] = value[0:1]
        bias_sums[4:8, :] = jnp.zeros((4, LANES), f32)

    staggered(frame(f) for f in range(styles.shape[0]))


def outer(left, right):
    return lax.dot_general(left, right, (((0,), (0,)), ((), ())), preferred_element_type=f32)


def accumulate(wins, tiles, sums, folds):
    win_one, win_two, win_level, win_coarse = wins
    tile_out, tile_level, tile_mid, coarse_pairs = tiles
    sum_one, sum_two, sum_down, sum_up = sums
    cells = win_one.shape[0] * BLOCK

    def operand(windows, slots):
        parts = []
        for slot in slots:
            for shift in (0, 1):
                parts.append(windows[:, slot, shift : shift + PAIRS].reshape(cells, LANES))
        return jnp.concatenate(parts, axis=1)

    def blocks(tiles):
        return jnp.concatenate([tiles[:, a].reshape(cells, LANES) for a in range(2)], axis=1)

    out_blocks = blocks(tile_out)
    sum_up[16 * C :, :] = outer(operand(win_coarse, range(3)), out_blocks)
    sum_up[: 16 * C, :] = outer(operand(win_level, range(4)), out_blocks)
    sum_down[...] = outer(operand(win_level, range(3)), coarse_pairs[...].reshape(cells, LANES))
    sum_two[...] = outer(operand(win_two, range(4)), blocks(tile_level))
    folds[0]()
    sum_one[...] = outer(operand(win_one, range(4)), blocks(tile_mid))
    folds[1]()
    folds[2]()


def taps():
    return [(p, q, (3 * p + q) * C) for p in range(3) for q in range(3)]


def fold(sums, p, q):
    return fold_slots(sums, 0, p, q, range(4))


def fold_coarse(sums, p, q):
    return fold_slots(sums, 16 * C, p, q, (0, 1, 1, 2))


def fold_slots(sums, base, p, q, slots):
    halves = []
    for b in range(2):
        rows = [base + (slots[a + p] * 4 + b + q) * C for a in range(2)]
        halves.append(sums[rows[0] : rows[0] + C, :LANES] + sums[rows[1] : rows[1] + C, LANES:])
    return halves[0] + swap_halves(halves[1])


def weight_kernel(*refs):
    wins, tiles, grads, sums = refs[:4], refs[4:8], refs[8:12], refs[12:]
    g_one, g_two, g_down, g_up = grads
    sum_one, sum_two, sum_down, sum_up = sums

    def fold_up():
        for p, q, at in taps():
            g_up[2 * at : 2 * at + C, :] = fold_coarse(sum_up, p, q)[:, :C]
            g_up[2 * at + C : 2 * at + 2 * C, :] = fold(sum_up, p, q)[:, :C]
            place = (p * 4 + q) * C
            g_down[at : at + C, :] = sum_down[place : place + C, :C]

    def fold_two():
        for p, q, at in taps():
            g_two[at : at + C, :] = fold(sum_two, p, q)[:, :C]

    def fold_one():
        for p, q, at in taps():
            g_one[at : at + C, :] = fold(sum_one, p, q)[:, :C]

    accumulate(wins, tiles, sums, (fold_up, fold_two, fold_one))


PARTS = 16
FAR_HINT = 90
PAIR_PARTS = 24


def three_parts(exact):
    high = exact.astype(bf16).astype(f32)
    rest = exact - high
    mid = rest.astype(bf16).astype(f32)
    return jnp.concatenate([high, mid, rest - mid], axis=0)


def below(block, rows):
    if block.shape[0] == rows:
        return block
    return jnp.concatenate([block, jnp.zeros((rows - block.shape[0], LANES), f32)], axis=0)


def message_kernel(count, rows, *refs):
    where_ref, wins, tiles = refs[0], refs[1:5], refs[5:9]
    pieces, bias_sums, ids, kept, small, theirs, hots = refs[9:16]
    sums = refs[16:20]
    g_pair, g_up, g_down = refs[20:]
    sum_one, sum_two, sum_down, sum_up = sums
    taken = 2 * pieces.shape[0]
    for at in range(ids.shape[0]):
        write_hots(hots, at * taken, where_ref[1] // 2 * taken, taken, ids[at])
    low_lanes = lane_ids((C, LANES)) < C

    def fold_up():
        for p, q, at in taps():
            g_up[2 * at : 2 * at + C, :] = fold_coarse(sum_up, p, q)
            g_up[2 * at + C : 2 * at + 2 * C, :] = fold(sum_up, p, q)
            place = (p * 4 + q) * C
            g_down[at : at + C, :] = sum_down[place : place + C, :]

    def fold_two():
        for p, q, at in taps():
            g_pair[at : at + C, :] = swap_halves(fold(sum_two, p, q))

    def fold_one():
        for p, q, at in taps():
            g_pair[at : at + C, :] = jnp.where(low_lanes, fold(sum_one, p, q), g_pair[at : at + C, :])

    accumulate(wins, tiles, sums, (fold_up, fold_two, fold_one))
    frames = pieces.shape[0]
    small[...] = jnp.zeros_like(small)
    total_bias = bias_sums[0, 0:4, :]
    for f in range(frames):
        small[4 * f : 4 * f + 4, :] = pieces[f, 0:4, :]
        if f > 0:
            total_bias = total_bias + bias_sums[f, 0:4, :]
    small[4 * frames : 4 * frames + 4, :] = total_bias
    sent = below(three_parts(small[...]), rows)
    low_lanes = lane_ids((rows, LANES)) < C
    half = count // 2
    for at in range(half):
        for ref, mine in ((kept, True), (theirs, False)):
            start = pl.multiple_of(seq_owner(where_ref[0], where_ref[1], half, at, mine) * rows, 8)
            blocks = (
                g_pair[pl.ds(start, rows), :],
                jnp.where(
                    low_lanes,
                    g_up[pl.ds(pl.multiple_of(2 * start, 8), rows), :],
                    swap_halves(g_up[pl.ds(pl.multiple_of(2 * start + rows, 8), rows), :]),
                ),
                jnp.where(low_lanes, g_down[pl.ds(start, rows), :], 0.0 if mine else sent),
            )
            ref[at * 3 * rows : (at + 1) * 3 * rows, :] = jnp.concatenate(blocks, axis=0).astype(ref.dtype)


def join_kernel(half, rows, frames, where_ref, kept, small, theirs, own, *messages):
    first = where_ref[1] % 2 == 0
    at = 2 * rows
    other = theirs[at : at + 3 * PARTS, :].astype(f32)
    other = other[:PARTS] + other[PARTS : 2 * PARTS] + other[2 * PARTS :]
    mine = small[...]
    n = 4 * frames
    exact = jnp.concatenate(
        [
            jnp.where(first, mine[:n], other[:n]),
            jnp.where(first, other[:n], mine[:n]),
            mine[n : n + 4] + other[n : n + 4],
            jnp.zeros((PAIR_PARTS - 2 * n - 4, LANES), f32),
        ],
        axis=0,
    )
    low_lanes = lane_ids((rows, LANES)) < C
    sent = below(three_parts(exact), rows)
    size = 3 * rows
    for k, message in enumerate(messages):
        block = kept[k * size : (k + 1) * size, :] + theirs[k * size : (k + 1) * size, :].astype(f32)
        message[:at, :] = block[:at].astype(bf16)
        message[at:, :] = jnp.where(low_lanes, block[at:], sent).astype(bf16)
        if k == half - 1:
            own[:at, :] = block[:at]
            own[at:, :] = jnp.where(low_lanes, block[at:], below(exact, rows))


def reduce_kernel(half, rows, cells, frames, *refs):
    where_ref, own = refs[:2]
    messages = refs[2 : 2 + half]
    hots, act_table, noise_table, ada_one, ada_two, out, pieces_one, pieces_two, table, high_one, high_two = refs[2 + half :]
    place, member = where_ref[0], where_ref[1]
    taken = 4 * frames
    bias = jnp.zeros((4, LANES), f32)
    sums = None
    lanes = lane_ids((1, LANES))
    low_lanes = lanes < C
    at = 2 * rows
    for k, ref in enumerate(messages):
        message = ref[...].astype(f32)
        if k == half - 1:
            message = jnp.where(member % 2 == 0, own[...], message)
        sums = message if sums is None else sums + message
        small = (
            message[at : at + PAIR_PARTS]
            + message[at + PAIR_PARTS : at + 2 * PAIR_PARTS]
            + message[at + 2 * PAIR_PARTS : at + 3 * PAIR_PARTS]
        )
        turned = swap_halves(small)
        bias = bias + small[taken : taken + 4]
        for f in range(frames):
            row = k * frames + f
            for kind, piece in ((0, pieces_one), (2, pieces_two)):
                low, high = 4 * f + kind, 4 * f + kind + 1
                piece[row : row + 1, :] = jnp.where(low_lanes, turned[low : low + 1], small[high : high + 1])
    hot = hots[:, :TABLE_ROWS]
    table[...] = jnp.zeros_like(table)
    table[ACT_ROW : ACT_ROW + NACT, :] = act_table[...].astype(f32)
    table[NOISE_ROW : NOISE_ROW + NLEV, :] = noise_table[...].astype(f32)
    embed = matmul(hot.astype(bf16), table[...].astype(bf16))

    def exact(left, right, dims):
        return lax.dot_general(left, right, (dims, ((), ())), precision=precise, preferred_element_type=f32)

    one, two = pieces_one[...], pieces_two[...]
    for ref, ada in ((high_one, ada_one), (high_two, ada_two)):
        ref[...] = jnp.zeros_like(ref)
        ref[C : C + cells, :] = ada[...].astype(f32)
    pieces = jnp.concatenate([one, two], axis=1)
    embed_grad = exact(pieces, jnp.concatenate([high_one[...], high_two[...]], axis=1), ((1,), (1,)))
    ada_grads = exact(embed, pieces, ((0,), (0,)))
    width = C // (2 * half)
    bias = pltpu.roll(jnp.concatenate([bias, bias], axis=0), (LANES - place * width) % LANES, axis=1)
    extra = below(jnp.concatenate([exact(hot, embed_grad, ((0,), (0,))), bias], axis=0), rows)
    at = 2 * rows
    blocks = (
        sums[:at],
        jnp.where(lane_ids((rows, LANES)) < C, sums[at:], extra),
        ada_grads[:, :LANES],
        ada_grads[:, LANES:],
    )
    out[...] = jnp.concatenate(blocks, axis=0).astype(out.dtype)


def finish_kernel(rows, cells, count, *refs):
    parts, outs = [ref[...].astype(f32) for ref in refs[:count]], refs[count:]
    act_grad, noise_grad, ada_one, ada_two, g_one, g_two, g_down, g_up = outs[:8]
    bias_grads = outs[8:12]
    while len(parts) > 1:
        parts = [parts[k] + parts[k + 1] for k in range(0, len(parts), 2)]
    sums = parts[0]

    def turn(block):
        return jnp.concatenate([block, jnp.zeros((LANES - rows, LANES), f32)], axis=0).T[:, :rows]

    pair, halves, down = (turn(sums[k * rows : (k + 1) * rows]) for k in range(3))
    g_one[...] = pair[:C]
    g_two[...] = pair[C:]
    g_up[:, :rows] = halves[:C]
    g_up[:, rows:] = halves[C:]
    g_down[...] = down[:C]
    at = 3 * rows
    ada_one[...] = sums[at : at + cells]
    ada_two[...] = sums[at + cells : at + 2 * cells]
    extra = swap_halves(sums[2 * rows : 3 * rows])
    act_grad[...] = extra[ACT_ROW : ACT_ROW + NACT, :cells]
    noise_grad[...] = extra[NOISE_ROW : NOISE_ROW + NLEV, :cells]
    for k, ref in enumerate(bias_grads):
        ref[...] = extra[BIAS_ROW + k : BIAS_ROW + k + 1, : ref.shape[0]].reshape(ref.shape)


def write_forward_operands(block, f_one, f_two, f_down, f_up):
    low_lanes = lane_ids((C, LANES)) < C
    zero = jnp.zeros((C, LANES), f32)

    def taps(name, base, step):
        return {(p, q): block(name, (3 * p + q) * step + base) for p in range(3) for q in range(3)}

    def write(ref, base, found):
        for w in range(4):
            for p in range(3):
                tile = jnp.where(low_lanes, found.get((p, w), zero), found.get((p, w - 1), zero)).astype(bf16)
                for a in range(2):
                    at = base + ((a + p) * 4 + w) * C
                    ref[at : at + C, a * LANES : (a + 1) * LANES] = tile
            for a in range(2):
                for r in range(4):
                    if not 0 <= r - a < 3:
                        at = base + (r * 4 + w) * C
                        ref[at : at + C, a * LANES : (a + 1) * LANES] = zero.astype(bf16)

    write(f_one, 0, taps("one", 0, C))
    yield
    write(f_two, 0, taps("two", 0, C))
    yield
    found = taps("down", 0, C)
    for p in range(3):
        for w in range(4):
            at = (p * 4 + w) * C
            f_down[at : at + C, :] = found.get((p, w), zero).astype(bf16)
    yield
    write(f_up, 0, taps("up", C, 2 * C))
    yield
    write(f_up, 16 * C, taps("up", 0, 2 * C))
    yield


def write_backward_operands(turned_pairs, b_one, b_two, b_down, b_up):
    low_lanes = lane_ids((C, LANES)) < C
    zero = jnp.zeros((C, LANES), f32)
    def taps(pairs, base, step, scale=1.0):
        found = {}
        for p in range(3):
            for q in range(3):
                at = (3 * p + q) * step + base
                pair = pairs[at // LANES]
                other = swap_halves(pair)
                low, high = (pair, other) if at % LANES == 0 else (other, pair)
                found[p, q] = jnp.where(low_lanes, low, high) * scale
        return found

    def write(ref, lane, found):
        for w in range(4):
            for p in range(3):
                tile = jnp.where(low_lanes, found.get((p, 2 - w), zero), found.get((p, 3 - w), zero)).astype(bf16)
                for a in range(2):
                    at = ((a + 2 - p) * 4 + w) * C
                    ref[at : at + C, lane + a * LANES : lane + (a + 1) * LANES] = tile
            for a in range(2):
                for r in range(4):
                    if not 0 <= a + 2 - r < 3:
                        at = (r * 4 + w) * C
                        ref[at : at + C, lane + a * LANES : lane + (a + 1) * LANES] = zero.astype(bf16)

    one, two = turned_pairs("one"), turned_pairs("two")
    write(b_one, 0, taps(one, 0, C, 0.5))
    yield
    write(b_two, 0, taps(two, 0, C, 0.5))
    yield
    pairs = turned_pairs("up")
    write(b_up, 0, taps(pairs, 0, 2 * C, 0.5))
    yield
    write(b_up, 2 * LANES, taps(pairs, C, 2 * C))
    yield
    found = taps(turned_pairs("down"), 0, C)
    for under in range(2):
        for right in range(2):
            at = (under * 2 + right) * C
            for a in range(2):
                p = {(0, 0): 1, (0, 1): 2, (1, 1): 0}.get((under, a))
                first, second = zero, zero
                if p is not None:
                    first = found[p, 1] if right == 0 else zero
                    second = found[p, 2] if right == 0 else found[p, 0]
                b_down[at : at + C, a * LANES : (a + 1) * LANES] = jnp.where(low_lanes, first, second).astype(bf16)


ACT_ROW, NOISE_ROW, TABLE_ROWS = 0, 24, 56
BIAS_ROW, ID_ROW = 56, 64


def pack_sizes(rows, cells):
    return 3 * rows, 3 * rows + 2 * cells, -(-(3 * rows + 2 * cells) // 16) * 16


def turned(values):
    wide = jnp.concatenate([values, jnp.zeros((C, LANES - values.shape[1]), f32)], axis=1)
    return jnp.concatenate([wide, jnp.zeros((C, LANES), f32)], axis=0).T[: values.shape[1]]


def copy_all(pairs, sent):
    copies = [pltpu.make_async_copy(source, target, sent.at[k]) for k, (source, target) in enumerate(pairs)]
    for copy in copies:
        copy.start()
    for copy in copies:
        copy.wait()


def far_part(member, array, out):
    half = out.shape[0]
    return array.at[pl.ds((1 - member // 2) * half, half)], out


def strip_parts(member, array, own, other):
    share = own.shape[0]
    return [
        (array.at[pl.ds(member * share, share)], own),
        (array.at[pl.ds((member ^ 1) * share, share)], other),
    ]


def far_kernel(member_ref, array, out, sent):
    copy_all([far_part(member_ref[0], array, out)], sent)


def cut_kernel(member_ref, frames, cotangent, own, other, far, cot_own, cot_other, sent):
    member = member_ref[0]
    pairs = strip_parts(member, frames, own, other) + strip_parts(member, cotangent, cot_own, cot_other)
    copy_all([far_part(member, cotangent, far)] + pairs, sent)


def share_kernel(member_ref, far, out):
    share = out.shape[0]
    out[...] = far[pl.ds((member_ref[0] ^ 1) % 2 * share, share)]


def mark_kernel(far, out):
    out[...] = far[0, :8, :LANES].astype(f32)


def near_kernel(other, shared, mark, out):
    share = out.shape[0] // 2
    out[:share] = other[...]
    out[share:] = shared[...]


def pack_kernel(*refs):
    actions, noise_ids, valid, conv_one, conv_two, down_kernel, up_kernel, ada_one, ada_two = refs[:9]
    act_table, noise_table = refs[9:11]
    biases = refs[11:15]
    out, work = refs[15:]
    rows, cells = conv_one.shape[1], ada_one.shape[0]
    style_at, end, _ = pack_sizes(rows, cells)
    wide = lambda ref: ref[...].astype(f32)
    low_lanes = lane_ids((rows, LANES)) < C
    up = wide(up_kernel)
    work[...] = jnp.zeros_like(work)
    for at, low, high in (
        (0, turned(wide(conv_one)), turned(wide(conv_two))),
        (rows, turned(up[:, :rows]), turned(up[:, rows:])),
    ):
        work[at : at + rows, :] = jnp.where(low_lanes, low, swap_halves(high))
    work[2 * rows : 3 * rows, :] = turned(wide(down_kernel))
    extra = 2 * rows
    for at, ref in ((ACT_ROW, act_table), (NOISE_ROW, noise_table)):
        size = ref.shape
        work[extra + at : extra + at + size[0], C : C + size[1]] = wide(ref)
    for k, ref in enumerate(biases):
        at = extra + BIAS_ROW + k
        work[at : at + 1, C : C + ref.shape[0]] = wide(ref).reshape(1, ref.shape[0])
    lanes = lane_ids((1, LANES))
    for k, ref in enumerate((actions, noise_ids, valid)):
        line = jnp.zeros((1, LANES), jnp.int32)
        for f in range(ref.shape[0]):
            line = jnp.where(lanes == C + f, ref[f], line)
        at = extra + ID_ROW + k
        work[at : at + 1, C:] = line.astype(f32)[:, C:]
    work[style_at : style_at + cells, :] = wide(ada_one)
    work[style_at + cells : end, :] = wide(ada_two)
    out[...] = work[...].astype(bf16)


def seq_owner(place, member, half, at, mine=True):
    side = member % 2 if mine else 1 - member % 2
    even, odd = sides(2 * half)
    return place ^ (even[at] + side * (odd[at] - even[at]))


def sides(count):
    ones = lambda offset: bin(offset).count("1") % 2
    return tuple([offset for offset in reversed(range(count)) if ones(offset) == side] for side in (0, 1))


def write_hots(hots, at, first, frames, ids):
    lanes = lane_ids((1, LANES)).astype(f32)
    for f in range(frames):
        mine = jnp.where(lane_ids(ids.shape) == C + first + f, ids, 0.0)
        mine = jnp.sum(mine, axis=1, keepdims=True)
        action, noise, valid = mine[0:1], mine[1:2], mine[2:3]
        hots[at + f : at + f + 1, :] = jnp.where(lanes == action + ACT_ROW, valid, 0.0) + jnp.where(
            lanes == noise + NOISE_ROW, 1.0, 0.0
        )


def prepare_kernel(count, rows, cells, *refs):
    where_ref, packed, mine, other = refs[:4]
    styles, biases, ids, work_pair, work_up, work_down, work_one, work_two, work_table, hots = refs[4:]
    place, member, frames = where_ref[0], where_ref[1], styles.shape[0]
    style_at, _, size = pack_sizes(rows, cells)
    bias_rows = jnp.zeros(SMALL, f32)
    half = count // 2
    for offset in range(count):
        ref = mine if offset < half else other
        at = offset % half
        pack = ref[at * size : (at + 1) * size, :].astype(f32)
        if at == half - 1:
            pack = jnp.where(member % 2 == offset // half, packed[...].astype(f32), pack)
        owner = seq_owner(place, member, half, at, offset < half)
        start = pl.multiple_of(owner * rows, 8)
        work_pair[pl.ds(start, rows), :] = pack[:rows]
        halves = pack[rows : 2 * rows]
        work_up[pl.ds(2 * start, rows), :] = halves
        work_up[pl.ds(pl.multiple_of(2 * start + rows, 8), rows), :] = swap_halves(halves)
        extra = pack[2 * rows : 3 * rows]
        work_down[pl.ds(start, rows), :] = extra
        work_one[offset * cells : (offset + 1) * cells, :] = pack[style_at : style_at + cells]
        work_two[offset * cells : (offset + 1) * cells, :] = pack[style_at + cells : style_at + 2 * cells]
        lane = (offset * cells) % LANES
        tables = pltpu.roll(extra[:TABLE_ROWS], (lane - C) % LANES, axis=1)
        kept = (lane_ids(tables.shape) >= lane) & (lane_ids(tables.shape) < lane + cells)
        column = offset * cells // LANES
        tables = jnp.where(kept, tables, 0.0)
        if lane == 0:
            work_table[column] = tables
        else:
            work_table[column] += tables
        slots = extra[BIAS_ROW : BIAS_ROW + 8]
        width = C // count
        slots = jnp.where((lane_ids(SMALL) >= C) & (lane_ids(SMALL) < C + width), slots, 0.0)
        bias_rows = bias_rows + pltpu.roll(slots, (owner * width + C) % LANES, axis=1)
        if offset < half:
            ids[at] = extra[ID_ROW : ID_ROW + 8]
    biases[...] = bias_rows + swap_halves(bias_rows)

    at = 2 * rows + ID_ROW
    hots[...] = jnp.zeros_like(hots)
    write_hots(hots, 0, member * frames, frames, packed[at : at + 8, :].astype(f32))
    hot = hots[:, :TABLE_ROWS].astype(bf16)
    embed = jnp.concatenate([matmul(hot, work_table[k].astype(bf16)) for k in range(work_table.shape[0])], axis=1)
    low_lanes = lane_ids(SMALL) < C
    for k, work in enumerate((work_one, work_two)):
        style = jnp.dot(embed, work[...], precision=precise, preferred_element_type=f32)
        other = swap_halves(style)
        scale = 1.0 + jnp.where(low_lanes, style, other)
        shift = jnp.where(low_lanes, other, style)
        for f in range(frames):
            styles[f, 2 * k : 2 * k + 1, :] = scale[f : f + 1]
            styles[f, 2 * k + 1 : 2 * k + 2, :] = shift[f : f + 1]
    for f in range(frames):
        styles[f, 4:8, :] = jnp.zeros((4, LANES), f32)


def shape(dims, kind):
    return jax.ShapeDtypeStruct(dims, kind)


def whole(dims):
    return pl.BlockSpec(dims, lambda f: (0,) * len(dims))


def per_frame(dims):
    return pl.BlockSpec((1,) + dims, lambda f: (f,) + (0,) * len(dims))


def strip_specs(count, strip):
    return [pl.BlockSpec((1, strip, W * C), lambda f: (f, 0, 0))] * count


SMALL = (8, LANES)
WINDOWS = (4, PAIRS + 1, HALF, LANES)
COARSE_WINDOWS = (3, PAIRS + 1, HALF, LANES)
TILES = (2, PAIRS, HALF, LANES)
COARSE = (PAIRS, HALF, LANES)
IMAGE = (PAIRS, H, LANES)
KEYS = 16 * C


def in_vmem():
    return pl.BlockSpec(memory_space=pltpu.VMEM)


def in_smem():
    return pl.BlockSpec(memory_space=pltpu.SMEM)


def params(limit=VMEM_LIMIT):
    return pltpu.CompilerParams(vmem_limit_bytes=limit)


def cost(macs, moved):
    return pl.CostEstimate(flops=2 * macs, bytes_accessed=moved, transcendentals=0)


def gather_frames(member, far, own, other, hint=0):
    near = trade(cut_near(member, other, far, hint), 1)
    frames = own.shape[0]
    return pl.pallas_call(
        gather_kernel,
        in_specs=[in_smem()] + [in_vmem()] * 3,
        out_specs=[in_vmem()] * 2,
        out_shape=[shape((frames,) + IMAGE, f32), shape((frames,) + SMALL, f32)],
        compiler_params=params(),
        name="frames",
    )(member, own, far, near)


def forward(member, frame_images, frame_stats, styles, biases, works, count):
    frames = frame_images.shape[0]
    strip = H // count
    return pl.pallas_call(
        lambda *refs: forward_kernel(count, *refs),
        in_specs=[in_smem()] + [in_vmem()] * 7,
        out_specs=[in_vmem()] * (count + 11),
        out_shape=[shape((frames, strip, W * C), bf16)] * count
        + [
            shape((frames,) + WINDOWS, bf16),
            shape((frames,) + WINDOWS, bf16),
            shape((frames,) + WINDOWS, bf16),
            shape((frames,) + COARSE_WINDOWS, bf16),
            shape((frames,) + TILES, f32),
            shape((frames,) + COARSE, f32),
            shape((frames,) + SMALL, f32),
        ]
        + [shape(dims, bf16) for dims in OPERANDS[4:]],
        scratch_shapes=[pltpu.VMEM((frames,) + IMAGE, f32), pltpu.VMEM((frames,) + TILES, f32)]
        + [pltpu.VMEM(dims, bf16) for dims in OPERANDS[:4]],
        compiler_params=params(),
        cost_estimate=cost(1 << 10, 1 << 10),
        name="forward",
    )(member, frame_images, frame_stats, styles, biases, *works)


def backward(member, cot, frame_images, styles, stats, middle, down, w_up, w_down, w_two, w_one, count):
    frames = frame_images.shape[0]
    strip = H // count
    return pl.pallas_call(
        lambda *refs: backward_kernel(count, *refs),
        in_specs=[in_smem()] + [in_vmem()] * 11,
        out_specs=[in_vmem()] * (count + 6),
        out_shape=[shape((frames, strip, W * C), bf16)] * count
        + [
            shape((frames,) + TILES, bf16),
            shape((frames,) + TILES, bf16),
            shape((frames,) + TILES, bf16),
            shape((frames,) + COARSE, bf16),
            shape((frames,) + SMALL, f32),
            shape((frames,) + SMALL, f32),
        ],
        scratch_shapes=[
            pltpu.VMEM((frames,) + IMAGE, f32),
            pltpu.VMEM((frames,) + TILES, f32),
            pltpu.VMEM((frames,) + TILES, f32),
            pltpu.VMEM((frames,) + WINDOWS, bf16),
            pltpu.VMEM((frames,) + COARSE, bf16),
        ],
        compiler_params=params(),
        cost_estimate=cost(frames * BLOCK * KEYS * 2 * LANES * 5, frames * (10 << 20)),
        name="backward",
    )(member, *cot, frame_images, styles, stats, middle, down, w_up, w_down, w_two, w_one)


def sum_scratch():
    return [
        pltpu.VMEM((KEYS, 2 * LANES), f32),
        pltpu.VMEM((KEYS, 2 * LANES), f32),
        pltpu.VMEM((6 * LANES, LANES), f32),
        pltpu.VMEM((KEYS + 6 * LANES, 2 * LANES), f32),
    ]


def weight_grads(wins, tiles):
    return pl.pallas_call(
        weight_kernel,
        in_specs=[in_vmem()] * 8,
        out_specs=[in_vmem()] * 4,
        out_shape=[shape((9 * C, C), f32)] * 3 + [shape((18 * C, C), f32)],
        scratch_shapes=sum_scratch(),
        compiler_params=params(),
        name="weights",
    )(*wins, *tiles)


def in_place(space=pl.ANY):
    return pl.BlockSpec(memory_space=space)


def cut_far(member, array):
    array = pltpu.with_memory_space_constraint(array, pltpu.HBM)
    return pl.pallas_call(
        far_kernel,
        in_specs=[in_smem(), in_place(pltpu.HBM)],
        out_specs=in_vmem(),
        out_shape=pltpu.VMEM((array.shape[0] // 2,) + array.shape[1:], array.dtype),
        scratch_shapes=[pltpu.SemaphoreType.DMA((1,))],
        compiler_params=params(),
        name="far",
    )(member, array)


def cut_others(member, frames, cotangent, count):
    half, share = ((frames.shape[0] // n,) + frames.shape[1:] for n in (2, count))
    frames, cotangent = (pltpu.with_memory_space_constraint(array, pltpu.HBM) for array in (frames, cotangent))
    return pl.pallas_call(
        cut_kernel,
        in_specs=[in_smem()] + [in_place(pltpu.HBM)] * 2,
        out_specs=[in_vmem()] * 5,
        out_shape=[pltpu.VMEM(dims, frames.dtype) for dims in (share, share, half, share, share)],
        scratch_shapes=[pltpu.SemaphoreType.DMA((5,))],
        compiler_params=params(),
        name="cut",
    )(member, frames, cotangent)


def cut_near(member, other, far, hint):
    shared = pl.pallas_call(
        share_kernel,
        in_specs=[in_smem(), in_vmem()],
        out_specs=in_vmem(),
        out_shape=shape(other.shape, other.dtype),
        compiler_params=params(),
        name="shared",
    )(member, far)
    mark = pl.pallas_call(
        mark_kernel,
        in_specs=[in_vmem()],
        out_specs=in_vmem(),
        out_shape=shape(SMALL, f32),
        compiler_params=params(),
        cost_estimate=cost(BLOCK * KEYS * 2 * LANES * hint, 1 << 20),
        name="mark",
    )(far)
    return pl.pallas_call(
        near_kernel,
        in_specs=[in_vmem()] * 3,
        out_specs=in_vmem(),
        out_shape=shape(far.shape, other.dtype),
        compiler_params=params(),
        name="near",
    )(other, shared, mark)


def pack(ids, kernels, ada_one, ada_two, act_table, noise_table, biases):
    _, _, size = pack_sizes(kernels[0].shape[0], ada_one.shape[0])
    args = (*[kernel.T for kernel in kernels], ada_one, ada_two, act_table, noise_table, *biases)
    return pl.pallas_call(
        pack_kernel,
        in_specs=[in_smem()] * 3 + [in_vmem()] * len(args),
        out_specs=in_vmem(),
        out_shape=shape((size, LANES), bf16),
        scratch_shapes=[pltpu.VMEM((size, LANES), f32)],
        compiler_params=params(VMEM_MOST),
        cost_estimate=cost(BLOCK * KEYS * 2 * LANES * 30, 1 << 20),
        name="pack",
    )(*ids, *args)


OPERANDS = (
    (KEYS, 2 * LANES),
    (KEYS, 2 * LANES),
    (6 * LANES, LANES),
    (2 * KEYS, 2 * LANES),
    (KEYS, 2 * LANES),
    (KEYS, 2 * LANES),
    (2 * LANES, 2 * LANES),
    (KEYS, 4 * LANES),
)


def prepare(where, packed, mine, other, count, rows, cells, frames):
    found = pl.pallas_call(
        lambda *refs: prepare_kernel(count, rows, cells, *refs),
        in_specs=[in_smem()] + [in_vmem()] * 3,
        out_specs=[in_vmem()] * 6,
        out_shape=[shape((frames,) + SMALL, f32), shape(SMALL, f32), shape((count // 2,) + SMALL, f32)]
        + [shape((n * C, LANES), f32) for n in (9, 18, 9)],
        scratch_shapes=[
            pltpu.VMEM((count * cells, LANES), f32),
            pltpu.VMEM((count * cells, LANES), f32),
            pltpu.VMEM((count * cells // LANES, TABLE_ROWS, LANES), f32),
            pltpu.VMEM(SMALL, f32),
        ],
        compiler_params=params(),
        name="prepare",
    )(where, packed, mine, other)
    return found[0], found[1], found[2], found[3:]


def weight_messages(where, wins, tiles, pieces, bias_sums, ids, count, rows):
    frames = pieces.shape[0]
    size = count // 2 * 3 * rows
    return pl.pallas_call(
        lambda *refs: message_kernel(count, rows, *refs),
        in_specs=[in_smem()] + [in_vmem()] * 11,
        out_specs=[in_vmem()] * 4,
        out_shape=[
            shape((size, LANES), f32),
            shape((PARTS, LANES), f32),
            shape((size, LANES), bf16),
            shape((count * frames, LANES), f32),
        ],
        scratch_shapes=sum_scratch()
        + [pltpu.VMEM((9 * C, LANES), f32), pltpu.VMEM((18 * C, LANES), f32), pltpu.VMEM((9 * C, LANES), f32)],
        compiler_params=params(),
        cost_estimate=cost(frames * BLOCK * KEYS * 2 * LANES * 5, frames * (6 << 20)),
        name="weights",
    )(where, *wins, *tiles, pieces, bias_sums, ids)


def join_messages(where, kept, small, theirs, half, rows, frames):
    return pl.pallas_call(
        lambda *refs: join_kernel(half, rows, frames, *refs),
        in_specs=[in_smem()] + [in_vmem()] * 3,
        out_specs=[in_vmem()] * (1 + half),
        out_shape=[shape((3 * rows, LANES), f32)] + [shape((3 * rows, LANES), bf16)] * half,
        compiler_params=params(),
        name="join",
    )(where, kept, small, theirs)


def reduce_messages(where, own, messages, hots, act_table, noise_table, ada_one, ada_two, rows, cells, frames):
    half = len(messages)
    return pl.pallas_call(
        lambda *refs: reduce_kernel(half, rows, cells, frames, *refs),
        in_specs=[in_smem()] + [in_vmem()] * (half + 6),
        out_specs=in_vmem(),
        out_shape=shape((3 * rows + 2 * cells, LANES), bf16),
        scratch_shapes=[
            pltpu.VMEM((half * frames, LANES), f32),
            pltpu.VMEM((half * frames, LANES), f32),
            pltpu.VMEM((TABLE_ROWS, cells), f32),
            pltpu.VMEM((LANES, LANES), f32),
            pltpu.VMEM((LANES, LANES), f32),
        ],
        compiler_params=params(),
        name="reduce",
    )(where, own, *messages, hots, act_table, noise_table, ada_one, ada_two)


def finish(parts, rows, cells, width):
    act_grad, noise_grad, one, two, *rest = pl.pallas_call(
        lambda *refs: finish_kernel(rows, cells, len(parts), *refs),
        in_specs=[in_vmem()] * len(parts),
        out_specs=[in_vmem()] * 12,
        out_shape=[
            shape((NACT, cells), f32),
            shape((NLEV, cells), f32),
            shape((cells, LANES), f32),
            shape((cells, LANES), f32),
            shape((C, rows), f32),
            shape((C, rows), f32),
            shape((C, rows), f32),
            shape((C, 2 * rows), f32),
        ]
        + [shape((width,), f32)] * 4,
        compiler_params=params(),
        name="finish",
    )(*parts)
    return (act_grad, noise_grad, one, two, *[grad.T for grad in rest[:4]], *rest[4:])


def collect_kernel(member_ref, *refs):
    strips, out = refs[:-1], refs[-1]
    for offset, strip in enumerate(strips):
        out[member_ref[0] ^ offset, 0] = strip[0].astype(out.dtype)


def trade_strips(strips):
    return tuple(trade(strip, offset) for offset, strip in enumerate(strips))


def collect_strips(member_box, strips, kind):
    count = len(strips)
    frames, rows, columns = strips[0].shape
    whole_strips = pl.pallas_call(
        collect_kernel,
        grid=(frames,),
        in_specs=[in_smem()] + [pl.BlockSpec((1, rows, columns), lambda f: (f, 0, 0))] * count,
        out_specs=pl.BlockSpec((count, 1, rows, columns), lambda f: (0, f, 0, 0)),
        out_shape=shape((count, frames, rows, columns), kind),
        compiler_params=params(),
        name="collect",
    )(member_box, *strips)
    return whole_strips.reshape(count * frames, rows, columns)


def twice(values):
    return jnp.concatenate([values, values], axis=-1)


def pad_small(rows):
    stacked = jnp.stack(rows, axis=-2)
    gaps = [(0, 0)] * (stacked.ndim - 2) + [(0, 8 - len(rows)), (0, 0)]
    return jnp.pad(stacked, gaps)


def trade(value, offset):
    if offset == 0:
        return value
    count = lax.axis_size("rows")
    return lax.ppermute(value, "rows", [(i, i ^ offset) for i in range(count)])


def half_trade(value, at):
    count, members = lax.axis_size("seq"), lax.axis_size("rows")
    pairs = []
    for place in range(count):
        for member in range(members):
            offset = sides(count)[member % 2][at]
            if offset:
                pairs.append((place * members + member, (place ^ offset) * members + member))
    return lax.ppermute(value, ("seq", "rows"), pairs)


def layers(member_box, frame_images, frame_stats, cot_fetched, styles, bias_rows, works):
    count = lax.axis_size("rows")
    *out, win_one, win_two, win_level, win_coarse, middle, down, stats, b_one, b_two, b_down, b_up = forward(
        member_box, frame_images, frame_stats, styles, bias_rows, works, count
    )
    out = trade_strips(out)
    down, cot_fetched = lax.optimization_barrier((down, cot_fetched))
    cot = gather_frames(member_box, *cot_fetched)
    *grad_strips, tile_out, tile_level, tile_mid, coarse_pairs, pieces, bias_sums = backward(
        member_box, cot, frame_images, styles, stats, middle, down, b_up, b_down, b_two, b_one, count
    )
    grad_strips = trade_strips(grad_strips)
    wins = (win_one, win_two, win_level, win_coarse)
    tiles = (tile_out, tile_level, tile_mid, coarse_pairs)
    return out, grad_strips, wins, tiles, pieces, bias_sums


def local_direct(
    frames,
    cotangent,
    actions,
    noise_ids,
    valid,
    act_table,
    noise_table,
    ada_one,
    ada_two,
    conv_one,
    conv_two,
    down_kernel,
    up_kernel,
    bias_one,
    bias_two,
    bias_down,
    bias_up,
):
    member = lax.axis_index("rows").astype(jnp.int32)
    place = lax.axis_index("seq").astype(jnp.int32)
    count = lax.axis_size("seq")
    share = frames.shape[0] // lax.axis_size("rows")
    rows, cells, width = conv_one.shape[0], ada_one.shape[0], bias_one.shape[0]
    half = count // 2
    member_box = member.reshape(1)
    where = jnp.stack([place, member])
    ids = (actions, noise_ids, valid)
    kernels = (conv_one, conv_two, down_kernel, up_kernel)
    biases = (bias_one, bias_two, bias_down, bias_up)
    far = trade(cut_far(member_box, frames), 2)
    packed = pack(ids, kernels, ada_one, ada_two, act_table, noise_table, biases)
    mine = jnp.concatenate([half_trade(packed, at) for at in range(half)], axis=0)
    other = trade(mine, 1)
    own, near, cot_far, *cot_rest = cut_others(member_box, frames, cotangent, lax.axis_size("rows"))
    cot_fetched = (trade(cot_far, 2), *cot_rest)
    frame_images, frame_stats = gather_frames(member_box, far, own, near, FAR_HINT)
    styles, bias_rows, group_ids, works = prepare(where, packed, mine, other, count, rows, cells, share)
    out, grad_strips, wins, tiles, pieces, bias_sums = layers(
        member_box, frame_images, frame_stats, cot_fetched, styles, bias_rows, works
    )
    kept, small, theirs, hots = weight_messages(where, wins, tiles, pieces, bias_sums, group_ids, count, rows)
    theirs, out = lax.optimization_barrier((theirs, out))
    own, *messages = join_messages(where, kept, small, trade(theirs, 1), half, rows, share)
    received = [half_trade(message, at) for at, message in enumerate(messages)]
    result = collect_strips(member_box, out, bf16)
    frames_grad = collect_strips(member_box, grad_strips, f32)
    received, result, frames_grad = lax.optimization_barrier((received, result, frames_grad))
    sums = reduce_messages(
        where, own, received, hots, act_table, noise_table, ada_one, ada_two, rows, cells, 2 * share
    )
    pair = (sums.astype(f32) + trade(sums, 1).astype(f32)).astype(bf16)
    parts = [pair, trade(pair, 2)]
    return (result, frames_grad, *finish(parts, rows, cells, width))


def local_general(
    frames,
    cotangent,
    actions,
    noise_ids,
    valid,
    act_table,
    noise_table,
    ada_one,
    ada_two,
    conv_one,
    conv_two,
    down_kernel,
    up_kernel,
    bias_one,
    bias_two,
    bias_down,
    bias_up,
):
    member = lax.axis_index("rows").astype(jnp.int32)
    share = frames.shape[0] // lax.axis_size("rows")
    member_box = member.reshape(1)

    def gathered(value, axis):
        return lax.all_gather(value, "seq", axis=axis, tiled=True)

    far = trade(cut_far(member_box, frames), 2)
    own, near, cot_far, *cot_rest = cut_others(member_box, frames, cotangent, lax.axis_size("rows"))
    cot_fetched = (trade(cot_far, 2), *cot_rest)
    frame_images, frame_stats = gather_frames(member_box, far, own, near)
    act_full = gathered(act_table, 1)
    noise_full = gathered(noise_table, 1)
    ada_full = gathered(jnp.concatenate([ada_one, ada_two], axis=1), 0).astype(f32)
    biases = gathered(jnp.stack([bias_one, bias_two, bias_down, bias_up]), 1).astype(f32)
    wide = lambda kernel: gathered(kernel, 0).astype(f32)
    works = (
        jnp.concatenate([wide(conv_one), wide(conv_two)], axis=1),
        twice(wide(up_kernel)),
        twice(wide(down_kernel)),
    )

    own = lambda ids: lax.dynamic_slice_in_dim(ids, member * share, share)
    own_actions, own_noise, own_valid = own(actions), own(noise_ids), own(valid)
    action_hot = (own_actions[:, None] == jnp.arange(NACT, dtype=jnp.int32)[None, :]).astype(f32) * own_valid[
        :, None
    ].astype(f32)
    noise_hot = (own_noise[:, None] == jnp.arange(NLEV, dtype=jnp.int32)[None, :]).astype(f32)
    embed = jnp.dot(action_hot, act_full.astype(f32), precision=precise) + jnp.dot(
        noise_hot, noise_full.astype(f32), precision=precise
    )
    style = jnp.dot(embed, ada_full, precision=precise)
    styles = pad_small(
        [
            twice(1.0 + style[:, :C]),
            twice(style[:, C : 2 * C]),
            twice(1.0 + style[:, 2 * C : 3 * C]),
            twice(style[:, 3 * C :]),
        ]
    )
    bias_rows = pad_small([twice(biases[k]) for k in range(4)])
    out, grad_strips, wins, tiles, pieces, bias_sums = layers(
        member_box, frame_images, frame_stats, cot_fetched, styles, bias_rows, works
    )
    g_one, g_two, g_down, g_up = weight_grads(wins, tiles)
    result = collect_strips(member_box, out, bf16)
    frames_grad = collect_strips(member_box, grad_strips, f32)

    pieces_one = jnp.concatenate([pieces[:, 0, :C], pieces[:, 1, :C]], axis=1)
    pieces_two = jnp.concatenate([pieces[:, 2, :C], pieces[:, 3, :C]], axis=1)
    ada_one_grad = jnp.dot(embed.T, pieces_one, precision=precise)
    ada_two_grad = jnp.dot(embed.T, pieces_two, precision=precise)
    embed_grad = jnp.dot(jnp.concatenate([pieces_one, pieces_two], axis=1), ada_full.T, precision=precise)
    act_table_grad = jnp.dot(action_hot.T, embed_grad, precision=precise)
    noise_table_grad = jnp.dot(noise_hot.T, embed_grad, precision=precise)
    bias_total = jnp.sum(bias_sums, axis=0)[:4, :C]

    def shard(value, axis):
        return lax.psum_scatter(value, "seq", scatter_dimension=axis, tiled=True)

    shards = (
        shard(act_table_grad, 1),
        shard(noise_table_grad, 1),
        shard(ada_one_grad, 0),
        shard(ada_two_grad, 0),
        shard(g_one, 0),
        shard(g_two, 0),
        shard(g_down, 0),
        shard(g_up, 0),
        shard(bias_total[0], 0),
        shard(bias_total[1], 0),
        shard(bias_total[2], 0),
        shard(bias_total[3], 0),
    )
    return (result, frames_grad) + lax.psum(shards, "rows")


def fits_direct(mesh):
    count = mesh.shape["seq"]
    rows, cells = 9 * C // count, 256 // count
    return count in (2, 4, 8) and rows % 8 == 0 and rows >= ID_ROW + 8 and cells % 8 == 0 and mesh.shape["rows"] == 4


def solution(mesh):
    in_specs = (
        P("seq", "rows", None),
        P("seq", "rows", None),
        P("seq"),
        P("seq"),
        P("seq"),
        P(None, "seq"),
        P(None, "seq"),
        P("seq", None),
        P("seq", None),
        P("seq", None),
        P("seq", None),
        P("seq", None),
        P("seq", None),
        P("seq"),
        P("seq"),
        P("seq"),
        P("seq"),
    )
    out_specs = (
        P("seq", "rows", None),
        P("seq", "rows", None),
        P(None, "seq"),
        P(None, "seq"),
        P("seq", None),
        P("seq", None),
        P("seq", None),
        P("seq", None),
        P("seq", None),
        P("seq", None),
        P("seq"),
        P("seq"),
        P("seq"),
        P("seq"),
    )
    local = local_direct if fits_direct(mesh) else local_general
    return jax.shard_map(local, mesh=mesh, in_specs=in_specs, out_specs=out_specs, check_vma=False)
```
